128 devices in a mesh: dp: 32 (over z, x, core), ctx: 4 (over y).
Axes of the slice: x: 4, y: 4, z: 4, core: 2. Of those that a mesh axis runs over, the one named last changes fastest.
Arguments:
- tokens: bfloat16 [32768, 1024], P(('dp', 'ctx')), may hold values from -6 to 6
- cotangent: bfloat16 [32768, 1024], P(('dp', 'ctx')), may hold values from -6 to 6
- span_order: int32 [8], replicated, may hold values from 0 to 7, each once
- w_qkv: float32 [1024, 4096], P(('dp', 'ctx')), may hold values from -0.1875 to 0.1875
- w_out: float32 [2048, 1024], P(('dp', 'ctx')), may hold values from -1 to 1
- w_gateup: float32 [1024, 6144], P(('dp', 'ctx')), may hold values from -0.1875 to 0.1875
- w_down: float32 [3072, 1024], P(('dp', 'ctx')), may hold values from -0.15625 to 0.15625
- gains: float32 [2304], P(('dp', 'ctx')), may hold values from 0.28 to 3
- first_qkv: float32 [1024, 4096], P(('dp', 'ctx')), may hold values from -0.0004272461 to 0.0004272461
- first_out: float32 [2048, 1024], P(('dp', 'ctx')), may hold values from -0.00010681152 to 0.00010681152
- first_gateup: float32 [1024, 6144], P(('dp', 'ctx')), may hold values from -0.0004272461 to 0.0004272461
- first_down: float32 [3072, 1024], P(('dp', 'ctx')), may hold values from -0.00018310547 to 0.00018310547
- first_gains: float32 [2304], P(('dp', 'ctx')), may hold values from -0.0012207031 to 0.0012207031
- second_qkv: float32 [1024, 4096], P(('dp', 'ctx')), may hold values from 6.3568976e-11 to 2.542759e-10
- second_out: float32 [2048, 1024], P(('dp', 'ctx')), may hold values from 2.542759e-12 to 1.0171036e-11
- second_gateup: float32 [1024, 6144], P(('dp', 'ctx')), may hold values from 6.3568976e-11 to 2.542759e-10
- second_down: float32 [3072, 1024], P(('dp', 'ctx')), may hold values from 1.5892244e-11 to 6.3568976e-11
- second_gains: float32 [2304], P(('dp', 'ctx')), may hold values from 5.721208e-10 to 2.2884832e-09
Outputs:
- layer_output: bfloat16 [32768, 1024], P(('dp', 'ctx'))
- input_grad: float32 [32768, 1024], P(('dp', 'ctx'))
- new_w_qkv: float32 [1024, 4096], P(('dp', 'ctx'))
- new_w_out: float32 [2048, 1024], P(('dp', 'ctx'))
- new_w_gateup: float32 [1024, 6144], P(('dp', 'ctx'))
- new_w_down: float32 [3072, 1024], P(('dp', 'ctx'))
- new_gains: float32 [2304], P(('dp', 'ctx'))
- new_first_qkv: float32 [1024, 4096], P(('dp', 'ctx'))
- new_first_out: float32 [2048, 1024], P(('dp', 'ctx'))
- new_first_gateup: float32 [1024, 6144], P(('dp', 'ctx'))
- new_first_down: float32 [3072, 1024], P(('dp', 'ctx'))
- new_first_gains: float32 [2304], P(('dp', 'ctx'))
- new_second_qkv: float32 [1024, 4096], P(('dp', 'ctx'))
- new_second_out: float32 [2048, 1024], P(('dp', 'ctx'))
- new_second_gateup: float32 [1024, 6144], P(('dp', 'ctx'))
- new_second_down: float32 [3072, 1024], P(('dp', 'ctx'))
- new_second_gains: float32 [2304], P(('dp', 'ctx'))
- grad_norm: float32 [], replicated
The draws below stay inside these ranges and needn't reach their ends.
Inputs may be any that keep to these rules, and one draw needn't show every extreme that they name: `span_order`: each stored block number holds a different block of the sequence.
All inputs are finite; a program needn't handle non-finite values.
Results may differ from the reference program's by a relative error of at most 0.038.
Values may be sent and summed in bfloat16 or wider, within the bound.
A program may use at most 192 MiB of HBM per device.

```python
import math
import jax
import jax.numpy as jnp
from jax import lax

D = 1024
HEADS = 16
KV_HEADS = 8
HEAD_WIDTH = 128
FF = 3072
TOK_DEV = 256
STEP = 10
LENGTH = 1024
TOKENS = 32768
GAIN_COUNT = 2304
PARAMS = 15730944
N_DP = 32
N_CTX = 4


def draw_gains(key, part):
    key = jax.random.fold_in(key, 11)
    first_key, second_key = jax.random.split(key, 2)
    steps = jnp.arange(D, dtype=jnp.float32) / (D - 1)
    ramp = 0.6 + 1.2 * steps
    rough = jax.random.uniform(first_key, (2, D), jnp.float32, 0.7, 1.4)
    heads = jax.random.uniform(second_key, (2 * HEAD_WIDTH,), jnp.float32, 1.0, 2.0)
    return jnp.concatenate([(ramp[None, :] * rough).reshape(-1), heads])


def block_scale(own_key, dims, pieces, low, high):
    factor_of, own = 1.0, jax.random.fold_in(own_key, 6)
    for axis_at, parts in pieces:
        heights = jnp.exp(jax.random.uniform(jax.random.fold_in(own, axis_at), (parts,), jnp.float32, low / len(pieces), high / len(pieces)))
        factor_of = factor_of * jnp.repeat(heights, dims[axis_at] // parts).reshape([-1 if axis == axis_at else 1 for axis in range(len(dims))])
    return factor_of


def gaussian(stream_key, extent, spread, most, pieces=(), kind=jnp.bfloat16):
    loudness = block_scale(stream_key, extent, pieces, -0.22, 0.18) if pieces else 1.0
    values = jax.random.normal(stream_key, extent, jnp.float32) * spread * loudness
    return jnp.minimum(jnp.maximum(values, -most), most).astype(kind)


def setup_inputs(seed: int = 0) -> dict:
    arg_keys = jax.random.split(jax.random.key(seed), 19)
    return {
        "tokens": gaussian(arg_keys[0], (TOKENS, D), 1.0, 6.0, ((0, 128),)),
        "cotangent": gaussian(arg_keys[1], (TOKENS, D), 1.0, 6.0, ((0, 128),)),
        "span_order": jax.random.permutation(arg_keys[2], 2 * N_CTX).astype(jnp.int32),
        "w_qkv": gaussian(arg_keys[3], (D, HEADS * HEAD_WIDTH + 2 * KV_HEADS * HEAD_WIDTH), D ** -0.5, 0.1875, ((0, 128),), jnp.float32),
        "w_out": gaussian(arg_keys[4], (HEADS * HEAD_WIDTH, D), (max(1, HEADS * HEAD_WIDTH * 16 // (TOK_DEV * N_CTX))) ** -0.5, 1.0, ((0, 128),), jnp.float32),
        "w_gateup": gaussian(arg_keys[5], (D, 2 * FF), D ** -0.5, 0.1875, ((0, 128),), jnp.float32),
        "w_down": gaussian(arg_keys[6], (FF, D), (FF // 2) ** -0.5, 0.15625, ((0, 128),), jnp.float32),
        "gains": draw_gains(jax.random.fold_in(arg_keys[18], 71), 0),
        "first_qkv": gaussian(arg_keys[8], (D, HEADS * HEAD_WIDTH + 2 * KV_HEADS * HEAD_WIDTH), (0.111 * PARAMS ** -0.5), 0.0004272461, ((0, 128),), jnp.float32),
        "first_out": gaussian(arg_keys[9], (HEADS * HEAD_WIDTH, D), (0.03 * PARAMS ** -0.5), 0.00010681152, ((0, 128),), jnp.float32),
        "first_gateup": gaussian(arg_keys[10], (D, 2 * FF), (0.111 * PARAMS ** -0.5), 0.0004272461, ((0, 128),), jnp.float32),
        "first_down": gaussian(arg_keys[11], (FF, D), (0.05 * PARAMS ** -0.5), 0.00018310547, ((0, 128),), jnp.float32),
        "first_gains": gaussian(arg_keys[12], (GAIN_COUNT,), (0.333 * PARAMS ** -0.5), 0.0012207031, ((0, 128),), jnp.float32),
        "second_qkv": jnp.clip(jnp.exp(math.log(2.5427590588655846e-10) - 1.3862944 * jax.random.uniform(arg_keys[13], (D, HEADS * HEAD_WIDTH + 2 * KV_HEADS * HEAD_WIDTH), jnp.float32) ** block_scale(arg_keys[13], (D, HEADS * HEAD_WIDTH + 2 * KV_HEADS * HEAD_WIDTH), ((0, 128),), -0.2, 0.2)), 6.356897647163962e-11, 2.5427590588655846e-10),
        "second_out": jnp.clip(jnp.exp(math.log(1.0171035888517643e-11) - 1.3862944 * jax.random.uniform(arg_keys[14], (HEADS * HEAD_WIDTH, D), jnp.float32) ** block_scale(arg_keys[14], (HEADS * HEAD_WIDTH, D), ((0, 128),), -0.2, 0.2)), 2.542758972129411e-12, 1.0171035888517643e-11),
        "second_gateup": jnp.clip(jnp.exp(math.log(2.5427590588655846e-10) - 1.3862944 * jax.random.uniform(arg_keys[15], (D, 2 * FF), jnp.float32) ** block_scale(arg_keys[15], (D, 2 * FF), ((0, 128),), -0.2, 0.2)), 6.356897647163962e-11, 2.5427590588655846e-10),
        "second_down": jnp.clip(jnp.exp(math.log(6.356897647163962e-11) - 1.3862944 * jax.random.uniform(arg_keys[16], (FF, D), jnp.float32) ** block_scale(arg_keys[16], (FF, D), ((0, 128),), -0.2, 0.2)), 1.5892244117909904e-11, 6.356897647163962e-11),
        "second_gains": jnp.clip(jnp.exp(math.log(2.2884831807346018e-09) - 1.3862944 * jax.random.uniform(arg_keys[17], (GAIN_COUNT,), jnp.float32) ** block_scale(arg_keys[17], (GAIN_COUNT,), ((0, 128),), -0.2, 0.2)), 5.721207951836504e-10, 2.2884831807346018e-09),
    }


@jax.custom_vjp
def low(v):
    return lax.optimization_barrier(v.astype(jnp.bfloat16)).astype(jnp.float32)

@jax.custom_vjp
def low_back(v):
    return v

def low_keep(v):
    return (low(v), None)

def low_pass(kept, grad):
    return (grad,)

def back_keep(v):
    return (v, None)

def back_low(kept, grad):
    return (low(grad),)
low.defvjp(low_keep, low_pass)
low_back.defvjp(back_keep, back_low)
norm_eps = 1e-06
rope_base = 1000000.0
beta_one = 0.9
beta_two = 0.999
adam_eps = 1e-08
clip_at = 1.0
matrix_rate = 0.05
out_rate = 0.25
matrix_decay = 0.1
gain_rate = 0.5
masked_score = -1e+30
highest_value = lax.Precision.HIGHEST

def normalize(value_rows):
    return value_rows * lax.rsqrt(lax.optimization_barrier(jnp.mean(value_rows * value_rows, axis=-1, keepdims=True)) + norm_eps)

def rotate(value_rows, cosine, sine):
    middle = value_rows.shape[-1] // 2
    turned = jnp.concatenate([-value_rows[..., middle:], value_rows[..., :middle]], axis=-1)
    return value_rows * cosine + turned * sine

def tables(positions):
    middle = HEAD_WIDTH // 2
    frequency = rope_base ** (-(jnp.arange(middle, dtype=jnp.float32) * 2.0) / HEAD_WIDTH)
    angle = positions.astype(jnp.float32)[:, None] * frequency[None, :]
    angle = jnp.concatenate([angle, angle], axis=1)
    return (jnp.cos(angle), jnp.sin(angle))

def attend(query, key_rows, value_rows, visible):
    group_size = HEADS // KV_HEADS
    seq_rows = query.shape[0]
    grouped_heads = query.reshape(seq_rows, KV_HEADS, group_size, HEAD_WIDTH)
    score_matrix = low_back(jnp.einsum('hkco,wko->kchw', grouped_heads, key_rows, precision=highest_value) * HEAD_WIDTH ** (-0.5))
    score_matrix = jnp.where(visible, score_matrix, masked_score)
    highest_score = lax.optimization_barrier(jnp.max(score_matrix, axis=-1, keepdims=True))
    log_total = highest_score + jnp.log(lax.optimization_barrier(jnp.sum(jnp.exp(score_matrix - highest_score), axis=-1, keepdims=True)))
    probabilities = low(jnp.exp(score_matrix - log_total))
    mixed_output = jnp.einsum('xwbq,qxm->bxwm', probabilities, value_rows, precision=highest_value)
    return mixed_output.reshape(seq_rows, HEADS * HEAD_WIDTH)

def block_layer(inputs, w_qkv, w_out, w_gateup, w_down, gains, cosine, sine, visible):
    w_qkv = low(w_qkv)
    w_out = low(w_out)
    w_gateup = low(w_gateup)
    w_down = low(w_down)
    gains = low(gains)
    g_attn = gains[:D]
    g_mlp = gains[D:2 * D]
    g_query = gains[2 * D:2 * D + HEAD_WIDTH]
    g_key = gains[2 * D + HEAD_WIDTH:]
    rows = inputs.shape[0]
    width_q = HEADS * HEAD_WIDTH
    width_kv = KV_HEADS * HEAD_WIDTH
    hidden = low(normalize(inputs) * g_attn)
    projected = low_back(jnp.dot(hidden, w_qkv, precision=highest_value))
    query = projected[:, :width_q].reshape(rows, HEADS, HEAD_WIDTH)
    key_rows = projected[:, width_q:width_q + width_kv].reshape(rows, KV_HEADS, HEAD_WIDTH)
    value_rows = low(projected[:, width_q + width_kv:]).reshape(rows, KV_HEADS, HEAD_WIDTH)
    query = low(rotate(normalize(query) * g_query, cosine[:, None, :], sine[:, None, :]))
    key_rows = low(rotate(normalize(key_rows) * g_key, cosine[:, None, :], sine[:, None, :]))
    seq_count = rows // LENGTH
    checked = jax.checkpoint(attend)
    attended_rows = lax.map(lambda trio: checked(trio[0], trio[1], trio[2], visible), (query.reshape(seq_count, LENGTH, HEADS, HEAD_WIDTH), key_rows.reshape(seq_count, LENGTH, KV_HEADS, HEAD_WIDTH), value_rows.reshape(seq_count, LENGTH, KV_HEADS, HEAD_WIDTH)))
    attended_rows = low(low_back(attended_rows.reshape(rows, width_q)))
    middle = inputs + low_back(jnp.dot(attended_rows, w_out, precision=highest_value))
    hidden2 = low(normalize(middle) * g_mlp)
    gate_up = low_back(jnp.dot(hidden2, w_gateup, precision=highest_value))
    product = low(jax.nn.silu(gate_up[:, :FF]) * gate_up[:, FF:])
    return middle + low_back(jnp.dot(product, w_down, precision=highest_value))

def adam_update(weight, first, second, grad, factor, rate, decay):
    clipped = grad * factor
    new_first = beta_one * first + (1.0 - beta_one) * clipped
    new_second = beta_two * second + (1.0 - beta_two) * clipped * clipped
    direction = new_first / (1.0 - beta_one ** STEP) / (jnp.sqrt(new_second / (1.0 - beta_two ** STEP)) + adam_eps)
    return (weight - rate * (direction + decay * weight), new_first, new_second)

def reference(tokens, cotangent, span_order, w_qkv, w_out, w_gateup, w_down, gains, first_qkv, first_out, first_gateup, first_down, first_gains, second_qkv, second_out, second_gateup, second_down, second_gains):
    half_block = TOK_DEV // 2
    seq_index = jnp.arange(LENGTH, dtype=jnp.int32)
    positions = span_order[seq_index // half_block] * half_block + seq_index % half_block
    visible = positions[None, :] <= positions[:, None]
    cosine, sine = tables(positions)
    per_block = math.gcd(N_DP, max(1, 4096 // LENGTH))
    block_rows = per_block * LENGTH
    blocks = TOKENS // block_rows
    cosine_rows = jnp.tile(cosine, (per_block, 1))
    sine_rows = jnp.tile(sine, (per_block, 1))
    masters = (w_qkv, w_out, w_gateup, w_down, gains)
    inputs_all = tokens.astype(jnp.float32).reshape(blocks, block_rows, D)
    incoming_all = cotangent.astype(jnp.float32).reshape(blocks, block_rows, D)

    def scan_step(grad_sums, block_pair):
        inputs, incoming = block_pair
        result, pullback = jax.vjp(lambda a, b, c, d, e, f: block_layer(a, b, c, d, e, f, cosine_rows, sine_rows, visible), inputs, *masters)
        grads = pullback(incoming)
        new_sums = tuple((total + part for total, part in zip(grad_sums, grads[1:])))
        return (new_sums, (result, grads[0]))
    init = tuple((jnp.zeros_like(weight) for weight in masters))
    grad_sums, (outputs, input_grads) = lax.scan(scan_step, init, (inputs_all, incoming_all))
    total = jnp.float32(0.0)
    for grad in grad_sums:
        total = total + jnp.sum(grad * grad)
    grad_norm = jnp.sqrt(total)
    factor = jnp.minimum(1.0, clip_at / (grad_norm + 1e-06))
    firsts = (first_qkv, first_out, first_gateup, first_down, first_gains)
    seconds = (second_qkv, second_out, second_gateup, second_down, second_gains)
    rates = (matrix_rate, out_rate, matrix_rate, matrix_rate, gain_rate)
    decays = (matrix_decay, matrix_decay, matrix_decay, matrix_decay, 0.0)
    news = []
    new_firsts = []
    new_seconds = []
    for which in range(5):
        weight, first, second = adam_update(masters[which], firsts[which], seconds[which], grad_sums[which], factor, rates[which], decays[which])
        news.append(weight)
        new_firsts.append(first)
        new_seconds.append(second)
    return (outputs.reshape(TOKENS, D).astype(jnp.bfloat16), input_grads.reshape(TOKENS, D), news[0], news[1], news[2], news[3], news[4], new_firsts[0], new_firsts[1], new_firsts[2], new_firsts[3], new_firsts[4], new_seconds[0], new_seconds[1], new_seconds[2], new_seconds[3], new_seconds[4], grad_norm)
```

```python
import jax
import jax.numpy as jnp
from jax import lax
from jax.experimental import pallas as pl
from jax.experimental.pallas import tpu as pltpu
from jax.sharding import PartitionSpec as P

D = 1024
HEADS = 16
KV_HEADS = 8
HEAD_WIDTH = 128
FF = 3072
STEP = 10

norm_eps = 1e-06
rope_base = 1000000.0
beta_one = 0.9
beta_two = 0.999
adam_eps = 1e-08
clip_at = 1.0
matrix_rate = 0.05
out_rate = 0.25
matrix_decay = 0.1
gain_rate = 0.5
masked_score = -1e30

MESH = pl.DeviceIdType.MESH
BF = jnp.bfloat16
F32 = jnp.float32
ROWS = 256
UNIT = 288
PART_A = 144
VMEM_LIMIT = 58 * 2**20
vmem = pl.BlockSpec(memory_space=pltpu.VMEM)
hbm = pl.BlockSpec(memory_space=pl.ANY)


class Place:
    def __init__(self):
        dp = lax.axis_index("dp")
        self.at = {
            "z": lax.div(dp, 8),
            "x": lax.rem(lax.div(dp, 2), 4),
            "k": lax.rem(dp, 2),
            "y": lax.axis_index("ctx"),
        }

    def __getitem__(self, axis):
        return self.at[axis]

    def device(self, **other):
        c = {**self.at, **other}
        return (c["z"] * 8 + c["x"] * 2 + c["k"], c["y"])

    def moved(self, axis, steps):
        return lax.rem(self.at[axis] + steps, 4)

    def peer(self, axis, steps):
        return self.device(**{axis: self.moved(axis, steps)})

    def sibling(self):
        return self.device(k=1 - self.at["k"])


def greet(devices):
    barrier = pltpu.get_barrier_semaphore()
    for device in devices:
        pl.semaphore_signal(barrier, inc=1, device_id=device, device_id_type=MESH)


def await_greetings(count):
    pl.semaphore_wait(pltpu.get_barrier_semaphore(), count)


def neighbours(place, axes):
    found = []
    for axis in axes:
        if axis == "k":
            found.append(place.sibling())
        else:
            found += [place.peer(axis, 1), place.peer(axis, 3)]
    return found


def remote(src, dst, send, recv, device):
    return pltpu.make_async_remote_copy(
        src_ref=src, dst_ref=dst, send_sem=send, recv_sem=recv, device_id=device, device_id_type=MESH
    )


class Gather:
    def __init__(self, place, axis, part, sems, own=None):
        self.part, self.send, self.recv = part, sems[0], sems[1]
        self.own = own or (lambda half: part(place[axis], half))
        self.next, self.prev = place.peer(axis, 1), place.peer(axis, 3)
        self.me, self.up, self.down, self.far = (place.moved(axis, n) for n in (0, 1, 3, 2))

    def copy(self, n, slot, half, device, src=None):
        view = self.part(slot, half)
        return remote(src if src is not None else view, view, self.send.at[n], self.recv.at[n], device)

    def outgoing(self, n):
        slot, half, device = [
            (self.me, 0, self.next),
            (self.me, 1, self.prev),
            (self.me, 1, self.next),
            (self.me, 0, self.prev),
            (self.down, 0, self.next),
            (self.up, 1, self.prev),
        ][n]
        return self.copy(n, slot, half, device, self.own(half) if n < 4 else None)

    def start(self):
        for n in range(4):
            self.outgoing(n).start()

    def forward(self):
        self.copy(0, self.down, 0, self.prev).wait_recv()
        self.outgoing(4).start()
        self.copy(1, self.up, 1, self.next).wait_recv()
        self.outgoing(5).start()

    def finish(self):
        self.copy(2, self.down, 1, self.prev).wait_recv()
        self.copy(3, self.up, 0, self.next).wait_recv()
        self.copy(4, self.far, 0, self.prev).wait_recv()
        self.copy(5, self.far, 1, self.next).wait_recv()
        for n in range(6):
            self.outgoing(n).wait_send()


class Scatter:
    def __init__(self, place, axis, part, boxes, sems, add):
        self.part, self.boxes, self.add = part, boxes, add
        self.send, self.recv = sems[0], sems[1]
        self.next, self.prev = place.peer(axis, 1), place.peer(axis, 3)
        self.me, self.up, self.down, self.far = (place.moved(axis, n) for n in (0, 1, 3, 2))

    def copy(self, n, src, device):
        return remote(src, self.boxes[n], self.send.at[n], self.recv.at[n], device)

    def outgoing(self, n):
        source, device = [
            (lambda: self.part(self.far, 0), self.prev),
            (lambda: self.part(self.far, 1), self.next),
            (lambda: self.part(self.down, 1), self.prev),
            (lambda: self.part(self.up, 0), self.next),
            (lambda: self.boxes[6], self.prev),
            (lambda: self.boxes[7], self.next),
        ][n]
        return self.copy(n, source(), device)

    def start(self):
        for n in range(4):
            self.outgoing(n).start()

    def forward(self):
        self.outgoing(0).wait_recv()
        self.add(self.boxes[6], [self.boxes[0], self.part(self.down, 0)])
        self.outgoing(4).start()
        self.outgoing(1).wait_recv()
        self.add(self.boxes[7], [self.boxes[1], self.part(self.up, 1)])
        self.outgoing(5).start()

    def finish(self, result):
        for n in (2, 3, 4, 5):
            self.outgoing(n).wait_recv()
        self.add(result(0), [self.part(self.me, 0), self.boxes[3], self.boxes[4]])
        self.add(result(1), [self.part(self.me, 1), self.boxes[2], self.boxes[5]])
        for n in range(6):
            self.outgoing(n).wait_send()


def add_rows(out, terms):
    shape = out.shape
    rows = shape[-2]

    def block(at):
        total = terms[0][at].astype(F32)
        for term in terms[1:]:
            total = total + term[at].astype(F32)
        out[at] = total.astype(out.dtype)

    if len(shape) == 2:

        @pl.loop(0, rows // 16)
        def _(r):
            block((pl.ds(pl.multiple_of(r * 16, 16), 16), slice(None)))

    else:

        @pl.loop(0, shape[0])
        def _(lead):
            @pl.loop(0, rows // 16)
            def _(r):
                block((lead, pl.ds(pl.multiple_of(r * 16, 16), 16), slice(None)))


def dma(*shape):
    return pltpu.SemaphoreType.DMA(shape)


def ring_sems():
    return [dma(6), dma(6)]


def params(which):
    return pltpu.CompilerParams(
        collective_id=which, has_side_effects=True, vmem_limit_bytes=VMEM_LIMIT
    )


def upper_rows(half, low, split, high):
    return pl.ds(low, split - low) if half == 0 else pl.ds(split, high - split)


def stage_one_a(place, w_all):
    return lambda i, half: w_all.at[place["z"], i, upper_rows(half, 0, 80, PART_A)]


def stage_one_b(place, w_all):
    return lambda i, half: w_all.at[i, place["x"], upper_rows(half, PART_A, 208, UNIT)]


def stage_two_a(place, w_all):
    return lambda i, half: w_all.at[i, pl.ds(2 * half, 2), pl.ds(0, PART_A)]


def stage_two_b(place, w_all):
    return lambda i, half: w_all.at[pl.ds(2 * half, 2), i, pl.ds(PART_A, UNIT - PART_A)]


def gather_kernel(
    tok, wq, wo, wgu, wd, gains,
    tok_all, wq_all, wo_all, w_all,
    q_send, q_recv, q_unit, o_send, g_recv, g_y, d_y, unit,
    local, qp_s, qp_r, op_s, op_r, gp, t_s, t_r, qx_s, qx_r, qz_s, qz_r, ox_s, ox_r,
    core, gy_s, gy_r, dy_s, dy_r, a_s, a_r, b_s, b_r,
):
    place = Place()
    z, x, k, y = (place[a] for a in "zxky")
    near = neighbours(place, "xyzk")
    greet(near + [place.peer("y", 2)])
    diagonal = z == y
    for other in range(4):

        @pl.when(jnp.logical_not(jnp.logical_and(diagonal, y == other)))
        def _():
            greet([place.device(z=y, y=jnp.int32(other))])

    for i in range(4):
        q_send[i, :, 0:512] = wq[:, 512 * i : 512 * i + 512]
        q_send[i, :, 512:768] = wq[:, 2048 + 256 * i : 2304 + 256 * i]
        q_send[i, :, 768:1024] = wq[:, 3072 + 256 * i : 3328 + 256 * i]
        q_send[i, :, 1024:1152] = gains[...]
    o_send[...] = wo[...].astype(BF)
    await_greetings(len(near) + 1 + jnp.where(diagonal, 3, 4))

    q_prep = [
        remote(q_send.at[place.moved("y", n)], q_recv.at[y], qp_s.at[n], qp_r.at[y], place.peer("y", n))
        for n in (1, 3, 2)
    ]
    for copy in q_prep:
        copy.start()
    g_prep = remote(wgu.at[1 - k], g_recv, gp.at[0], gp.at[1], place.sibling())
    g_prep.start()
    tok_own = pltpu.make_async_copy(tok, tok_all.at[y], local.at[0])
    tok_own.start()

    def o_slot(source):
        return wo_all.at[x, k, pl.ds(pl.multiple_of(16 * source, 16), 16)]

    for other in range(4):

        @pl.when(jnp.logical_not(jnp.logical_and(diagonal, z == other)))
        def _():
            remote(o_send, o_slot(y), op_s.at[other], op_r.at[y], place.device(z=jnp.int32(other), y=z)).start()

    @pl.when(diagonal)
    def _():
        pltpu.make_async_copy(o_send, o_slot(y), local.at[1]).start()

    tokens_ring = Gather(
        place, "y", lambda i, h: tok_all.at[i, pl.ds(128 * h, 128)], (t_s, t_r),
        own=lambda h: tok.at[pl.ds(128 * h, 128)],
    )
    tokens_ring.start()

    q_recv[y] = q_send[y]
    for n in (1, 3, 2):
        source = place.moved("y", n)
        remote(q_send.at[0], q_recv.at[source], qp_s.at[n], qp_r.at[source], place.peer("y", n)).wait_recv()
    q_unit[...] = q_recv[...].reshape(32, 1152).astype(BF)
    q_own = pltpu.make_async_copy(q_unit, wq_all.at[z, x, k], local.at[2])
    q_own.start()
    q_x = Gather(
        place, "x", lambda i, h: wq_all.at[z, i, k, pl.ds(16 * h, 16)], (qx_s, qx_r),
        own=lambda h: q_unit.at[pl.ds(16 * h, 16)],
    )
    q_x.start()

    g_prep.wait_recv()
    g_own = wgu[k]
    g_other = g_recv[...]
    lower = k == 0
    first = jnp.where(lower, g_own, g_other)
    second = jnp.where(lower, g_other, g_own)
    both = jnp.concatenate([first, second], axis=1)
    g_y[y] = both.reshape(48, 1024).astype(BF)
    d_y[y] = wd[...]
    g_ring = Gather(place, "y", lambda i, h: g_y.at[i, upper_rows(h, 0, 32, 48)], (gy_s, gy_r))
    d_ring = Gather(place, "y", lambda i, h: d_y.at[i, upper_rows(h, 0, 16, 24)], (dy_s, dy_r))
    g_ring.start()
    d_ring.start()

    for other in range(4):
        here = jnp.logical_and(diagonal, y == other)

        @pl.when(jnp.logical_not(here))
        def _():
            remote(o_send, o_slot(other), op_s.at[0], op_r.at[other], place.device(z=y, y=jnp.int32(other))).wait_recv()

    @pl.when(diagonal)
    def _():
        pltpu.make_async_copy(o_send, o_slot(y), local.at[1]).wait()

    o_x = Gather(place, "x", lambda i, h: wo_all.at[i, k, pl.ds(32 * h, 32)], (ox_s, ox_r))
    o_x.start()

    q_x.forward()
    g_ring.forward()
    d_ring.forward()
    q_x.finish()
    q_own.wait()
    q_z = Gather(place, "z", lambda i, h: wq_all.at[i, pl.ds(2 * h, 2), k], (qz_s, qz_r))
    q_z.start()
    o_x.forward()
    g_ring.finish()
    d_ring.finish()

    for b in range(3):
        pieces = [g_y[c, 16 * b : 16 * b + 16].astype(F32) for c in range(4)]
        for core_row in range(2):
            rows = jnp.concatenate([piece[8 * core_row : 8 * core_row + 8] for piece in pieces], axis=0)
            at = 64 * b + 32 * core_row
            unit[at : at + 32] = rows.astype(BF)
    unit[192:288] = d_y[...].reshape(96, 1024).astype(BF)
    u_own = pltpu.make_async_copy(unit, w_all.at[z, x], local.at[3])
    u_own.start()
    a_ring = Gather(
        place, "x", stage_one_a(place, w_all), (a_s, a_r),
        own=lambda h: unit.at[upper_rows(h, 0, 80, PART_A)],
    )
    b_ring = Gather(
        place, "z", stage_one_b(place, w_all), (b_s, b_r),
        own=lambda h: unit.at[upper_rows(h, PART_A, 208, UNIT)],
    )
    a_ring.start()
    b_ring.start()
    tokens_ring.forward()
    q_z.forward()
    o_x.finish()
    o_core = remote(wo_all.at[:, k], wo_all.at[:, k], core.at[0], core.at[1], place.sibling())
    o_core.start()
    a_ring.forward()
    b_ring.forward()
    q_z.finish()
    q_core = remote(wq_all.at[:, :, k], wq_all.at[:, :, k], core.at[2], core.at[3], place.sibling())
    q_core.start()
    a_ring.finish()
    b_ring.finish()
    tokens_ring.finish()
    tok_own.wait()
    u_own.wait()
    for copy in q_prep:
        copy.wait_send()
    g_prep.wait_send()
    for other in range(4):

        @pl.when(jnp.logical_not(jnp.logical_and(diagonal, z == other)))
        def _():
            remote(o_send, o_slot(y), op_s.at[other], op_r.at[y], place.device(z=jnp.int32(other), y=z)).wait_send()

    remote(wo_all.at[:, 1 - k], wo_all.at[:, 1 - k], core.at[0], core.at[1], place.sibling()).wait_recv()
    remote(wq_all.at[:, :, 1 - k], wq_all.at[:, :, 1 - k], core.at[2], core.at[3], place.sibling()).wait_recv()
    o_core.wait_send()
    q_core.wait_send()


def gather_all(tok, wq, wo, wgu, wd, gains):
    shape = jax.ShapeDtypeStruct
    return pl.pallas_call(
        gather_kernel,
        out_shape=(
            shape((4, ROWS, D), BF),
            shape((4, 4, 2, 32, 1152), BF),
            shape((4, 2, 64, D), BF),
            shape((4, 4, UNIT, D), BF),
        ),
        in_specs=[vmem] * 6,
        out_specs=(hbm,) * 4,
        scratch_shapes=[
            pltpu.VMEM((4, 8, 1152), F32),
            pltpu.VMEM((4, 8, 1152), F32),
            pltpu.VMEM((32, 1152), BF),
            pltpu.VMEM((16, D), BF),
            pltpu.VMEM((3, 8, D), F32),
            pltpu.VMEM((4, 48, D), BF),
            pltpu.VMEM((4, 24, D), F32),
            pltpu.VMEM((UNIT, D), BF),
            dma(4), dma(4), dma(4), dma(4), dma(4), dma(2),
            *ring_sems(), *ring_sems(), *ring_sems(), *ring_sems(),
            dma(4),
            *ring_sems(), *ring_sems(), *ring_sems(), *ring_sems(),
        ],
        compiler_params=params(1),
        name="gather_weights_tokens",
    )(tok, wq, wo, wgu, wd, gains)


def middle_kernel(
    terms, tok, cot, gain, w_in,
    middle, hidden_pair, cot_pair, w_all,
    boxes, total, local, y_s, y_r, core, a_s, a_r, b_s, b_r,
):
    place = Place()
    near = neighbours(place, "xyzk")
    greet(near)
    await_greetings(len(near))
    a_ring = Gather(place, "z", stage_two_a(place, w_all), (a_s, a_r))
    b_ring = Gather(place, "x", stage_two_b(place, w_all), (b_s, b_r))
    reduce = Scatter(
        place, "y", lambda i, h: terms.at[i, pl.ds(128 * h, 128)],
        [boxes.at[n] for n in range(8)], (y_s, y_r), add_rows,
    )
    reduce.start()
    a_ring.start()
    b_ring.start()
    cot_copy = remote(cot, cot_pair.at[1], core.at[0], core.at[1], place.sibling())
    cot_copy.start()
    cot_own = pltpu.make_async_copy(cot, cot_pair.at[0], local)
    cot_own.start()
    reduce.forward()
    a_ring.forward()
    b_ring.forward()
    reduce.finish(lambda h: total.at[pl.ds(128 * h, 128)])

    @pl.loop(0, ROWS // 16)
    def _(r):
        at = pl.ds(pl.multiple_of(r * 16, 16), 16)
        rows = tok[at].astype(F32) + total[at]
        middle[at] = rows
        scale = lax.rsqrt(jnp.mean(rows * rows, axis=-1, keepdims=True) + norm_eps)
        hidden_pair[0, at] = (rows * scale * gain[...]).astype(BF)

    hid_copy = remote(hidden_pair.at[0], hidden_pair.at[1], core.at[2], core.at[3], place.sibling())
    hid_copy.start()
    a_ring.finish()
    b_ring.finish()
    cot_own.wait()
    cot_copy.wait()
    hid_copy.wait()


def middle_step(terms, tok, cot, gain, w_all):
    shape = jax.ShapeDtypeStruct
    return pl.pallas_call(
        middle_kernel,
        out_shape=(
            shape((ROWS, D), F32),
            shape((2, ROWS, D), BF),
            shape((2, ROWS, D), BF),
            shape((4, 4, UNIT, D), BF),
        ),
        in_specs=[vmem] * 4 + [hbm],
        out_specs=(vmem, vmem, vmem, hbm),
        scratch_shapes=[
            pltpu.VMEM((8, 128, D), BF),
            pltpu.VMEM((ROWS, D), F32),
            pltpu.SemaphoreType.DMA,
            *ring_sems(), dma(4), *ring_sems(), *ring_sems(),
        ],
        input_output_aliases={4: 3},
        compiler_params=params(2),
        name="reduce_attention_gather_ff",
    )(terms, tok, cot, gain, w_all)


def back_kernel(
    out_own, out_sib, dh_own, dh_sib, mid, cot, gain, d_w,
    layer_out, d_middle, d_attn_all, gain_grad, a_one, b_one,
    out_box, dh_box, own, a_box, b_box,
    local, core, y_s, y_r, a_s, a_r, b_s, b_r,
):
    place = Place()
    y = place["y"]
    near = neighbours(place, "xyzk")
    greet(near)
    await_greetings(len(near))
    dh_copy = remote(dh_sib, dh_box, core.at[0], core.at[1], place.sibling())
    out_copy = remote(out_sib, out_box, core.at[2], core.at[3], place.sibling())
    dh_copy.start()
    out_copy.start()
    a_ring = Scatter(
        place, "z", lambda i, h: d_w.at[i, pl.ds(2 * h, 2), pl.ds(0, PART_A)],
        [a_box.at[n] for n in range(8)], (a_s, a_r), add_rows,
    )
    b_ring = Scatter(
        place, "x", lambda i, h: d_w.at[pl.ds(2 * h, 2), i, pl.ds(PART_A, UNIT - PART_A)],
        [b_box.at[n] for n in range(8)], (b_s, b_r), add_rows,
    )
    a_ring.start()
    b_ring.start()
    gain_grad[...] = jnp.zeros_like(gain_grad)
    dh_copy.wait_recv()

    @pl.loop(0, ROWS // 16)
    def _(r):
        at = pl.ds(pl.multiple_of(r * 16, 16), 16)
        rows = mid[at]
        scale = lax.rsqrt(jnp.mean(rows * rows, axis=-1, keepdims=True) + norm_eps)
        normed = rows * scale
        incoming = dh_own[at] + dh_box[at].astype(F32)
        product = incoming * normed
        gain_grad[...] += product[0:8] + product[8:16]
        incoming = incoming * gain[...]
        mean = jnp.mean(incoming * normed, axis=-1, keepdims=True)
        d_mid = cot[at].astype(F32) + scale * (incoming - normed * mean)
        d_middle[at] = d_mid
        own[at] = d_mid.astype(BF)

    ring = Gather(
        place, "y", lambda i, h: d_attn_all.at[i, pl.ds(128 * h, 128)], (y_s, y_r),
        own=lambda h: own.at[pl.ds(128 * h, 128)],
    )
    ring.start()
    own_copy = pltpu.make_async_copy(own, d_attn_all.at[y], local)
    own_copy.start()
    out_copy.wait_recv()

    @pl.loop(0, ROWS // 16)
    def _(r):
        at = pl.ds(pl.multiple_of(r * 16, 16), 16)
        layer_out[at] = (mid[at] + out_own[at] + out_box[at].astype(F32)).astype(BF)

    ring.forward()
    a_ring.forward()
    b_ring.forward()
    ring.finish()
    a_ring.finish(lambda h: a_one.at[pl.ds(2 * h, 2)])
    b_ring.finish(lambda h: b_one.at[pl.ds(2 * h, 2)])
    own_copy.wait()
    dh_copy.wait_send()
    out_copy.wait_send()


def back_step(out_own, out_sib, dh_own, dh_sib, mid, cot, gain, d_w):
    shape = jax.ShapeDtypeStruct
    return pl.pallas_call(
        back_kernel,
        out_shape=(
            shape((ROWS, D), BF),
            shape((ROWS, D), F32),
            shape((4, ROWS, D), BF),
            shape((8, D), F32),
            shape((4, PART_A, D), BF),
            shape((4, PART_A, D), BF),
        ),
        in_specs=[vmem] * 8,
        out_specs=(vmem,) * 6,
        scratch_shapes=[
            pltpu.VMEM((ROWS, D), BF),
            pltpu.VMEM((ROWS, D), BF),
            pltpu.VMEM((ROWS, D), BF),
            pltpu.VMEM((8, 2, PART_A, D), BF),
            pltpu.VMEM((8, 2, PART_A, D), BF),
            pltpu.SemaphoreType.DMA,
            dma(4), *ring_sems(), *ring_sems(), *ring_sems(),
        ],
        compiler_params=params(3),
        name="reduce_ff_gather_gradient",
    )(out_own, out_sib, dh_own, dh_sib, mid, cot, gain, d_w)


def owner_kernel(
    dh_terms, d_q, d_o, a_one, b_one,
    dh_out, q_out, o_out, g_out, d_out,
    y_box, dh_total, q_box, q_one, qz_box, q_two, qx_box, q_three,
    o_box, o_one, ox_box, o_two, o_slots, a_box, b_box, total, g_send, g_slots, d_slots, g_sum,
    core, y_s, y_r, qz_s, qz_r, qx_s, qx_r, ox_s, ox_r, a_s, a_r, b_s, b_r,
    qy_s, qy_r, oy_s, oy_r, gy_s, gy_r, dy_s, dy_r, local,
):
    place = Place()
    z, x, k, y = (place[a] for a in "zxky")
    diagonal = z == y
    near = neighbours(place, "xyzk")
    greet(near + [place.peer("y", 2)])
    for other in range(4):

        @pl.when(jnp.logical_not(jnp.logical_and(diagonal, z == other)))
        def _():
            greet([place.device(z=jnp.int32(other), y=z)])

    await_greetings(len(near) + 1 + jnp.where(diagonal, 3, 4))

    q_core = remote(d_q.at[:, :, 1 - k], q_box, core.at[0], core.at[1], place.sibling())
    o_core = remote(d_o.at[:, 1 - k], o_box, core.at[2], core.at[3], place.sibling())
    o_core.start()
    q_core.start()
    dh_ring = Scatter(
        place, "y", lambda i, h: dh_terms.at[i, pl.ds(128 * h, 128)],
        [y_box.at[n] for n in range(8)], (y_s, y_r), add_rows,
    )
    dh_ring.start()
    a_part = lambda i, h: a_one.at[i, upper_rows(h, 0, 80, PART_A)]
    b_part = lambda i, h: b_one.at[i, upper_rows(h, 0, 64, PART_A)]
    a_ring = Scatter(
        place, "x", a_part,
        [a_box.at[n, pl.ds(0, 80 if n in (0, 3, 4, 6) else 64)] for n in range(8)],
        (a_s, a_r), add_rows,
    )
    b_ring = Scatter(
        place, "z", b_part,
        [b_box.at[n, pl.ds(0, 64 if n in (0, 3, 4, 6) else 80)] for n in range(8)],
        (b_s, b_r), add_rows,
    )
    a_ring.start()
    b_ring.start()

    o_core.wait_recv()

    @pl.loop(0, 4)
    def _(i):
        @pl.loop(0, 4)
        def _(r):
            at = pl.ds(pl.multiple_of(r * 16, 16), 16)
            o_one[i, at] = (d_o[i, k, at].astype(F32) + o_box[i, at].astype(F32)).astype(BF)

    o_x = Scatter(
        place, "x", lambda i, h: o_one.at[i, pl.ds(32 * h, 32)],
        [ox_box.at[n] for n in range(8)], (ox_s, ox_r), add_rows,
    )
    o_x.start()
    q_core.wait_recv()

    @pl.loop(0, 4)
    def _(i):
        @pl.loop(0, 4)
        def _(j):
            @pl.loop(0, 2)
            def _(r):
                at = pl.ds(pl.multiple_of(r * 16, 16), 16)
                q_one[i, j, at] = (d_q[i, j, k, at].astype(F32) + q_box[i, j, at].astype(F32)).astype(BF)

    q_z = Scatter(
        place, "z", lambda i, h: q_one.at[i, pl.ds(2 * h, 2)],
        [qz_box.at[n] for n in range(8)], (qz_s, qz_r), add_rows,
    )
    q_z.start()
    a_ring.forward()
    b_ring.forward()
    o_x.forward()
    q_z.forward()
    dh_ring.forward()

    a_ring.finish(lambda h: total.at[upper_rows(h, 0, 80, PART_A)])
    b_ring.finish(lambda h: total.at[upper_rows(h, PART_A, 208, UNIT)])
    for c in range(4):
        for b in range(3):
            at = 64 * b + 8 * c
            rows = jnp.concatenate([total[at : at + 8], total[at + 32 : at + 40]], axis=0)
            g_send[c, 16 * b : 16 * b + 16] = rows.astype(BF)
    g_slots[y] = g_send[y]
    d_slots[y] = total[pl.ds(pl.multiple_of(192 + 24 * y, 8), 24)]
    y_copies = []
    for n in (1, 3, 2):
        to = place.moved("y", n)
        y_copies.append(remote(g_send.at[to], g_slots.at[y], gy_s.at[n], gy_r.at[y], place.peer("y", n)))
        rows = pl.ds(pl.multiple_of(192 + 24 * to, 8), 24)
        y_copies.append(remote(total.at[rows], d_slots.at[y], dy_s.at[n], dy_r.at[y], place.peer("y", n)))
    for copy in y_copies:
        copy.start()

    q_z.finish(lambda h: q_two.at[pl.ds(2 * h, 2)])
    q_x = Scatter(
        place, "x", lambda i, h: q_two.at[i, pl.ds(16 * h, 16)],
        [qx_box.at[n] for n in range(8)], (qx_s, qx_r), add_rows,
    )
    q_x.start()
    o_x.finish(lambda h: o_two.at[pl.ds(32 * h, 32)])
    for other in range(4):
        piece = o_two.at[pl.ds(16 * other, 16)]

        @pl.when(jnp.logical_not(jnp.logical_and(diagonal, y == other)))
        def _():
            remote(piece, o_slots.at[z], oy_s.at[other], oy_r.at[z], place.device(z=y, y=jnp.int32(other))).start()

        @pl.when(jnp.logical_and(diagonal, y == other))
        def _():
            pltpu.make_async_copy(piece, o_slots.at[z], local).start()

    q_x.forward()
    dh_ring.finish(lambda h: dh_out.at[pl.ds(128 * h, 128)])

    for n in (1, 3, 2):
        source = place.moved("y", n)
        remote(g_send.at[0], g_slots.at[source], gy_s.at[n], gy_r.at[source], place.peer("y", n)).wait_recv()
        remote(total.at[pl.ds(192, 24)], d_slots.at[source], dy_s.at[n], dy_r.at[source], place.peer("y", n)).wait_recv()
    d_out[...] = d_slots[0] + d_slots[1] + d_slots[2] + d_slots[3]
    summed = g_slots[0].astype(F32)
    for c in range(1, 4):
        summed = summed + g_slots[c].astype(F32)
    summed = summed.reshape(3, 2, 8, D)
    g_sum[0] = summed[:, 0]
    g_sum[1] = summed[:, 1]
    g_out[k] = g_sum[k]
    g_core = remote(g_sum.at[1 - k], g_out.at[k], core.at[4], core.at[5], place.sibling())
    g_core.start()

    q_x.finish(lambda h: q_three.at[pl.ds(16 * h, 16)])
    q_out[y] = q_three[pl.ds(pl.multiple_of(8 * y, 8), 8)]
    q_copies = []
    for n in (1, 3, 2):
        rows = pl.ds(pl.multiple_of(8 * place.moved("y", n), 8), 8)
        q_copies.append(remote(q_three.at[rows], q_out.at[y], qy_s.at[n], qy_r.at[y], place.peer("y", n)))
    for copy in q_copies:
        copy.start()

    for other in range(4):
        here = jnp.logical_and(diagonal, z == other)

        @pl.when(jnp.logical_not(here))
        def _():
            remote(o_two.at[pl.ds(0, 16)], o_slots.at[other], oy_s.at[0], oy_r.at[other], place.device(z=jnp.int32(other), y=z)).wait_recv()

        @pl.when(here)
        def _():
            pltpu.make_async_copy(o_two.at[pl.ds(0, 16)], o_slots.at[other], local).wait()

    o_sum = o_slots[0].astype(F32)
    for c in range(1, 4):
        o_sum = o_sum + o_slots[c].astype(F32)
    o_out[...] = o_sum
    for n in (1, 3, 2):
        source = place.moved("y", n)
        remote(q_three.at[pl.ds(0, 8)], q_out.at[source], qy_s.at[n], qy_r.at[source], place.peer("y", n)).wait_recv()
    remote(g_sum.at[0], g_out.at[1 - k], core.at[4], core.at[5], place.sibling()).wait_recv()
    for copy in [o_core, q_core, g_core] + y_copies + q_copies:
        copy.wait_send()
    for other in range(4):

        @pl.when(jnp.logical_not(jnp.logical_and(diagonal, y == other)))
        def _():
            remote(o_two.at[pl.ds(16 * other, 16)], o_slots.at[z], oy_s.at[other], oy_r.at[z], place.device(z=y, y=jnp.int32(other))).wait_send()


def owner_step(dh_terms, d_q, d_o, a_one, b_one):
    shape = jax.ShapeDtypeStruct
    return pl.pallas_call(
        owner_kernel,
        out_shape=(
            shape((ROWS, D), F32),
            shape((4, 8, D), F32),
            shape((16, D), F32),
            shape((2, 3, 8, D), F32),
            shape((24, D), F32),
        ),
        in_specs=[vmem] * 5,
        out_specs=(vmem,) * 5,
        scratch_shapes=[
            pltpu.VMEM((8, 128, D), BF),
            pltpu.VMEM((8, 128), F32),
            pltpu.VMEM((4, 4, 32, D), BF),
            pltpu.VMEM((4, 4, 32, D), BF),
            pltpu.VMEM((8, 2, 32, D), BF),
            pltpu.VMEM((4, 32, D), BF),
            pltpu.VMEM((8, 16, D), BF),
            pltpu.VMEM((32, D), F32),
            pltpu.VMEM((4, 64, D), BF),
            pltpu.VMEM((4, 64, D), BF),
            pltpu.VMEM((8, 32, D), BF),
            pltpu.VMEM((64, D), BF),
            pltpu.VMEM((4, 16, D), BF),
            pltpu.VMEM((8, 80, D), BF),
            pltpu.VMEM((8, 80, D), BF),
            pltpu.VMEM((UNIT, D), F32),
            pltpu.VMEM((4, 48, D), BF),
            pltpu.VMEM((4, 48, D), BF),
            pltpu.VMEM((4, 24, D), F32),
            pltpu.VMEM((2, 3, 8, D), F32),
            dma(6),
            *ring_sems(), *ring_sems(), *ring_sems(), *ring_sems(), *ring_sems(), *ring_sems(),
            dma(4), dma(4), dma(4), dma(4), dma(4), dma(4), dma(4), dma(4),
            pltpu.SemaphoreType.DMA,
        ],
        compiler_params=params(4),
        name="reduce_gradients",
    )(dh_terms, d_q, d_o, a_one, b_one)


def sum_kernel(value, result, first, second, held, s_one, r_one, s_two, r_two):
    place = Place()
    z, x, k, y = (place[a] for a in "zxky")
    ours = [(dy, dk) for dy in range(4) for dk in range(2) if (dy, dk) != (0, 0)]
    theirs = [(dz, dx) for dz in range(4) for dx in range(4) if (dz, dx) != (0, 0)]

    def near(dy, dk):
        return place.device(y=place.moved("y", dy), k=lax.rem(k + dk, 2))

    def far(dz, dx):
        return place.device(z=place.moved("z", dz), x=place.moved("x", dx))

    greet([near(*o) for o in ours] + [far(*o) for o in theirs])
    await_greetings(len(ours) + len(theirs))

    def stage(source, slots, send, recv, offsets, device, me, slot_of):
        slots[me] = source[...]
        copies = []
        for n, offset in enumerate(offsets):
            copies.append(remote(source, slots.at[me], send.at[n], recv.at[me], device(*offset)))
        for copy in copies:
            copy.start()
        for n, offset in enumerate(offsets):
            slot = slot_of(*offset)
            remote(source, slots.at[slot], send.at[n], recv.at[slot], device(*offset)).wait_recv()
        for copy in copies:
            copy.wait_send()

    stage(value, first, s_one, r_one, ours, near, y * 2 + k,
          lambda dy, dk: place.moved("y", dy) * 2 + lax.rem(k + dk, 2))
    held[...] = jnp.sum(first[...], axis=0)
    stage(held, second, s_two, r_two, theirs, far, z * 4 + x,
          lambda dz, dx: place.moved("z", dz) * 4 + place.moved("x", dx))
    result[...] = jnp.sum(second[...], axis=0)


def sum_all(value):
    return pl.pallas_call(
        sum_kernel,
        out_shape=jax.ShapeDtypeStruct((24, 128), F32),
        in_specs=[vmem],
        out_specs=vmem,
        scratch_shapes=[
            pltpu.VMEM((8, 24, 128), F32),
            pltpu.VMEM((16, 24, 128), F32),
            pltpu.VMEM((24, 128), F32),
            dma(7), dma(8), dma(15), dma(16),
        ],
        compiler_params=params(5),
        name="sum_squares",
    )(value)


def rms_parts(value_rows):
    factor = lax.rsqrt(jnp.mean(value_rows * value_rows, axis=-1, keepdims=True) + norm_eps)
    return (value_rows * factor, factor)


def rms_back(incoming, normed, factor):
    return factor * (incoming - normed * jnp.mean(incoming * normed, axis=-1, keepdims=True))


def rotate(value_rows, cosine, sine):
    middle = value_rows.shape[-1] // 2
    turned = jnp.concatenate([-value_rows[..., middle:], value_rows[..., :middle]], axis=-1)
    return value_rows * cosine + turned * sine


def rotate_back(incoming, cosine, sine):
    middle = incoming.shape[-1] // 2
    moved = incoming * sine
    return incoming * cosine + jnp.concatenate([moved[..., middle:], -moved[..., :middle]], axis=-1)


def tables(positions):
    middle = HEAD_WIDTH // 2
    frequency = rope_base ** (-(jnp.arange(middle, dtype=jnp.float32) * 2.0) / HEAD_WIDTH)
    angle = positions.astype(jnp.float32)[:, None] * frequency[None, :]
    angle = jnp.concatenate([angle, angle], axis=1)
    return (jnp.cos(angle)[:, None, :], jnp.sin(angle)[:, None, :])


def contract_rows(left, right):
    return lax.dot_general(
        left, right, (((0,), (0,)), ((), ())), preferred_element_type=jnp.float32
    )


def contract_cols(left, right):
    return lax.dot_general(
        left, right, (((1,), (1,)), ((), ())), preferred_element_type=jnp.float32
    )


def adam_update(weight, first, second, grad, factor, rate, decay):
    clipped = grad * factor
    new_first = beta_one * first + (1.0 - beta_one) * clipped
    new_second = beta_two * second + (1.0 - beta_two) * clipped * clipped
    direction = (
        new_first
        / (1.0 - beta_one**STEP)
        / (jnp.sqrt(new_second / (1.0 - beta_two**STEP)) + adam_eps)
    )
    return (weight - rate * (direction + decay * weight), new_first, new_second)


def pack_gateup(w):
    rows = w.shape[0]
    v = w.reshape(rows, 2, 16, 2, 96).transpose(3, 0, 1, 2, 4).reshape(2, rows, 2, 3, 512)
    return v.transpose(0, 3, 1, 2, 4).reshape(2, 3, rows, 1024)


def unpack_gateup(v):
    rows = v.shape[2]
    w = v.reshape(2, 3, rows, 2, 512).transpose(0, 2, 3, 1, 4).reshape(2, rows, 2, 16, 96)
    return w.transpose(1, 2, 3, 0, 4).reshape(rows, 2 * FF)


def body(
    tokens, cotangent, span_order,
    w_qkv, w_out, w_gateup, w_down, gains,
    first_qkv, first_out, first_gateup, first_down, first_gains,
    second_qkv, second_out, second_gateup, second_down, second_gains,
):
    seq_length = 4 * ROWS
    half_block = ROWS // 2
    heads, kv_heads, group_size = HEADS // 4, KV_HEADS // 4, HEADS // KV_HEADS
    width_q, width_kv = heads * HEAD_WIDTH, kv_heads * HEAD_WIDTH
    score_scale = HEAD_WIDTH ** (-0.5)
    own_gains = jnp.pad(gains[None, :], ((0, 7), (0, 128 - gains.shape[0])))
    tok_all, wq_all, wo_all, w_part = gather_all(
        tokens, w_qkv, w_out, pack_gateup(w_gateup), w_down, own_gains
    )
    wq_all = wq_all.reshape(D, 1152)
    full_qkv = wq_all[:, :D]
    full_out = wo_all.reshape(width_q, D)
    gain_values = wq_all.reshape(128, 8, 1152)[:, 0, D : D + 18].reshape(-1).astype(F32)
    g_attn = gain_values[:D]
    g_mlp = gain_values[D : 2 * D]
    g_query = gain_values[2 * D : 2 * D + HEAD_WIDTH]
    g_key = gain_values[2 * D + HEAD_WIDTH :]

    seq_index = jnp.arange(seq_length, dtype=jnp.int32)
    positions = span_order[seq_index // half_block] * half_block + seq_index % half_block
    cosine, sine = tables(positions)
    visible = positions[None, :] <= positions[:, None]
    normed1, _ = rms_parts(tok_all.reshape(seq_length, D).astype(F32))
    hidden = (normed1 * g_attn).astype(BF)
    projected = jnp.dot(hidden, full_qkv, preferred_element_type=F32)
    query_raw = projected[:, :width_q].reshape(seq_length, heads, HEAD_WIDTH)
    key_raw = projected[:, width_q : width_q + width_kv].reshape(seq_length, kv_heads, HEAD_WIDTH)
    q_normed, q_scale = rms_parts(query_raw)
    query = rotate(q_normed * g_query, cosine, sine).astype(BF)
    k_normed, k_scale = rms_parts(key_raw)
    keys = rotate(k_normed * g_key, cosine, sine).astype(BF)
    values = projected[:, width_q + width_kv :].astype(BF).reshape(seq_length, kv_heads, HEAD_WIDTH)
    grouped = query.reshape(seq_length, kv_heads, group_size, HEAD_WIDTH)

    def score_of():
        raw = jnp.einsum("hkco,wko->kchw", grouped, keys, preferred_element_type=F32) * score_scale
        return jnp.where(visible, raw, masked_score)

    scores = score_of()
    highest = jnp.max(scores, axis=-1, keepdims=True)
    log_total = highest + jnp.log(jnp.sum(jnp.exp(scores - highest), axis=-1, keepdims=True))
    probs = jnp.exp(scores - log_total).astype(BF)
    attended = jnp.einsum("xwbq,qxm->bxwm", probs, values, preferred_element_type=F32)
    attended = attended.reshape(seq_length, width_q).astype(BF)
    terms = jnp.dot(attended, full_out, preferred_element_type=F32).astype(BF)
    middle, hidden_pair, cot_pair, w_all = middle_step(
        terms.reshape(4, ROWS, D), tokens, cotangent, g_mlp[None, :], w_part
    )

    hidden2 = hidden_pair.reshape(2 * ROWS, D)
    cot = cot_pair.reshape(2 * ROWS, D)
    w_all = w_all.reshape(16, UNIT, D)
    w_down_half = w_all[:, 192:].reshape(1536, D)
    out_part = jnp.zeros((2 * ROWS, D), F32)
    dh_part = jnp.zeros((2 * ROWS, D), F32)
    d_w = []
    d_downs = []
    for b in range(3):
        w_gu = w_all[:, 64 * b : 64 * b + 64].reshape(D, D)
        w_dn = w_down_half[512 * b : 512 * b + 512]
        gate_up = jnp.dot(hidden2, w_gu, preferred_element_type=F32)
        gate, up = gate_up[:, :512], gate_up[:, 512:]
        sigmoid = jax.nn.sigmoid(gate)
        active = gate * sigmoid
        product = (active * up).astype(BF)
        out_part += jnp.dot(product, w_dn, preferred_element_type=F32)
        d_downs.append(contract_rows(product, cot).astype(BF))
        d_product = contract_cols(cot, w_dn)
        d_gate = d_product * up * sigmoid * (1.0 + gate * (1.0 - sigmoid))
        d_gate_up = jnp.concatenate([d_gate, d_product * active], axis=1).astype(BF)
        d_w.append(contract_rows(hidden2, d_gate_up).astype(BF).reshape(16, 64, D))
        dh_part += contract_cols(d_gate_up, w_gu)
    d_w.append(jnp.concatenate(d_downs, axis=0).reshape(16, 96, D))
    d_w = jnp.concatenate(d_w, axis=1).reshape(4, 4, UNIT, D)

    layer_output, d_middle, d_attn_all, mlp_gain, a_one, b_one = back_step(
        out_part[:ROWS], out_part[ROWS:].astype(BF), dh_part[:ROWS], dh_part[ROWS:].astype(BF),
        middle, cotangent, g_mlp[None, :], d_w,
    )

    d_attn = d_attn_all.reshape(seq_length, D)
    grad_out = contract_rows(attended, d_attn)
    d_attended = contract_cols(d_attn, full_out).astype(BF)
    grouped_gradient = d_attended.reshape(seq_length, kv_heads, group_size, HEAD_WIDTH)
    probabilities = jnp.exp(score_of() - log_total)
    probability_gradient = jnp.einsum(
        "hkco,wko->kchw", grouped_gradient, values, preferred_element_type=F32
    )
    score_gradient = (
        probabilities
        * (
            probability_gradient
            - jnp.sum(probabilities * probability_gradient, axis=-1, keepdims=True)
        )
    ).astype(BF)
    d_query = (
        jnp.einsum("xwbq,qxm->bxwm", score_gradient, keys, preferred_element_type=F32) * score_scale
    )
    d_keys = (
        jnp.einsum("ixnp,nixa->pia", score_gradient, grouped, preferred_element_type=F32)
        * score_scale
    )
    d_values = jnp.einsum(
        "ixnp,nixa->pia", probabilities.astype(BF), grouped_gradient, preferred_element_type=F32
    )
    d_query_gained = rotate_back(d_query.reshape(seq_length, heads, HEAD_WIDTH), cosine, sine)
    grad_query_gain = jnp.sum(d_query_gained * q_normed, axis=(0, 1))
    d_query_raw = rms_back(d_query_gained * g_query, q_normed, q_scale)
    d_key_gained = rotate_back(d_keys.reshape(seq_length, kv_heads, HEAD_WIDTH), cosine, sine)
    grad_key_gain = jnp.sum(d_key_gained * k_normed, axis=(0, 1))
    d_key_raw = rms_back(d_key_gained * g_key, k_normed, k_scale)
    d_projected = jnp.concatenate(
        [
            d_query_raw.reshape(seq_length, width_q),
            d_key_raw.reshape(seq_length, width_kv),
            d_values.reshape(seq_length, width_kv),
        ],
        axis=1,
    ).astype(BF)
    grad_qkv = contract_rows(hidden, d_projected).astype(BF)
    dh_terms = contract_cols(d_projected, full_qkv).astype(BF)

    d_hidden, q_grad, o_grad, gu_grad, down_grad = owner_step(
        dh_terms.reshape(4, ROWS, D),
        grad_qkv.reshape(4, 4, 2, 32, D),
        grad_out.astype(BF).reshape(4, 2, 64, D),
        a_one,
        b_one,
    )
    own_normed, own_scale = rms_parts(tokens.astype(F32))
    grad_attn_gain = jnp.sum(d_hidden * own_normed, axis=0)
    input_grad = d_middle + rms_back(d_hidden * g_attn, own_normed, own_scale)

    q_shard = jnp.concatenate(
        [
            q_grad[:, :, :512].transpose(1, 0, 2).reshape(8, 2048),
            q_grad[:, :, 512:768].transpose(1, 0, 2).reshape(8, 1024),
            q_grad[:, :, 768:].transpose(1, 0, 2).reshape(8, 1024),
        ],
        axis=1,
    )
    shards = [q_shard, o_grad, unpack_gateup(gu_grad), down_grad]
    squares = jnp.float32(0.0)
    for shard in (q_grad, o_grad, gu_grad, down_grad):
        squares = squares + jnp.sum(shard * shard)
    grad_gains = jnp.concatenate(
        [grad_attn_gain, jnp.sum(mlp_gain, axis=0), grad_query_gain, grad_key_gain]
    )
    extra = jnp.zeros((6, 128), F32).at[0, 0].set(squares)
    sums = sum_all(jnp.concatenate([grad_gains.reshape(18, 128), extra], axis=0))
    all_gains = sums[:18].reshape(-1)
    grad_norm = jnp.sqrt(sums[18, 0] + jnp.sum(all_gains * all_gains))
    index = lax.axis_index("dp") * 4 + lax.axis_index("ctx")
    shards.append(lax.dynamic_slice_in_dim(all_gains, index * 18, 18))

    factor = jnp.minimum(1.0, clip_at / (grad_norm + 1e-06))
    masters = (w_qkv, w_out, w_gateup, w_down, gains)
    firsts = (first_qkv, first_out, first_gateup, first_down, first_gains)
    seconds = (second_qkv, second_out, second_gateup, second_down, second_gains)
    rates = (matrix_rate, out_rate, matrix_rate, matrix_rate, gain_rate)
    decays = (matrix_decay, matrix_decay, matrix_decay, matrix_decay, 0.0)
    news, new_firsts, new_seconds = [], [], []
    for which in range(5):
        weight, first, second = adam_update(
            masters[which], firsts[which], seconds[which], shards[which], factor,
            rates[which], decays[which],
        )
        news.append(weight)
        new_firsts.append(first)
        new_seconds.append(second)
    return (layer_output, input_grad, *news, *new_firsts, *new_seconds, grad_norm)


def solution(mesh):
    rows, flat = P(("dp", "ctx"), None), P(("dp", "ctx"))
    state = (rows, rows, rows, rows, flat)
    in_specs = (rows, rows, P()) + state * 3
    out_specs = (rows, rows) + state * 3 + (P(),)
    return jax.shard_map(body, mesh=mesh, in_specs=in_specs, out_specs=out_specs, check_vma=False)
```

```python
import jax
import jax.numpy as jnp
import numpy as np
from jax import lax
from jax.experimental import pallas as pl
from jax.experimental.pallas import tpu as pltpu
from jax.sharding import PartitionSpec as P

D = 1024
HEADS = 16
KV_HEADS = 8
HEAD_WIDTH = 128
FF = 3072
STEP = 10

norm_eps = 1e-06
rope_base = 1000000.0
beta_one = 0.9
beta_two = 0.999
adam_eps = 1e-08
clip_at = 1.0
matrix_rate = 0.05
out_rate = 0.25
matrix_decay = 0.1
gain_rate = 0.5
masked_score = -1e30

MESH = pl.DeviceIdType.MESH
BF = jnp.bfloat16
F32 = jnp.float32
ROWS = 256
UNIT = 288
PART_A = 144
VMEM_LIMIT = 58 * 2**20
vmem = pl.BlockSpec(memory_space=pltpu.VMEM)
hbm = pl.BlockSpec(memory_space=pl.ANY)


class Place:
    def __init__(self):
        dp = lax.axis_index("dp")
        self.at = {
            "z": lax.div(dp, 8),
            "x": lax.rem(lax.div(dp, 2), 4),
            "k": lax.rem(dp, 2),
            "y": lax.axis_index("ctx"),
        }

    def __getitem__(self, axis):
        return self.at[axis]

    def device(self, **other):
        c = {**self.at, **other}
        return (c["z"] * 8 + c["x"] * 2 + c["k"], c["y"])

    def moved(self, axis, steps):
        return lax.rem(self.at[axis] + steps, 4)

    def peer(self, axis, steps):
        return self.device(**{axis: self.moved(axis, steps)})

    def sibling(self):
        return self.device(k=1 - self.at["k"])


def greet(devices):
    barrier = pltpu.get_barrier_semaphore()
    for device in devices:
        pl.semaphore_signal(barrier, inc=1, device_id=device, device_id_type=MESH)


def await_greetings(count):
    pl.semaphore_wait(pltpu.get_barrier_semaphore(), count)


def neighbours(place, axes):
    found = []
    for axis in axes:
        if axis == "k":
            found.append(place.sibling())
        else:
            found += [place.peer(axis, 1), place.peer(axis, 3)]
    return found


def remote(src, dst, send, recv, device):
    return pltpu.make_async_remote_copy(
        src_ref=src, dst_ref=dst, send_sem=send, recv_sem=recv, device_id=device, device_id_type=MESH
    )


class Gather:
    def __init__(self, place, axis, part, sems, own=None):
        self.part, self.send, self.recv = part, sems[0], sems[1]
        self.own = own or (lambda half: part(place[axis], half))
        self.next, self.prev = place.peer(axis, 1), place.peer(axis, 3)
        self.me, self.up, self.down, self.far = (place.moved(axis, n) for n in (0, 1, 3, 2))

    def copy(self, n, slot, half, device, src=None):
        view = self.part(slot, half)
        return remote(src if src is not None else view, view, self.send.at[n], self.recv.at[n], device)

    def outgoing(self, n):
        slot, half, device = [
            (self.me, 0, self.next),
            (self.me, 1, self.prev),
            (self.me, 1, self.next),
            (self.me, 0, self.prev),
            (self.down, 0, self.next),
            (self.up, 1, self.prev),
        ][n]
        return self.copy(n, slot, half, device, self.own(half) if n < 4 else None)

    def start(self):
        for n in range(4):
            self.outgoing(n).start()

    def forward(self):
        self.copy(0, self.down, 0, self.prev).wait_recv()
        self.outgoing(4).start()
        self.copy(1, self.up, 1, self.next).wait_recv()
        self.outgoing(5).start()

    def finish(self):
        self.copy(2, self.down, 1, self.prev).wait_recv()
        self.copy(3, self.up, 0, self.next).wait_recv()
        self.copy(4, self.far, 0, self.prev).wait_recv()
        self.copy(5, self.far, 1, self.next).wait_recv()
        for n in range(6):
            self.outgoing(n).wait_send()


class Scatter:
    def __init__(self, place, axis, part, boxes, sems, add):
        self.part, self.boxes, self.add = part, boxes, add
        self.send, self.recv = sems[0], sems[1]
        self.next, self.prev = place.peer(axis, 1), place.peer(axis, 3)
        self.me, self.up, self.down, self.far = (place.moved(axis, n) for n in (0, 1, 3, 2))

    def copy(self, n, src, device):
        return remote(src, self.boxes[n], self.send.at[n], self.recv.at[n], device)

    def outgoing(self, n):
        source, device = [
            (lambda: self.part(self.far, 0), self.prev),
            (lambda: self.part(self.far, 1), self.next),
            (lambda: self.part(self.down, 1), self.prev),
            (lambda: self.part(self.up, 0), self.next),
            (lambda: self.boxes[6], self.prev),
            (lambda: self.boxes[7], self.next),
        ][n]
        return self.copy(n, source(), device)

    def start(self):
        for n in range(4):
            self.outgoing(n).start()

    def forward(self):
        self.outgoing(0).wait_recv()
        self.add(self.boxes[6], [self.boxes[0], self.part(self.down, 0)])
        self.outgoing(4).start()
        self.outgoing(1).wait_recv()
        self.add(self.boxes[7], [self.boxes[1], self.part(self.up, 1)])
        self.outgoing(5).start()

    def finish(self, result):
        for n in (2, 3, 4, 5):
            self.outgoing(n).wait_recv()
        self.add(result(0), [self.part(self.me, 0), self.boxes[3], self.boxes[4]])
        self.add(result(1), [self.part(self.me, 1), self.boxes[2], self.boxes[5]])
        for n in range(6):
            self.outgoing(n).wait_send()


def add_rows(out, terms):
    shape = out.shape
    rows = shape[-2]

    def block(at):
        total = terms[0][at].astype(F32)
        for term in terms[1:]:
            total = total + term[at].astype(F32)
        out[at] = total.astype(out.dtype)

    if len(shape) == 2:

        @pl.loop(0, rows // 16)
        def _(r):
            block((pl.ds(pl.multiple_of(r * 16, 16), 16), slice(None)))

    else:

        @pl.loop(0, shape[0])
        def _(lead):
            @pl.loop(0, rows // 16)
            def _(r):
                block((lead, pl.ds(pl.multiple_of(r * 16, 16), 16), slice(None)))


def dma(*shape):
    return pltpu.SemaphoreType.DMA(shape)


def ring_sems():
    return [dma(6), dma(6)]


def params(which):
    return pltpu.CompilerParams(
        collective_id=which, has_side_effects=True, vmem_limit_bytes=VMEM_LIMIT
    )


def upper_rows(half, low, split, high):
    return pl.ds(low, split - low) if half == 0 else pl.ds(split, high - split)


def stage_one_a(place, w_all):
    return lambda i, half: w_all.at[place["z"], i, upper_rows(half, 0, 80, PART_A)]


def stage_one_b(place, w_all):
    return lambda i, half: w_all.at[i, place["x"], upper_rows(half, PART_A, 208, UNIT)]


def stage_two_a(place, w_all):
    return lambda i, half: w_all.at[i, pl.ds(2 * half, 2), pl.ds(0, PART_A)]


def stage_two_b(place, w_all):
    return lambda i, half: w_all.at[pl.ds(2 * half, 2), i, pl.ds(PART_A, UNIT - PART_A)]


def gather_kernel(
    tok, wq, wo, wgu, wd, gains,
    tok_all, wq_all, wo_all, w_all,
    q_send, q_recv, q_unit, o_send, g_recv, g_y, d_y, unit,
    local, qp_s, qp_r, op_s, op_r, gp, t_s, t_r, qx_s, qx_r, qz_s, qz_r, ox_s, ox_r,
    core, gy_s, gy_r, dy_s, dy_r, a_s, a_r, b_s, b_r,
):
    place = Place()
    z, x, k, y = (place[a] for a in "zxky")
    near = neighbours(place, "xyzk")
    greet(near + [place.peer("y", 2)])
    diagonal = z == y
    for other in range(4):

        @pl.when(jnp.logical_not(jnp.logical_and(diagonal, y == other)))
        def _():
            greet([place.device(z=y, y=jnp.int32(other))])

    for i in range(4):
        q_send[i, :, 0:512] = wq[:, 512 * i : 512 * i + 512]
        q_send[i, :, 512:768] = wq[:, 2048 + 256 * i : 2304 + 256 * i]
        q_send[i, :, 768:1024] = wq[:, 3072 + 256 * i : 3328 + 256 * i]
        q_send[i, :, 1024:1152] = gains[...]
    o_send[...] = wo[...].astype(BF)
    await_greetings(len(near) + 1 + jnp.where(diagonal, 3, 4))

    q_prep = [
        remote(q_send.at[place.moved("y", n)], q_recv.at[y], qp_s.at[n], qp_r.at[y], place.peer("y", n))
        for n in (1, 3, 2)
    ]
    for copy in q_prep:
        copy.start()
    g_prep = remote(wgu.at[1 - k], g_recv, gp.at[0], gp.at[1], place.sibling())
    g_prep.start()
    tok_own = pltpu.make_async_copy(tok, tok_all.at[y], local.at[0])
    tok_own.start()

    def o_slot(source):
        return wo_all.at[x, k, pl.ds(pl.multiple_of(16 * source, 16), 16)]

    for other in range(4):

        @pl.when(jnp.logical_not(jnp.logical_and(diagonal, z == other)))
        def _():
            remote(o_send, o_slot(y), op_s.at[other], op_r.at[y], place.device(z=jnp.int32(other), y=z)).start()

    @pl.when(diagonal)
    def _():
        pltpu.make_async_copy(o_send, o_slot(y), local.at[1]).start()

    tokens_ring = Gather(
        place, "y", lambda i, h: tok_all.at[i, pl.ds(128 * h, 128)], (t_s, t_r),
        own=lambda h: tok.at[pl.ds(128 * h, 128)],
    )
    tokens_ring.start()

    q_recv[y] = q_send[y]
    for n in (1, 3, 2):
        source = place.moved("y", n)
        remote(q_send.at[0], q_recv.at[source], qp_s.at[n], qp_r.at[source], place.peer("y", n)).wait_recv()
    q_unit[...] = q_recv[...].reshape(32, 1152).astype(BF)
    q_own = pltpu.make_async_copy(q_unit, wq_all.at[z, x, k], local.at[2])
    q_own.start()
    q_x = Gather(
        place, "x", lambda i, h: wq_all.at[z, i, k, pl.ds(16 * h, 16)], (qx_s, qx_r),
        own=lambda h: q_unit.at[pl.ds(16 * h, 16)],
    )
    q_x.start()

    g_prep.wait_recv()
    g_own = wgu[k]
    g_other = g_recv[...]
    lower = k == 0
    first = jnp.where(lower, g_own, g_other)
    second = jnp.where(lower, g_other, g_own)
    both = jnp.concatenate([first, second], axis=1)
    g_y[y] = both.reshape(48, 1024).astype(BF)
    d_y[y] = wd[...]
    g_ring = Gather(place, "y", lambda i, h: g_y.at[i, upper_rows(h, 0, 32, 48)], (gy_s, gy_r))
    d_ring = Gather(place, "y", lambda i, h: d_y.at[i, upper_rows(h, 0, 16, 24)], (dy_s, dy_r))
    g_ring.start()
    d_ring.start()

    for other in range(4):
        here = jnp.logical_and(diagonal, y == other)

        @pl.when(jnp.logical_not(here))
        def _():
            remote(o_send, o_slot(other), op_s.at[0], op_r.at[other], place.device(z=y, y=jnp.int32(other))).wait_recv()

    @pl.when(diagonal)
    def _():
        pltpu.make_async_copy(o_send, o_slot(y), local.at[1]).wait()

    o_x = Gather(place, "x", lambda i, h: wo_all.at[i, k, pl.ds(32 * h, 32)], (ox_s, ox_r))
    o_x.start()

    q_x.forward()
    g_ring.forward()
    d_ring.forward()
    q_x.finish()
    q_own.wait()
    q_z = Gather(place, "z", lambda i, h: wq_all.at[i, pl.ds(2 * h, 2), k], (qz_s, qz_r))
    q_z.start()
    o_x.forward()
    g_ring.finish()
    d_ring.finish()

    for b in range(3):
        pieces = [g_y[c, 16 * b : 16 * b + 16].astype(F32) for c in range(4)]
        for core_row in range(2):
            rows = jnp.concatenate([piece[8 * core_row : 8 * core_row + 8] for piece in pieces], axis=0)
            at = 64 * b + 32 * core_row
            unit[at : at + 32] = rows.astype(BF)
    unit[192:288] = d_y[...].reshape(96, 1024).astype(BF)
    u_own = pltpu.make_async_copy(unit, w_all.at[z, x], local.at[3])
    u_own.start()
    a_ring = Gather(
        place, "x", stage_one_a(place, w_all), (a_s, a_r),
        own=lambda h: unit.at[upper_rows(h, 0, 80, PART_A)],
    )
    b_ring = Gather(
        place, "z", stage_one_b(place, w_all), (b_s, b_r),
        own=lambda h: unit.at[upper_rows(h, PART_A, 208, UNIT)],
    )
    a_ring.start()
    b_ring.start()
    tokens_ring.forward()
    q_z.forward()
    o_x.finish()
    o_core = remote(wo_all.at[:, k], wo_all.at[:, k], core.at[0], core.at[1], place.sibling())
    o_core.start()
    a_ring.forward()
    b_ring.forward()
    q_z.finish()
    q_core = remote(wq_all.at[:, :, k], wq_all.at[:, :, k], core.at[2], core.at[3], place.sibling())
    q_core.start()
    a_ring.finish()
    b_ring.finish()
    tokens_ring.finish()
    tok_own.wait()
    u_own.wait()
    for copy in q_prep:
        copy.wait_send()
    g_prep.wait_send()
    for other in range(4):

        @pl.when(jnp.logical_not(jnp.logical_and(diagonal, z == other)))
        def _():
            remote(o_send, o_slot(y), op_s.at[other], op_r.at[y], place.device(z=jnp.int32(other), y=z)).wait_send()

    remote(wo_all.at[:, 1 - k], wo_all.at[:, 1 - k], core.at[0], core.at[1], place.sibling()).wait_recv()
    remote(wq_all.at[:, :, 1 - k], wq_all.at[:, :, 1 - k], core.at[2], core.at[3], place.sibling()).wait_recv()
    o_core.wait_send()
    q_core.wait_send()


def gather_all(tok, wq, wo, wgu, wd, gains):
    shape = jax.ShapeDtypeStruct
    return pl.pallas_call(
        gather_kernel,
        out_shape=(
            shape((4, ROWS, D), BF),
            shape((4, 4, 2, 32, 1152), BF),
            shape((4, 2, 64, D), BF),
            shape((4, 4, UNIT, D), BF),
        ),
        in_specs=[vmem] * 6,
        out_specs=(hbm,) * 4,
        scratch_shapes=[
            pltpu.VMEM((4, 8, 1152), F32),
            pltpu.VMEM((4, 8, 1152), F32),
            pltpu.VMEM((32, 1152), BF),
            pltpu.VMEM((16, D), BF),
            pltpu.VMEM((3, 8, D), F32),
            pltpu.VMEM((4, 48, D), BF),
            pltpu.VMEM((4, 24, D), F32),
            pltpu.VMEM((UNIT, D), BF),
            dma(4), dma(4), dma(4), dma(4), dma(4), dma(2),
            *ring_sems(), *ring_sems(), *ring_sems(), *ring_sems(),
            dma(4),
            *ring_sems(), *ring_sems(), *ring_sems(), *ring_sems(),
        ],
        compiler_params=params(1),
        name="gather_weights_tokens",
    )(tok, wq, wo, wgu, wd, gains)


def middle_kernel(
    terms, tok, cot, gain, w_in,
    middle, hidden_pair, cot_pair, w_all,
    boxes, total, local, y_s, y_r, core, a_s, a_r, b_s, b_r,
):
    place = Place()
    near = neighbours(place, "xyzk")
    greet(near)
    await_greetings(len(near))
    a_ring = Gather(place, "z", stage_two_a(place, w_all), (a_s, a_r))
    b_ring = Gather(place, "x", stage_two_b(place, w_all), (b_s, b_r))
    reduce = Scatter(
        place, "y", lambda i, h: terms.at[i, pl.ds(128 * h, 128)],
        [boxes.at[n] for n in range(8)], (y_s, y_r), add_rows,
    )
    reduce.start()
    a_ring.start()
    b_ring.start()
    cot_copy = remote(cot, cot_pair.at[1], core.at[0], core.at[1], place.sibling())
    cot_copy.start()
    cot_own = pltpu.make_async_copy(cot, cot_pair.at[0], local)
    cot_own.start()
    reduce.forward()
    a_ring.forward()
    b_ring.forward()
    reduce.finish(lambda h: total.at[pl.ds(128 * h, 128)])

    @pl.loop(0, ROWS // 16)
    def _(r):
        at = pl.ds(pl.multiple_of(r * 16, 16), 16)
        rows = tok[at].astype(F32) + total[at]
        middle[at] = rows
        scale = lax.rsqrt(jnp.mean(rows * rows, axis=-1, keepdims=True) + norm_eps)
        hidden_pair[0, at] = (rows * scale * gain[...]).astype(BF)

    hid_copy = remote(hidden_pair.at[0], hidden_pair.at[1], core.at[2], core.at[3], place.sibling())
    hid_copy.start()
    a_ring.finish()
    b_ring.finish()
    cot_own.wait()
    cot_copy.wait()
    hid_copy.wait()


def middle_step(terms, tok, cot, gain, w_all):
    shape = jax.ShapeDtypeStruct
    return pl.pallas_call(
        middle_kernel,
        out_shape=(
            shape((ROWS, D), F32),
            shape((2, ROWS, D), BF),
            shape((2, ROWS, D), BF),
            shape((4, 4, UNIT, D), BF),
        ),
        in_specs=[vmem] * 4 + [hbm],
        out_specs=(vmem, vmem, vmem, hbm),
        scratch_shapes=[
            pltpu.VMEM((8, 128, D), BF),
            pltpu.VMEM((ROWS, D), F32),
            pltpu.SemaphoreType.DMA,
            *ring_sems(), dma(4), *ring_sems(), *ring_sems(),
        ],
        input_output_aliases={4: 3},
        compiler_params=params(2),
        name="reduce_attention_gather_ff",
    )(terms, tok, cot, gain, w_all)


def back_kernel(
    out_own, out_sib, dh_own, dh_sib, mid, cot, gain, d_w,
    layer_out, d_middle, d_attn_all, gain_grad, a_one, b_one,
    out_box, dh_box, own, a_box, b_box,
    local, core, y_s, y_r, a_s, a_r, b_s, b_r,
):
    place = Place()
    y = place["y"]
    near = neighbours(place, "xyzk")
    greet(near)
    await_greetings(len(near))
    dh_copy = remote(dh_sib, dh_box, core.at[0], core.at[1], place.sibling())
    out_copy = remote(out_sib, out_box, core.at[2], core.at[3], place.sibling())
    dh_copy.start()
    out_copy.start()
    a_ring = Scatter(
        place, "z", lambda i, h: d_w.at[i, pl.ds(2 * h, 2), pl.ds(0, PART_A)],
        [a_box.at[n] for n in range(8)], (a_s, a_r), add_rows,
    )
    b_ring = Scatter(
        place, "x", lambda i, h: d_w.at[pl.ds(2 * h, 2), i, pl.ds(PART_A, UNIT - PART_A)],
        [b_box.at[n] for n in range(8)], (b_s, b_r), add_rows,
    )
    a_ring.start()
    b_ring.start()
    gain_grad[...] = jnp.zeros_like(gain_grad)
    dh_copy.wait_recv()

    @pl.loop(0, ROWS // 16)
    def _(r):
        at = pl.ds(pl.multiple_of(r * 16, 16), 16)
        rows = mid[at]
        scale = lax.rsqrt(jnp.mean(rows * rows, axis=-1, keepdims=True) + norm_eps)
        normed = rows * scale
        incoming = dh_own[at] + dh_box[at].astype(F32)
        product = incoming * normed
        gain_grad[...] += product[0:8] + product[8:16]
        incoming = incoming * gain[...]
        mean = jnp.mean(incoming * normed, axis=-1, keepdims=True)
        d_mid = cot[at].astype(F32) + scale * (incoming - normed * mean)
        d_middle[at] = d_mid
        own[at] = d_mid.astype(BF)

    ring = Gather(
        place, "y", lambda i, h: d_attn_all.at[i, pl.ds(128 * h, 128)], (y_s, y_r),
        own=lambda h: own.at[pl.ds(128 * h, 128)],
    )
    ring.start()
    own_copy = pltpu.make_async_copy(own, d_attn_all.at[y], local)
    own_copy.start()
    out_copy.wait_recv()

    @pl.loop(0, ROWS // 16)
    def _(r):
        at = pl.ds(pl.multiple_of(r * 16, 16), 16)
        layer_out[at] = (mid[at] + out_own[at] + out_box[at].astype(F32)).astype(BF)

    ring.forward()
    a_ring.forward()
    b_ring.forward()
    ring.finish()
    a_ring.finish(lambda h: a_one.at[pl.ds(2 * h, 2)])
    b_ring.finish(lambda h: b_one.at[pl.ds(2 * h, 2)])
    own_copy.wait()
    dh_copy.wait_send()
    out_copy.wait_send()


def back_step(out_own, out_sib, dh_own, dh_sib, mid, cot, gain, d_w):
    shape = jax.ShapeDtypeStruct
    return pl.pallas_call(
        back_kernel,
        out_shape=(
            shape((ROWS, D), BF),
            shape((ROWS, D), F32),
            shape((4, ROWS, D), BF),
            shape((8, D), F32),
            shape((4, PART_A, D), BF),
            shape((4, PART_A, D), BF),
        ),
        in_specs=[vmem] * 8,
        out_specs=(vmem,) * 6,
        scratch_shapes=[
            pltpu.VMEM((ROWS, D), BF),
            pltpu.VMEM((ROWS, D), BF),
            pltpu.VMEM((ROWS, D), BF),
            pltpu.VMEM((8, 2, PART_A, D), BF),
            pltpu.VMEM((8, 2, PART_A, D), BF),
            pltpu.SemaphoreType.DMA,
            dma(4), *ring_sems(), *ring_sems(), *ring_sems(),
        ],
        compiler_params=params(3),
        name="reduce_ff_gather_gradient",
    )(out_own, out_sib, dh_own, dh_sib, mid, cot, gain, d_w)


def owner_kernel(
    dh_terms, d_q, d_o, a_one, b_one,
    dh_out, q_out, o_out, g_out, d_out,
    y_box, dh_total, q_box, q_one, qz_box, q_two, qx_box, q_three,
    o_box, o_one, ox_box, o_two, o_slots, a_box, b_box, total, g_send, g_slots, d_slots, g_sum,
    core, y_s, y_r, qz_s, qz_r, qx_s, qx_r, ox_s, ox_r, a_s, a_r, b_s, b_r,
    qy_s, qy_r, oy_s, oy_r, gy_s, gy_r, dy_s, dy_r, local,
):
    place = Place()
    z, x, k, y = (place[a] for a in "zxky")
    diagonal = z == y
    near = neighbours(place, "xyzk")
    greet(near + [place.peer("y", 2)])
    for other in range(4):

        @pl.when(jnp.logical_not(jnp.logical_and(diagonal, z == other)))
        def _():
            greet([place.device(z=jnp.int32(other), y=z)])

    await_greetings(len(near) + 1 + jnp.where(diagonal, 3, 4))

    q_core = remote(d_q.at[:, :, 1 - k], q_box, core.at[0], core.at[1], place.sibling())
    o_core = remote(d_o.at[:, 1 - k], o_box, core.at[2], core.at[3], place.sibling())
    o_core.start()
    q_core.start()
    dh_ring = Scatter(
        place, "y", lambda i, h: dh_terms.at[i, pl.ds(128 * h, 128)],
        [y_box.at[n] for n in range(8)], (y_s, y_r), add_rows,
    )
    dh_ring.start()
    a_part = lambda i, h: a_one.at[i, upper_rows(h, 0, 80, PART_A)]
    b_part = lambda i, h: b_one.at[i, upper_rows(h, 0, 64, PART_A)]
    a_ring = Scatter(
        place, "x", a_part,
        [a_box.at[n, pl.ds(0, 80 if n in (0, 3, 4, 6) else 64)] for n in range(8)],
        (a_s, a_r), add_rows,
    )
    b_ring = Scatter(
        place, "z", b_part,
        [b_box.at[n, pl.ds(0, 64 if n in (0, 3, 4, 6) else 80)] for n in range(8)],
        (b_s, b_r), add_rows,
    )
    a_ring.start()
    b_ring.start()

    o_core.wait_recv()

    @pl.loop(0, 4)
    def _(i):
        @pl.loop(0, 4)
        def _(r):
            at = pl.ds(pl.multiple_of(r * 16, 16), 16)
            o_one[i, at] = (d_o[i, k, at].astype(F32) + o_box[i, at].astype(F32)).astype(BF)

    o_x = Scatter(
        place, "x", lambda i, h: o_one.at[i, pl.ds(32 * h, 32)],
        [ox_box.at[n] for n in range(8)], (ox_s, ox_r), add_rows,
    )
    o_x.start()
    q_core.wait_recv()

    @pl.loop(0, 4)
    def _(i):
        @pl.loop(0, 4)
        def _(j):
            @pl.loop(0, 2)
            def _(r):
                at = pl.ds(pl.multiple_of(r * 16, 16), 16)
                q_one[i, j, at] = (d_q[i, j, k, at].astype(F32) + q_box[i, j, at].astype(F32)).astype(BF)

    q_z = Scatter(
        place, "z", lambda i, h: q_one.at[i, pl.ds(2 * h, 2)],
        [qz_box.at[n] for n in range(8)], (qz_s, qz_r), add_rows,
    )
    q_z.start()
    a_ring.forward()
    b_ring.forward()
    o_x.forward()
    q_z.forward()
    dh_ring.forward()

    a_ring.finish(lambda h: total.at[upper_rows(h, 0, 80, PART_A)])
    b_ring.finish(lambda h: total.at[upper_rows(h, PART_A, 208, UNIT)])
    for c in range(4):
        for b in range(3):
            at = 64 * b + 8 * c
            rows = jnp.concatenate([total[at : at + 8], total[at + 32 : at + 40]], axis=0)
            g_send[c, 16 * b : 16 * b + 16] = rows.astype(BF)
    g_slots[y] = g_send[y]
    d_slots[y] = total[pl.ds(pl.multiple_of(192 + 24 * y, 8), 24)]
    y_copies = []
    for n in (1, 3, 2):
        to = place.moved("y", n)
        y_copies.append(remote(g_send.at[to], g_slots.at[y], gy_s.at[n], gy_r.at[y], place.peer("y", n)))
        rows = pl.ds(pl.multiple_of(192 + 24 * to, 8), 24)
        y_copies.append(remote(total.at[rows], d_slots.at[y], dy_s.at[n], dy_r.at[y], place.peer("y", n)))
    for copy in y_copies:
        copy.start()

    q_z.finish(lambda h: q_two.at[pl.ds(2 * h, 2)])
    q_x = Scatter(
        place, "x", lambda i, h: q_two.at[i, pl.ds(16 * h, 16)],
        [qx_box.at[n] for n in range(8)], (qx_s, qx_r), add_rows,
    )
    q_x.start()
    o_x.finish(lambda h: o_two.at[pl.ds(32 * h, 32)])
    for other in range(4):
        piece = o_two.at[pl.ds(16 * other, 16)]

        @pl.when(jnp.logical_not(jnp.logical_and(diagonal, y == other)))
        def _():
            remote(piece, o_slots.at[z], oy_s.at[other], oy_r.at[z], place.device(z=y, y=jnp.int32(other))).start()

        @pl.when(jnp.logical_and(diagonal, y == other))
        def _():
            pltpu.make_async_copy(piece, o_slots.at[z], local).start()

    q_x.forward()
    dh_ring.finish(lambda h: dh_out.at[pl.ds(128 * h, 128)])

    for n in (1, 3, 2):
        source = place.moved("y", n)
        remote(g_send.at[0], g_slots.at[source], gy_s.at[n], gy_r.at[source], place.peer("y", n)).wait_recv()
        remote(total.at[pl.ds(192, 24)], d_slots.at[source], dy_s.at[n], dy_r.at[source], place.peer("y", n)).wait_recv()
    d_out[...] = d_slots[0] + d_slots[1] + d_slots[2] + d_slots[3]
    summed = g_slots[0].astype(F32)
    for c in range(1, 4):
        summed = summed + g_slots[c].astype(F32)
    summed = summed.reshape(3, 2, 8, D)
    g_sum[0] = summed[:, 0]
    g_sum[1] = summed[:, 1]
    g_out[k] = g_sum[k]
    g_core = remote(g_sum.at[1 - k], g_out.at[k], core.at[4], core.at[5], place.sibling())
    g_core.start()

    q_x.finish(lambda h: q_three.at[pl.ds(16 * h, 16)])
    q_out[y] = q_three[pl.ds(pl.multiple_of(8 * y, 8), 8)]
    q_copies = []
    for n in (1, 3, 2):
        rows = pl.ds(pl.multiple_of(8 * place.moved("y", n), 8), 8)
        q_copies.append(remote(q_three.at[rows], q_out.at[y], qy_s.at[n], qy_r.at[y], place.peer("y", n)))
    for copy in q_copies:
        copy.start()

    for other in range(4):
        here = jnp.logical_and(diagonal, z == other)

        @pl.when(jnp.logical_not(here))
        def _():
            remote(o_two.at[pl.ds(0, 16)], o_slots.at[other], oy_s.at[0], oy_r.at[other], place.device(z=jnp.int32(other), y=z)).wait_recv()

        @pl.when(here)
        def _():
            pltpu.make_async_copy(o_two.at[pl.ds(0, 16)], o_slots.at[other], local).wait()

    o_sum = o_slots[0].astype(F32)
    for c in range(1, 4):
        o_sum = o_sum + o_slots[c].astype(F32)
    o_out[...] = o_sum
    for n in (1, 3, 2):
        source = place.moved("y", n)
        remote(q_three.at[pl.ds(0, 8)], q_out.at[source], qy_s.at[n], qy_r.at[source], place.peer("y", n)).wait_recv()
    remote(g_sum.at[0], g_out.at[1 - k], core.at[4], core.at[5], place.sibling()).wait_recv()
    for copy in [o_core, q_core, g_core] + y_copies + q_copies:
        copy.wait_send()
    for other in range(4):

        @pl.when(jnp.logical_not(jnp.logical_and(diagonal, y == other)))
        def _():
            remote(o_two.at[pl.ds(16 * other, 16)], o_slots.at[z], oy_s.at[other], oy_r.at[z], place.device(z=y, y=jnp.int32(other))).wait_send()


def owner_step(dh_terms, d_q, d_o, a_one, b_one):
    shape = jax.ShapeDtypeStruct
    return pl.pallas_call(
        owner_kernel,
        out_shape=(
            shape((ROWS, D), F32),
            shape((4, 8, D), F32),
            shape((16, D), F32),
            shape((2, 3, 8, D), F32),
            shape((24, D), F32),
        ),
        in_specs=[vmem] * 5,
        out_specs=(vmem,) * 5,
        scratch_shapes=[
            pltpu.VMEM((8, 128, D), BF),
            pltpu.VMEM((8, 128), F32),
            pltpu.VMEM((4, 4, 32, D), BF),
            pltpu.VMEM((4, 4, 32, D), BF),
            pltpu.VMEM((8, 2, 32, D), BF),
            pltpu.VMEM((4, 32, D), BF),
            pltpu.VMEM((8, 16, D), BF),
            pltpu.VMEM((32, D), F32),
            pltpu.VMEM((4, 64, D), BF),
            pltpu.VMEM((4, 64, D), BF),
            pltpu.VMEM((8, 32, D), BF),
            pltpu.VMEM((64, D), BF),
            pltpu.VMEM((4, 16, D), BF),
            pltpu.VMEM((8, 80, D), BF),
            pltpu.VMEM((8, 80, D), BF),
            pltpu.VMEM((UNIT, D), F32),
            pltpu.VMEM((4, 48, D), BF),
            pltpu.VMEM((4, 48, D), BF),
            pltpu.VMEM((4, 24, D), F32),
            pltpu.VMEM((2, 3, 8, D), F32),
            dma(6),
            *ring_sems(), *ring_sems(), *ring_sems(), *ring_sems(), *ring_sems(), *ring_sems(),
            dma(4), dma(4), dma(4), dma(4), dma(4), dma(4), dma(4), dma(4),
            pltpu.SemaphoreType.DMA,
        ],
        compiler_params=params(4),
        name="reduce_gradients",
    )(dh_terms, d_q, d_o, a_one, b_one)


def sum_kernel(value, result, first, second, held, s_one, r_one, s_two, r_two):
    place = Place()
    z, x, k, y = (place[a] for a in "zxky")
    ours = [(dy, dk) for dy in range(4) for dk in range(2) if (dy, dk) != (0, 0)]
    theirs = [(dz, dx) for dz in range(4) for dx in range(4) if (dz, dx) != (0, 0)]

    def near(dy, dk):
        return place.device(y=place.moved("y", dy), k=lax.rem(k + dk, 2))

    def far(dz, dx):
        return place.device(z=place.moved("z", dz), x=place.moved("x", dx))

    greet([near(*o) for o in ours] + [far(*o) for o in theirs])
    await_greetings(len(ours) + len(theirs))

    def stage(source, slots, send, recv, offsets, device, me, slot_of):
        slots[me] = source[...]
        copies = []
        for n, offset in enumerate(offsets):
            copies.append(remote(source, slots.at[me], send.at[n], recv.at[me], device(*offset)))
        for copy in copies:
            copy.start()
        for n, offset in enumerate(offsets):
            slot = slot_of(*offset)
            remote(source, slots.at[slot], send.at[n], recv.at[slot], device(*offset)).wait_recv()
        for copy in copies:
            copy.wait_send()

    stage(value, first, s_one, r_one, ours, near, y * 2 + k,
          lambda dy, dk: place.moved("y", dy) * 2 + lax.rem(k + dk, 2))
    held[...] = jnp.sum(first[...], axis=0)
    stage(held, second, s_two, r_two, theirs, far, z * 4 + x,
          lambda dz, dx: place.moved("z", dz) * 4 + place.moved("x", dx))
    result[...] = jnp.sum(second[...], axis=0)


def sum_all(value):
    return pl.pallas_call(
        sum_kernel,
        out_shape=jax.ShapeDtypeStruct((24, 128), F32),
        in_specs=[vmem],
        out_specs=vmem,
        scratch_shapes=[
            pltpu.VMEM((8, 24, 128), F32),
            pltpu.VMEM((16, 24, 128), F32),
            pltpu.VMEM((24, 128), F32),
            dma(7), dma(8), dma(15), dma(16),
        ],
        compiler_params=params(5),
        name="sum_squares",
    )(value)


TILE = 256
SEQ = 4 * ROWS
BLOCK = ROWS // 2
OWN_HEADS = HEADS // 4
OWN_KV = KV_HEADS // 4
LOG2E = 1.4426950408889634


def turn(value_rows):
    return pltpu.roll(value_rows, HEAD_WIDTH // 2, 1)


def head_norm(raw):
    scale = lax.rsqrt(jnp.mean(raw * raw, axis=-1, keepdims=True) + norm_eps)
    return raw * scale, scale


def pair_of(ref, order, tile):
    return jnp.concatenate([ref[order[2 * tile]], ref[order[2 * tile + 1]]], axis=0)


def dot_nt(left, right):
    return lax.dot_general(left, right, (((1,), (1,)), ((), ())), preferred_element_type=F32)


def dot_nn(left, right):
    return jnp.dot(left, right, preferred_element_type=F32)


def causal(scores):
    keys = lax.broadcasted_iota(jnp.int32, scores.shape, 0)
    queries = lax.broadcasted_iota(jnp.int32, scores.shape, 1)
    return jnp.where(keys <= queries, scores, masked_score)


def project(stored, tok, wq, g_attn, g_query, g_key, cosine, sine, hidden, raw, query, key, key_t, value, value_t):
    @pl.loop(0, SEQ // TILE)
    def _(t):
        at = pl.ds(pl.multiple_of(t * TILE, TILE), TILE)
        rows = pair_of(tok, stored, t).astype(F32)
        scale = lax.rsqrt(jnp.mean(rows * rows, axis=-1, keepdims=True) + norm_eps)
        hid = (rows * scale * g_attn[...]).astype(BF)
        hidden[at] = hid
        cos_t, sin_t = cosine[at], sine[at]
        for h in range(OWN_HEADS):
            part = dot_nn(hid, wq[:, 128 * h : 128 * h + 128])
            raw[h, at] = part
            normed = head_norm(part)[0] * g_query[...]
            query[h, at] = (normed * cos_t + turn(normed) * sin_t).astype(BF)
        for h in range(OWN_KV):
            part = dot_nn(hid, wq[:, 512 + 128 * h : 640 + 128 * h])
            raw[OWN_HEADS + h, at] = part
            normed = head_norm(part)[0] * g_key[...]
            rotated = normed * cos_t + turn(normed) * sin_t
            key[h, at] = rotated.astype(BF)
            key_t[h, :, at] = rotated.T.astype(BF)
            part = dot_nn(hid, wq[:, 768 + 128 * h : 896 + 128 * h])
            value[h, at] = part.astype(BF)
            value_t[h, :, at] = part.T.astype(BF)


def attend(query, key, value_t, attended, attended_t, log_total):
    factor = HEAD_WIDTH ** (-0.5) * LOG2E

    @pl.loop(0, OWN_HEADS)
    def _(h):
        kv = lax.div(h, 2)
        for t in range(SEQ // TILE):
            low, high = t * TILE, (t + 1) * TILE
            q = query[h, low:high]
            scores = [causal(dot_nt(key[kv, low:high], q))]
            if t:
                scores.append(dot_nt(key[kv, 0:low], q))
            top = jnp.max(scores[0], axis=0, keepdims=True)
            if t:
                top = jnp.maximum(top, jnp.max(scores[1], axis=0, keepdims=True))
            top = top * factor
            probs = [jnp.exp2(s * factor - top) for s in scores]
            total = jnp.sum(probs[0], axis=0, keepdims=True)
            mixed = dot_nn(value_t[kv, :, low:high], probs[0].astype(BF))
            if t:
                total = total + jnp.sum(probs[1], axis=0, keepdims=True)
                mixed = mixed + dot_nn(value_t[kv, :, 0:low], probs[1].astype(BF))
            mixed = mixed * (1.0 / total)
            attended_t[h, :, low:high] = mixed.astype(BF)
            attended[h, low:high] = mixed.T.astype(BF)
            log_total[h, :, low:high] = jnp.broadcast_to(top + jnp.log2(total), (8, TILE))


def heads_of(ref, count, at):
    return jnp.concatenate([ref[h, at] for h in range(count)], axis=1)


def block_rows(block):
    return pl.ds(pl.multiple_of(block * BLOCK, BLOCK), BLOCK)


def forward_kernel(
    span, stored, tok, wq, wo, g_attn, g_query, g_key, cosine, sine,
    terms, hidden, raw, query, key, key_t, value, attended, attended_t, log_total, value_t,
):
    project(stored, tok, wq, g_attn, g_query, g_key, cosine, sine, hidden, raw, query, key, key_t, value, value_t)
    attend(query, key, value_t, attended, attended_t, log_total)

    @pl.loop(0, 4)
    def _(i):
        rows = jnp.concatenate(
            [heads_of(attended, OWN_HEADS, block_rows(span[2 * i + n])) for n in range(2)], axis=0
        )
        terms[i] = dot_nn(rows, wo[...]).astype(BF)


smem = pl.BlockSpec(memory_space=pltpu.SMEM)


def local_params():
    return pltpu.CompilerParams(vmem_limit_bytes=VMEM_LIMIT)


def attention_forward(span, stored, tok, wq, wo, g_attn, g_query, g_key, cosine, sine):
    shape = jax.ShapeDtypeStruct
    return pl.pallas_call(
        forward_kernel,
        out_shape=(
            shape((4, ROWS, D), BF),
            shape((SEQ, D), BF),
            shape((OWN_HEADS + OWN_KV, SEQ, HEAD_WIDTH), F32),
            shape((OWN_HEADS, SEQ, HEAD_WIDTH), BF),
            shape((OWN_KV, SEQ, HEAD_WIDTH), BF),
            shape((OWN_KV, HEAD_WIDTH, SEQ), BF),
            shape((OWN_KV, SEQ, HEAD_WIDTH), BF),
            shape((OWN_HEADS, SEQ, HEAD_WIDTH), BF),
            shape((OWN_HEADS, HEAD_WIDTH, SEQ), BF),
            shape((OWN_HEADS, 8, SEQ), F32),
        ),
        in_specs=[smem] * 2 + [vmem] * 8,
        out_specs=(vmem,) * 10,
        scratch_shapes=[pltpu.VMEM((OWN_KV, HEAD_WIDTH, SEQ), BF)],
        compiler_params=local_params(),
        name="attention_forward",
    )(span, stored, tok, wq, wo, g_attn, g_query, g_key, cosine, sine)


def attend_back(query, key, key_t, value, d_attended, log_total, d_query, d_key, d_value):
    factor = HEAD_WIDTH ** (-0.5) * LOG2E
    plain = HEAD_WIDTH ** (-0.5)
    d_key[...] = jnp.zeros_like(d_key)
    d_value[...] = jnp.zeros_like(d_value)

    @pl.loop(0, OWN_HEADS)
    def _(h):
        kv = lax.div(h, 2)
        for t in range(SEQ // TILE):
            low, high = t * TILE, (t + 1) * TILE
            q = query[h, low:high]
            da = d_attended[h, low:high]
            total = log_total[h, 0:1, low:high]
            spans = [(low, high)] + ([(0, low)] if t else [])
            probs, mixes = [], []
            for n, (first, last) in enumerate(spans):
                scores = dot_nt(key[kv, first:last], q)
                if n == 0:
                    scores = causal(scores)
                p = jnp.exp2(scores * factor - total)
                d_value[kv, first:last] += dot_nn(p.astype(BF), da)
                probs.append(p)
                mixes.append(p * dot_nt(value[kv, first:last], da))
            delta = jnp.sum(mixes[0], axis=0, keepdims=True)
            if t:
                delta = delta + jnp.sum(mixes[1], axis=0, keepdims=True)
            back = None
            for (first, last), p, mix in zip(spans, probs, mixes):
                ds = (mix - p * delta).astype(BF)
                d_key[kv, first:last] += dot_nn(ds, q)
                part = dot_nn(key_t[kv, :, first:last], ds)
                back = part if back is None else back + part
            d_query[h, low:high] = (back * plain).T


def backward_kernel(
    span, stored, d_attn, wq, wo, g_query, g_key, cosine, sine,
    raw, query, key, key_t, value, log_total,
    terms, d_sorted, d_proj, gain_grads,
    d_attended, d_query, d_key, d_value,
):
    plain = HEAD_WIDTH ** (-0.5)

    @pl.loop(0, SEQ // TILE)
    def _(t):
        at = pl.ds(pl.multiple_of(t * TILE, TILE), TILE)
        rows = pair_of(d_attn, stored, t)
        d_sorted[at] = rows
        for h in range(OWN_HEADS):
            d_attended[h, at] = dot_nt(rows, wo[128 * h : 128 * h + 128]).astype(BF)

    attend_back(query, key, key_t, value, d_attended, log_total, d_query, d_key, d_value)
    gain_grads[...] = jnp.zeros_like(gain_grads)

    @pl.loop(0, SEQ // TILE)
    def _(t):
        at = pl.ds(pl.multiple_of(t * TILE, TILE), TILE)
        cos_t, sin_t = cosine[at], sine[at]
        for h in range(OWN_HEADS + OWN_KV):
            mine = h < OWN_HEADS
            d_rows = d_query[h, at] if mine else d_key[h - OWN_HEADS, at] * plain
            gain = g_query if mine else g_key
            d_gained = d_rows * cos_t - turn(d_rows) * sin_t
            normed, scale = head_norm(raw[h, at])
            product = d_gained * normed
            which = 0 if mine else 1
            gain_grads[which] += jnp.sum(product.reshape(TILE // 8, 8, HEAD_WIDTH), axis=0)
            incoming = d_gained * gain[...]
            mean = jnp.mean(incoming * normed, axis=-1, keepdims=True)
            d_proj[at, 128 * h : 128 * h + 128] = (scale * (incoming - normed * mean)).astype(BF)
        for h in range(OWN_KV):
            d_proj[at, 768 + 128 * h : 896 + 128 * h] = d_value[h, at].astype(BF)

    @pl.loop(0, 4)
    def _(i):
        rows = jnp.concatenate([d_proj[block_rows(span[2 * i + n])] for n in range(2)], axis=0)
        terms[i] = dot_nt(rows, wq[:, 0:D]).astype(BF)


def attention_backward(span, stored, d_attn, wq, wo, g_query, g_key, cosine, sine, raw, query, key, key_t, value, log_total):
    shape = jax.ShapeDtypeStruct
    return pl.pallas_call(
        backward_kernel,
        out_shape=(
            shape((4, ROWS, D), BF),
            shape((SEQ, D), BF),
            shape((SEQ, D), BF),
            shape((2, 8, HEAD_WIDTH), F32),
        ),
        in_specs=[smem] * 2 + [vmem] * 13,
        out_specs=(vmem,) * 4,
        scratch_shapes=[
            pltpu.VMEM((OWN_HEADS, SEQ, HEAD_WIDTH), BF),
            pltpu.VMEM((OWN_HEADS, SEQ, HEAD_WIDTH), F32),
            pltpu.VMEM((OWN_KV, SEQ, HEAD_WIDTH), F32),
            pltpu.VMEM((OWN_KV, SEQ, HEAD_WIDTH), F32),
        ],
        compiler_params=local_params(),
        name="attention_backward",
    )(span, stored, d_attn, wq, wo, g_query, g_key, cosine, sine, raw, query, key, key_t, value, log_total)


def rms_parts(value_rows):
    factor = lax.rsqrt(jnp.mean(value_rows * value_rows, axis=-1, keepdims=True) + norm_eps)
    return (value_rows * factor, factor)


def rms_back(incoming, normed, factor):
    return factor * (incoming - normed * jnp.mean(incoming * normed, axis=-1, keepdims=True))


def rope_tables():
    middle = HEAD_WIDTH // 2
    frequency = rope_base ** (-(np.arange(middle) * 2.0) / HEAD_WIDTH)
    angle = np.arange(SEQ)[:, None] * frequency[None, :]
    cosine, sine = np.cos(angle), np.sin(angle)
    return (
        jnp.asarray(np.concatenate([cosine, cosine], axis=1), F32),
        jnp.asarray(np.concatenate([-sine, sine], axis=1), F32),
    )


def contract_rows(left, right):
    return lax.dot_general(
        left, right, (((0,), (0,)), ((), ())), preferred_element_type=jnp.float32
    )


def contract_cols(left, right):
    return lax.dot_general(
        left, right, (((1,), (1,)), ((), ())), preferred_element_type=jnp.float32
    )


def adam_update(weight, first, second, grad, factor, rate, decay):
    clipped = grad * factor
    new_first = beta_one * first + (1.0 - beta_one) * clipped
    new_second = beta_two * second + (1.0 - beta_two) * clipped * clipped
    direction = (
        new_first
        / (1.0 - beta_one**STEP)
        / (jnp.sqrt(new_second / (1.0 - beta_two**STEP)) + adam_eps)
    )
    return (weight - rate * (direction + decay * weight), new_first, new_second)


def pack_gateup(w):
    rows = w.shape[0]
    v = w.reshape(rows, 2, 16, 2, 96).transpose(3, 0, 1, 2, 4).reshape(2, rows, 2, 3, 512)
    return v.transpose(0, 3, 1, 2, 4).reshape(2, 3, rows, 1024)


def unpack_gateup(v):
    rows = v.shape[2]
    w = v.reshape(2, 3, rows, 2, 512).transpose(0, 2, 3, 1, 4).reshape(2, rows, 2, 16, 96)
    return w.transpose(1, 2, 3, 0, 4).reshape(rows, 2 * FF)


def body(
    tokens, cotangent, span_order,
    w_qkv, w_out, w_gateup, w_down, gains,
    first_qkv, first_out, first_gateup, first_down, first_gains,
    second_qkv, second_out, second_gateup, second_down, second_gains,
):
    own_gains = jnp.pad(gains[None, :], ((0, 7), (0, 128 - gains.shape[0])))
    tok_all, wq_all, wo_all, w_part = gather_all(
        tokens, w_qkv, w_out, pack_gateup(w_gateup), w_down, own_gains
    )
    wq_all = wq_all.reshape(D, 1152)
    wo_all = wo_all.reshape(OWN_HEADS * HEAD_WIDTH, D)
    gain_values = wq_all.reshape(128, 8, 1152)[:, 0, D : D + 18].reshape(1, -1).astype(F32)
    g_attn = gain_values[:, :D]
    g_mlp = gain_values[:, D : 2 * D]
    g_query = gain_values[:, 2 * D : 2 * D + HEAD_WIDTH]
    g_key = gain_values[:, 2 * D + HEAD_WIDTH :]
    block = jnp.arange(8, dtype=jnp.int32)
    stored = jnp.sum(jnp.where(span_order[None, :] == block[:, None], block[None, :], 0), axis=1)
    cosine, sine = rope_tables()
    terms, hidden, raw, query, key, key_t, value, _, attended_t, log_total = attention_forward(
        span_order, stored, tok_all.reshape(8, BLOCK, D), wq_all, wo_all,
        g_attn, g_query, g_key, cosine, sine,
    )
    middle, hidden_pair, cot_pair, w_all = middle_step(
        terms, tokens, cotangent, g_mlp, w_part
    )

    hidden2 = hidden_pair.reshape(2 * ROWS, D)
    cot = cot_pair.reshape(2 * ROWS, D)
    w_all = w_all.reshape(16, UNIT, D)
    w_down_half = w_all[:, 192:].reshape(1536, D)
    out_part = jnp.zeros((2 * ROWS, D), F32)
    dh_part = jnp.zeros((2 * ROWS, D), F32)
    d_w = []
    d_downs = []
    for b in range(3):
        w_gu = w_all[:, 64 * b : 64 * b + 64].reshape(D, D)
        w_dn = w_down_half[512 * b : 512 * b + 512]
        gate_up = jnp.dot(hidden2, w_gu, preferred_element_type=F32)
        gate, up = gate_up[:, :512], gate_up[:, 512:]
        sigmoid = jax.nn.sigmoid(gate)
        active = gate * sigmoid
        product = (active * up).astype(BF)
        out_part += jnp.dot(product, w_dn, preferred_element_type=F32)
        d_downs.append(contract_rows(product, cot).astype(BF))
        d_product = contract_cols(cot, w_dn)
        d_gate = d_product * up * sigmoid * (1.0 + gate * (1.0 - sigmoid))
        d_gate_up = jnp.concatenate([d_gate, d_product * active], axis=1).astype(BF)
        d_w.append(contract_rows(hidden2, d_gate_up).astype(BF).reshape(16, 64, D))
        dh_part += contract_cols(d_gate_up, w_gu)
    d_w.append(jnp.concatenate(d_downs, axis=0).reshape(16, 96, D))
    d_w = jnp.concatenate(d_w, axis=1).reshape(4, 4, UNIT, D)

    layer_output, d_middle, d_attn_all, mlp_gain, a_one, b_one = back_step(
        out_part[:ROWS], out_part[ROWS:].astype(BF), dh_part[:ROWS], dh_part[ROWS:].astype(BF),
        middle, cotangent, g_mlp, d_w,
    )

    dh_terms, d_attn, d_projected, head_gains = attention_backward(
        span_order, stored, d_attn_all.reshape(8, BLOCK, D), wq_all, wo_all,
        g_query, g_key, cosine, sine, raw, query, key, key_t, value, log_total,
    )
    grad_out = jnp.dot(
        attended_t.reshape(OWN_HEADS * HEAD_WIDTH, SEQ), d_attn, preferred_element_type=F32
    ).astype(BF)
    grad_qkv = contract_rows(hidden, d_projected).astype(BF)
    d_hidden, q_grad, o_grad, gu_grad, down_grad = owner_step(
        dh_terms, grad_qkv.reshape(4, 4, 2, 32, D), grad_out.reshape(4, 2, 64, D), a_one, b_one
    )
    own_normed, own_scale = rms_parts(tokens.astype(F32))
    grad_attn_gain = jnp.sum(d_hidden * own_normed, axis=0)
    input_grad = d_middle + rms_back(d_hidden * g_attn, own_normed, own_scale)

    q_shard = jnp.concatenate(
        [
            q_grad[:, :, :512].transpose(1, 0, 2).reshape(8, 2048),
            q_grad[:, :, 512:768].transpose(1, 0, 2).reshape(8, 1024),
            q_grad[:, :, 768:].transpose(1, 0, 2).reshape(8, 1024),
        ],
        axis=1,
    )
    shards = [q_shard, o_grad, unpack_gateup(gu_grad), down_grad]
    squares = jnp.float32(0.0)
    for shard in (q_grad, o_grad, gu_grad, down_grad):
        squares = squares + jnp.sum(shard * shard)
    grad_gains = jnp.concatenate(
        [grad_attn_gain, jnp.sum(mlp_gain, axis=0), jnp.sum(head_gains, axis=1).reshape(-1)]
    )
    extra = jnp.zeros((6, 128), F32).at[0, 0].set(squares)
    sums = sum_all(jnp.concatenate([grad_gains.reshape(18, 128), extra], axis=0))
    all_gains = sums[:18].reshape(-1)
    grad_norm = jnp.sqrt(sums[18, 0] + jnp.sum(all_gains * all_gains))
    index = lax.axis_index("dp") * 4 + lax.axis_index("ctx")
    shards.append(lax.dynamic_slice_in_dim(all_gains, index * 18, 18))

    factor = jnp.minimum(1.0, clip_at / (grad_norm + 1e-06))
    masters = (w_qkv, w_out, w_gateup, w_down, gains)
    firsts = (first_qkv, first_out, first_gateup, first_down, first_gains)
    seconds = (second_qkv, second_out, second_gateup, second_down, second_gains)
    rates = (matrix_rate, out_rate, matrix_rate, matrix_rate, gain_rate)
    decays = (matrix_decay, matrix_decay, matrix_decay, matrix_decay, 0.0)
    news, new_firsts, new_seconds = [], [], []
    for which in range(5):
        weight, first, second = adam_update(
            masters[which], firsts[which], seconds[which], shards[which], factor,
            rates[which], decays[which],
        )
        news.append(weight)
        new_firsts.append(first)
        new_seconds.append(second)
    return (layer_output, input_grad, *news, *new_firsts, *new_seconds, grad_norm)


def solution(mesh):
    rows, flat = P(("dp", "ctx"), None), P(("dp", "ctx"))
    state = (rows, rows, rows, rows, flat)
    in_specs = (rows, rows, P()) + state * 3
    out_specs = (rows, rows) + state * 3 + (P(),)
    return jax.shard_map(body, mesh=mesh, in_specs=in_specs, out_specs=out_specs, check_vma=False)
```

```python
import jax
import jax.numpy as jnp
import numpy as np
from jax import lax
from jax.experimental import pallas as pl
from jax.experimental.pallas import tpu as pltpu
from jax.sharding import PartitionSpec as P

D = 1024
HEADS = 16
KV_HEADS = 8
HEAD_WIDTH = 128
FF = 3072
STEP = 10

norm_eps = 1e-06
rope_base = 1000000.0
beta_one = 0.9
beta_two = 0.999
adam_eps = 1e-08
clip_at = 1.0
matrix_rate = 0.05
out_rate = 0.25
matrix_decay = 0.1
gain_rate = 0.5
masked_score = -1e30

MESH = pl.DeviceIdType.MESH
BF = jnp.bfloat16
F32 = jnp.float32
ROWS = 256
UNIT = 288
PART_A = 144
VMEM_LIMIT = 62 * 2**20
vmem = pl.BlockSpec(memory_space=pltpu.VMEM)
hbm = pl.BlockSpec(memory_space=pl.ANY)


class Place:
    def __init__(self):
        dp = lax.axis_index("dp")
        self.at = {
            "z": lax.div(dp, 8),
            "x": lax.rem(lax.div(dp, 2), 4),
            "k": lax.rem(dp, 2),
            "y": lax.axis_index("ctx"),
        }

    def __getitem__(self, axis):
        return self.at[axis]

    def device(self, **other):
        c = {**self.at, **other}
        return (c["z"] * 8 + c["x"] * 2 + c["k"], c["y"])

    def moved(self, axis, steps):
        return lax.rem(self.at[axis] + steps, 4)

    def peer(self, axis, steps):
        return self.device(**{axis: self.moved(axis, steps)})

    def sibling(self):
        return self.device(k=1 - self.at["k"])


def greet(devices):
    barrier = pltpu.get_barrier_semaphore()
    for device in devices:
        pl.semaphore_signal(barrier, inc=1, device_id=device, device_id_type=MESH)


def await_greetings(count):
    pl.semaphore_wait(pltpu.get_barrier_semaphore(), count)


def neighbours(place, axes):
    found = []
    for axis in axes:
        if axis == "k":
            found.append(place.sibling())
        else:
            found += [place.peer(axis, 1), place.peer(axis, 3)]
    return found


def remote(src, dst, send, recv, device):
    return pltpu.make_async_remote_copy(
        src_ref=src, dst_ref=dst, send_sem=send, recv_sem=recv, device_id=device, device_id_type=MESH
    )


class Gather:
    def __init__(self, place, axis, part, sems, own=None):
        self.part, self.send, self.recv = part, sems[0], sems[1]
        self.own = own or (lambda half: part(place[axis], half))
        self.next, self.prev = place.peer(axis, 1), place.peer(axis, 3)
        self.me, self.up, self.down, self.far = (place.moved(axis, n) for n in (0, 1, 3, 2))

    def copy(self, n, slot, half, device, src=None):
        view = self.part(slot, half)
        return remote(src if src is not None else view, view, self.send.at[n], self.recv.at[n], device)

    def outgoing(self, n):
        slot, half, device = [
            (self.me, 0, self.next),
            (self.me, 1, self.prev),
            (self.me, 1, self.next),
            (self.me, 0, self.prev),
            (self.down, 0, self.next),
            (self.up, 1, self.prev),
        ][n]
        return self.copy(n, slot, half, device, self.own(half) if n < 4 else None)

    def start(self):
        for n in range(4):
            self.outgoing(n).start()

    def forward(self):
        self.copy(0, self.down, 0, self.prev).wait_recv()
        self.outgoing(4).start()
        self.copy(1, self.up, 1, self.next).wait_recv()
        self.outgoing(5).start()

    def finish(self):
        self.copy(2, self.down, 1, self.prev).wait_recv()
        self.copy(3, self.up, 0, self.next).wait_recv()
        self.copy(4, self.far, 0, self.prev).wait_recv()
        self.copy(5, self.far, 1, self.next).wait_recv()
        for n in range(6):
            self.outgoing(n).wait_send()


class Scatter:
    def __init__(self, place, axis, part, boxes, sems, mine=None):
        self.part, self.boxes = part, boxes
        self.send, self.recv = sems[0], sems[1]
        self.next, self.prev = place.peer(axis, 1), place.peer(axis, 3)
        self.me, self.up, self.down, self.far = (place.moved(axis, n) for n in (0, 1, 3, 2))
        self.mine = mine or self.own_part

    def own_part(self, n):
        slot, half = [(self.down, 0), (self.up, 1), (self.me, 0), (self.me, 1)][n]
        return self.part(slot, half)

    def copy(self, n, src, device):
        return remote(src, self.boxes[n], self.send.at[n], self.recv.at[n], device)

    def outgoing(self, n):
        source, device = [
            (lambda: self.part(self.far, 0), self.prev),
            (lambda: self.part(self.far, 1), self.next),
            (lambda: self.part(self.down, 1), self.prev),
            (lambda: self.part(self.up, 0), self.next),
            (lambda: self.boxes[0], self.prev),
            (lambda: self.boxes[1], self.next),
        ][n]
        return self.copy(n, source(), device)

    def start(self):
        for n in range(4):
            self.outgoing(n).start()

    def forward(self):
        for n in range(2):
            self.outgoing(n).wait_recv()
            add_rows(self.boxes[n], [self.boxes[n], self.mine(n)])
            self.outgoing(4 + n).start()

    def finish(self, result):
        for n in (2, 3, 4, 5):
            self.outgoing(n).wait_recv()
        add_rows(result(0), [self.mine(2), self.boxes[3], self.boxes[4]])
        add_rows(result(1), [self.mine(3), self.boxes[2], self.boxes[5]])
        for n in range(6):
            self.outgoing(n).wait_send()


def add_rows(out, terms):
    shape = out.shape
    rows = shape[-2]

    def block(at):
        total = terms[0][at].astype(F32)
        for term in terms[1:]:
            total = total + term[at].astype(F32)
        out[at] = total.astype(out.dtype)

    if len(shape) == 2:

        @pl.loop(0, rows // 16)
        def _(r):
            block((pl.ds(pl.multiple_of(r * 16, 16), 16), slice(None)))

    else:

        @pl.loop(0, shape[0])
        def _(lead):
            @pl.loop(0, rows // 16)
            def _(r):
                block((lead, pl.ds(pl.multiple_of(r * 16, 16), 16), slice(None)))


def dma(*shape):
    return pltpu.SemaphoreType.DMA(shape)


def ring_sems():
    return [dma(6), dma(6)]


def params(which):
    return pltpu.CompilerParams(
        collective_id=which, has_side_effects=True, vmem_limit_bytes=VMEM_LIMIT
    )


TILE = 256
SEQ = 4 * ROWS
BLOCK = ROWS // 2
OWN_HEADS = HEADS // 4
OWN_KV = KV_HEADS // 4
LOG2E = 1.4426950408889634


def turn(value_rows):
    return pltpu.roll(value_rows, HEAD_WIDTH // 2, 1)


def head_norm(raw):
    scale = lax.rsqrt(jnp.mean(raw * raw, axis=-1, keepdims=True) + norm_eps)
    return raw * scale, scale


def pair_of(ref, order, tile):
    return jnp.concatenate([ref[order[2 * tile]], ref[order[2 * tile + 1]]], axis=0)


def dot_nt(left, right):
    return lax.dot_general(left, right, (((1,), (1,)), ((), ())), preferred_element_type=F32)


def dot_nn(left, right):
    return jnp.dot(left, right, preferred_element_type=F32)


def causal(scores):
    keys = lax.broadcasted_iota(jnp.int32, scores.shape, 0)
    queries = lax.broadcasted_iota(jnp.int32, scores.shape, 1)
    return jnp.where(keys <= queries, scores, masked_score)


def project(r, g_attn, g_query, g_key):
    stored, tok, cosine, sine = r.stored, r.tok_all, r.cosine, r.sine
    hidden, raw, query, key, key_t = r.hidden, r.raw, r.query, r.key, r.key_t
    value, value_t = r.value, r.value_t

    def columns(pair):
        return r.wq_all[:, :, :, :, 256 * pair : 256 * pair + 256].reshape(D, 256)

    @pl.loop(0, SEQ // TILE)
    def _(t):
        at = pl.ds(pl.multiple_of(t * TILE, TILE), TILE)
        rows = pair_of(tok, stored, t).astype(F32)
        scale = lax.rsqrt(jnp.mean(rows * rows, axis=-1, keepdims=True) + norm_eps)
        hid = (rows * scale * g_attn[...]).astype(BF)
        hidden[at] = hid
        cos_t, sin_t = cosine[at], sine[at]
        for pair in range(OWN_HEADS // 2):
            both = dot_nn(hid, columns(pair))
            for n in range(2):
                h, part = 2 * pair + n, both[:, 128 * n : 128 * n + 128]
                raw[h, at] = part
                normed = head_norm(part)[0] * g_query[...]
                query[h, at] = (normed * cos_t + turn(normed) * sin_t).astype(BF)
        both = dot_nn(hid, columns(2))
        for h in range(OWN_KV):
            part = both[:, 128 * h : 128 * h + 128]
            raw[OWN_HEADS + h, at] = part
            normed = head_norm(part)[0] * g_key[...]
            rotated = normed * cos_t + turn(normed) * sin_t
            key[h, at] = rotated.astype(BF)
            key_t[h, :, at] = rotated.T.astype(BF)
        both = dot_nn(hid, columns(3))
        for h in range(OWN_KV):
            part = both[:, 128 * h : 128 * h + 128]
            value[h, at] = part.astype(BF)
            value_t[h, :, at] = part.T.astype(BF)


def attend(r, first_head, last_head):
    query, key, value_t, attended = r.query, r.key, r.value_t, r.attended
    attended_t, log_total = r.attended_t, r.log_total
    factor = HEAD_WIDTH ** (-0.5) * LOG2E

    @pl.loop(first_head, last_head)
    def _(h):
        kv = lax.div(h, 2)
        for t in range(SEQ // TILE):
            low, high = t * TILE, (t + 1) * TILE
            q = query[h, low:high]
            scores = [causal(dot_nt(key[kv, low:high], q))]
            if t:
                scores.append(dot_nt(key[kv, 0:low], q))
            top = jnp.max(scores[0], axis=0, keepdims=True)
            if t:
                top = jnp.maximum(top, jnp.max(scores[1], axis=0, keepdims=True))
            top = top * factor
            probs = [jnp.exp2(s * factor - top) for s in scores]
            total = jnp.sum(probs[0], axis=0, keepdims=True)
            mixed = dot_nn(value_t[kv, :, low:high], probs[0].astype(BF))
            if t:
                total = total + jnp.sum(probs[1], axis=0, keepdims=True)
                mixed = mixed + dot_nn(value_t[kv, :, 0:low], probs[1].astype(BF))
            mixed = mixed * (1.0 / total)
            attended_t[h, :, low:high] = mixed.astype(BF)
            attended[h, 2 * t : 2 * t + 2] = mixed.T.astype(BF).reshape(2, BLOCK, HEAD_WIDTH)
            log_total[h, :, low:high] = jnp.broadcast_to(top + jnp.log2(total), (8, TILE))


def attend_back(r, first_head, last_head):
    query, key, key_t, value = r.query, r.key, r.key_t, r.value
    d_attended, log_total, d_query = r.d_attended, r.log_total, r.d_query
    d_key, d_value = r.d_key, r.d_value
    factor = HEAD_WIDTH ** (-0.5) * LOG2E
    plain = HEAD_WIDTH ** (-0.5)

    @pl.loop(first_head, last_head)
    def _(h):
        kv = lax.div(h, 2)
        for t in range(SEQ // TILE):
            low, high = t * TILE, (t + 1) * TILE
            q = query[h, low:high]
            da = d_attended[h, low:high]
            total = log_total[h, 0:1, low:high]
            spans = [(low, high)] + ([(0, low)] if t else [])
            probs, mixes = [], []
            for n, (first, last) in enumerate(spans):
                scores = dot_nt(key[kv, first:last], q)
                if n == 0:
                    scores = causal(scores)
                p = jnp.exp2(scores * factor - total)
                d_value[kv, first:last] += dot_nn(p.astype(BF), da)
                probs.append(p)
                mixes.append(p * dot_nt(value[kv, first:last], da))
            delta = jnp.sum(mixes[0], axis=0, keepdims=True)
            if t:
                delta = delta + jnp.sum(mixes[1], axis=0, keepdims=True)
            back = None
            for (first, last), p, mix in zip(spans, probs, mixes):
                ds = (mix - p * delta).astype(BF)
                d_key[kv, first:last] += dot_nn(ds, q)
                part = dot_nn(key_t[kv, :, first:last], ds)
                back = part if back is None else back + part
            d_query[h, low:high] = (back * plain).T


GAINS = 2 * D + 2 * HEAD_WIDTH
smem = pl.BlockSpec(memory_space=pltpu.SMEM)
regular = pltpu.SemaphoreType.DMA


class Names:
    def __init__(self, names, refs):
        self.__dict__.update(zip(names, refs))


def named_call(kernel, which, name, given, spaces, outputs, scratch):
    names = list(given) + ["out_" + n for n in outputs] + list(scratch)
    results = pl.pallas_call(
        lambda *refs: kernel(Names(names, refs)),
        out_shape=tuple(jax.ShapeDtypeStruct(shape, kind) for shape, kind, _ in outputs.values()),
        in_specs=[spaces.get(n, vmem) for n in given],
        out_specs=tuple(space for _, _, space in outputs.values()),
        scratch_shapes=list(scratch.values()),
        compiler_params=params(which),
        name=name,
    )(*given.values())
    return dict(zip(outputs, results))


SAVED = {
    "wq_all": ((4, 4, 2, 32, 1152), BF),
    "wo_all": ((4, 2, 64, D), BF),
    "hidden": ((SEQ, D), BF),
    "raw": ((OWN_HEADS + OWN_KV, SEQ, HEAD_WIDTH), F32),
    "query": ((OWN_HEADS, SEQ, HEAD_WIDTH), BF),
    "key": ((OWN_KV, SEQ, HEAD_WIDTH), BF),
    "key_t": ((OWN_KV, HEAD_WIDTH, SEQ), BF),
    "value": ((OWN_KV, SEQ, HEAD_WIDTH), BF),
    "attended_t": ((OWN_HEADS, HEAD_WIDTH, SEQ), BF),
    "log_total": ((OWN_HEADS, 8, SEQ), F32),
}


def heads_of(ref, count, at):
    return jnp.concatenate([ref[h, at] for h in range(count)], axis=1)


def row_tile(r, size):
    return pl.ds(pl.multiple_of(r * size, size), size)


def from_to(half, low, split, high):
    return pl.ds(low, split - low) if half == 0 else pl.ds(split, high - split)


def not_here(condition, other, coordinate):
    return jnp.logical_not(jnp.logical_and(condition, coordinate == other))


def forward_kernel(r):
    place = Place()
    z, x, k, y = (place[a] for a in "zxky")
    near = neighbours(place, "xyzk")
    diagonal = z == y
    greet(near + [place.peer("y", 2)])
    for other in range(4):

        @pl.when(not_here(diagonal, other, y))
        def _():
            greet([place.device(z=y, y=jnp.int32(other))])

    for i in range(4):
        r.q_send[i, :, 0:512] = r.wq[:, 512 * i : 512 * i + 512]
        r.q_send[i, :, 512:768] = r.wq[:, 2048 + 256 * i : 2304 + 256 * i]
        r.q_send[i, :, 768:1024] = r.wq[:, 3072 + 256 * i : 3328 + 256 * i]
        r.q_send[i, :, 1024:1152] = r.gains[...]
    r.q_recv[y] = r.q_send[y]
    r.o_send[...] = r.wo[...].astype(BF)
    r.tok_all[pl.ds(2 * y, 2)] = r.tok[...].reshape(2, BLOCK, D)
    r.out_cot_pair[0] = r.cot[...]
    await_greetings(len(near) + 1 + jnp.where(diagonal, 3, 4))

    g_prep = remote(r.wgu.at[1 - k], r.g_recv, r.pair.at[0], r.pair.at[1], place.sibling())
    g_prep.start()
    q_prep = [
        remote(r.q_send.at[place.moved("y", n)], r.q_recv.at[y], r.qp_s.at[n], r.qp_r.at[y], place.peer("y", n))
        for n in (1, 3, 2)
    ]
    for copy in q_prep:
        copy.start()

    def o_slot(source):
        return r.wo_all.at[x, k, row_tile(source, 16)]

    for other in range(4):

        @pl.when(not_here(diagonal, other, z))
        def _():
            remote(r.o_send, o_slot(y), r.op_s.at[other], r.op_r.at[y], place.device(z=jnp.int32(other), y=z)).start()

    @pl.when(diagonal)
    def _():
        r.wo_all[x, k, row_tile(y, 16)] = r.o_send[...]

    cot_copy = remote(r.cot, r.out_cot_pair.at[1], r.pair.at[2], r.pair.at[3], place.sibling())
    cot_copy.start()

    g_prep.wait_recv()
    g_own, g_other, lower = r.wgu[k], r.g_recv[...], k == 0
    both = jnp.concatenate([jnp.where(lower, g_own, g_other), jnp.where(lower, g_other, g_own)], axis=1)
    r.g_y[y] = both.reshape(48, D).astype(BF)
    r.d_y[y] = r.wd[...]
    g_ring = Gather(place, "y", lambda i, h: r.g_y.at[i, from_to(h, 0, 32, 48)], (r.gy_s, r.gy_r))
    d_ring = Gather(place, "y", lambda i, h: r.d_y.at[i, from_to(h, 0, 16, 24)], (r.dy_s, r.dy_r))
    g_ring.start()
    d_ring.start()

    for n in (1, 3, 2):
        source = place.moved("y", n)
        remote(r.q_send.at[0], r.q_recv.at[source], r.qp_s.at[n], r.qp_r.at[source], place.peer("y", n)).wait_recv()
    r.wq_all[z, x, k] = r.q_recv[...].reshape(32, 1152).astype(BF)
    q_x = Gather(place, "x", lambda i, h: r.wq_all.at[z, i, k, pl.ds(16 * h, 16)], (r.qx_s, r.qx_r))
    q_x.start()
    tokens = Gather(place, "y", lambda i, h: r.tok_all.at[2 * i + h], (r.t_s, r.t_r))
    tokens.start()

    for other in range(4):

        @pl.when(not_here(diagonal, other, y))
        def _():
            remote(r.o_send, o_slot(other), r.op_s.at[0], r.op_r.at[other], place.device(z=y, y=jnp.int32(other))).wait_recv()

    o_x = Gather(place, "x", lambda i, h: r.wo_all.at[i, k, pl.ds(32 * h, 32)], (r.ox_s, r.ox_r))
    o_x.start()
    g_ring.forward()
    d_ring.forward()
    q_x.forward()
    q_x.finish()
    q_z = Gather(place, "z", lambda i, h: r.wq_all.at[i, pl.ds(2 * h, 2), k], (r.qz_s, r.qz_r))
    q_z.start()
    o_x.forward()
    g_ring.finish()
    d_ring.finish()

    for b in range(3):
        pieces = [r.g_y[c, 16 * b : 16 * b + 16].astype(F32) for c in range(4)]
        for core_row in range(2):
            rows = jnp.concatenate([piece[8 * core_row : 8 * core_row + 8] for piece in pieces], axis=0)
            at = 64 * b + 32 * core_row
            r.unit[at : at + 32] = rows.astype(BF)
    r.unit[192:288] = r.d_y[...].reshape(96, D).astype(BF)
    w_all = r.out_w_all
    u_own = pltpu.make_async_copy(r.unit, w_all.at[z, x], r.pair.at[4])
    u_own.start()
    a_one = Gather(
        place, "x", lambda i, h: w_all.at[z, i, from_to(h, 0, 80, PART_A)], (r.a1_s, r.a1_r),
        own=lambda h: r.unit.at[from_to(h, 0, 80, PART_A)],
    )
    b_one = Gather(
        place, "z", lambda i, h: w_all.at[i, x, from_to(h, PART_A, 208, UNIT)], (r.b1_s, r.b1_r),
        own=lambda h: r.unit.at[from_to(h, PART_A, 208, UNIT)],
    )
    a_one.start()
    b_one.start()
    tokens.forward()
    q_z.forward()
    o_x.finish()
    o_core = remote(r.wo_all.at[:, k], r.wo_all.at[:, k], r.core.at[0], r.core.at[1], place.sibling())
    o_core.start()
    a_one.forward()
    b_one.forward()
    q_z.finish()
    q_core = remote(r.wq_all.at[:, :, k], r.wq_all.at[:, :, k], r.core.at[2], r.core.at[3], place.sibling())
    q_core.start()
    a_one.finish()
    b_one.finish()
    u_own.wait()
    a_two = Gather(place, "z", lambda i, h: w_all.at[i, pl.ds(2 * h, 2), pl.ds(0, PART_A)], (r.a2_s, r.a2_r))
    b_two = Gather(place, "x", lambda i, h: w_all.at[pl.ds(2 * h, 2), i, pl.ds(PART_A, UNIT - PART_A)], (r.b2_s, r.b2_r))
    a_two.start()
    b_two.start()
    remote(r.wo_all.at[:, 1 - k], r.wo_all.at[:, 1 - k], r.core.at[0], r.core.at[1], place.sibling()).wait_recv()
    remote(r.wq_all.at[:, :, 1 - k], r.wq_all.at[:, :, 1 - k], r.core.at[2], r.core.at[3], place.sibling()).wait_recv()
    tokens.finish()

    lanes = r.wq_all[:, :, :, :, D:1152].reshape(128, 8, 128).astype(F32)
    spread = dot_nn(jnp.sum(lanes, axis=1).astype(BF), r.spread[...])
    owner = lax.broadcasted_iota(jnp.int32, (128, GAINS), 0) * 18
    spot = lax.broadcasted_iota(jnp.int32, (128, GAINS), 1)
    mine = jnp.logical_and(spot >= owner, spot < owner + 18)
    r.out_gain_row[...] = jnp.sum(jnp.where(mine, spread, 0.0), axis=0, keepdims=True)
    gain = r.out_gain_row
    project(r, gain.at[:, 0:D], gain.at[:, 2 * D : 2 * D + 128], gain.at[:, 2 * D + 128 : GAINS])
    attend(r, 0, 2)
    a_two.forward()
    b_two.forward()
    attend(r, 2, 4)

    wo = r.wo_all[...].reshape(OWN_HEADS * HEAD_WIDTH, D)

    @pl.loop(0, 4)
    def _(i):
        rows = jnp.concatenate(
            [heads_of(r.attended, OWN_HEADS, r.span[2 * i + n]) for n in range(2)], axis=0
        )
        r.terms[i] = dot_nn(rows, wo).astype(BF)

    reduce = Scatter(
        place, "y", lambda i, h: r.terms.at[i, pl.ds(128 * h, 128)],
        [r.boxes.at[n] for n in range(6)], (r.y_s, r.y_r),
    )
    reduce.start()
    saves = [
        pltpu.make_async_copy(getattr(r, n), getattr(r, "out_" + n), r.save.at[i]) for i, n in enumerate(SAVED)
    ]
    for copy in saves:
        copy.start()
    reduce.forward()
    reduce.finish(lambda h: r.total.at[pl.ds(128 * h, 128)])

    @pl.loop(0, ROWS // 16)
    def _(t):
        at = row_tile(t, 16)
        rows = r.tok[at].astype(F32) + r.total[at]
        r.out_middle[at] = rows
        scale = lax.rsqrt(jnp.mean(rows * rows, axis=-1, keepdims=True) + norm_eps)
        r.out_hidden_pair[0, at] = (rows * scale * gain[:, D : 2 * D]).astype(BF)

    hid_copy = remote(r.out_hidden_pair.at[0], r.out_hidden_pair.at[1], r.core.at[4], r.core.at[5], place.sibling())
    hid_copy.start()
    a_two.finish()
    b_two.finish()
    for copy in saves:
        copy.wait()
    for copy in q_prep + [g_prep, o_core, q_core]:
        copy.wait_send()
    cot_copy.wait()
    hid_copy.wait()
    for other in range(4):

        @pl.when(not_here(diagonal, other, z))
        def _():
            remote(r.o_send, o_slot(y), r.op_s.at[other], r.op_r.at[y], place.device(z=jnp.int32(other), y=z)).wait_send()


def rings(*names):
    return {f"{name}_{end}": dma(6) for name in names for end in "sr"}


def forward_step(**given):
    outputs = {
        "middle": ((ROWS, D), F32, vmem),
        "hidden_pair": ((2, ROWS, D), BF, vmem),
        "cot_pair": ((2, ROWS, D), BF, vmem),
        "gain_row": ((1, GAINS), F32, vmem),
        "w_all": ((4, 4, UNIT, D), BF, hbm),
        **{n: (*what, hbm) for n, what in SAVED.items()},
    }
    scratch = {
        "q_send": pltpu.VMEM((4, 8, 1152), F32),
        "q_recv": pltpu.VMEM((4, 8, 1152), F32),
        "o_send": pltpu.VMEM((16, D), BF),
        "g_recv": pltpu.VMEM((3, 8, D), F32),
        "g_y": pltpu.VMEM((4, 48, D), BF),
        "d_y": pltpu.VMEM((4, 24, D), F32),
        "unit": pltpu.VMEM((UNIT, D), BF),
        "tok_all": pltpu.VMEM((8, BLOCK, D), BF),
        "value_t": pltpu.VMEM((OWN_KV, HEAD_WIDTH, SEQ), BF),
        "attended": pltpu.VMEM((OWN_HEADS, 8, BLOCK, HEAD_WIDTH), BF),
        "terms": pltpu.VMEM((4, ROWS, D), BF),
        "boxes": pltpu.VMEM((6, BLOCK, D), BF),
        "total": pltpu.VMEM((ROWS, D), F32),
        **{n: pltpu.VMEM(*what) for n, what in SAVED.items()},
        "pair": dma(5),
        "core": dma(6),
        "save": dma(len(SAVED)),
        **{n: dma(4) for n in ("qp_s", "qp_r", "op_s", "op_r")},
        **rings("gy", "dy", "qx", "qz", "ox", "t", "a1", "b1", "a2", "b2", "y"),
    }
    spaces = {"span": smem, "stored": smem}
    return named_call(forward_kernel, 1, "forward_attention", given, spaces, outputs, scratch)


def sum_everywhere(r, place):
    z, x, k, y = (place[a] for a in "zxky")

    def stage(source, slots, send, recv, offsets, device, me, slot_of):
        slots[me] = source[...]
        copies = [
            remote(source, slots.at[me], send.at[n], recv.at[me], device(*offset))
            for n, offset in enumerate(offsets)
        ]
        for copy in copies:
            copy.start()
        for n, offset in enumerate(offsets):
            slot = slot_of(*offset)
            remote(source, slots.at[slot], send.at[n], recv.at[slot], device(*offset)).wait_recv()
        for copy in copies:
            copy.wait_send()

    stage(r.value_row, r.first, r.s1_s, r.s1_r, OURS, lambda *o: ours_at(place, *o), y * 2 + k,
          lambda dy, dk: place.moved("y", dy) * 2 + lax.rem(k + dk, 2))
    r.held[...] = jnp.sum(r.first[...], axis=0)
    stage(r.held, r.second, r.s2_s, r.s2_r, THEIRS, lambda *o: theirs_at(place, *o), z * 4 + x,
          lambda dz, dx: place.moved("z", dz) * 4 + place.moved("x", dx))
    r.out_sums[...] = jnp.sum(r.second[...], axis=0)


OURS = [(dy, dk) for dy in range(4) for dk in range(2) if (dy, dk) != (0, 0)]
THEIRS = [(dz, dx) for dz in range(4) for dx in range(4) if (dz, dx) != (0, 0)]


def ours_at(place, dy, dk):
    return place.device(y=place.moved("y", dy), k=lax.rem(place["k"] + dk, 2))


def theirs_at(place, dz, dx):
    return place.device(z=place.moved("z", dz), x=place.moved("x", dx))


def back_through_norm(r, gain):
    r.mlp_gain[...] = jnp.zeros_like(r.mlp_gain)

    @pl.loop(0, ROWS // 16)
    def _(t):
        at = row_tile(t, 16)
        rows = r.middle[at]
        scale = lax.rsqrt(jnp.mean(rows * rows, axis=-1, keepdims=True) + norm_eps)
        normed = rows * scale
        incoming = r.dh_own[at] + r.dh_box[at].astype(F32)
        product = incoming * normed
        r.mlp_gain[...] += product[0:8] + product[8:16]
        incoming = incoming * gain[:, D : 2 * D]
        mean = jnp.mean(incoming * normed, axis=-1, keepdims=True)
        d_mid = r.cot[at].astype(F32) + scale * (incoming - normed * mean)
        r.out_input_grad[at] = d_mid
        r.own[at] = d_mid.astype(BF)


def back_to_input(r, gain):
    r.attn_gain[...] = jnp.zeros_like(r.attn_gain)

    @pl.loop(0, ROWS // 16)
    def _(t):
        at = row_tile(t, 16)
        rows = r.tok[at].astype(F32)
        scale = lax.rsqrt(jnp.mean(rows * rows, axis=-1, keepdims=True) + norm_eps)
        normed = rows * scale
        incoming = r.dh_total[at]
        product = incoming * normed
        r.attn_gain[...] += product[0:8] + product[8:16]
        incoming = incoming * gain[:, 0:D]
        mean = jnp.mean(incoming * normed, axis=-1, keepdims=True)
        r.out_input_grad[at] += scale * (incoming - normed * mean)


def back_to_projections(r, gain):
    plain = HEAD_WIDTH ** (-0.5)
    r.head_gain[...] = jnp.zeros_like(r.head_gain)

    @pl.loop(0, SEQ // TILE)
    def _(t):
        at = row_tile(t, TILE)
        cos_t, sin_t = r.cosine[at], r.sine[at]
        for h in range(OWN_HEADS + OWN_KV):
            mine = h < OWN_HEADS
            d_rows = r.d_query[h, at] if mine else r.d_key[h - OWN_HEADS, at] * plain
            first = 2 * D if mine else 2 * D + HEAD_WIDTH
            d_gained = d_rows * cos_t - turn(d_rows) * sin_t
            normed, scale = head_norm(r.raw[h, at])
            product = d_gained * normed
            r.head_gain[0 if mine else 1] += jnp.sum(product.reshape(TILE // 8, 8, HEAD_WIDTH), axis=0)
            incoming = d_gained * gain[:, first : first + HEAD_WIDTH]
            mean = jnp.mean(incoming * normed, axis=-1, keepdims=True)
            r.d_proj[pl.ds(2 * t, 2), :, 128 * h : 128 * h + 128] = (
                (scale * (incoming - normed * mean)).astype(BF).reshape(2, BLOCK, HEAD_WIDTH)
            )
        for h in range(OWN_KV):
            r.d_proj[pl.ds(2 * t, 2), :, 768 + 128 * h : 896 + 128 * h] = (
                r.d_value[h, at].astype(BF).reshape(2, BLOCK, HEAD_WIDTH)
            )


def backward_kernel(r):
    place = Place()
    z, x, k, y = (place[a] for a in "zxky")
    diagonal = z == y
    gain = r.gain_row
    near = neighbours(place, "xyzk")
    everyone = [ours_at(place, *o) for o in OURS] + [theirs_at(place, *o) for o in THEIRS]
    greet(near + everyone)
    for other in range(4):

        @pl.when(not_here(diagonal, other, z))
        def _():
            greet([place.device(z=jnp.int32(other), y=z)])

    loads = {
        n: pltpu.make_async_copy(getattr(r, "in_" + n), getattr(r, n), r.load.at[i]) for i, n in enumerate(SAVED)
    }
    for copy in loads.values():
        copy.start()

    def a_part(i, h):
        return r.d_w.at[i, pl.ds(2 * h, 2), pl.ds(0, PART_A)]

    def b_part(i, h):
        return r.d_w.at[pl.ds(2 * h, 2), i, pl.ds(PART_A, UNIT - PART_A)]

    a_one = Scatter(place, "z", a_part, [r.a_box.at[n] for n in range(6)], (r.a1_s, r.a1_r), lambda n: r.a_mine.at[n])
    b_one = Scatter(place, "x", b_part, [r.b_box.at[n] for n in range(6)], (r.b1_s, r.b1_r), lambda n: r.b_mine.at[n])
    mine = [
        pltpu.make_async_copy(ring.own_part(n), ring.mine(n), r.mine_sem.at[4 * i + n])
        for i, ring in enumerate((a_one, b_one))
        for n in range(4)
    ]
    for copy in mine:
        copy.start()
    await_greetings(len(near) + len(everyone) + jnp.where(diagonal, 3, 4))

    dh_copy = remote(r.dh_sib, r.dh_box, r.core.at[0], r.core.at[1], place.sibling())
    out_copy = remote(r.out_sib, r.out_box, r.core.at[2], r.core.at[3], place.sibling())
    dh_copy.start()
    out_copy.start()
    a_one.start()
    b_one.start()
    dh_copy.wait_recv()
    back_through_norm(r, gain)
    ring = Gather(
        place, "y", lambda i, h: r.d_attn_all.at[2 * i + h], (r.t_s, r.t_r),
        own=lambda h: r.own.at[pl.ds(BLOCK * h, BLOCK)],
    )
    ring.start()
    r.d_attn_all[pl.ds(2 * y, 2)] = r.own[...].reshape(2, BLOCK, D)
    out_copy.wait_recv()

    @pl.loop(0, ROWS // 16)
    def _(t):
        at = row_tile(t, 16)
        r.out_layer_out[at] = (r.middle[at] + r.out_own[at] + r.out_box[at].astype(F32)).astype(BF)

    for copy in mine:
        copy.wait()
    for copy in loads.values():
        copy.wait()
    r.d_key[...] = jnp.zeros_like(r.d_key)
    r.d_value[...] = jnp.zeros_like(r.d_value)
    ring.forward()
    a_one.forward()
    b_one.forward()
    ring.finish()

    wo = r.wo_all[...].reshape(OWN_HEADS * HEAD_WIDTH, D)

    @pl.loop(0, SEQ // TILE)
    def _(t):
        at = row_tile(t, TILE)
        rows = pair_of(r.d_attn_all, r.stored, t)
        r.d_q[t] = rows.reshape(4, 2, 32, D)
        both = dot_nt(rows, wo)
        for h in range(OWN_HEADS):
            r.d_attended[h, at] = both[:, 128 * h : 128 * h + 128].astype(BF)

    d_sorted = r.d_q[...].reshape(SEQ, D)

    @pl.loop(0, 4)
    def _(i):
        r.d_o[i] = dot_nn(r.attended_t[i], d_sorted).astype(BF).reshape(2, 64, D)

    o_core = remote(r.d_o.at[:, 1 - k], r.o_box, r.core.at[4], r.core.at[5], place.sibling())
    o_core.start()
    attend_back(r, 0, 2)
    o_core.wait_recv()

    @pl.loop(0, 4)
    def _(i):
        add_rows(r.o_box.at[i], [r.o_box.at[i], r.d_o.at[i, k]])

    o_x = Scatter(
        place, "x", lambda i, h: r.o_box.at[i, pl.ds(32 * h, 32)],
        [r.ox_box.at[n] for n in range(6)], (r.ox_s, r.ox_r),
    )
    o_x.start()
    a_one.finish(lambda h: r.a_sum.at[pl.ds(2 * h, 2)])
    b_one.finish(lambda h: r.b_sum.at[pl.ds(2 * h, 2)])
    a_two = Scatter(
        place, "x", lambda i, h: r.a_sum.at[i, from_to(h, 0, 80, PART_A)],
        [r.a_box2.at[n, pl.ds(0, 80 if n in (0, 3, 4) else 64)] for n in range(6)], (r.a2_s, r.a2_r),
    )
    b_two = Scatter(
        place, "z", lambda i, h: r.b_sum.at[i, from_to(h, 0, 64, PART_A)],
        [r.b_box2.at[n, pl.ds(0, 64 if n in (0, 3, 4) else 80)] for n in range(6)], (r.b2_s, r.b2_r),
    )
    a_two.start()
    b_two.start()
    attend_back(r, 2, 4)
    o_x.forward()
    back_to_projections(r, gain)

    wq = r.wq_all[:, :, :, :, 0:D].reshape(D, D)

    @pl.loop(0, 4)
    def _(i):
        rows = jnp.concatenate([r.d_proj[r.span[2 * i + n]] for n in range(2)], axis=0)
        r.d_attn_all[pl.ds(2 * i, 2)] = dot_nt(rows, wq).astype(BF).reshape(2, BLOCK, D)

    dh_ring = Scatter(
        place, "y", lambda i, h: r.d_attn_all.at[2 * i + h],
        [r.y_box.at[n] for n in range(6)], (r.y_s, r.y_r),
    )
    dh_ring.start()

    d_proj = r.d_proj[...].reshape(SEQ, D)

    @pl.loop(0, 4)
    def _(t):
        left = r.hidden[:, pl.ds(pl.multiple_of(t * 256, 256), 256)]
        rows = lax.dot_general(left, d_proj, (((0,), (0,)), ((), ())), preferred_element_type=F32)
        r.d_q[t] = rows.astype(BF).reshape(4, 2, 32, D)

    q_core = remote(r.d_q.at[:, :, 1 - k], r.q_box, r.core.at[6], r.core.at[7], place.sibling())
    q_core.start()
    a_two.forward()
    b_two.forward()
    dh_ring.forward()
    o_x.finish(lambda h: r.o_two.at[pl.ds(32 * h, 32)])

    def o_target(other):
        return place.device(z=y, y=jnp.int32(other))

    for other in range(4):
        piece = r.o_two.at[pl.ds(16 * other, 16)]

        @pl.when(not_here(diagonal, other, y))
        def _():
            remote(piece, r.o_slots.at[z], r.oy_s.at[other], r.oy_r.at[z], o_target(other)).start()

    @pl.when(diagonal)
    def _():
        r.o_slots[z] = r.o_two[row_tile(y, 16)]

    q_core.wait_recv()

    @pl.loop(0, 4)
    def _(i):
        @pl.loop(0, 4)
        def _(j):
            add_rows(r.q_box.at[i, j], [r.q_box.at[i, j], r.d_q.at[i, j, k]])

    q_z = Scatter(
        place, "z", lambda i, h: r.q_box.at[i, pl.ds(2 * h, 2)],
        [r.qz_box.at[n] for n in range(6)], (r.qz_s, r.qz_r),
    )
    q_z.start()

    a_two.finish(lambda h: r.total.at[from_to(h, 0, 80, PART_A)])
    b_two.finish(lambda h: r.total.at[from_to(h, PART_A, 208, UNIT)])
    for c in range(4):
        for b in range(3):
            at = 64 * b + 8 * c
            rows = jnp.concatenate([r.total[at : at + 8], r.total[at + 32 : at + 40]], axis=0)
            r.g_send[c, 16 * b : 16 * b + 16] = rows.astype(BF)
    r.g_slots[y] = r.g_send[y]

    def down_rows(c):
        return pl.ds(pl.multiple_of(192 + 24 * c, 8), 24)

    r.d_slots[y] = r.total[down_rows(y)]
    y_copies = []
    for n in (1, 3, 2):
        to = place.moved("y", n)
        y_copies.append(remote(r.g_send.at[to], r.g_slots.at[y], r.gy_s.at[n], r.gy_r.at[y], place.peer("y", n)))
        y_copies.append(remote(r.total.at[down_rows(to)], r.d_slots.at[y], r.dy_s.at[n], r.dy_r.at[y], place.peer("y", n)))
    for copy in y_copies:
        copy.start()
    q_z.forward()
    dh_ring.finish(lambda h: r.dh_total.at[pl.ds(BLOCK * h, BLOCK)])
    back_to_input(r, gain)

    for n in (1, 3, 2):
        source = place.moved("y", n)
        remote(r.g_send.at[0], r.g_slots.at[source], r.gy_s.at[n], r.gy_r.at[source], place.peer("y", n)).wait_recv()
        remote(r.total.at[pl.ds(192, 24)], r.d_slots.at[source], r.dy_s.at[n], r.dy_r.at[source], place.peer("y", n)).wait_recv()
    r.out_d_out[...] = r.d_slots[0] + r.d_slots[1] + r.d_slots[2] + r.d_slots[3]
    summed = r.g_slots[0].astype(F32)
    for c in range(1, 4):
        summed = summed + r.g_slots[c].astype(F32)
    summed = summed.reshape(3, 2, 8, D)
    r.g_sum[0] = summed[:, 0]
    r.g_sum[1] = summed[:, 1]
    r.out_g_out[k] = r.g_sum[k]
    g_core = remote(r.g_sum.at[1 - k], r.out_g_out.at[k], r.core.at[8], r.core.at[9], place.sibling())
    g_core.start()
    for other in range(4):

        @pl.when(not_here(diagonal, other, z))
        def _():
            remote(r.o_two.at[pl.ds(0, 16)], r.o_slots.at[other], r.oy_s.at[0], r.oy_r.at[other], place.device(z=jnp.int32(other), y=z)).wait_recv()

    o_sum = r.o_slots[0].astype(F32)
    for c in range(1, 4):
        o_sum = o_sum + r.o_slots[c].astype(F32)
    r.out_o_out[...] = o_sum

    q_z.finish(lambda h: r.q_two.at[pl.ds(2 * h, 2)])
    q_x = Scatter(
        place, "x", lambda i, h: r.q_two.at[i, pl.ds(16 * h, 16)],
        [r.qx_box.at[n] for n in range(6)], (r.qx_s, r.qx_r),
    )
    q_x.start()
    q_x.forward()
    q_x.finish(lambda h: r.q_three.at[pl.ds(16 * h, 16)])
    r.out_q_out[y] = r.q_three[row_tile(y, 8)]
    q_copies = [
        remote(r.q_three.at[row_tile(place.moved("y", n), 8)], r.out_q_out.at[y], r.qy_s.at[n], r.qy_r.at[y], place.peer("y", n))
        for n in (1, 3, 2)
    ]
    for copy in q_copies:
        copy.start()
    remote(r.g_sum.at[0], r.out_g_out.at[1 - k], r.core.at[8], r.core.at[9], place.sibling()).wait_recv()
    for n in (1, 3, 2):
        source = place.moved("y", n)
        remote(r.q_three.at[pl.ds(0, 8)], r.out_q_out.at[source], r.qy_s.at[n], r.qy_r.at[source], place.peer("y", n)).wait_recv()

    squares = jnp.zeros((8, D), F32)
    for part in [r.out_q_out[c] for c in range(4)] + [r.out_g_out[c, b] for c in range(2) for b in range(3)]:
        squares = squares + part * part
    for c in range(2):
        part = r.out_o_out[8 * c : 8 * c + 8]
        squares = squares + part * part
    for c in range(3):
        part = r.out_d_out[8 * c : 8 * c + 8]
        squares = squares + part * part
    attn = jnp.sum(r.attn_gain[...], axis=0, keepdims=True)
    mlp = jnp.sum(r.mlp_gain[...], axis=0, keepdims=True)
    squares = jnp.sum(squares, axis=0, keepdims=True)
    r.value_row[...] = jnp.zeros_like(r.value_row)
    lanes = jnp.zeros((1, 128), F32)
    for c in range(8):
        at = slice(128 * c, 128 * c + 128)
        r.value_row[c : c + 1] = attn[:, at]
        r.value_row[8 + c : 9 + c] = mlp[:, at]
        lanes = lanes + squares[:, at]
    for c in range(2):
        r.value_row[16 + c : 17 + c] = jnp.sum(r.head_gain[c], axis=0, keepdims=True)
    r.value_row[18:19] = lanes
    sum_everywhere(r, place)

    for copy in [dh_copy, out_copy, o_core, q_core, g_core] + y_copies + q_copies:
        copy.wait_send()
    for other in range(4):

        @pl.when(not_here(diagonal, other, y))
        def _():
            remote(r.o_two.at[pl.ds(16 * other, 16)], r.o_slots.at[z], r.oy_s.at[other], r.oy_r.at[z], o_target(other)).wait_send()


def backward_step(**given):
    given = {("in_" + n if n in SAVED else n): v for n, v in given.items()}
    outputs = {
        "layer_out": ((ROWS, D), BF, vmem),
        "input_grad": ((ROWS, D), F32, vmem),
        "q_out": ((4, 8, D), F32, vmem),
        "o_out": ((16, D), F32, vmem),
        "g_out": ((2, 3, 8, D), F32, vmem),
        "d_out": ((24, D), F32, vmem),
        "sums": ((24, 128), F32, vmem),
    }
    head_rows = (OWN_HEADS, SEQ, HEAD_WIDTH)
    kv_rows = (OWN_KV, SEQ, HEAD_WIDTH)
    scratch = {
        **{n: pltpu.VMEM(*what) for n, what in SAVED.items()},
        "out_box": pltpu.VMEM((ROWS, D), BF),
        "dh_box": pltpu.VMEM((ROWS, D), BF),
        "own": pltpu.VMEM((ROWS, D), BF),
        "d_attn_all": pltpu.VMEM((8, BLOCK, D), BF),
        "d_attended": pltpu.VMEM(head_rows, BF),
        "d_query": pltpu.VMEM(head_rows, F32),
        "d_key": pltpu.VMEM(kv_rows, F32),
        "d_value": pltpu.VMEM(kv_rows, F32),
        "d_proj": pltpu.VMEM((8, BLOCK, D), BF),
        "y_box": pltpu.VMEM((6, BLOCK, D), BF),
        "dh_total": pltpu.VMEM((ROWS, D), F32),
        "a_box": pltpu.VMEM((6, 2, PART_A, D), BF),
        "b_box": pltpu.VMEM((6, 2, PART_A, D), BF),
        "a_mine": pltpu.VMEM((4, 2, PART_A, D), BF),
        "b_mine": pltpu.VMEM((4, 2, PART_A, D), BF),
        "a_sum": pltpu.VMEM((4, PART_A, D), BF),
        "b_sum": pltpu.VMEM((4, PART_A, D), BF),
        "a_box2": pltpu.VMEM((6, 80, D), BF),
        "b_box2": pltpu.VMEM((6, 80, D), BF),
        "total": pltpu.VMEM((UNIT, D), F32),
        "g_send": pltpu.VMEM((4, 48, D), BF),
        "g_slots": pltpu.VMEM((4, 48, D), BF),
        "d_slots": pltpu.VMEM((4, 24, D), F32),
        "g_sum": pltpu.VMEM((2, 3, 8, D), F32),
        "d_q": pltpu.VMEM((4, 4, 2, 32, D), BF),
        "d_o": pltpu.VMEM((4, 2, 64, D), BF),
        "q_box": pltpu.VMEM((4, 4, 32, D), BF),
        "qz_box": pltpu.VMEM((6, 2, 32, D), BF),
        "q_two": pltpu.VMEM((4, 32, D), BF),
        "qx_box": pltpu.VMEM((6, 16, D), BF),
        "q_three": pltpu.VMEM((32, D), F32),
        "o_box": pltpu.VMEM((4, 64, D), BF),
        "ox_box": pltpu.VMEM((6, 32, D), BF),
        "o_two": pltpu.VMEM((64, D), BF),
        "o_slots": pltpu.VMEM((4, 16, D), BF),
        "mlp_gain": pltpu.VMEM((8, D), F32),
        "attn_gain": pltpu.VMEM((8, D), F32),
        "head_gain": pltpu.VMEM((2, 8, HEAD_WIDTH), F32),
        "value_row": pltpu.VMEM((24, 128), F32),
        "first": pltpu.VMEM((8, 24, 128), F32),
        "second": pltpu.VMEM((16, 24, 128), F32),
        "held": pltpu.VMEM((24, 128), F32),
        "core": dma(10),
        "load": dma(len(SAVED)),
        "mine_sem": dma(8),
        **{n: dma(4) for n in ("gy_s", "gy_r", "dy_s", "dy_r", "qy_s", "qy_r", "oy_s", "oy_r")},
        **{"s1_s": dma(7), "s1_r": dma(8), "s2_s": dma(15), "s2_r": dma(16)},
        **rings("t", "y", "a1", "b1", "a2", "b2", "qz", "qx", "ox"),
    }
    spaces = {"span": smem, "stored": smem, "d_w": hbm, **{"in_" + n: hbm for n in SAVED}}
    return named_call(backward_kernel, 2, "backward_attention", given, spaces, outputs, scratch)


def gain_spread():
    return jnp.asarray(np.arange(128)[:, None] == np.arange(GAINS)[None, :] % 18, BF)


def rope_tables():
    middle = HEAD_WIDTH // 2
    frequency = rope_base ** (-(np.arange(middle) * 2.0) / HEAD_WIDTH)
    angle = np.arange(SEQ)[:, None] * frequency[None, :]
    cosine, sine = np.cos(angle), np.sin(angle)
    return (
        jnp.asarray(np.concatenate([cosine, cosine], axis=1), F32),
        jnp.asarray(np.concatenate([-sine, sine], axis=1), F32),
    )


def contract_rows(left, right):
    return lax.dot_general(
        left, right, (((0,), (0,)), ((), ())), preferred_element_type=jnp.float32
    )


def contract_cols(left, right):
    return lax.dot_general(
        left, right, (((1,), (1,)), ((), ())), preferred_element_type=jnp.float32
    )


def adam_update(weight, first, second, grad, factor, rate, decay):
    clipped = grad * factor
    new_first = beta_one * first + (1.0 - beta_one) * clipped
    new_second = beta_two * second + (1.0 - beta_two) * clipped * clipped
    direction = (
        new_first
        / (1.0 - beta_one**STEP)
        / (jnp.sqrt(new_second / (1.0 - beta_two**STEP)) + adam_eps)
    )
    return (weight - rate * (direction + decay * weight), new_first, new_second)


def pack_gateup(w):
    rows = w.shape[0]
    v = w.reshape(rows, 2, 16, 2, 96).transpose(3, 0, 1, 2, 4).reshape(2, rows, 2, 3, 512)
    return v.transpose(0, 3, 1, 2, 4).reshape(2, 3, rows, 1024)


def unpack_gateup(v):
    rows = v.shape[2]
    w = v.reshape(2, 3, rows, 2, 512).transpose(0, 2, 3, 1, 4).reshape(2, rows, 2, 16, 96)
    return w.transpose(1, 2, 3, 0, 4).reshape(rows, 2 * FF)


def body(
    tokens, cotangent, span_order,
    w_qkv, w_out, w_gateup, w_down, gains,
    first_qkv, first_out, first_gateup, first_down, first_gains,
    second_qkv, second_out, second_gateup, second_down, second_gains,
):
    own_gains = jnp.pad(gains[None, :], ((0, 7), (0, 128 - gains.shape[0])))
    block = jnp.arange(8, dtype=jnp.int32)
    stored = jnp.sum(jnp.where(span_order[None, :] == block[:, None], block[None, :], 0), axis=1)
    cosine, sine = rope_tables()
    fwd = forward_step(
        span=span_order, stored=stored, tok=tokens, cot=cotangent, wq=w_qkv, wo=w_out,
        wgu=pack_gateup(w_gateup), wd=w_down, gains=own_gains, spread=gain_spread(),
        cosine=cosine, sine=sine,
    )

    hidden2 = fwd["hidden_pair"].reshape(2 * ROWS, D)
    cot = fwd["cot_pair"].reshape(2 * ROWS, D)
    w_all = fwd["w_all"].reshape(16, UNIT, D)
    w_down_half = w_all[:, 192:].reshape(1536, D)
    out_part = jnp.zeros((2 * ROWS, D), F32)
    dh_part = jnp.zeros((2 * ROWS, D), F32)
    d_w = []
    d_downs = []
    for b in range(3):
        w_gu = w_all[:, 64 * b : 64 * b + 64].reshape(D, D)
        w_dn = w_down_half[512 * b : 512 * b + 512]
        gate_up = jnp.dot(hidden2, w_gu, preferred_element_type=F32)
        gate, up = gate_up[:, :512], gate_up[:, 512:]
        sigmoid = jax.nn.sigmoid(gate)
        active = gate * sigmoid
        product = (active * up).astype(BF)
        out_part += jnp.dot(product, w_dn, preferred_element_type=F32)
        d_downs.append(contract_rows(product, cot).astype(BF))
        d_product = contract_cols(cot, w_dn)
        d_gate = d_product * up * sigmoid * (1.0 + gate * (1.0 - sigmoid))
        d_gate_up = jnp.concatenate([d_gate, d_product * active], axis=1).astype(BF)
        d_w.append(contract_rows(hidden2, d_gate_up).astype(BF).reshape(16, 64, D))
        dh_part += contract_cols(d_gate_up, w_gu)
    d_w.append(jnp.concatenate(d_downs, axis=0).reshape(16, 96, D))
    d_w = jnp.concatenate(d_w, axis=1).reshape(4, 4, UNIT, D)

    bwd = backward_step(
        span=span_order, stored=stored, tok=tokens, cot=cotangent, middle=fwd["middle"],
        gain_row=fwd["gain_row"], cosine=cosine, sine=sine,
        out_own=out_part[:ROWS], out_sib=out_part[ROWS:].astype(BF),
        dh_own=dh_part[:ROWS], dh_sib=dh_part[ROWS:].astype(BF), d_w=d_w,
        **{name: fwd[name] for name in SAVED},
    )
    q_grad, o_grad, gu_grad, down_grad = (bwd[n] for n in ("q_out", "o_out", "g_out", "d_out"))
    q_shard = jnp.concatenate(
        [
            q_grad[:, :, :512].transpose(1, 0, 2).reshape(8, 2048),
            q_grad[:, :, 512:768].transpose(1, 0, 2).reshape(8, 1024),
            q_grad[:, :, 768:].transpose(1, 0, 2).reshape(8, 1024),
        ],
        axis=1,
    )
    shards = [q_shard, o_grad, unpack_gateup(gu_grad), down_grad]
    sums = bwd["sums"]
    all_gains = sums[:18].reshape(-1)
    grad_norm = jnp.sqrt(jnp.sum(sums[18]) + jnp.sum(all_gains * all_gains))
    index = lax.axis_index("dp") * 4 + lax.axis_index("ctx")
    shards.append(lax.dynamic_slice_in_dim(all_gains, index * 18, 18))

    factor = jnp.minimum(1.0, clip_at / (grad_norm + 1e-06))
    masters = (w_qkv, w_out, w_gateup, w_down, gains)
    firsts = (first_qkv, first_out, first_gateup, first_down, first_gains)
    seconds = (second_qkv, second_out, second_gateup, second_down, second_gains)
    rates = (matrix_rate, out_rate, matrix_rate, matrix_rate, gain_rate)
    decays = (matrix_decay, matrix_decay, matrix_decay, matrix_decay, 0.0)
    news, new_firsts, new_seconds = [], [], []
    for which in range(5):
        weight, first, second = adam_update(
            masters[which], firsts[which], seconds[which], shards[which], factor,
            rates[which], decays[which],
        )
        news.append(weight)
        new_firsts.append(first)
        new_seconds.append(second)
    return (bwd["layer_out"], bwd["input_grad"], *news, *new_firsts, *new_seconds, grad_norm)


def solution(mesh):
    rows, flat = P(("dp", "ctx"), None), P(("dp", "ctx"))
    state = (rows, rows, rows, rows, flat)
    in_specs = (rows, rows, P()) + state * 3
    out_specs = (rows, rows) + state * 3 + (P(),)
    return jax.shard_map(body, mesh=mesh, in_specs=in_specs, out_specs=out_specs, check_vma=False)
```

```python
import jax
import jax.numpy as jnp
import numpy as np
from jax import lax
from jax.experimental import pallas as pl
from jax.experimental.pallas import tpu as pltpu
from jax.sharding import PartitionSpec as P

D = 1024
HEADS = 16
KV_HEADS = 8
HEAD_WIDTH = 128
FF = 3072
STEP = 10

norm_eps = 1e-06
rope_base = 1000000.0
beta_one = 0.9
beta_two = 0.999
adam_eps = 1e-08
clip_at = 1.0
matrix_rate = 0.05
out_rate = 0.25
matrix_decay = 0.1
gain_rate = 0.5
masked_score = -1e30

MESH = pl.DeviceIdType.MESH
BF = jnp.bfloat16
F32 = jnp.float32
ROWS = 256
UNIT = 288
PART_A = 144
VMEM_LIMIT = 62 * 2**20
vmem = pl.BlockSpec(memory_space=pltpu.VMEM)
hbm = pl.BlockSpec(memory_space=pl.ANY)


class Place:
    def __init__(self):
        dp = lax.axis_index("dp")
        self.at = {
            "z": lax.div(dp, 8),
            "x": lax.rem(lax.div(dp, 2), 4),
            "k": lax.rem(dp, 2),
            "y": lax.axis_index("ctx"),
        }

    def __getitem__(self, axis):
        return self.at[axis]

    def device(self, **other):
        c = {**self.at, **other}
        return (c["z"] * 8 + c["x"] * 2 + c["k"], c["y"])

    def moved(self, axis, steps):
        return lax.rem(self.at[axis] + steps, 4)

    def peer(self, axis, steps):
        return self.device(**{axis: self.moved(axis, steps)})

    def sibling(self):
        return self.device(k=1 - self.at["k"])


def greet(devices):
    barrier = pltpu.get_barrier_semaphore()
    for device in devices:
        pl.semaphore_signal(barrier, inc=1, device_id=device, device_id_type=MESH)


def await_greetings(count):
    pl.semaphore_wait(pltpu.get_barrier_semaphore(), count)


def neighbours(place, axes):
    found = []
    for axis in axes:
        if axis == "k":
            found.append(place.sibling())
        else:
            found += [place.peer(axis, 1), place.peer(axis, 3)]
    return found


def remote(src, dst, send, recv, device):
    return pltpu.make_async_remote_copy(
        src_ref=src, dst_ref=dst, send_sem=send, recv_sem=recv, device_id=device, device_id_type=MESH
    )


class Gather:
    def __init__(self, place, axis, part, sems, own=None):
        self.part, self.send, self.recv = part, sems[0], sems[1]
        self.own = own or (lambda half: part(place[axis], half))
        self.next, self.prev = place.peer(axis, 1), place.peer(axis, 3)
        self.me, self.up, self.down, self.far = (place.moved(axis, n) for n in (0, 1, 3, 2))

    def copy(self, n, slot, half, device, src=None):
        view = self.part(slot, half)
        return remote(src if src is not None else view, view, self.send.at[n], self.recv.at[n], device)

    def outgoing(self, n):
        slot, half, device = [
            (self.me, 0, self.next),
            (self.me, 1, self.prev),
            (self.me, 1, self.next),
            (self.me, 0, self.prev),
            (self.down, 0, self.next),
            (self.up, 1, self.prev),
        ][n]
        return self.copy(n, slot, half, device, self.own(half) if n < 4 else None)

    def start(self):
        for n in range(4):
            self.outgoing(n).start()

    def forward(self):
        self.copy(0, self.down, 0, self.prev).wait_recv()
        self.outgoing(4).start()
        self.copy(1, self.up, 1, self.next).wait_recv()
        self.outgoing(5).start()

    def finish(self):
        self.copy(2, self.down, 1, self.prev).wait_recv()
        self.copy(3, self.up, 0, self.next).wait_recv()
        self.copy(4, self.far, 0, self.prev).wait_recv()
        self.copy(5, self.far, 1, self.next).wait_recv()
        for n in range(6):
            self.outgoing(n).wait_send()


class Scatter:
    def __init__(self, place, axis, part, boxes, sems, mine=None):
        self.part, self.boxes = part, boxes
        self.send, self.recv = sems[0], sems[1]
        self.next, self.prev = place.peer(axis, 1), place.peer(axis, 3)
        self.me, self.up, self.down, self.far = (place.moved(axis, n) for n in (0, 1, 3, 2))
        self.mine = mine or self.own_part

    def own_part(self, n):
        slot, half = [(self.down, 0), (self.up, 1), (self.me, 0), (self.me, 1)][n]
        return self.part(slot, half)

    def copy(self, n, src, device):
        return remote(src, self.boxes[n], self.send.at[n], self.recv.at[n], device)

    def outgoing(self, n):
        source, device = [
            (lambda: self.part(self.far, 0), self.prev),
            (lambda: self.part(self.far, 1), self.next),
            (lambda: self.part(self.down, 1), self.prev),
            (lambda: self.part(self.up, 0), self.next),
            (lambda: self.boxes[0], self.prev),
            (lambda: self.boxes[1], self.next),
        ][n]
        return self.copy(n, source(), device)

    def start(self):
        for n in range(4):
            self.outgoing(n).start()

    def forward(self):
        for n in range(2):
            self.outgoing(n).wait_recv()
            add_rows(self.boxes[n], [self.boxes[n], self.mine(n)])
            self.outgoing(4 + n).start()

    def finish(self, result):
        for n in (2, 3, 4, 5):
            self.outgoing(n).wait_recv()
        add_rows(result(0), [self.mine(2), self.boxes[3], self.boxes[4]])
        add_rows(result(1), [self.mine(3), self.boxes[2], self.boxes[5]])
        for n in range(6):
            self.outgoing(n).wait_send()


def add_rows(out, terms):
    shape = out.shape
    rows = shape[-2]

    def block(at):
        total = terms[0][at].astype(F32)
        for term in terms[1:]:
            total = total + term[at].astype(F32)
        out[at] = total.astype(out.dtype)

    if len(shape) == 2:

        @pl.loop(0, rows // 16)
        def _(r):
            block((pl.ds(pl.multiple_of(r * 16, 16), 16), slice(None)))

    else:

        @pl.loop(0, shape[0])
        def _(lead):
            @pl.loop(0, rows // 16)
            def _(r):
                block((lead, pl.ds(pl.multiple_of(r * 16, 16), 16), slice(None)))


def dma(*shape):
    return pltpu.SemaphoreType.DMA(shape)


def ring_sems():
    return [dma(6), dma(6)]


def params(which):
    return pltpu.CompilerParams(
        collective_id=which, has_side_effects=True, vmem_limit_bytes=VMEM_LIMIT
    )


TILE = 256
SEQ = 4 * ROWS
BLOCK = ROWS // 2
OWN_HEADS = HEADS // 4
OWN_KV = KV_HEADS // 4
LOG2E = 1.4426950408889634


def turn(value_rows):
    return pltpu.roll(value_rows, HEAD_WIDTH // 2, 1)


def head_norm(raw):
    scale = lax.rsqrt(jnp.mean(raw * raw, axis=-1, keepdims=True) + norm_eps)
    return raw * scale, scale


def pair_of(ref, order, tile):
    return jnp.concatenate([ref[order[2 * tile]], ref[order[2 * tile + 1]]], axis=0)


def dot_nt(left, right):
    return lax.dot_general(left, right, (((1,), (1,)), ((), ())), preferred_element_type=F32)


def dot_nn(left, right):
    return jnp.dot(left, right, preferred_element_type=F32)


def causal(scores):
    keys = lax.broadcasted_iota(jnp.int32, scores.shape, 0)
    queries = lax.broadcasted_iota(jnp.int32, scores.shape, 1)
    return jnp.where(keys <= queries, scores, masked_score)


def project(r, g_attn, g_query, g_key):
    stored, tok, cosine, sine = r.stored, r.tok_all, r.cosine, r.sine
    hidden, raw, query, key, key_t = r.hidden, r.raw, r.query, r.key, r.key_t
    value, value_t = r.value, r.value_t

    def columns(pair):
        return r.wq_all[:, :, :, :, 256 * pair : 256 * pair + 256].reshape(D, 256)

    @pl.loop(0, SEQ // TILE)
    def _(t):
        at = pl.ds(pl.multiple_of(t * TILE, TILE), TILE)
        rows = pair_of(tok, stored, t).astype(F32)
        scale = lax.rsqrt(jnp.mean(rows * rows, axis=-1, keepdims=True) + norm_eps)
        hid = (rows * scale * g_attn[...]).astype(BF)
        hidden[at] = hid
        cos_t, sin_t = cosine[at], sine[at]
        for pair in range(OWN_HEADS // 2):
            both = dot_nn(hid, columns(pair))
            for n in range(2):
                h, part = 2 * pair + n, both[:, 128 * n : 128 * n + 128]
                raw[h, at] = part.astype(BF)
                normed = head_norm(part)[0] * g_query[...]
                query[h, at] = (normed * cos_t + turn(normed) * sin_t).astype(BF)
        both = dot_nn(hid, columns(2))
        for h in range(OWN_KV):
            part = both[:, 128 * h : 128 * h + 128]
            raw[OWN_HEADS + h, at] = part.astype(BF)
            normed = head_norm(part)[0] * g_key[...]
            rotated = normed * cos_t + turn(normed) * sin_t
            key[h, at] = rotated.astype(BF)
            key_t[h, :, at] = rotated.T.astype(BF)
        both = dot_nn(hid, columns(3))
        for h in range(OWN_KV):
            part = both[:, 128 * h : 128 * h + 128]
            value[h, at] = part.astype(BF)
            value_t[h, :, at] = part.T.astype(BF)


def attend(r, first_head, last_head):
    query, key, value_t, attended = r.query, r.key, r.value_t, r.attended
    attended_t, log_total = r.attended_t, r.log_total
    factor = HEAD_WIDTH ** (-0.5) * LOG2E

    @pl.loop(first_head, last_head)
    def _(h):
        kv = lax.div(h, 2)
        for t in range(SEQ // TILE):
            low, high = t * TILE, (t + 1) * TILE
            q = query[h, low:high]
            scores = [causal(dot_nt(key[kv, low:high], q))]
            if t:
                scores.append(dot_nt(key[kv, 0:low], q))
            top = jnp.max(scores[0], axis=0, keepdims=True)
            if t:
                top = jnp.maximum(top, jnp.max(scores[1], axis=0, keepdims=True))
            top = top * factor
            probs = [jnp.exp2(s * factor - top) for s in scores]
            total = jnp.sum(probs[0], axis=0, keepdims=True)
            mixed = dot_nn(value_t[kv, :, low:high], probs[0].astype(BF))
            if t:
                total = total + jnp.sum(probs[1], axis=0, keepdims=True)
                mixed = mixed + dot_nn(value_t[kv, :, 0:low], probs[1].astype(BF))
            mixed = mixed * (1.0 / total)
            attended_t[h, :, low:high] = mixed.astype(BF)
            attended[h, 2 * t : 2 * t + 2] = mixed.T.astype(BF).reshape(2, BLOCK, HEAD_WIDTH)
            log_total[h, :, low:high] = jnp.broadcast_to(top + jnp.log2(total), (8, TILE))


def attend_back(r, first_head, last_head):
    query, key, key_t, value = r.query, r.key, r.key_t, r.value
    d_attended, log_total, d_query = r.d_attended, r.log_total, r.d_query
    d_key, d_value = r.d_key, r.d_value
    factor = HEAD_WIDTH ** (-0.5) * LOG2E
    plain = HEAD_WIDTH ** (-0.5)

    @pl.loop(first_head, last_head)
    def _(h):
        kv = lax.div(h, 2)
        for t in range(SEQ // TILE):
            low, high = t * TILE, (t + 1) * TILE
            q = query[h, low:high]
            da = d_attended[h, low:high]
            total = log_total[h, 0:1, low:high]
            spans = [(low, high)] + ([(0, low)] if t else [])
            probs, mixes = [], []
            for n, (first, last) in enumerate(spans):
                scores = dot_nt(key[kv, first:last], q)
                if n == 0:
                    scores = causal(scores)
                p = jnp.exp2(scores * factor - total)
                d_value[kv, first:last] += dot_nn(p.astype(BF), da)
                probs.append(p)
                mixes.append(p * dot_nt(value[kv, first:last], da))
            delta = jnp.sum(mixes[0], axis=0, keepdims=True)
            if t:
                delta = delta + jnp.sum(mixes[1], axis=0, keepdims=True)
            back = None
            for (first, last), p, mix in zip(spans, probs, mixes):
                ds = (mix - p * delta).astype(BF)
                d_key[kv, first:last] += dot_nn(ds, q)
                part = dot_nn(key_t[kv, :, first:last], ds)
                back = part if back is None else back + part
            d_query[h, low:high] = (back * plain).T


GAINS = 2 * D + 2 * HEAD_WIDTH
smem = pl.BlockSpec(memory_space=pltpu.SMEM)
regular = pltpu.SemaphoreType.DMA


class Names:
    def __init__(self, names, refs):
        self.__dict__.update(zip(names, refs))


def named_call(kernel, which, name, given, spaces, outputs, scratch):
    names = list(given) + ["out_" + n for n in outputs] + list(scratch)
    results = pl.pallas_call(
        lambda *refs: kernel(Names(names, refs)),
        out_shape=tuple(jax.ShapeDtypeStruct(shape, kind) for shape, kind, _ in outputs.values()),
        in_specs=[spaces.get(n, vmem) for n in given],
        out_specs=tuple(space for _, _, space in outputs.values()),
        scratch_shapes=list(scratch.values()),
        compiler_params=params(which),
        name=name,
    )(*given.values())
    return dict(zip(outputs, results))


SAVED = {
    "wq_all": ((4, 4, 2, 32, 1152), BF),
    "wo_all": ((4, 2, 64, D), BF),
    "hidden": ((SEQ, D), BF),
    "raw": ((OWN_HEADS + OWN_KV, SEQ, HEAD_WIDTH), BF),
    "query": ((OWN_HEADS, SEQ, HEAD_WIDTH), BF),
    "key": ((OWN_KV, SEQ, HEAD_WIDTH), BF),
    "key_t": ((OWN_KV, HEAD_WIDTH, SEQ), BF),
    "value": ((OWN_KV, SEQ, HEAD_WIDTH), BF),
    "attended_t": ((OWN_HEADS, HEAD_WIDTH, SEQ), BF),
    "log_total": ((OWN_HEADS, 8, SEQ), F32),
}


def heads_of(ref, count, at):
    return jnp.concatenate([ref[h, at] for h in range(count)], axis=1)


def row_tile(r, size):
    return pl.ds(pl.multiple_of(r * size, size), size)


def from_to(half, low, split, high):
    return pl.ds(low, split - low) if half == 0 else pl.ds(split, high - split)


def not_here(condition, other, coordinate):
    return jnp.logical_not(jnp.logical_and(condition, coordinate == other))


def forward_kernel(r):
    place = Place()
    z, x, k, y = (place[a] for a in "zxky")
    near = neighbours(place, "xyzk")
    diagonal = z == y
    greet(near + [place.peer("y", 2)])
    for other in range(4):

        @pl.when(not_here(diagonal, other, y))
        def _():
            greet([place.device(z=y, y=jnp.int32(other))])

    for i in range(4):
        r.q_send[i, :, 0:512] = r.wq[:, 512 * i : 512 * i + 512]
        r.q_send[i, :, 512:768] = r.wq[:, 2048 + 256 * i : 2304 + 256 * i]
        r.q_send[i, :, 768:1024] = r.wq[:, 3072 + 256 * i : 3328 + 256 * i]
        r.q_send[i, :, 1024:1152] = r.gains[...]
    r.q_recv[y] = r.q_send[y]
    r.o_send[...] = r.wo[...].astype(BF)
    r.tok_all[pl.ds(2 * y, 2)] = r.tok[...].reshape(2, BLOCK, D)
    r.out_cot_pair[0:ROWS] = r.cot[...]
    await_greetings(len(near) + 1 + jnp.where(diagonal, 3, 4))

    g_prep = remote(r.wgu.at[1 - k], r.g_recv, r.pair.at[0], r.pair.at[1], place.sibling())
    g_prep.start()
    q_prep = [
        remote(r.q_send.at[place.moved("y", n)], r.q_recv.at[y], r.qp_s.at[n], r.qp_r.at[y], place.peer("y", n))
        for n in (1, 3, 2)
    ]
    for copy in q_prep:
        copy.start()

    def o_slot(source):
        return r.wo_all.at[x, k, row_tile(source, 16)]

    for other in range(4):

        @pl.when(not_here(diagonal, other, z))
        def _():
            remote(r.o_send, o_slot(y), r.op_s.at[other], r.op_r.at[y], place.device(z=jnp.int32(other), y=z)).start()

    @pl.when(diagonal)
    def _():
        r.wo_all[x, k, row_tile(y, 16)] = r.o_send[...]

    cot_copy = remote(r.cot, r.out_cot_pair.at[pl.ds(ROWS, ROWS)], r.pair.at[2], r.pair.at[3], place.sibling())
    cot_copy.start()

    g_prep.wait_recv()
    g_own, g_other, lower = r.wgu[k], r.g_recv[...], k == 0
    both = jnp.concatenate([jnp.where(lower, g_own, g_other), jnp.where(lower, g_other, g_own)], axis=1)
    r.g_y[y] = both.reshape(48, D).astype(BF)
    r.d_y[y] = r.wd[...]
    g_ring = Gather(place, "y", lambda i, h: r.g_y.at[i, from_to(h, 0, 32, 48)], (r.gy_s, r.gy_r))
    d_ring = Gather(place, "y", lambda i, h: r.d_y.at[i, from_to(h, 0, 16, 24)], (r.dy_s, r.dy_r))
    g_ring.start()
    d_ring.start()

    for n in (1, 3, 2):
        source = place.moved("y", n)
        remote(r.q_send.at[0], r.q_recv.at[source], r.qp_s.at[n], r.qp_r.at[source], place.peer("y", n)).wait_recv()
    r.wq_all[z, x, k] = r.q_recv[...].reshape(32, 1152).astype(BF)
    q_x = Gather(place, "x", lambda i, h: r.wq_all.at[z, i, k, pl.ds(16 * h, 16)], (r.qx_s, r.qx_r))
    q_x.start()
    tokens = Gather(place, "y", lambda i, h: r.tok_all.at[2 * i + h], (r.t_s, r.t_r))
    tokens.start()

    for other in range(4):

        @pl.when(not_here(diagonal, other, y))
        def _():
            remote(r.o_send, o_slot(other), r.op_s.at[0], r.op_r.at[other], place.device(z=y, y=jnp.int32(other))).wait_recv()

    o_x = Gather(place, "x", lambda i, h: r.wo_all.at[i, k, pl.ds(32 * h, 32)], (r.ox_s, r.ox_r))
    o_x.start()
    g_ring.forward()
    d_ring.forward()
    q_x.forward()
    q_x.finish()
    q_z = Gather(place, "z", lambda i, h: r.wq_all.at[i, pl.ds(2 * h, 2), k], (r.qz_s, r.qz_r))
    q_z.start()
    o_x.forward()
    g_ring.finish()
    d_ring.finish()

    for b in range(3):
        pieces = [r.g_y[c, 16 * b : 16 * b + 16].astype(F32) for c in range(4)]
        for core_row in range(2):
            rows = jnp.concatenate([piece[8 * core_row : 8 * core_row + 8] for piece in pieces], axis=0)
            at = 64 * b + 32 * core_row
            r.unit[at : at + 32] = rows.astype(BF)
    r.unit[192:288] = r.d_y[...].reshape(96, D).astype(BF)
    w_all = r.out_w_all
    u_own = pltpu.make_async_copy(r.unit, w_all.at[z, x], r.pair.at[4])
    u_own.start()
    a_one = Gather(
        place, "x", lambda i, h: w_all.at[z, i, from_to(h, 0, 80, PART_A)], (r.a1_s, r.a1_r),
        own=lambda h: r.unit.at[from_to(h, 0, 80, PART_A)],
    )
    b_one = Gather(
        place, "z", lambda i, h: w_all.at[i, x, from_to(h, PART_A, 208, UNIT)], (r.b1_s, r.b1_r),
        own=lambda h: r.unit.at[from_to(h, PART_A, 208, UNIT)],
    )
    a_one.start()
    b_one.start()
    tokens.forward()
    q_z.forward()
    o_x.finish()
    o_core = remote(r.wo_all.at[:, k], r.wo_all.at[:, k], r.core.at[0], r.core.at[1], place.sibling())
    o_core.start()
    a_one.forward()
    b_one.forward()
    q_z.finish()
    q_core = remote(r.wq_all.at[:, :, k], r.wq_all.at[:, :, k], r.core.at[2], r.core.at[3], place.sibling())
    q_core.start()
    a_one.finish()
    b_one.finish()
    u_own.wait()
    a_two = Gather(place, "z", lambda i, h: w_all.at[i, pl.ds(2 * h, 2), pl.ds(0, PART_A)], (r.a2_s, r.a2_r))
    b_two = Gather(place, "x", lambda i, h: w_all.at[pl.ds(2 * h, 2), i, pl.ds(PART_A, UNIT - PART_A)], (r.b2_s, r.b2_r))
    a_two.start()
    b_two.start()
    remote(r.wo_all.at[:, 1 - k], r.wo_all.at[:, 1 - k], r.core.at[0], r.core.at[1], place.sibling()).wait_recv()
    remote(r.wq_all.at[:, :, 1 - k], r.wq_all.at[:, :, 1 - k], r.core.at[2], r.core.at[3], place.sibling()).wait_recv()
    tokens.finish()

    lanes = r.wq_all[:, :, :, :, D:1152].reshape(128, 8, 128).astype(F32)
    spread = dot_nn(jnp.sum(lanes, axis=1).astype(BF), r.spread[...])
    owner = lax.broadcasted_iota(jnp.int32, (128, GAINS), 0) * 18
    spot = lax.broadcasted_iota(jnp.int32, (128, GAINS), 1)
    mine = jnp.logical_and(spot >= owner, spot < owner + 18)
    r.out_gain_row[...] = jnp.sum(jnp.where(mine, spread, 0.0), axis=0, keepdims=True)
    gain = r.out_gain_row
    project(r, gain.at[:, 0:D], gain.at[:, 2 * D : 2 * D + 128], gain.at[:, 2 * D + 128 : GAINS])
    attend(r, 0, 2)
    a_two.forward()
    b_two.forward()
    attend(r, 2, 4)

    wo = r.wo_all[...].reshape(OWN_HEADS * HEAD_WIDTH, D)

    @pl.loop(0, 4)
    def _(i):
        rows = jnp.concatenate(
            [heads_of(r.attended, OWN_HEADS, r.span[2 * i + n]) for n in range(2)], axis=0
        )
        r.terms[i] = dot_nn(rows, wo).astype(BF)

    reduce = Scatter(
        place, "y", lambda i, h: r.terms.at[i, pl.ds(128 * h, 128)],
        [r.boxes.at[n] for n in range(6)], (r.y_s, r.y_r),
    )
    reduce.start()
    saves = [
        pltpu.make_async_copy(getattr(r, n), getattr(r, "out_" + n), r.save.at[i]) for i, n in enumerate(SAVED)
    ]
    for copy in saves:
        copy.start()
    reduce.forward()
    reduce.finish(lambda h: r.total.at[pl.ds(128 * h, 128)])

    @pl.loop(0, ROWS // 16)
    def _(t):
        at = row_tile(t, 16)
        rows = r.tok[at].astype(F32) + r.total[at]
        r.out_middle[at] = rows
        scale = lax.rsqrt(jnp.mean(rows * rows, axis=-1, keepdims=True) + norm_eps)
        r.out_hidden_pair[at] = (rows * scale * gain[:, D : 2 * D]).astype(BF)

    hid_copy = remote(r.out_hidden_pair.at[pl.ds(0, ROWS)], r.out_hidden_pair.at[pl.ds(ROWS, ROWS)], r.core.at[4], r.core.at[5], place.sibling())
    hid_copy.start()
    a_two.finish()
    b_two.finish()
    for copy in saves:
        copy.wait()
    for copy in q_prep + [g_prep, o_core, q_core]:
        copy.wait_send()
    cot_copy.wait()
    hid_copy.wait()
    for other in range(4):

        @pl.when(not_here(diagonal, other, z))
        def _():
            remote(r.o_send, o_slot(y), r.op_s.at[other], r.op_r.at[y], place.device(z=jnp.int32(other), y=z)).wait_send()


def rings(*names):
    return {f"{name}_{end}": dma(6) for name in names for end in "sr"}


def forward_step(**given):
    outputs = {
        "middle": ((ROWS, D), F32, vmem),
        "hidden_pair": ((2 * ROWS, D), BF, vmem),
        "cot_pair": ((2 * ROWS, D), BF, vmem),
        "gain_row": ((1, GAINS), F32, vmem),
        "w_all": ((4, 4, UNIT, D), BF, hbm),
        **{n: (*what, hbm) for n, what in SAVED.items()},
    }
    scratch = {
        "q_send": pltpu.VMEM((4, 8, 1152), F32),
        "q_recv": pltpu.VMEM((4, 8, 1152), F32),
        "o_send": pltpu.VMEM((16, D), BF),
        "g_recv": pltpu.VMEM((3, 8, D), F32),
        "g_y": pltpu.VMEM((4, 48, D), BF),
        "d_y": pltpu.VMEM((4, 24, D), F32),
        "unit": pltpu.VMEM((UNIT, D), BF),
        "tok_all": pltpu.VMEM((8, BLOCK, D), BF),
        "value_t": pltpu.VMEM((OWN_KV, HEAD_WIDTH, SEQ), BF),
        "attended": pltpu.VMEM((OWN_HEADS, 8, BLOCK, HEAD_WIDTH), BF),
        "terms": pltpu.VMEM((4, ROWS, D), BF),
        "boxes": pltpu.VMEM((6, BLOCK, D), BF),
        "total": pltpu.VMEM((ROWS, D), F32),
        **{n: pltpu.VMEM(*what) for n, what in SAVED.items()},
        "pair": dma(5),
        "core": dma(6),
        "save": dma(len(SAVED)),
        **{n: dma(4) for n in ("qp_s", "qp_r", "op_s", "op_r")},
        **rings("gy", "dy", "qx", "qz", "ox", "t", "a1", "b1", "a2", "b2", "y"),
    }
    spaces = {"span": smem, "stored": smem}
    return named_call(forward_kernel, 1, "forward_attention", given, spaces, outputs, scratch)


def sum_everywhere(r, place):
    z, x, k, y = (place[a] for a in "zxky")

    def stage(source, slots, send, recv, offsets, device, me, slot_of):
        slots[me] = source[...]
        copies = [
            remote(source, slots.at[me], send.at[n], recv.at[me], device(*offset))
            for n, offset in enumerate(offsets)
        ]
        for copy in copies:
            copy.start()
        for n, offset in enumerate(offsets):
            slot = slot_of(*offset)
            remote(source, slots.at[slot], send.at[n], recv.at[slot], device(*offset)).wait_recv()
        for copy in copies:
            copy.wait_send()

    stage(r.value_row, r.first, r.s1_s, r.s1_r, OURS, lambda *o: ours_at(place, *o), y * 2 + k,
          lambda dy, dk: place.moved("y", dy) * 2 + lax.rem(k + dk, 2))
    r.held[...] = jnp.sum(r.first[...], axis=0)
    stage(r.held, r.second, r.s2_s, r.s2_r, THEIRS, lambda *o: theirs_at(place, *o), z * 4 + x,
          lambda dz, dx: place.moved("z", dz) * 4 + place.moved("x", dx))
    r.out_sums[...] = jnp.sum(r.second[...], axis=0)


OURS = [(dy, dk) for dy in range(4) for dk in range(2) if (dy, dk) != (0, 0)]
THEIRS = [(dz, dx) for dz in range(4) for dx in range(4) if (dz, dx) != (0, 0)]


def ours_at(place, dy, dk):
    return place.device(y=place.moved("y", dy), k=lax.rem(place["k"] + dk, 2))


def theirs_at(place, dz, dx):
    return place.device(z=place.moved("z", dz), x=place.moved("x", dx))


def back_through_norm(r, gain):
    r.mlp_gain[...] = jnp.zeros_like(r.mlp_gain)

    @pl.loop(0, ROWS // 16)
    def _(t):
        at = row_tile(t, 16)
        rows = r.middle[at]
        scale = lax.rsqrt(jnp.mean(rows * rows, axis=-1, keepdims=True) + norm_eps)
        normed = rows * scale
        incoming = r.out_input_grad[at] + r.dh_box[at].astype(F32)
        product = incoming * normed
        r.mlp_gain[...] += product[0:8] + product[8:16]
        incoming = incoming * gain[:, D : 2 * D]
        mean = jnp.mean(incoming * normed, axis=-1, keepdims=True)
        d_mid = r.cot[at].astype(F32) + scale * (incoming - normed * mean)
        r.out_input_grad[at] = d_mid
        r.own[at] = d_mid.astype(BF)


def back_to_input(r, gain):
    r.attn_gain[...] = jnp.zeros_like(r.attn_gain)

    @pl.loop(0, ROWS // 16)
    def _(t):
        at = row_tile(t, 16)
        rows = r.tok[at].astype(F32)
        scale = lax.rsqrt(jnp.mean(rows * rows, axis=-1, keepdims=True) + norm_eps)
        normed = rows * scale
        incoming = r.dh_total[at]
        product = incoming * normed
        r.attn_gain[...] += product[0:8] + product[8:16]
        incoming = incoming * gain[:, 0:D]
        mean = jnp.mean(incoming * normed, axis=-1, keepdims=True)
        r.out_input_grad[at] += scale * (incoming - normed * mean)


def back_to_projections(r, gain):
    plain = HEAD_WIDTH ** (-0.5)
    r.head_gain[...] = jnp.zeros_like(r.head_gain)

    @pl.loop(0, SEQ // TILE)
    def _(t):
        at = row_tile(t, TILE)
        cos_t, sin_t = r.cosine[at], r.sine[at]
        for h in range(OWN_HEADS + OWN_KV):
            mine = h < OWN_HEADS
            d_rows = r.d_query[h, at] if mine else r.d_key[h - OWN_HEADS, at] * plain
            first = 2 * D if mine else 2 * D + HEAD_WIDTH
            d_gained = d_rows * cos_t - turn(d_rows) * sin_t
            normed, scale = head_norm(r.raw[h, at].astype(F32))
            product = d_gained * normed
            r.head_gain[0 if mine else 1] += jnp.sum(product.reshape(TILE // 8, 8, HEAD_WIDTH), axis=0)
            incoming = d_gained * gain[:, first : first + HEAD_WIDTH]
            mean = jnp.mean(incoming * normed, axis=-1, keepdims=True)
            r.d_proj[pl.ds(2 * t, 2), :, 128 * h : 128 * h + 128] = (
                (scale * (incoming - normed * mean)).astype(BF).reshape(2, BLOCK, HEAD_WIDTH)
            )
        for h in range(OWN_KV):
            r.d_proj[pl.ds(2 * t, 2), :, 768 + 128 * h : 896 + 128 * h] = (
                r.d_value[h, at].astype(BF).reshape(2, BLOCK, HEAD_WIDTH)
            )


def block_weights(r, b):
    return r.w[:, :, 64 * b : 64 * b + 64].reshape(D, D)


def block_down(r, b):
    return r.w[:, :, 192:UNIT].reshape(FF // 2, D)[512 * b : 512 * b + 512]


def product_rows(r, first, last):
    parts = []
    if first < D:
        parts.append(r.d_o[...].reshape(2 * ROWS, D)[:, first : min(last, D)])
    if last > D:
        parts.append(r.d_q[2:4].reshape(2 * ROWS, D)[:, max(first, D) - D : last - D])
    return parts[0] if len(parts) == 1 else jnp.concatenate(parts, axis=1)


def d_gate_up_rows(r, b, t):
    if b < 2:
        return r.d_proj[pl.ds(4 * b + 2 * t, 2)].reshape(ROWS, D)
    return r.d_q[t].reshape(ROWS, D)


def feed_forward(r, w_loads):
    w_loads[0].wait()
    w_loads[1].wait()
    for b in range(3):
        if b:
            w_loads[1 + b].wait()
        weights, down = block_weights(r, b), block_down(r, b)

        @pl.loop(0, 2)
        def _(t):
            gate_up = dot_nn(r.hidden[row_tile(t, ROWS)], weights)
            d_product = dot_nt(r.hidden[row_tile(2 + t, ROWS)], down)
            gate, up = gate_up[:, :512], gate_up[:, 512:]
            sigmoid = 1.0 / (1.0 + jnp.exp(-gate))
            active = gate * sigmoid
            product = (active * up).astype(BF).reshape(4, 64, 512)
            if b < 2:
                r.d_o[pl.ds(2 * t, 2), :, :, 512 * b : 512 * b + 512] = product.reshape(2, 2, 64, 512)
            else:
                r.d_q[2 + t, :, :, :, 0:512] = product.reshape(4, 2, 32, 512)
            d_gate = d_product * up * sigmoid * (1.0 + gate * (1.0 - sigmoid))
            d_both = jnp.concatenate([d_gate, d_product * active], axis=1).astype(BF)
            if b < 2:
                r.d_proj[pl.ds(4 * b + 2 * t, 2)] = d_both.reshape(2, BLOCK, D)
            else:
                r.d_q[t] = d_both.reshape(4, 2, 32, D)


def feed_forward_inputs(r):
    def half(t):
        total = dot_nt(d_gate_up_rows(r, 0, t), block_weights(r, 0))
        for b in (1, 2):
            total = total + dot_nt(d_gate_up_rows(r, b, t), block_weights(r, b))
        return total

    r.dh_sib[...] = half(1).astype(BF)
    r.out_input_grad[...] = half(0)


def feed_forward_outputs(r):
    down = r.w[:, :, 192:UNIT].reshape(FF // 2, D)

    def half(t):
        first = dot_nn(r.d_o[2 * t : 2 * t + 2].reshape(ROWS, D), down[:D])
        return first + dot_nn(r.d_q[2 + t, :, :, :, 0:512].reshape(ROWS, 512), down[D:])

    r.out_sib[...] = half(1).astype(BF)
    r.dh_total[...] = half(0)


def dot_tn(left, right):
    return lax.dot_general(left, right, (((0,), (0,)), ((), ())), preferred_element_type=F32)


def feed_forward_gradients(r):
    for b in range(3):
        d_both = jnp.concatenate([d_gate_up_rows(r, b, 0), d_gate_up_rows(r, b, 1)], axis=0)

        @pl.loop(0, 4)
        def _(i):
            columns = pl.ds(pl.multiple_of(i * 256, 256), 256)
            left = r.hidden[0 : 2 * ROWS, columns]
            r.w[i, :, 64 * b : 64 * b + 64] = dot_tn(left, d_both).astype(BF).reshape(4, 64, D)

    cot = r.hidden[2 * ROWS : SEQ]
    for i in range(4):
        left = product_rows(r, 384 * i, 384 * i + 384)
        r.w[i, :, 192:UNIT] = dot_tn(left, cot).astype(BF).reshape(4, 96, D)


def backward_kernel(r):
    place = Place()
    z, x, k, y = (place[a] for a in "zxky")
    diagonal = z == y
    gain = r.gain_row
    near = neighbours(place, "xyzk")
    everyone = [ours_at(place, *o) for o in OURS] + [theirs_at(place, *o) for o in THEIRS]
    greet(near + everyone)
    for other in range(4):

        @pl.when(not_here(diagonal, other, z))
        def _():
            greet([place.device(z=jnp.int32(other), y=z)])

    loads = {
        n: pltpu.make_async_copy(getattr(r, "in_" + n), getattr(r, n), r.load.at[i]) for i, n in enumerate(SAVED)
    }
    pair_loads = [
        pltpu.make_async_copy(pair, r.hidden.at[rows], r.w_sem.at[4 + i])
        for i, (pair, rows) in enumerate([(r.hidden_pair, pl.ds(0, 2 * ROWS)), (r.cot_pair, pl.ds(2 * ROWS, 2 * ROWS))])
    ]
    w_loads = [
        pltpu.make_async_copy(r.w_all.at[:, :, rows], r.w.at[:, :, rows], r.w_sem.at[i])
        for i, rows in enumerate([pl.ds(0, 64), pl.ds(192, 96), pl.ds(64, 64), pl.ds(128, 64)])
    ]
    hidden_load = loads.pop("hidden")
    for copy in pair_loads + w_loads + list(loads.values()):
        copy.start()

    def a_part(i, h):
        return r.w.at[i, pl.ds(2 * h, 2), pl.ds(0, PART_A)]

    def b_part(i, h):
        return r.w.at[pl.ds(2 * h, 2), i, pl.ds(PART_A, UNIT - PART_A)]

    a_one = Scatter(place, "z", a_part, [r.a_box.at[n] for n in range(6)], (r.a1_s, r.a1_r))
    b_one = Scatter(place, "x", b_part, [r.b_box.at[n] for n in range(6)], (r.b1_s, r.b1_r))
    await_greetings(len(near) + len(everyone) + jnp.where(diagonal, 3, 4))

    dh_copy = remote(r.dh_sib, r.dh_box, r.core.at[0], r.core.at[1], place.sibling())
    out_copy = remote(r.out_sib, r.out_box, r.core.at[2], r.core.at[3], place.sibling())
    for copy in pair_loads:
        copy.wait()
    feed_forward(r, w_loads)
    feed_forward_inputs(r)
    dh_copy.start()
    feed_forward_outputs(r)
    out_copy.start()
    dh_copy.wait_recv()
    back_through_norm(r, gain)
    ring = Gather(
        place, "y", lambda i, h: r.d_attn_all.at[2 * i + h], (r.t_s, r.t_r),
        own=lambda h: r.own.at[pl.ds(BLOCK * h, BLOCK)],
    )
    ring.start()
    r.d_attn_all[pl.ds(2 * y, 2)] = r.own[...].reshape(2, BLOCK, D)
    feed_forward_gradients(r)
    hidden_load.start()
    a_one.start()
    b_one.start()
    out_copy.wait_recv()

    @pl.loop(0, ROWS // 16)
    def _(t):
        at = row_tile(t, 16)
        r.out_layer_out[at] = (r.middle[at] + r.dh_total[at] + r.out_box[at].astype(F32)).astype(BF)

    for copy in [hidden_load, *loads.values()]:
        copy.wait()
    r.d_key[...] = jnp.zeros_like(r.d_key)
    r.d_value[...] = jnp.zeros_like(r.d_value)
    ring.forward()
    a_one.forward()
    b_one.forward()
    ring.finish()

    wo = r.wo_all[...].reshape(OWN_HEADS * HEAD_WIDTH, D)

    @pl.loop(0, SEQ // TILE)
    def _(t):
        at = row_tile(t, TILE)
        rows = pair_of(r.d_attn_all, r.stored, t)
        r.d_q[t] = rows.reshape(4, 2, 32, D)
        both = dot_nt(rows, wo)
        for h in range(OWN_HEADS):
            r.d_attended[h, at] = both[:, 128 * h : 128 * h + 128].astype(BF)

    d_sorted = r.d_q[...].reshape(SEQ, D)

    @pl.loop(0, 4)
    def _(i):
        r.d_o[i] = dot_nn(r.attended_t[i], d_sorted).astype(BF).reshape(2, 64, D)

    o_core = remote(r.d_o.at[:, 1 - k], r.o_box, r.core.at[4], r.core.at[5], place.sibling())
    o_core.start()
    attend_back(r, 0, 2)
    o_core.wait_recv()

    @pl.loop(0, 4)
    def _(i):
        add_rows(r.o_box.at[i], [r.o_box.at[i], r.d_o.at[i, k]])

    o_x = Scatter(
        place, "x", lambda i, h: r.o_box.at[i, pl.ds(32 * h, 32)],
        [r.ox_box.at[n] for n in range(6)], (r.ox_s, r.ox_r),
    )
    o_x.start()
    a_one.finish(lambda h: a_part(z, h))
    b_one.finish(lambda h: b_part(x, h))
    a_two = Scatter(
        place, "x", lambda i, h: r.w.at[z, i, from_to(h, 0, 80, PART_A)],
        [r.a_box2.at[n, pl.ds(0, 80 if n in (0, 3, 4) else 64)] for n in range(6)], (r.a2_s, r.a2_r),
    )
    b_two = Scatter(
        place, "z", lambda i, h: r.w.at[i, x, from_to(h, PART_A, 208, UNIT)],
        [r.b_box2.at[n, pl.ds(0, 64 if n in (0, 3, 4) else 80)] for n in range(6)], (r.b2_s, r.b2_r),
    )
    a_two.start()
    b_two.start()
    attend_back(r, 2, 4)
    o_x.forward()
    back_to_projections(r, gain)

    wq = r.wq_all[:, :, :, :, 0:D].reshape(D, D)

    @pl.loop(0, 4)
    def _(i):
        rows = jnp.concatenate([r.d_proj[r.span[2 * i + n]] for n in range(2)], axis=0)
        r.d_attn_all[pl.ds(2 * i, 2)] = dot_nt(rows, wq).astype(BF).reshape(2, BLOCK, D)

    dh_ring = Scatter(
        place, "y", lambda i, h: r.d_attn_all.at[2 * i + h],
        [r.y_box.at[n] for n in range(6)], (r.y_s, r.y_r),
    )
    dh_ring.start()

    d_proj = r.d_proj[...].reshape(SEQ, D)

    @pl.loop(0, 4)
    def _(t):
        left = r.hidden[:, pl.ds(pl.multiple_of(t * 256, 256), 256)]
        rows = dot_tn(left, d_proj)
        r.d_q[t] = rows.astype(BF).reshape(4, 2, 32, D)

    q_core = remote(r.d_q.at[:, :, 1 - k], r.q_box, r.core.at[6], r.core.at[7], place.sibling())
    q_core.start()
    a_two.forward()
    b_two.forward()
    dh_ring.forward()
    o_x.finish(lambda h: r.o_two.at[pl.ds(32 * h, 32)])

    def o_target(other):
        return place.device(z=y, y=jnp.int32(other))

    for other in range(4):
        piece = r.o_two.at[pl.ds(16 * other, 16)]

        @pl.when(not_here(diagonal, other, y))
        def _():
            remote(piece, r.o_slots.at[z], r.oy_s.at[other], r.oy_r.at[z], o_target(other)).start()

    @pl.when(diagonal)
    def _():
        r.o_slots[z] = r.o_two[row_tile(y, 16)]

    q_core.wait_recv()

    @pl.loop(0, 4)
    def _(i):
        @pl.loop(0, 4)
        def _(j):
            add_rows(r.q_box.at[i, j], [r.q_box.at[i, j], r.d_q.at[i, j, k]])

    q_z = Scatter(
        place, "z", lambda i, h: r.q_box.at[i, pl.ds(2 * h, 2)],
        [r.qz_box.at[n] for n in range(6)], (r.qz_s, r.qz_r),
    )
    q_z.start()

    a_two.finish(lambda h: r.total.at[from_to(h, 0, 80, PART_A)])
    b_two.finish(lambda h: r.total.at[from_to(h, PART_A, 208, UNIT)])
    for c in range(4):
        for b in range(3):
            at = 64 * b + 8 * c
            rows = jnp.concatenate([r.total[at : at + 8], r.total[at + 32 : at + 40]], axis=0)
            r.g_send[c, 16 * b : 16 * b + 16] = rows.astype(BF)
    r.g_slots[y] = r.g_send[y]

    def down_rows(c):
        return pl.ds(pl.multiple_of(192 + 24 * c, 8), 24)

    r.d_slots[y] = r.total[down_rows(y)]
    y_copies = []
    for n in (1, 3, 2):
        to = place.moved("y", n)
        y_copies.append(remote(r.g_send.at[to], r.g_slots.at[y], r.gy_s.at[n], r.gy_r.at[y], place.peer("y", n)))
        y_copies.append(remote(r.total.at[down_rows(to)], r.d_slots.at[y], r.dy_s.at[n], r.dy_r.at[y], place.peer("y", n)))
    for copy in y_copies:
        copy.start()
    q_z.forward()
    dh_ring.finish(lambda h: r.dh_total.at[pl.ds(BLOCK * h, BLOCK)])
    back_to_input(r, gain)

    for n in (1, 3, 2):
        source = place.moved("y", n)
        remote(r.g_send.at[0], r.g_slots.at[source], r.gy_s.at[n], r.gy_r.at[source], place.peer("y", n)).wait_recv()
        remote(r.total.at[pl.ds(192, 24)], r.d_slots.at[source], r.dy_s.at[n], r.dy_r.at[source], place.peer("y", n)).wait_recv()
    r.out_d_out[...] = r.d_slots[0] + r.d_slots[1] + r.d_slots[2] + r.d_slots[3]
    summed = r.g_slots[0].astype(F32)
    for c in range(1, 4):
        summed = summed + r.g_slots[c].astype(F32)
    summed = summed.reshape(3, 2, 8, D)
    r.g_sum[0] = summed[:, 0]
    r.g_sum[1] = summed[:, 1]
    r.out_g_out[k] = r.g_sum[k]
    g_core = remote(r.g_sum.at[1 - k], r.out_g_out.at[k], r.core.at[8], r.core.at[9], place.sibling())
    g_core.start()
    for other in range(4):

        @pl.when(not_here(diagonal, other, z))
        def _():
            remote(r.o_two.at[pl.ds(0, 16)], r.o_slots.at[other], r.oy_s.at[0], r.oy_r.at[other], place.device(z=jnp.int32(other), y=z)).wait_recv()

    o_sum = r.o_slots[0].astype(F32)
    for c in range(1, 4):
        o_sum = o_sum + r.o_slots[c].astype(F32)
    r.out_o_out[...] = o_sum

    q_z.finish(lambda h: r.q_two.at[pl.ds(2 * h, 2)])
    q_x = Scatter(
        place, "x", lambda i, h: r.q_two.at[i, pl.ds(16 * h, 16)],
        [r.qx_box.at[n] for n in range(6)], (r.qx_s, r.qx_r),
    )
    q_x.start()
    q_x.forward()
    q_x.finish(lambda h: r.q_three.at[pl.ds(16 * h, 16)])
    r.out_q_out[y] = r.q_three[row_tile(y, 8)]
    q_copies = [
        remote(r.q_three.at[row_tile(place.moved("y", n), 8)], r.out_q_out.at[y], r.qy_s.at[n], r.qy_r.at[y], place.peer("y", n))
        for n in (1, 3, 2)
    ]
    for copy in q_copies:
        copy.start()
    remote(r.g_sum.at[0], r.out_g_out.at[1 - k], r.core.at[8], r.core.at[9], place.sibling()).wait_recv()
    for n in (1, 3, 2):
        source = place.moved("y", n)
        remote(r.q_three.at[pl.ds(0, 8)], r.out_q_out.at[source], r.qy_s.at[n], r.qy_r.at[source], place.peer("y", n)).wait_recv()

    squares = jnp.zeros((8, D), F32)
    for part in [r.out_q_out[c] for c in range(4)] + [r.out_g_out[c, b] for c in range(2) for b in range(3)]:
        squares = squares + part * part
    for c in range(2):
        part = r.out_o_out[8 * c : 8 * c + 8]
        squares = squares + part * part
    for c in range(3):
        part = r.out_d_out[8 * c : 8 * c + 8]
        squares = squares + part * part
    attn = jnp.sum(r.attn_gain[...], axis=0, keepdims=True)
    mlp = jnp.sum(r.mlp_gain[...], axis=0, keepdims=True)
    squares = jnp.sum(squares, axis=0, keepdims=True)
    r.value_row[...] = jnp.zeros_like(r.value_row)
    lanes = jnp.zeros((1, 128), F32)
    for c in range(8):
        at = slice(128 * c, 128 * c + 128)
        r.value_row[c : c + 1] = attn[:, at]
        r.value_row[8 + c : 9 + c] = mlp[:, at]
        lanes = lanes + squares[:, at]
    for c in range(2):
        r.value_row[16 + c : 17 + c] = jnp.sum(r.head_gain[c], axis=0, keepdims=True)
    r.value_row[18:19] = lanes
    sum_everywhere(r, place)

    for copy in [dh_copy, out_copy, o_core, q_core, g_core] + y_copies + q_copies:
        copy.wait_send()
    for other in range(4):

        @pl.when(not_here(diagonal, other, y))
        def _():
            remote(r.o_two.at[pl.ds(16 * other, 16)], r.o_slots.at[z], r.oy_s.at[other], r.oy_r.at[z], o_target(other)).wait_send()


def backward_step(**given):
    given = {("in_" + n if n in SAVED else n): v for n, v in given.items()}
    outputs = {
        "layer_out": ((ROWS, D), BF, vmem),
        "input_grad": ((ROWS, D), F32, vmem),
        "q_out": ((4, 8, D), F32, vmem),
        "o_out": ((16, D), F32, vmem),
        "g_out": ((2, 3, 8, D), F32, vmem),
        "d_out": ((24, D), F32, vmem),
        "sums": ((24, 128), F32, vmem),
    }
    head_rows = (OWN_HEADS, SEQ, HEAD_WIDTH)
    kv_rows = (OWN_KV, SEQ, HEAD_WIDTH)
    scratch = {
        **{n: pltpu.VMEM(*what) for n, what in SAVED.items()},
        "out_box": pltpu.VMEM((ROWS, D), BF),
        "dh_box": pltpu.VMEM((ROWS, D), BF),
        "own": pltpu.VMEM((ROWS, D), BF),
        "d_attn_all": pltpu.VMEM((8, BLOCK, D), BF),
        "d_attended": pltpu.VMEM(head_rows, BF),
        "d_query": pltpu.VMEM(head_rows, F32),
        "d_key": pltpu.VMEM(kv_rows, F32),
        "d_value": pltpu.VMEM(kv_rows, F32),
        "d_proj": pltpu.VMEM((8, BLOCK, D), BF),
        "y_box": pltpu.VMEM((6, BLOCK, D), BF),
        "dh_total": pltpu.VMEM((ROWS, D), F32),
        "a_box": pltpu.VMEM((6, 2, PART_A, D), BF),
        "b_box": pltpu.VMEM((6, 2, PART_A, D), BF),
        "w": pltpu.VMEM((4, 4, UNIT, D), BF),
        "out_sib": pltpu.VMEM((ROWS, D), BF),
        "dh_sib": pltpu.VMEM((ROWS, D), BF),
        "a_box2": pltpu.VMEM((6, 80, D), BF),
        "b_box2": pltpu.VMEM((6, 80, D), BF),
        "total": pltpu.VMEM((UNIT, D), F32),
        "g_send": pltpu.VMEM((4, 48, D), BF),
        "g_slots": pltpu.VMEM((4, 48, D), BF),
        "d_slots": pltpu.VMEM((4, 24, D), F32),
        "g_sum": pltpu.VMEM((2, 3, 8, D), F32),
        "d_q": pltpu.VMEM((4, 4, 2, 32, D), BF),
        "d_o": pltpu.VMEM((4, 2, 64, D), BF),
        "q_box": pltpu.VMEM((4, 4, 32, D), BF),
        "qz_box": pltpu.VMEM((6, 2, 32, D), BF),
        "q_two": pltpu.VMEM((4, 32, D), BF),
        "qx_box": pltpu.VMEM((6, 16, D), BF),
        "q_three": pltpu.VMEM((32, D), F32),
        "o_box": pltpu.VMEM((4, 64, D), BF),
        "ox_box": pltpu.VMEM((6, 32, D), BF),
        "o_two": pltpu.VMEM((64, D), BF),
        "o_slots": pltpu.VMEM((4, 16, D), BF),
        "mlp_gain": pltpu.VMEM((8, D), F32),
        "attn_gain": pltpu.VMEM((8, D), F32),
        "head_gain": pltpu.VMEM((2, 8, HEAD_WIDTH), F32),
        "value_row": pltpu.VMEM((24, 128), F32),
        "first": pltpu.VMEM((8, 24, 128), F32),
        "second": pltpu.VMEM((16, 24, 128), F32),
        "held": pltpu.VMEM((24, 128), F32),
        "core": dma(10),
        "load": dma(len(SAVED)),
        "w_sem": dma(6),
        **{n: dma(4) for n in ("gy_s", "gy_r", "dy_s", "dy_r", "qy_s", "qy_r", "oy_s", "oy_r")},
        **{"s1_s": dma(7), "s1_r": dma(8), "s2_s": dma(15), "s2_r": dma(16)},
        **rings("t", "y", "a1", "b1", "a2", "b2", "qz", "qx", "ox"),
    }
    spaces = {"span": smem, "stored": smem, "w_all": hbm, "hidden_pair": hbm, "cot_pair": hbm, **{"in_" + n: hbm for n in SAVED}}
    return named_call(backward_kernel, 2, "backward_attention", given, spaces, outputs, scratch)


def gain_spread():
    return jnp.asarray(np.arange(128)[:, None] == np.arange(GAINS)[None, :] % 18, BF)


def rope_tables():
    middle = HEAD_WIDTH // 2
    frequency = rope_base ** (-(np.arange(middle) * 2.0) / HEAD_WIDTH)
    angle = np.arange(SEQ)[:, None] * frequency[None, :]
    cosine, sine = np.cos(angle), np.sin(angle)
    return (
        jnp.asarray(np.concatenate([cosine, cosine], axis=1), F32),
        jnp.asarray(np.concatenate([-sine, sine], axis=1), F32),
    )


def adam_update(weight, first, second, grad, factor, rate, decay):
    clipped = grad * factor
    new_first = beta_one * first + (1.0 - beta_one) * clipped
    new_second = beta_two * second + (1.0 - beta_two) * clipped * clipped
    direction = (
        new_first
        / (1.0 - beta_one**STEP)
        / (jnp.sqrt(new_second / (1.0 - beta_two**STEP)) + adam_eps)
    )
    return (weight - rate * (direction + decay * weight), new_first, new_second)


def pack_gateup(w):
    rows = w.shape[0]
    v = w.reshape(rows, 2, 16, 2, 96).transpose(3, 0, 1, 2, 4).reshape(2, rows, 2, 3, 512)
    return v.transpose(0, 3, 1, 2, 4).reshape(2, 3, rows, 1024)


def unpack_gateup(v):
    rows = v.shape[2]
    w = v.reshape(2, 3, rows, 2, 512).transpose(0, 2, 3, 1, 4).reshape(2, rows, 2, 16, 96)
    return w.transpose(1, 2, 3, 0, 4).reshape(rows, 2 * FF)


def body(
    tokens, cotangent, span_order,
    w_qkv, w_out, w_gateup, w_down, gains,
    first_qkv, first_out, first_gateup, first_down, first_gains,
    second_qkv, second_out, second_gateup, second_down, second_gains,
):
    own_gains = jnp.pad(gains[None, :], ((0, 7), (0, 128 - gains.shape[0])))
    block = jnp.arange(8, dtype=jnp.int32)
    stored = jnp.sum(jnp.where(span_order[None, :] == block[:, None], block[None, :], 0), axis=1)
    cosine, sine = rope_tables()
    fwd = forward_step(
        span=span_order, stored=stored, tok=tokens, cot=cotangent, wq=w_qkv, wo=w_out,
        wgu=pack_gateup(w_gateup), wd=w_down, gains=own_gains, spread=gain_spread(),
        cosine=cosine, sine=sine,
    )

    bwd = backward_step(
        span=span_order, stored=stored, tok=tokens, cot=cotangent, middle=fwd["middle"],
        gain_row=fwd["gain_row"], cosine=cosine, sine=sine,
        hidden_pair=fwd["hidden_pair"], cot_pair=fwd["cot_pair"], w_all=fwd["w_all"],
        **{name: fwd[name] for name in SAVED},
    )
    q_grad, o_grad, gu_grad, down_grad = (bwd[n] for n in ("q_out", "o_out", "g_out", "d_out"))
    q_shard = jnp.concatenate(
        [
            q_grad[:, :, :512].transpose(1, 0, 2).reshape(8, 2048),
            q_grad[:, :, 512:768].transpose(1, 0, 2).reshape(8, 1024),
            q_grad[:, :, 768:].transpose(1, 0, 2).reshape(8, 1024),
        ],
        axis=1,
    )
    shards = [q_shard, o_grad, unpack_gateup(gu_grad), down_grad]
    sums = bwd["sums"]
    all_gains = sums[:18].reshape(-1)
    grad_norm = jnp.sqrt(jnp.sum(sums[18]) + jnp.sum(all_gains * all_gains))
    index = lax.axis_index("dp") * 4 + lax.axis_index("ctx")
    shards.append(lax.dynamic_slice_in_dim(all_gains, index * 18, 18))

    factor = jnp.minimum(1.0, clip_at / (grad_norm + 1e-06))
    masters = (w_qkv, w_out, w_gateup, w_down, gains)
    firsts = (first_qkv, first_out, first_gateup, first_down, first_gains)
    seconds = (second_qkv, second_out, second_gateup, second_down, second_gains)
    rates = (matrix_rate, out_rate, matrix_rate, matrix_rate, gain_rate)
    decays = (matrix_decay, matrix_decay, matrix_decay, matrix_decay, 0.0)
    news, new_firsts, new_seconds = [], [], []
    for which in range(5):
        weight, first, second = adam_update(
            masters[which], firsts[which], seconds[which], shards[which], factor,
            rates[which], decays[which],
        )
        news.append(weight)
        new_firsts.append(first)
        new_seconds.append(second)
    return (bwd["layer_out"], bwd["input_grad"], *news, *new_firsts, *new_seconds, grad_norm)


def solution(mesh):
    rows, flat = P(("dp", "ctx"), None), P(("dp", "ctx"))
    state = (rows, rows, rows, rows, flat)
    in_specs = (rows, rows, P()) + state * 3
    out_specs = (rows, rows) + state * 3 + (P(),)
    return jax.shard_map(body, mesh=mesh, in_specs=in_specs, out_specs=out_specs, check_vma=False)
```

```python
import jax
import jax.numpy as jnp
import numpy as np
from jax import lax
from jax.experimental import pallas as pl
from jax.experimental.pallas import tpu as pltpu
from jax.sharding import PartitionSpec as P

D = 1024
HEADS = 16
KV_HEADS = 8
HEAD_WIDTH = 128
FF = 3072
STEP = 10

norm_eps = 1e-06
rope_base = 1000000.0
beta_one = 0.9
beta_two = 0.999
adam_eps = 1e-08
clip_at = 1.0
matrix_rate = 0.05
out_rate = 0.25
matrix_decay = 0.1
gain_rate = 0.5
masked_score = -1e30

MESH = pl.DeviceIdType.MESH
BF = jnp.bfloat16
F32 = jnp.float32
ROWS = 256
UNIT = 224
PART_A = 112
DOWN = 128
VMEM_LIMIT = 62 * 2**20
vmem = pl.BlockSpec(memory_space=pltpu.VMEM)
hbm = pl.BlockSpec(memory_space=pl.ANY)


class Place:
    def __init__(self):
        dp = lax.axis_index("dp")
        self.at = {
            "z": lax.div(dp, 8),
            "x": lax.rem(lax.div(dp, 2), 4),
            "k": lax.rem(dp, 2),
            "y": lax.axis_index("ctx"),
        }

    def __getitem__(self, axis):
        return self.at[axis]

    def device(self, **other):
        c = {**self.at, **other}
        return (c["z"] * 8 + c["x"] * 2 + c["k"], c["y"])

    def moved(self, axis, steps):
        return lax.rem(self.at[axis] + steps, 4)

    def peer(self, axis, steps):
        return self.device(**{axis: self.moved(axis, steps)})

    def sibling(self):
        return self.device(k=1 - self.at["k"])


def greet(devices):
    barrier = pltpu.get_barrier_semaphore()
    for device in devices:
        pl.semaphore_signal(barrier, inc=1, device_id=device, device_id_type=MESH)


def await_greetings(count):
    pl.semaphore_wait(pltpu.get_barrier_semaphore(), count)


def neighbours(place, axes):
    found = []
    for axis in axes:
        if axis == "k":
            found.append(place.sibling())
        else:
            found += [place.peer(axis, 1), place.peer(axis, 3)]
    return found


def remote(src, dst, send, recv, device):
    return pltpu.make_async_remote_copy(
        src_ref=src, dst_ref=dst, send_sem=send, recv_sem=recv, device_id=device, device_id_type=MESH
    )


class Gather:
    def __init__(self, place, axis, part, sems, own=None):
        self.part, self.send, self.recv = part, sems[0], sems[1]
        self.own = own or (lambda half: part(place[axis], half))
        self.next, self.prev = place.peer(axis, 1), place.peer(axis, 3)
        self.me, self.up, self.down, self.far = (place.moved(axis, n) for n in (0, 1, 3, 2))

    def copy(self, n, slot, half, device, src=None):
        view = self.part(slot, half)
        return remote(src if src is not None else view, view, self.send.at[n], self.recv.at[n], device)

    def outgoing(self, n):
        slot, half, device = [
            (self.me, 0, self.next),
            (self.me, 1, self.prev),
            (self.me, 1, self.next),
            (self.me, 0, self.prev),
            (self.down, 0, self.next),
            (self.up, 1, self.prev),
        ][n]
        return self.copy(n, slot, half, device, self.own(half) if n < 4 else None)

    def start(self):
        for n in range(4):
            self.outgoing(n).start()

    def forward(self):
        self.copy(0, self.down, 0, self.prev).wait_recv()
        self.outgoing(4).start()
        self.copy(1, self.up, 1, self.next).wait_recv()
        self.outgoing(5).start()

    def finish(self):
        self.copy(2, self.down, 1, self.prev).wait_recv()
        self.copy(3, self.up, 0, self.next).wait_recv()
        self.copy(4, self.far, 0, self.prev).wait_recv()
        self.copy(5, self.far, 1, self.next).wait_recv()
        for n in range(6):
            self.outgoing(n).wait_send()


class Scatter:
    def __init__(self, place, axis, part, boxes, sems, mine=None):
        self.part, self.boxes = part, boxes
        self.send, self.recv = sems[0], sems[1]
        self.next, self.prev = place.peer(axis, 1), place.peer(axis, 3)
        self.me, self.up, self.down, self.far = (place.moved(axis, n) for n in (0, 1, 3, 2))
        self.mine = mine or self.own_part

    def own_part(self, n):
        slot, half = [(self.down, 0), (self.up, 1), (self.me, 0), (self.me, 1)][n]
        return self.part(slot, half)

    def copy(self, n, src, device):
        return remote(src, self.boxes[n], self.send.at[n], self.recv.at[n], device)

    def outgoing(self, n):
        source, device = [
            (lambda: self.part(self.far, 0), self.prev),
            (lambda: self.part(self.far, 1), self.next),
            (lambda: self.part(self.down, 1), self.prev),
            (lambda: self.part(self.up, 0), self.next),
            (lambda: self.boxes[0], self.prev),
            (lambda: self.boxes[1], self.next),
        ][n]
        return self.copy(n, source(), device)

    def start(self):
        for n in range(4):
            self.outgoing(n).start()

    def forward(self):
        for n in range(2):
            self.outgoing(n).wait_recv()
            add_rows(self.boxes[n], [self.boxes[n], self.mine(n)])
            self.outgoing(4 + n).start()

    def finish(self, result):
        for n in (2, 3, 4, 5):
            self.outgoing(n).wait_recv()
        add_rows(result(0), [self.mine(2), self.boxes[3], self.boxes[4]])
        add_rows(result(1), [self.mine(3), self.boxes[2], self.boxes[5]])
        for n in range(6):
            self.outgoing(n).wait_send()


def add_rows(out, terms):
    shape = out.shape
    rows = shape[-2]

    def block(at):
        total = terms[0][at].astype(F32)
        for term in terms[1:]:
            total = total + term[at].astype(F32)
        out[at] = total.astype(out.dtype)

    if len(shape) == 2:

        @pl.loop(0, rows // 16)
        def _(r):
            block((pl.ds(pl.multiple_of(r * 16, 16), 16), slice(None)))

    else:

        @pl.loop(0, shape[0])
        def _(lead):
            @pl.loop(0, rows // 16)
            def _(r):
                block((lead, pl.ds(pl.multiple_of(r * 16, 16), 16), slice(None)))


def dma(*shape):
    return pltpu.SemaphoreType.DMA(shape)


def ring_sems():
    return [dma(6), dma(6)]


def params(which):
    return pltpu.CompilerParams(
        collective_id=which, has_side_effects=True, vmem_limit_bytes=VMEM_LIMIT
    )


TILE = 256
SEQ = 4 * ROWS
BLOCK = ROWS // 2
OWN_HEADS = HEADS // 4
OWN_KV = KV_HEADS // 4
LOG2E = 1.4426950408889634


def turn(value_rows):
    return pltpu.roll(value_rows, HEAD_WIDTH // 2, 1)


def head_norm(raw):
    scale = lax.rsqrt(jnp.mean(raw * raw, axis=-1, keepdims=True) + norm_eps)
    return raw * scale, scale


def pair_of(ref, order, tile):
    return jnp.concatenate([ref[order[2 * tile]], ref[order[2 * tile + 1]]], axis=0)


def dot_nt(left, right):
    return lax.dot_general(left, right, (((1,), (1,)), ((), ())), preferred_element_type=F32)


def dot_nn(left, right):
    return jnp.dot(left, right, preferred_element_type=F32)


def causal(scores):
    keys = lax.broadcasted_iota(jnp.int32, scores.shape, 0)
    queries = lax.broadcasted_iota(jnp.int32, scores.shape, 1)
    return jnp.where(keys <= queries, scores, masked_score)


def project(r, g_attn, g_query, g_key):
    stored, tok, cosine, sine = r.stored, r.tok_all, r.cosine, r.sine
    hidden, raw, query, key, key_t = r.hidden, r.raw, r.query, r.key, r.key_t
    value, value_t = r.value, r.value_t

    def columns(pair):
        return r.wq_all[:, :, :, :, 256 * pair : 256 * pair + 256].reshape(D, 256)

    @pl.loop(0, SEQ // TILE)
    def _(t):
        at = pl.ds(pl.multiple_of(t * TILE, TILE), TILE)
        rows = pair_of(tok, stored, t).astype(F32)
        scale = lax.rsqrt(jnp.mean(rows * rows, axis=-1, keepdims=True) + norm_eps)
        hid = (rows * scale * g_attn[...]).astype(BF)
        hidden[at] = hid
        cos_t, sin_t = cosine[at], sine[at]
        for pair in range(OWN_HEADS // 2):
            both = dot_nn(hid, columns(pair))
            for n in range(2):
                h, part = 2 * pair + n, both[:, 128 * n : 128 * n + 128]
                raw[h, at] = part.astype(BF)
                normed = head_norm(part)[0] * g_query[...]
                query[h, at] = (normed * cos_t + turn(normed) * sin_t).astype(BF)
        both = dot_nn(hid, columns(2))
        for h in range(OWN_KV):
            part = both[:, 128 * h : 128 * h + 128]
            raw[OWN_HEADS + h, at] = part.astype(BF)
            normed = head_norm(part)[0] * g_key[...]
            rotated = normed * cos_t + turn(normed) * sin_t
            key[h, at] = rotated.astype(BF)
            key_t[h, :, at] = rotated.T.astype(BF)
        both = dot_nn(hid, columns(3))
        for h in range(OWN_KV):
            part = both[:, 128 * h : 128 * h + 128]
            value[h, at] = part.astype(BF)
            value_t[h, :, at] = part.T.astype(BF)


def attend(r, first_head, last_head):
    query, key, value_t, attended = r.query, r.key, r.value_t, r.attended
    attended_t, log_total = r.attended_t, r.log_total
    factor = HEAD_WIDTH ** (-0.5) * LOG2E

    @pl.loop(first_head, last_head)
    def _(h):
        kv = lax.div(h, 2)
        for t in range(SEQ // TILE):
            low, high = t * TILE, (t + 1) * TILE
            q = query[h, low:high]
            scores = [causal(dot_nt(key[kv, low:high], q))]
            if t:
                scores.append(dot_nt(key[kv, 0:low], q))
            top = jnp.max(scores[0], axis=0, keepdims=True)
            if t:
                top = jnp.maximum(top, jnp.max(scores[1], axis=0, keepdims=True))
            top = top * factor
            probs = [jnp.exp2(s * factor - top) for s in scores]
            total = jnp.sum(probs[0], axis=0, keepdims=True)
            mixed = dot_nn(value_t[kv, :, low:high], probs[0].astype(BF))
            if t:
                total = total + jnp.sum(probs[1], axis=0, keepdims=True)
                mixed = mixed + dot_nn(value_t[kv, :, 0:low], probs[1].astype(BF))
            mixed = mixed * (1.0 / total)
            attended_t[h, :, low:high] = mixed.astype(BF)
            attended[h, 2 * t : 2 * t + 2] = mixed.T.astype(BF).reshape(2, BLOCK, HEAD_WIDTH)
            log_total[h, :, low:high] = jnp.broadcast_to(top + jnp.log2(total), (8, TILE))


def attend_back(r, first_head, last_head):
    query, key, key_t, value = r.query, r.key, r.key_t, r.value
    d_attended, log_total, d_query = r.d_attended, r.log_total, r.d_query
    d_key, d_value = r.d_key, r.d_value
    factor = HEAD_WIDTH ** (-0.5) * LOG2E
    plain = HEAD_WIDTH ** (-0.5)

    @pl.loop(first_head, last_head)
    def _(h):
        kv = lax.div(h, 2)
        for t in range(SEQ // TILE):
            low, high = t * TILE, (t + 1) * TILE
            q = query[h, low:high]
            da = d_attended[h, low:high]
            total = log_total[h, 0:1, low:high]
            spans = [(low, high)] + ([(0, low)] if t else [])
            probs, mixes = [], []
            for n, (first, last) in enumerate(spans):
                scores = dot_nt(key[kv, first:last], q)
                if n == 0:
                    scores = causal(scores)
                p = jnp.exp2(scores * factor - total)
                d_value[kv, first:last] += dot_nn(p.astype(BF), da)
                probs.append(p)
                mixes.append(p * dot_nt(value[kv, first:last], da))
            delta = jnp.sum(mixes[0], axis=0, keepdims=True)
            if t:
                delta = delta + jnp.sum(mixes[1], axis=0, keepdims=True)
            back = None
            for (first, last), p, mix in zip(spans, probs, mixes):
                ds = (mix - p * delta).astype(BF)
                d_key[kv, first:last] += dot_nn(ds, q)
                part = dot_nn(key_t[kv, :, first:last], ds)
                back = part if back is None else back + part
            d_query[h, low:high] = (back * plain).T


GAINS = 2 * D + 2 * HEAD_WIDTH
smem = pl.BlockSpec(memory_space=pltpu.SMEM)
regular = pltpu.SemaphoreType.DMA


class Names:
    def __init__(self, names, refs):
        self.__dict__.update(zip(names, refs))


def named_call(kernel, which, name, given, spaces, outputs, scratch):
    names = list(given) + ["out_" + n for n in outputs] + list(scratch)
    results = pl.pallas_call(
        lambda *refs: kernel(Names(names, refs)),
        out_shape=tuple(jax.ShapeDtypeStruct(shape, kind) for shape, kind, _ in outputs.values()),
        in_specs=[spaces.get(n, vmem) for n in given],
        out_specs=tuple(space for _, _, space in outputs.values()),
        scratch_shapes=list(scratch.values()),
        compiler_params=params(which),
        name=name,
    )(*given.values())
    return dict(zip(outputs, results))


SAVED = {
    "wq_all": ((4, 4, 2, 32, 1152), BF),
    "wo_all": ((4, 2, 64, D), BF),
    "hidden": ((SEQ, D), BF),
    "raw": ((OWN_HEADS + OWN_KV, SEQ, HEAD_WIDTH), BF),
    "query": ((OWN_HEADS, SEQ, HEAD_WIDTH), BF),
    "key": ((OWN_KV, SEQ, HEAD_WIDTH), BF),
    "key_t": ((OWN_KV, HEAD_WIDTH, SEQ), BF),
    "value": ((OWN_KV, SEQ, HEAD_WIDTH), BF),
    "attended_t": ((OWN_HEADS, HEAD_WIDTH, SEQ), BF),
    "log_total": ((OWN_HEADS, 8, SEQ), F32),
}


def heads_of(ref, count, at):
    return jnp.concatenate([ref[h, at] for h in range(count)], axis=1)


def row_tile(r, size):
    return pl.ds(pl.multiple_of(r * size, size), size)


def from_to(half, low, split, high):
    return pl.ds(low, split - low) if half == 0 else pl.ds(split, high - split)


def not_here(condition, other, coordinate):
    return jnp.logical_not(jnp.logical_and(condition, coordinate == other))


def forward_kernel(r):
    place = Place()
    z, x, k, y = (place[a] for a in "zxky")
    near = neighbours(place, "xyzk")
    diagonal = z == y
    plane = [theirs_at(place, *o) for o in THEIRS]
    greet(near + [place.peer("y", 2)] + plane)
    for other in range(4):

        @pl.when(not_here(diagonal, other, y))
        def _():
            greet([place.device(z=y, y=jnp.int32(other))])

    for i in range(4):
        r.q_send[i, :, 0:512] = r.wq[:, 512 * i : 512 * i + 512]
        r.q_send[i, :, 512:768] = r.wq[:, 2048 + 256 * i : 2304 + 256 * i]
        r.q_send[i, :, 768:1024] = r.wq[:, 3072 + 256 * i : 3328 + 256 * i]
        r.q_send[i, :, 1024:1152] = r.gains[...]
    r.q_recv[y] = r.q_send[y]
    r.o_send[...] = r.wo[...].astype(BF)
    r.tok_all[pl.ds(2 * y, 2)] = r.tok[...].reshape(2, BLOCK, D)
    r.out_cot_pair[0:ROWS] = r.cot[...]
    await_greetings(len(near) + 1 + len(plane) + jnp.where(diagonal, 3, 4))

    g_prep = remote(r.wgu.at[1 - k], r.g_recv, r.pair.at[0], r.pair.at[1], place.sibling())
    g_prep.start()
    q_prep = [
        remote(r.q_send.at[place.moved("y", n)], r.q_recv.at[y], r.qp_s.at[n], r.qp_r.at[y], place.peer("y", n))
        for n in (1, 3, 2)
    ]
    for copy in q_prep:
        copy.start()

    def o_slot(source):
        return r.wo_all.at[x, k, row_tile(source, 16)]

    for other in range(4):

        @pl.when(not_here(diagonal, other, z))
        def _():
            remote(r.o_send, o_slot(y), r.op_s.at[other], r.op_r.at[y], place.device(z=jnp.int32(other), y=z)).start()

    @pl.when(diagonal)
    def _():
        r.wo_all[x, k, row_tile(y, 16)] = r.o_send[...]

    cot_copy = remote(r.cot, r.out_cot_pair.at[pl.ds(ROWS, ROWS)], r.pair.at[2], r.pair.at[3], place.sibling())
    cot_copy.start()

    g_prep.wait_recv()
    g_own, g_other, lower = r.wgu[k], r.g_recv[...], k == 0
    both = jnp.concatenate([jnp.where(lower, g_own, g_other), jnp.where(lower, g_other, g_own)], axis=1)
    r.g_y[y] = both[0:2].reshape(32, D).astype(BF)
    r.w_c[y, 4 * z + x] = both[2].astype(BF)
    c_x = Gather(place, "x", lambda i, h: r.w_c.at[y, 4 * z + i, :, pl.ds(512 * h, 512)], (r.cx_s, r.cx_r))
    c_z = Gather(place, "z", lambda i, h: r.w_c.at[y, pl.ds(4 * i + 2 * h, 2)], (r.cz_s, r.cz_r))
    c_y = Gather(place, "y", lambda i, h: r.w_c.at[i, pl.ds(8 * h, 8)], (r.cy_s, r.cy_r))
    r.d_y[y] = r.wd[...]
    g_ring = Gather(place, "y", lambda i, h: r.g_y.at[i, pl.ds(16 * h, 16)], (r.gy_s, r.gy_r))
    d_ring = Gather(place, "y", lambda i, h: r.d_y.at[i, from_to(h, 0, 16, 24)], (r.dy_s, r.dy_r))
    g_ring.start()
    d_ring.start()
    c_x.start()

    for n in (1, 3, 2):
        source = place.moved("y", n)
        remote(r.q_send.at[0], r.q_recv.at[source], r.qp_s.at[n], r.qp_r.at[source], place.peer("y", n)).wait_recv()
    r.wq_all[z, x, k] = r.q_recv[...].reshape(32, 1152).astype(BF)
    q_direct = []
    for n, (dz, dx) in enumerate(THEIRS):
        unit = r.wq_all.at[z, x, k]
        q_direct.append(remote(unit, unit, r.qd_s.at[n], r.qd_r.at[4 * z + x], theirs_at(place, dz, dx)))
    for copy in q_direct:
        copy.start()
    tokens = Gather(place, "y", lambda i, h: r.tok_all.at[2 * i + h], (r.t_s, r.t_r))
    tokens.start()

    for other in range(4):

        @pl.when(not_here(diagonal, other, y))
        def _():
            remote(r.o_send, o_slot(other), r.op_s.at[0], r.op_r.at[other], place.device(z=y, y=jnp.int32(other))).wait_recv()

    o_x = Gather(place, "x", lambda i, h: r.wo_all.at[i, k, pl.ds(32 * h, 32)], (r.ox_s, r.ox_r))
    o_x.start()
    g_ring.forward()
    d_ring.forward()
    c_x.forward()
    c_x.finish()
    c_z.start()
    o_x.forward()
    g_ring.finish()
    d_ring.finish()

    for b in range(2):
        pieces = [r.g_y[c, 16 * b : 16 * b + 16].astype(F32) for c in range(4)]
        for core_row in range(2):
            rows = jnp.concatenate([piece[8 * core_row : 8 * core_row + 8] for piece in pieces], axis=0)
            at = 64 * b + 32 * core_row
            r.unit[at : at + 32] = rows.astype(BF)
    r.unit[DOWN:UNIT] = r.d_y[...].reshape(96, D).astype(BF)
    w_all = r.out_w_all
    u_own = pltpu.make_async_copy(r.unit, w_all.at[z, x], r.pair.at[4])
    u_own.start()
    a_one = Gather(
        place, "x", lambda i, h: w_all.at[z, i, from_to(h, 0, 64, PART_A)], (r.a1_s, r.a1_r),
        own=lambda h: r.unit.at[from_to(h, 0, 64, PART_A)],
    )
    b_one = Gather(
        place, "z", lambda i, h: w_all.at[i, x, from_to(h, PART_A, 160, UNIT)], (r.b1_s, r.b1_r),
        own=lambda h: r.unit.at[from_to(h, PART_A, 160, UNIT)],
    )
    a_one.start()
    b_one.start()
    tokens.forward()
    c_z.forward()
    o_x.finish()
    o_core = remote(r.wo_all.at[:, k], r.wo_all.at[:, k], r.core.at[0], r.core.at[1], place.sibling())
    o_core.start()
    a_one.forward()
    b_one.forward()
    for dz, dx in THEIRS:
        other = r.wq_all.at[place.moved("z", dz), place.moved("x", dx), k]
        at = 4 * place.moved("z", dz) + place.moved("x", dx)
        remote(other, other, r.qd_s.at[0], r.qd_r.at[at], theirs_at(place, dz, dx)).wait_recv()
    q_core = remote(r.wq_all.at[:, :, k], r.wq_all.at[:, :, k], r.core.at[2], r.core.at[3], place.sibling())
    q_core.start()
    a_one.finish()
    b_one.finish()
    u_own.wait()
    a_two = Gather(place, "z", lambda i, h: w_all.at[i, pl.ds(2 * h, 2), pl.ds(0, PART_A)], (r.a2_s, r.a2_r))
    b_two = Gather(place, "x", lambda i, h: w_all.at[pl.ds(2 * h, 2), i, pl.ds(PART_A, UNIT - PART_A)], (r.b2_s, r.b2_r))
    a_two.start()
    b_two.start()
    c_z.finish()
    c_y.start()
    remote(r.wo_all.at[:, 1 - k], r.wo_all.at[:, 1 - k], r.core.at[0], r.core.at[1], place.sibling()).wait_recv()
    remote(r.wq_all.at[:, :, 1 - k], r.wq_all.at[:, :, 1 - k], r.core.at[2], r.core.at[3], place.sibling()).wait_recv()
    tokens.finish()

    lanes = r.wq_all[:, :, :, :, D:1152].reshape(128, 8, 128).astype(F32)
    spread = dot_nn(jnp.sum(lanes, axis=1).astype(BF), r.spread[...])
    owner = lax.broadcasted_iota(jnp.int32, (128, GAINS), 0) * 18
    spot = lax.broadcasted_iota(jnp.int32, (128, GAINS), 1)
    mine = jnp.logical_and(spot >= owner, spot < owner + 18)
    r.out_gain_row[...] = jnp.sum(jnp.where(mine, spread, 0.0), axis=0, keepdims=True)
    gain = r.out_gain_row
    project(r, gain.at[:, 0:D], gain.at[:, 2 * D : 2 * D + 128], gain.at[:, 2 * D + 128 : GAINS])
    attend(r, 0, 2)
    c_y.forward()
    a_two.forward()
    b_two.forward()
    attend(r, 2, 4)

    wo = r.wo_all[...].reshape(OWN_HEADS * HEAD_WIDTH, D)

    @pl.loop(0, 4)
    def _(i):
        rows = jnp.concatenate(
            [heads_of(r.attended, OWN_HEADS, r.span[2 * i + n]) for n in range(2)], axis=0
        )
        r.terms[i] = dot_nn(rows, wo).astype(BF)

    reduce = Scatter(
        place, "y", lambda i, h: r.terms.at[i, pl.ds(128 * h, 128)],
        [r.boxes.at[n] for n in range(6)], (r.y_s, r.y_r),
    )
    reduce.start()
    saves = [
        pltpu.make_async_copy(getattr(r, n), getattr(r, "out_" + n), r.save.at[i]) for i, n in enumerate(SAVED)
    ]
    for copy in saves:
        copy.start()
    c_y.finish()

    @pl.loop(0, 16)
    def _(j):
        pieces = [r.w_c[c, j].astype(F32) for c in range(4)]
        rows = [piece[8 * core_row : 8 * core_row + 8] for core_row in range(2) for piece in pieces]
        r.w_two[j] = jnp.concatenate(rows, axis=0).astype(BF)

    two_copy = pltpu.make_async_copy(r.w_two, r.out_w_two, r.pair.at[5])
    two_copy.start()
    reduce.forward()
    reduce.finish(lambda h: r.total.at[pl.ds(128 * h, 128)])

    @pl.loop(0, ROWS // 16)
    def _(t):
        at = row_tile(t, 16)
        rows = r.tok[at].astype(F32) + r.total[at]
        r.out_middle[at] = rows
        scale = lax.rsqrt(jnp.mean(rows * rows, axis=-1, keepdims=True) + norm_eps)
        r.out_hidden_pair[at] = (rows * scale * gain[:, D : 2 * D]).astype(BF)

    hid_copy = remote(r.out_hidden_pair.at[pl.ds(0, ROWS)], r.out_hidden_pair.at[pl.ds(ROWS, ROWS)], r.core.at[4], r.core.at[5], place.sibling())
    hid_copy.start()
    a_two.finish()
    b_two.finish()
    two_copy.wait()
    for copy in saves:
        copy.wait()
    for copy in q_prep + q_direct + [g_prep, o_core, q_core]:
        copy.wait_send()
    cot_copy.wait()
    hid_copy.wait()
    for other in range(4):

        @pl.when(not_here(diagonal, other, z))
        def _():
            remote(r.o_send, o_slot(y), r.op_s.at[other], r.op_r.at[y], place.device(z=jnp.int32(other), y=z)).wait_send()


def rings(*names):
    return {f"{name}_{end}": dma(6) for name in names for end in "sr"}


def forward_step(**given):
    outputs = {
        "middle": ((ROWS, D), F32, vmem),
        "hidden_pair": ((2 * ROWS, D), BF, vmem),
        "cot_pair": ((2 * ROWS, D), BF, vmem),
        "gain_row": ((1, GAINS), F32, vmem),
        "w_all": ((4, 4, UNIT, D), BF, hbm),
        "w_two": ((16, 64, D), BF, hbm),
        **{n: (*what, hbm) for n, what in SAVED.items()},
    }
    scratch = {
        "q_send": pltpu.VMEM((4, 8, 1152), F32),
        "q_recv": pltpu.VMEM((4, 8, 1152), F32),
        "o_send": pltpu.VMEM((16, D), BF),
        "g_recv": pltpu.VMEM((3, 8, D), F32),
        "g_y": pltpu.VMEM((4, 32, D), BF),
        "w_c": pltpu.VMEM((4, 16, 16, D), BF),
        "w_two": pltpu.VMEM((16, 64, D), BF),
        "d_y": pltpu.VMEM((4, 24, D), F32),
        "unit": pltpu.VMEM((UNIT, D), BF),
        "tok_all": pltpu.VMEM((8, BLOCK, D), BF),
        "value_t": pltpu.VMEM((OWN_KV, HEAD_WIDTH, SEQ), BF),
        "attended": pltpu.VMEM((OWN_HEADS, 8, BLOCK, HEAD_WIDTH), BF),
        "terms": pltpu.VMEM((4, ROWS, D), BF),
        "boxes": pltpu.VMEM((6, BLOCK, D), BF),
        "total": pltpu.VMEM((ROWS, D), F32),
        **{n: pltpu.VMEM(*what) for n, what in SAVED.items()},
        "pair": dma(6),
        "core": dma(6),
        "save": dma(len(SAVED)),
        **{n: dma(4) for n in ("qp_s", "qp_r", "op_s", "op_r")},
        **{"qd_s": dma(15), "qd_r": dma(16)},
        **rings("gy", "dy", "cx", "cz", "cy", "ox", "t", "a1", "b1", "a2", "b2", "y"),
    }
    spaces = {"span": smem, "stored": smem}
    return named_call(forward_kernel, 1, "forward_attention", given, spaces, outputs, scratch)


def sum_everywhere(r, place):
    z, x, k, y = (place[a] for a in "zxky")

    def stage(source, slots, send, recv, offsets, device, me, slot_of):
        slots[me] = source[...]
        copies = [
            remote(source, slots.at[me], send.at[n], recv.at[me], device(*offset))
            for n, offset in enumerate(offsets)
        ]
        for copy in copies:
            copy.start()
        for n, offset in enumerate(offsets):
            slot = slot_of(*offset)
            remote(source, slots.at[slot], send.at[n], recv.at[slot], device(*offset)).wait_recv()
        for copy in copies:
            copy.wait_send()

    stage(r.value_row, r.first, r.s1_s, r.s1_r, OURS, lambda *o: ours_at(place, *o), y * 2 + k,
          lambda dy, dk: place.moved("y", dy) * 2 + lax.rem(k + dk, 2))
    r.held[...] = jnp.sum(r.first[...], axis=0)
    stage(r.held, r.second, r.s2_s, r.s2_r, THEIRS, lambda *o: theirs_at(place, *o), z * 4 + x,
          lambda dz, dx: place.moved("z", dz) * 4 + place.moved("x", dx))
    r.out_sums[...] = jnp.sum(r.second[...], axis=0)


OURS = [(dy, dk) for dy in range(4) for dk in range(2) if (dy, dk) != (0, 0)]
THEIRS = [(dz, dx) for dz in range(4) for dx in range(4) if (dz, dx) != (0, 0)]


def ours_at(place, dy, dk):
    return place.device(y=place.moved("y", dy), k=lax.rem(place["k"] + dk, 2))


def theirs_at(place, dz, dx):
    return place.device(z=place.moved("z", dz), x=place.moved("x", dx))


def back_through_norm(r, gain):
    r.mlp_gain[...] = jnp.zeros_like(r.mlp_gain)

    @pl.loop(0, ROWS // 16)
    def _(t):
        at = row_tile(t, 16)
        rows = r.middle[at]
        scale = lax.rsqrt(jnp.mean(rows * rows, axis=-1, keepdims=True) + norm_eps)
        normed = rows * scale
        incoming = r.out_input_grad[at] + r.dh_box[at].astype(F32)
        product = incoming * normed
        r.mlp_gain[...] += product[0:8] + product[8:16]
        incoming = incoming * gain[:, D : 2 * D]
        mean = jnp.mean(incoming * normed, axis=-1, keepdims=True)
        d_mid = r.cot[at].astype(F32) + scale * (incoming - normed * mean)
        r.out_input_grad[at] = d_mid
        r.own[at] = d_mid.astype(BF)


def back_to_input(r, gain):
    r.attn_gain[...] = jnp.zeros_like(r.attn_gain)

    @pl.loop(0, ROWS // 16)
    def _(t):
        at = row_tile(t, 16)
        rows = r.tok[at].astype(F32)
        scale = lax.rsqrt(jnp.mean(rows * rows, axis=-1, keepdims=True) + norm_eps)
        normed = rows * scale
        incoming = r.dh_total[at]
        product = incoming * normed
        r.attn_gain[...] += product[0:8] + product[8:16]
        incoming = incoming * gain[:, 0:D]
        mean = jnp.mean(incoming * normed, axis=-1, keepdims=True)
        r.out_input_grad[at] += scale * (incoming - normed * mean)


def back_to_projections(r, gain):
    plain = HEAD_WIDTH ** (-0.5)
    r.head_gain[...] = jnp.zeros_like(r.head_gain)

    @pl.loop(0, SEQ // TILE)
    def _(t):
        at = row_tile(t, TILE)
        cos_t, sin_t = r.cosine[at], r.sine[at]
        for h in range(OWN_HEADS + OWN_KV):
            mine = h < OWN_HEADS
            d_rows = r.d_query[h, at] if mine else r.d_key[h - OWN_HEADS, at] * plain
            first = 2 * D if mine else 2 * D + HEAD_WIDTH
            d_gained = d_rows * cos_t - turn(d_rows) * sin_t
            normed, scale = head_norm(r.raw[h, at].astype(F32))
            product = d_gained * normed
            r.head_gain[0 if mine else 1] += jnp.sum(product.reshape(TILE // 8, 8, HEAD_WIDTH), axis=0)
            incoming = d_gained * gain[:, first : first + HEAD_WIDTH]
            mean = jnp.mean(incoming * normed, axis=-1, keepdims=True)
            r.d_proj[pl.ds(2 * t, 2), :, 128 * h : 128 * h + 128] = (
                (scale * (incoming - normed * mean)).astype(BF).reshape(2, BLOCK, HEAD_WIDTH)
            )
        for h in range(OWN_KV):
            r.d_proj[pl.ds(2 * t, 2), :, 768 + 128 * h : 896 + 128 * h] = (
                r.d_value[h, at].astype(BF).reshape(2, BLOCK, HEAD_WIDTH)
            )


def block_weights(r, b):
    if b == 2:
        return r.c[...].reshape(D, D)
    return r.w[:, :, 64 * b : 64 * b + 64].reshape(D, D)


def block_down(r, b):
    return r.w[:, :, DOWN:UNIT].reshape(FF // 2, D)[512 * b : 512 * b + 512]


def product_rows(r, first, last):
    parts = []
    if first < D:
        parts.append(r.d_o[...].reshape(2 * ROWS, D)[:, first : min(last, D)])
    if last > D:
        parts.append(r.d_q[2:4].reshape(2 * ROWS, D)[:, max(first, D) - D : last - D])
    return parts[0] if len(parts) == 1 else jnp.concatenate(parts, axis=1)


def d_gate_up_rows(r, b, t):
    if b < 2:
        return r.d_proj[pl.ds(4 * b + 2 * t, 2)].reshape(ROWS, D)
    return r.d_q[t].reshape(ROWS, D)


def feed_forward(r, w_loads):
    w_loads[0].wait()
    w_loads[1].wait()
    for b in range(3):
        if b:
            w_loads[1 + b].wait()
        weights, down = block_weights(r, b), block_down(r, b)

        @pl.loop(0, 2)
        def _(t):
            gate_up = dot_nn(r.hidden[row_tile(t, ROWS)], weights)
            d_product = dot_nt(r.hidden[row_tile(2 + t, ROWS)], down)
            gate, up = gate_up[:, :512], gate_up[:, 512:]
            sigmoid = 1.0 / (1.0 + jnp.exp(-gate))
            active = gate * sigmoid
            product = (active * up).astype(BF).reshape(4, 64, 512)
            if b < 2:
                r.d_o[pl.ds(2 * t, 2), :, :, 512 * b : 512 * b + 512] = product.reshape(2, 2, 64, 512)
            else:
                r.d_q[2 + t, :, :, :, 0:512] = product.reshape(4, 2, 32, 512)
            d_gate = d_product * up * sigmoid * (1.0 + gate * (1.0 - sigmoid))
            d_both = jnp.concatenate([d_gate, d_product * active], axis=1).astype(BF)
            if b < 2:
                r.d_proj[pl.ds(4 * b + 2 * t, 2)] = d_both.reshape(2, BLOCK, D)
            else:
                r.d_q[t] = d_both.reshape(4, 2, 32, D)


def feed_forward_inputs(r):
    def half(t):
        total = dot_nt(d_gate_up_rows(r, 0, t), block_weights(r, 0))
        for b in (1, 2):
            total = total + dot_nt(d_gate_up_rows(r, b, t), block_weights(r, b))
        return total

    r.dh_sib[...] = half(1).astype(BF)
    r.out_input_grad[...] = half(0)


def feed_forward_outputs(r):
    down = r.w[:, :, DOWN:UNIT].reshape(FF // 2, D)

    def half(t):
        first = dot_nn(r.d_o[2 * t : 2 * t + 2].reshape(ROWS, D), down[:D])
        return first + dot_nn(r.d_q[2 + t, :, :, :, 0:512].reshape(ROWS, 512), down[D:])

    r.out_sib[...] = half(1).astype(BF)
    r.dh_total[...] = half(0)


def dot_tn(left, right):
    return lax.dot_general(left, right, (((0,), (0,)), ((), ())), preferred_element_type=F32)


def feed_forward_gradients(r):
    for b in range(3):
        d_both = jnp.concatenate([d_gate_up_rows(r, b, 0), d_gate_up_rows(r, b, 1)], axis=0)

        @pl.loop(0, 4)
        def _(i):
            columns = pl.ds(pl.multiple_of(i * 256, 256), 256)
            rows = dot_tn(r.hidden[0 : 2 * ROWS, columns], d_both)
            if b < 2:
                r.w[i, :, 64 * b : 64 * b + 64] = rows.astype(BF).reshape(4, 64, D)
            else:
                rows = rows.reshape(4, 2, 4, 8, D)
                for c in range(4):
                    r.c[c, pl.ds(4 * i, 4)] = rows[:, :, c].reshape(4, 16, D).astype(BF)

    cot = r.hidden[2 * ROWS : SEQ]
    for i in range(4):
        left = product_rows(r, 384 * i, 384 * i + 384)
        r.w[i, :, DOWN:UNIT] = dot_tn(left, cot).astype(BF).reshape(4, 96, D)


def backward_kernel(r):
    place = Place()
    z, x, k, y = (place[a] for a in "zxky")
    diagonal = z == y
    gain = r.gain_row
    near = neighbours(place, "xyzk")
    everyone = [ours_at(place, *o) for o in OURS] + [theirs_at(place, *o) for o in THEIRS]
    greet(near + everyone)
    for other in range(4):

        @pl.when(not_here(diagonal, other, z))
        def _():
            greet([place.device(z=jnp.int32(other), y=z)])

    loads = {
        n: pltpu.make_async_copy(getattr(r, "in_" + n), getattr(r, n), r.load.at[i]) for i, n in enumerate(SAVED)
    }
    pair_loads = [
        pltpu.make_async_copy(pair, r.hidden.at[rows], r.w_sem.at[4 + i])
        for i, (pair, rows) in enumerate([(r.hidden_pair, pl.ds(0, 2 * ROWS)), (r.cot_pair, pl.ds(2 * ROWS, 2 * ROWS))])
    ]
    w_loads = [
        pltpu.make_async_copy(r.w_all.at[:, :, rows], r.w.at[:, :, rows], r.w_sem.at[i])
        for i, rows in enumerate([pl.ds(0, 64), pl.ds(DOWN, 96), pl.ds(64, 64)])
    ]
    w_loads.append(pltpu.make_async_copy(r.w_two, r.c, r.w_sem.at[3]))
    hidden_load = loads.pop("hidden")
    for copy in pair_loads + w_loads + list(loads.values()):
        copy.start()

    def a_part(i, h):
        return r.w.at[i, pl.ds(2 * h, 2), pl.ds(0, PART_A)]

    def b_part(i, h):
        return r.w.at[pl.ds(2 * h, 2), i, pl.ds(PART_A, UNIT - PART_A)]

    a_one = Scatter(place, "z", a_part, [r.a_box.at[n] for n in range(6)], (r.a1_s, r.a1_r))
    b_one = Scatter(place, "x", b_part, [r.b_box.at[n] for n in range(6)], (r.b1_s, r.b1_r))
    await_greetings(len(near) + len(everyone) + jnp.where(diagonal, 3, 4))

    dh_copy = remote(r.dh_sib, r.dh_box, r.core.at[0], r.core.at[1], place.sibling())
    out_copy = remote(r.out_sib, r.out_box, r.core.at[2], r.core.at[3], place.sibling())
    for copy in pair_loads:
        copy.wait()
    feed_forward(r, w_loads)
    feed_forward_inputs(r)
    dh_copy.start()
    feed_forward_outputs(r)
    out_copy.start()
    dh_copy.wait_recv()
    back_through_norm(r, gain)
    ring = Gather(
        place, "y", lambda i, h: r.d_attn_all.at[2 * i + h], (r.t_s, r.t_r),
        own=lambda h: r.own.at[pl.ds(BLOCK * h, BLOCK)],
    )
    ring.start()
    r.d_attn_all[pl.ds(2 * y, 2)] = r.own[...].reshape(2, BLOCK, D)
    feed_forward_gradients(r)
    hidden_load.start()
    a_one.start()
    b_one.start()
    out_copy.wait_recv()

    @pl.loop(0, ROWS // 16)
    def _(t):
        at = row_tile(t, 16)
        r.out_layer_out[at] = (r.middle[at] + r.dh_total[at] + r.out_box[at].astype(F32)).astype(BF)

    for copy in [hidden_load, *loads.values()]:
        copy.wait()
    r.d_key[...] = jnp.zeros_like(r.d_key)
    r.d_value[...] = jnp.zeros_like(r.d_value)
    ring.forward()
    a_one.forward()
    b_one.forward()
    ring.finish()
    c_y = Scatter(
        place, "y", lambda i, h: r.c.at[i, pl.ds(8 * h, 8)],
        [r.cy_box.at[n] for n in range(6)], (r.cy_s, r.cy_r),
    )
    c_z = Scatter(
        place, "z", lambda i, h: r.c.at[y, pl.ds(4 * i + 2 * h, 2)],
        [r.cz_box.at[n] for n in range(6)], (r.cz_s, r.cz_r),
    )
    c_x = Scatter(
        place, "x", lambda i, h: r.c.at[y, 4 * z + i, :, pl.ds(512 * h, 512)],
        [r.cx_box.at[n] for n in range(6)], (r.cx_s, r.cx_r),
    )
    c_y.start()

    wo = r.wo_all[...].reshape(OWN_HEADS * HEAD_WIDTH, D)

    @pl.loop(0, SEQ // TILE)
    def _(t):
        at = row_tile(t, TILE)
        rows = pair_of(r.d_attn_all, r.stored, t)
        r.d_q[t] = rows.reshape(4, 2, 32, D)
        both = dot_nt(rows, wo)
        for h in range(OWN_HEADS):
            r.d_attended[h, at] = both[:, 128 * h : 128 * h + 128].astype(BF)

    d_sorted = r.d_q[...].reshape(SEQ, D)

    @pl.loop(0, 4)
    def _(i):
        r.d_o[i] = dot_nn(r.attended_t[i], d_sorted).astype(BF).reshape(2, 64, D)

    o_core = remote(r.d_o.at[:, 1 - k], r.o_box, r.core.at[4], r.core.at[5], place.sibling())
    o_core.start()
    attend_back(r, 0, 2)
    c_y.forward()
    o_core.wait_recv()

    @pl.loop(0, 4)
    def _(i):
        add_rows(r.o_box.at[i], [r.o_box.at[i], r.d_o.at[i, k]])

    o_x = Scatter(
        place, "x", lambda i, h: r.o_box.at[i, pl.ds(32 * h, 32)],
        [r.ox_box.at[n] for n in range(6)], (r.ox_s, r.ox_r),
    )
    o_x.start()
    a_one.finish(lambda h: a_part(z, h))
    b_one.finish(lambda h: b_part(x, h))
    a_two = Scatter(
        place, "x", lambda i, h: r.w.at[z, i, from_to(h, 0, 64, PART_A)],
        [r.a_box2.at[n, pl.ds(0, 64 if n in (0, 3, 4) else 48)] for n in range(6)], (r.a2_s, r.a2_r),
    )
    b_two = Scatter(
        place, "z", lambda i, h: r.w.at[i, x, from_to(h, PART_A, 160, UNIT)],
        [r.b_box2.at[n, pl.ds(0, 48 if n in (0, 3, 4) else 64)] for n in range(6)], (r.b2_s, r.b2_r),
    )
    a_two.start()
    b_two.start()
    attend_back(r, 2, 4)
    c_y.finish(lambda h: r.c.at[y, pl.ds(8 * h, 8)])
    c_z.start()
    o_x.forward()
    back_to_projections(r, gain)

    wq = r.wq_all[:, :, :, :, 0:D].reshape(D, D)

    @pl.loop(0, 4)
    def _(i):
        rows = jnp.concatenate([r.d_proj[r.span[2 * i + n]] for n in range(2)], axis=0)
        r.d_attn_all[pl.ds(2 * i, 2)] = dot_nt(rows, wq).astype(BF).reshape(2, BLOCK, D)

    dh_ring = Scatter(
        place, "y", lambda i, h: r.d_attn_all.at[2 * i + h],
        [r.y_box.at[n] for n in range(6)], (r.y_s, r.y_r),
    )
    dh_ring.start()

    d_proj = r.d_proj[...].reshape(SEQ, D)

    @pl.loop(0, 4)
    def _(t):
        left = r.hidden[:, pl.ds(pl.multiple_of(t * 256, 256), 256)]
        rows = dot_tn(left, d_proj)
        r.d_q[t] = rows.astype(BF).reshape(4, 2, 32, D)

    q_core = remote(r.d_q.at[:, :, 1 - k], r.q_box, r.core.at[6], r.core.at[7], place.sibling())
    q_core.start()
    c_z.forward()
    a_two.forward()
    b_two.forward()
    dh_ring.forward()
    c_z.finish(lambda h: r.c.at[y, pl.ds(4 * z + 2 * h, 2)])
    c_x.start()
    o_x.finish(lambda h: r.o_two.at[pl.ds(32 * h, 32)])

    def o_target(other):
        return place.device(z=y, y=jnp.int32(other))

    for other in range(4):
        piece = r.o_two.at[pl.ds(16 * other, 16)]

        @pl.when(not_here(diagonal, other, y))
        def _():
            remote(piece, r.o_slots.at[z], r.oy_s.at[other], r.oy_r.at[z], o_target(other)).start()

    @pl.when(diagonal)
    def _():
        r.o_slots[z] = r.o_two[row_tile(y, 16)]

    q_core.wait_recv()

    @pl.loop(0, 4)
    def _(i):
        @pl.loop(0, 4)
        def _(j):
            add_rows(r.q_box.at[i, j], [r.q_box.at[i, j], r.d_q.at[i, j, k]])

    q_direct = []
    for n, (dz, dx) in enumerate(THEIRS):
        unit = r.q_box.at[place.moved("z", dz), place.moved("x", dx)]
        q_direct.append(remote(unit, r.q_slots.at[4 * z + x], r.qd_s.at[n], r.qd_r.at[4 * z + x], theirs_at(place, dz, dx)))
    for copy in q_direct:
        copy.start()
    r.q_slots[4 * z + x] = r.q_box[z, x]
    c_x.forward()

    a_two.finish(lambda h: r.total.at[from_to(h, 0, 64, PART_A)])
    b_two.finish(lambda h: r.total.at[from_to(h, PART_A, 160, UNIT)])
    for c in range(4):
        for b in range(2):
            at = 64 * b + 8 * c
            rows = jnp.concatenate([r.total[at : at + 8], r.total[at + 32 : at + 40]], axis=0)
            r.g_send[c, 16 * b : 16 * b + 16] = rows.astype(BF)
    r.g_slots[y] = r.g_send[y]

    def down_rows(c):
        return pl.ds(pl.multiple_of(DOWN + 24 * c, 8), 24)

    r.d_slots[y] = r.total[down_rows(y)]
    y_copies = []
    for n in (1, 3, 2):
        to = place.moved("y", n)
        y_copies.append(remote(r.g_send.at[to], r.g_slots.at[y], r.gy_s.at[n], r.gy_r.at[y], place.peer("y", n)))
        y_copies.append(remote(r.total.at[down_rows(to)], r.d_slots.at[y], r.dy_s.at[n], r.dy_r.at[y], place.peer("y", n)))
    for copy in y_copies:
        copy.start()
    c_x.finish(lambda h: r.c_sum.at[:, pl.ds(512 * h, 512)])
    dh_ring.finish(lambda h: r.dh_total.at[pl.ds(BLOCK * h, BLOCK)])
    back_to_input(r, gain)

    for n in (1, 3, 2):
        source = place.moved("y", n)
        remote(r.g_send.at[0], r.g_slots.at[source], r.gy_s.at[n], r.gy_r.at[source], place.peer("y", n)).wait_recv()
        remote(r.total.at[pl.ds(DOWN, 24)], r.d_slots.at[source], r.dy_s.at[n], r.dy_r.at[source], place.peer("y", n)).wait_recv()
    r.out_d_out[...] = r.d_slots[0] + r.d_slots[1] + r.d_slots[2] + r.d_slots[3]
    summed = r.g_slots[0].astype(F32)
    for c in range(1, 4):
        summed = summed + r.g_slots[c].astype(F32)
    summed = summed.reshape(2, 2, 8, D)
    last = r.c_sum[...].reshape(2, 8, D)
    for n in range(2):
        r.g_sum[n, 0:2] = summed[:, n]
        r.g_sum[n, 2] = last[n]
    r.out_g_out[k] = r.g_sum[k]
    g_core = remote(r.g_sum.at[1 - k], r.out_g_out.at[k], r.core.at[8], r.core.at[9], place.sibling())
    g_core.start()
    for other in range(4):

        @pl.when(not_here(diagonal, other, z))
        def _():
            remote(r.o_two.at[pl.ds(0, 16)], r.o_slots.at[other], r.oy_s.at[0], r.oy_r.at[other], place.device(z=jnp.int32(other), y=z)).wait_recv()

    o_sum = r.o_slots[0].astype(F32)
    for c in range(1, 4):
        o_sum = o_sum + r.o_slots[c].astype(F32)
    r.out_o_out[...] = o_sum

    for dz, dx in THEIRS:
        at = 4 * place.moved("z", dz) + place.moved("x", dx)
        remote(r.q_box.at[0, 0], r.q_slots.at[at], r.qd_s.at[0], r.qd_r.at[at], theirs_at(place, dz, dx)).wait_recv()

    @pl.loop(0, 2)
    def _(t):
        at = row_tile(t, 16)
        total = r.q_slots[0, at].astype(F32)
        for n in range(1, 16):
            total = total + r.q_slots[n, at].astype(F32)
        r.q_three[at] = total

    r.out_q_out[y] = r.q_three[row_tile(y, 8)]
    q_copies = [
        remote(r.q_three.at[row_tile(place.moved("y", n), 8)], r.out_q_out.at[y], r.qy_s.at[n], r.qy_r.at[y], place.peer("y", n))
        for n in (1, 3, 2)
    ]
    for copy in q_copies:
        copy.start()
    remote(r.g_sum.at[0], r.out_g_out.at[1 - k], r.core.at[8], r.core.at[9], place.sibling()).wait_recv()
    for n in (1, 3, 2):
        source = place.moved("y", n)
        remote(r.q_three.at[pl.ds(0, 8)], r.out_q_out.at[source], r.qy_s.at[n], r.qy_r.at[source], place.peer("y", n)).wait_recv()

    squares = jnp.zeros((8, D), F32)
    for part in [r.out_q_out[c] for c in range(4)] + [r.out_g_out[c, b] for c in range(2) for b in range(3)]:
        squares = squares + part * part
    for c in range(2):
        part = r.out_o_out[8 * c : 8 * c + 8]
        squares = squares + part * part
    for c in range(3):
        part = r.out_d_out[8 * c : 8 * c + 8]
        squares = squares + part * part
    attn = jnp.sum(r.attn_gain[...], axis=0, keepdims=True)
    mlp = jnp.sum(r.mlp_gain[...], axis=0, keepdims=True)
    squares = jnp.sum(squares, axis=0, keepdims=True)
    r.value_row[...] = jnp.zeros_like(r.value_row)
    lanes = jnp.zeros((1, 128), F32)
    for c in range(8):
        at = slice(128 * c, 128 * c + 128)
        r.value_row[c : c + 1] = attn[:, at]
        r.value_row[8 + c : 9 + c] = mlp[:, at]
        lanes = lanes + squares[:, at]
    for c in range(2):
        r.value_row[16 + c : 17 + c] = jnp.sum(r.head_gain[c], axis=0, keepdims=True)
    r.value_row[18:19] = lanes
    sum_everywhere(r, place)

    for copy in [dh_copy, out_copy, o_core, q_core, g_core] + y_copies + q_copies + q_direct:
        copy.wait_send()
    for other in range(4):

        @pl.when(not_here(diagonal, other, y))
        def _():
            remote(r.o_two.at[pl.ds(16 * other, 16)], r.o_slots.at[z], r.oy_s.at[other], r.oy_r.at[z], o_target(other)).wait_send()


def backward_step(**given):
    given = {("in_" + n if n in SAVED else n): v for n, v in given.items()}
    outputs = {
        "layer_out": ((ROWS, D), BF, vmem),
        "input_grad": ((ROWS, D), F32, vmem),
        "q_out": ((4, 8, D), F32, vmem),
        "o_out": ((16, D), F32, vmem),
        "g_out": ((2, 3, 8, D), F32, vmem),
        "d_out": ((24, D), F32, vmem),
        "sums": ((24, 128), F32, vmem),
    }
    head_rows = (OWN_HEADS, SEQ, HEAD_WIDTH)
    kv_rows = (OWN_KV, SEQ, HEAD_WIDTH)
    scratch = {
        **{n: pltpu.VMEM(*what) for n, what in SAVED.items()},
        "out_box": pltpu.VMEM((ROWS, D), BF),
        "dh_box": pltpu.VMEM((ROWS, D), BF),
        "own": pltpu.VMEM((ROWS, D), BF),
        "d_attn_all": pltpu.VMEM((8, BLOCK, D), BF),
        "d_attended": pltpu.VMEM(head_rows, BF),
        "d_query": pltpu.VMEM(head_rows, F32),
        "d_key": pltpu.VMEM(kv_rows, F32),
        "d_value": pltpu.VMEM(kv_rows, F32),
        "d_proj": pltpu.VMEM((8, BLOCK, D), BF),
        "y_box": pltpu.VMEM((6, BLOCK, D), BF),
        "dh_total": pltpu.VMEM((ROWS, D), F32),
        "a_box": pltpu.VMEM((6, 2, PART_A, D), BF),
        "b_box": pltpu.VMEM((6, 2, PART_A, D), BF),
        "w": pltpu.VMEM((4, 4, UNIT, D), BF),
        "out_sib": pltpu.VMEM((ROWS, D), BF),
        "dh_sib": pltpu.VMEM((ROWS, D), BF),
        "a_box2": pltpu.VMEM((6, 64, D), BF),
        "b_box2": pltpu.VMEM((6, 64, D), BF),
        "total": pltpu.VMEM((UNIT, D), F32),
        "g_send": pltpu.VMEM((4, 32, D), BF),
        "g_slots": pltpu.VMEM((4, 32, D), BF),
        "d_slots": pltpu.VMEM((4, 24, D), F32),
        "g_sum": pltpu.VMEM((2, 3, 8, D), F32),
        "d_q": pltpu.VMEM((4, 4, 2, 32, D), BF),
        "d_o": pltpu.VMEM((4, 2, 64, D), BF),
        "q_box": pltpu.VMEM((4, 4, 32, D), BF),
        "q_slots": pltpu.VMEM((16, 32, D), BF),
        "c": pltpu.VMEM((4, 16, 16, D), BF),
        "cy_box": pltpu.VMEM((6, 8, 16, D), BF),
        "cz_box": pltpu.VMEM((6, 2, 16, D), BF),
        "cx_box": pltpu.VMEM((6, 16, 512), BF),
        "c_sum": pltpu.VMEM((16, D), F32),
        "q_three": pltpu.VMEM((32, D), F32),
        "o_box": pltpu.VMEM((4, 64, D), BF),
        "ox_box": pltpu.VMEM((6, 32, D), BF),
        "o_two": pltpu.VMEM((64, D), BF),
        "o_slots": pltpu.VMEM((4, 16, D), BF),
        "mlp_gain": pltpu.VMEM((8, D), F32),
        "attn_gain": pltpu.VMEM((8, D), F32),
        "head_gain": pltpu.VMEM((2, 8, HEAD_WIDTH), F32),
        "value_row": pltpu.VMEM((24, 128), F32),
        "first": pltpu.VMEM((8, 24, 128), F32),
        "second": pltpu.VMEM((16, 24, 128), F32),
        "held": pltpu.VMEM((24, 128), F32),
        "core": dma(10),
        "load": dma(len(SAVED)),
        "w_sem": dma(6),
        **{n: dma(4) for n in ("gy_s", "gy_r", "dy_s", "dy_r", "qy_s", "qy_r", "oy_s", "oy_r")},
        **{"s1_s": dma(7), "s1_r": dma(8), "s2_s": dma(15), "s2_r": dma(16)},
        **{"qd_s": dma(15), "qd_r": dma(16)},
        **rings("t", "y", "a1", "b1", "a2", "b2", "cx", "cy", "cz", "ox"),
    }
    spaces = {"span": smem, "stored": smem, "w_all": hbm, "w_two": hbm, "hidden_pair": hbm, "cot_pair": hbm, **{"in_" + n: hbm for n in SAVED}}
    return named_call(backward_kernel, 2, "backward_attention", given, spaces, outputs, scratch)


def gain_spread():
    return jnp.asarray(np.arange(128)[:, None] == np.arange(GAINS)[None, :] % 18, BF)


def rope_tables():
    middle = HEAD_WIDTH // 2
    frequency = rope_base ** (-(np.arange(middle) * 2.0) / HEAD_WIDTH)
    angle = np.arange(SEQ)[:, None] * frequency[None, :]
    cosine, sine = np.cos(angle), np.sin(angle)
    return (
        jnp.asarray(np.concatenate([cosine, cosine], axis=1), F32),
        jnp.asarray(np.concatenate([-sine, sine], axis=1), F32),
    )


def adam_update(weight, first, second, grad, factor, rate, decay):
    clipped = grad * factor
    new_first = beta_one * first + (1.0 - beta_one) * clipped
    new_second = beta_two * second + (1.0 - beta_two) * clipped * clipped
    direction = (
        new_first
        / (1.0 - beta_one**STEP)
        / (jnp.sqrt(new_second / (1.0 - beta_two**STEP)) + adam_eps)
    )
    return (weight - rate * (direction + decay * weight), new_first, new_second)


def pack_gateup(w):
    rows = w.shape[0]
    v = w.reshape(rows, 2, 16, 2, 96).transpose(3, 0, 1, 2, 4).reshape(2, rows, 2, 3, 512)
    return v.transpose(0, 3, 1, 2, 4).reshape(2, 3, rows, 1024)


def unpack_gateup(v):
    rows = v.shape[2]
    w = v.reshape(2, 3, rows, 2, 512).transpose(0, 2, 3, 1, 4).reshape(2, rows, 2, 16, 96)
    return w.transpose(1, 2, 3, 0, 4).reshape(rows, 2 * FF)


def body(
    tokens, cotangent, span_order,
    w_qkv, w_out, w_gateup, w_down, gains,
    first_qkv, first_out, first_gateup, first_down, first_gains,
    second_qkv, second_out, second_gateup, second_down, second_gains,
):
    own_gains = jnp.pad(gains[None, :], ((0, 7), (0, 128 - gains.shape[0])))
    block = jnp.arange(8, dtype=jnp.int32)
    stored = jnp.sum(jnp.where(span_order[None, :] == block[:, None], block[None, :], 0), axis=1)
    cosine, sine = rope_tables()
    fwd = forward_step(
        span=span_order, stored=stored, tok=tokens, cot=cotangent, wq=w_qkv, wo=w_out,
        wgu=pack_gateup(w_gateup), wd=w_down, gains=own_gains, spread=gain_spread(),
        cosine=cosine, sine=sine,
    )

    bwd = backward_step(
        span=span_order, stored=stored, tok=tokens, cot=cotangent, middle=fwd["middle"],
        gain_row=fwd["gain_row"], cosine=cosine, sine=sine,
        hidden_pair=fwd["hidden_pair"], cot_pair=fwd["cot_pair"], w_all=fwd["w_all"],
        w_two=fwd["w_two"].reshape(4, 16, 16, D),
        **{name: fwd[name] for name in SAVED},
    )
    q_grad, o_grad, gu_grad, down_grad = (bwd[n] for n in ("q_out", "o_out", "g_out", "d_out"))
    q_shard = jnp.concatenate(
        [
            q_grad[:, :, :512].transpose(1, 0, 2).reshape(8, 2048),
            q_grad[:, :, 512:768].transpose(1, 0, 2).reshape(8, 1024),
            q_grad[:, :, 768:].transpose(1, 0, 2).reshape(8, 1024),
        ],
        axis=1,
    )
    shards = [q_shard, o_grad, unpack_gateup(gu_grad), down_grad]
    sums = bwd["sums"]
    all_gains = sums[:18].reshape(-1)
    grad_norm = jnp.sqrt(jnp.sum(sums[18]) + jnp.sum(all_gains * all_gains))
    index = lax.axis_index("dp") * 4 + lax.axis_index("ctx")
    shards.append(lax.dynamic_slice_in_dim(all_gains, index * 18, 18))

    factor = jnp.minimum(1.0, clip_at / (grad_norm + 1e-06))
    masters = (w_qkv, w_out, w_gateup, w_down, gains)
    firsts = (first_qkv, first_out, first_gateup, first_down, first_gains)
    seconds = (second_qkv, second_out, second_gateup, second_down, second_gains)
    rates = (matrix_rate, out_rate, matrix_rate, matrix_rate, gain_rate)
    decays = (matrix_decay, matrix_decay, matrix_decay, matrix_decay, 0.0)
    news, new_firsts, new_seconds = [], [], []
    for which in range(5):
        weight, first, second = adam_update(
            masters[which], firsts[which], seconds[which], shards[which], factor,
            rates[which], decays[which],
        )
        news.append(weight)
        new_firsts.append(first)
        new_seconds.append(second)
    return (bwd["layer_out"], bwd["input_grad"], *news, *new_firsts, *new_seconds, grad_norm)


def solution(mesh):
    rows, flat = P(("dp", "ctx"), None), P(("dp", "ctx"))
    state = (rows, rows, rows, rows, flat)
    in_specs = (rows, rows, P()) + state * 3
    out_specs = (rows, rows) + state * 3 + (P(),)
    return jax.shard_map(body, mesh=mesh, in_specs=in_specs, out_specs=out_specs, check_vma=False)
```

```python
import jax
import jax.numpy as jnp
import numpy as np
from jax import lax
from jax.experimental import pallas as pl
from jax.experimental.pallas import tpu as pltpu
from jax.sharding import PartitionSpec as P

D = 1024
HEADS = 16
KV_HEADS = 8
HEAD_WIDTH = 128
FF = 3072
STEP = 10

norm_eps = 1e-06
rope_base = 1000000.0
beta_one = 0.9
beta_two = 0.999
adam_eps = 1e-08
clip_at = 1.0
matrix_rate = 0.05
out_rate = 0.25
matrix_decay = 0.1
gain_rate = 0.5
masked_score = -1e30

MESH = pl.DeviceIdType.MESH
BF = jnp.bfloat16
F32 = jnp.float32
ROWS = 256
UNIT = 224
PART_A = 112
DOWN = 128
VMEM_LIMIT = 62 * 2**20
vmem = pl.BlockSpec(memory_space=pltpu.VMEM)
hbm = pl.BlockSpec(memory_space=pl.ANY)


class Place:
    def __init__(self):
        dp = lax.axis_index("dp")
        self.at = {
            "z": lax.div(dp, 8),
            "x": lax.rem(lax.div(dp, 2), 4),
            "k": lax.rem(dp, 2),
            "y": lax.axis_index("ctx"),
        }

    def __getitem__(self, axis):
        return self.at[axis]

    def device(self, **other):
        c = {**self.at, **other}
        return (c["z"] * 8 + c["x"] * 2 + c["k"], c["y"])

    def moved(self, axis, steps):
        return lax.rem(self.at[axis] + steps, 4)

    def peer(self, axis, steps):
        return self.device(**{axis: self.moved(axis, steps)})

    def sibling(self):
        return self.device(k=1 - self.at["k"])


def greet(devices):
    barrier = pltpu.get_barrier_semaphore()
    for device in devices:
        pl.semaphore_signal(barrier, inc=1, device_id=device, device_id_type=MESH)


def await_greetings(count):
    pl.semaphore_wait(pltpu.get_barrier_semaphore(), count)


def neighbours(place, axes):
    found = []
    for axis in axes:
        if axis == "k":
            found.append(place.sibling())
        else:
            found += [place.peer(axis, 1), place.peer(axis, 3)]
    return found


def remote(src, dst, send, recv, device):
    return pltpu.make_async_remote_copy(
        src_ref=src, dst_ref=dst, send_sem=send, recv_sem=recv, device_id=device, device_id_type=MESH
    )


class Gather:
    def __init__(self, place, axis, part, sems, own=None):
        self.part, self.send, self.recv = part, sems[0], sems[1]
        self.own = own or (lambda half: part(place[axis], half))
        self.next, self.prev = place.peer(axis, 1), place.peer(axis, 3)
        self.me, self.up, self.down, self.far = (place.moved(axis, n) for n in (0, 1, 3, 2))

    def copy(self, n, slot, half, device, src=None):
        view = self.part(slot, half)
        return remote(src if src is not None else view, view, self.send.at[n], self.recv.at[n], device)

    def outgoing(self, n):
        slot, half, device = [
            (self.me, 0, self.next),
            (self.me, 1, self.prev),
            (self.me, 1, self.next),
            (self.me, 0, self.prev),
            (self.down, 0, self.next),
            (self.up, 1, self.prev),
        ][n]
        return self.copy(n, slot, half, device, self.own(half) if n < 4 else None)

    def start(self, halves=(0, 1)):
        for half in halves:
            for n in ((0, 3), (1, 2))[half]:
                self.outgoing(n).start()

    def forward(self):
        self.copy(0, self.down, 0, self.prev).wait_recv()
        self.outgoing(4).start()
        self.copy(1, self.up, 1, self.next).wait_recv()
        self.outgoing(5).start()

    def finish(self):
        self.copy(2, self.down, 1, self.prev).wait_recv()
        self.copy(3, self.up, 0, self.next).wait_recv()
        self.copy(4, self.far, 0, self.prev).wait_recv()
        self.copy(5, self.far, 1, self.next).wait_recv()
        for n in range(6):
            self.outgoing(n).wait_send()


class Scatter:
    def __init__(self, place, axis, part, boxes, sems, mine=None):
        self.part, self.boxes = part, boxes
        self.send, self.recv = sems[0], sems[1]
        self.next, self.prev = place.peer(axis, 1), place.peer(axis, 3)
        self.me, self.up, self.down, self.far = (place.moved(axis, n) for n in (0, 1, 3, 2))
        self.mine = mine or self.own_part

    def own_part(self, n):
        slot, half = [(self.down, 0), (self.up, 1), (self.me, 0), (self.me, 1)][n]
        return self.part(slot, half)

    def copy(self, n, src, device):
        return remote(src, self.boxes[n], self.send.at[n], self.recv.at[n], device)

    def outgoing(self, n):
        source, device = [
            (lambda: self.part(self.far, 0), self.prev),
            (lambda: self.part(self.far, 1), self.next),
            (lambda: self.part(self.down, 1), self.prev),
            (lambda: self.part(self.up, 0), self.next),
            (lambda: self.boxes[0], self.prev),
            (lambda: self.boxes[1], self.next),
        ][n]
        return self.copy(n, source(), device)

    def start(self):
        for n in range(4):
            self.outgoing(n).start()

    def forward(self):
        for n in range(2):
            self.outgoing(n).wait_recv()
            add_rows(self.boxes[n], [self.boxes[n], self.mine(n)])
            self.outgoing(4 + n).start()

    def finish(self, result):
        for n in (2, 3, 4, 5):
            self.outgoing(n).wait_recv()
        add_rows(result(0), [self.mine(2), self.boxes[3], self.boxes[4]])
        add_rows(result(1), [self.mine(3), self.boxes[2], self.boxes[5]])
        for n in range(6):
            self.outgoing(n).wait_send()


def add_rows(out, terms):
    shape = out.shape
    rows = shape[-2]

    def block(at):
        total = terms[0][at].astype(F32)
        for term in terms[1:]:
            total = total + term[at].astype(F32)
        out[at] = total.astype(out.dtype)

    if len(shape) == 2:

        @pl.loop(0, rows // 16)
        def _(r):
            block((pl.ds(pl.multiple_of(r * 16, 16), 16), slice(None)))

    else:

        @pl.loop(0, shape[0])
        def _(lead):
            @pl.loop(0, rows // 16)
            def _(r):
                block((lead, pl.ds(pl.multiple_of(r * 16, 16), 16), slice(None)))


def dma(*shape):
    return pltpu.SemaphoreType.DMA(shape)


def ring_sems():
    return [dma(6), dma(6)]


def params(which):
    if which is None:
        return pltpu.CompilerParams(vmem_limit_bytes=VMEM_LIMIT)
    return pltpu.CompilerParams(
        collective_id=which, has_side_effects=True, vmem_limit_bytes=VMEM_LIMIT
    )


TILE = 256
SEQ = 4 * ROWS
BLOCK = ROWS // 2
OWN_HEADS = HEADS // 4
OWN_KV = KV_HEADS // 4
LOG2E = 1.4426950408889634


def turn(value_rows):
    return pltpu.roll(value_rows, HEAD_WIDTH // 2, 1)


def head_norm(raw):
    scale = lax.rsqrt(jnp.mean(raw * raw, axis=-1, keepdims=True) + norm_eps)
    return raw * scale, scale


def stored_block(span, position):
    found = jnp.int32(0)
    for block in range(1, 8):
        found = jnp.where(span[block] == position, block, found)
    return found


def pair_of(ref, span, tile):
    return jnp.concatenate([ref[stored_block(span, 2 * tile + n)] for n in range(2)], axis=0)


def dot_nt(left, right):
    return lax.dot_general(left, right, (((1,), (1,)), ((), ())), preferred_element_type=F32)


def dot_nn(left, right):
    return jnp.dot(left, right, preferred_element_type=F32)


def causal(scores):
    keys = lax.broadcasted_iota(jnp.int32, scores.shape, 0)
    queries = lax.broadcasted_iota(jnp.int32, scores.shape, 1)
    return jnp.where(keys <= queries, scores, masked_score)


def project(r, g_attn, g_query, g_key):
    span, tok, cosine, sine = r.span, r.tok_all, r.cosine, r.sine
    hidden, raw, query, key, key_t = r.hidden, r.raw, r.query, r.key, r.key_t
    value, value_t = r.value, r.value_t

    def columns(pair):
        return r.wq_all[:, :, :, :, 256 * pair : 256 * pair + 256].reshape(D, 256)

    @pl.loop(0, SEQ // TILE)
    def _(t):
        at = pl.ds(pl.multiple_of(t * TILE, TILE), TILE)
        rows = pair_of(tok, span, t).astype(F32)
        scale = lax.rsqrt(jnp.mean(rows * rows, axis=-1, keepdims=True) + norm_eps)
        hid = (rows * scale * g_attn[...]).astype(BF)
        hidden[at] = hid
        cos_t, sin_t = cosine[at], sine[at]
        for pair in range(OWN_HEADS // 2):
            both = dot_nn(hid, columns(pair))
            for n in range(2):
                h, part = 2 * pair + n, both[:, 128 * n : 128 * n + 128]
                raw[h, at] = part.astype(BF)
                normed = head_norm(part)[0] * g_query[...]
                query[h, at] = (normed * cos_t + turn(normed) * sin_t).astype(BF)
        both = dot_nn(hid, columns(2))
        for h in range(OWN_KV):
            part = both[:, 128 * h : 128 * h + 128]
            raw[OWN_HEADS + h, at] = part.astype(BF)
            normed = head_norm(part)[0] * g_key[...]
            rotated = normed * cos_t + turn(normed) * sin_t
            key[h, at] = rotated.astype(BF)
            key_t[h, :, at] = rotated.T.astype(BF)
        both = dot_nn(hid, columns(3))
        for h in range(OWN_KV):
            part = both[:, 128 * h : 128 * h + 128]
            value[h, at] = part.astype(BF)
            value_t[h, :, at] = part.T.astype(BF)


def attend(r, first_head, last_head):
    query, key, value_t, attended = r.query, r.key, r.value_t, r.attended
    attended_t, log_total = r.attended_t, r.log_total
    factor = HEAD_WIDTH ** (-0.5) * LOG2E

    @pl.loop(first_head, last_head)
    def _(h):
        kv = lax.div(h, 2)
        for t in range(SEQ // TILE):
            low, high = t * TILE, (t + 1) * TILE
            q = query[h, low:high]
            scores = [causal(dot_nt(key[kv, low:high], q))]
            if t:
                scores.append(dot_nt(key[kv, 0:low], q))
            top = jnp.max(scores[0], axis=0, keepdims=True)
            if t:
                top = jnp.maximum(top, jnp.max(scores[1], axis=0, keepdims=True))
            top = top * factor
            probs = [jnp.exp2(s * factor - top) for s in scores]
            total = jnp.sum(probs[0], axis=0, keepdims=True)
            mixed = dot_nn(value_t[kv, :, low:high], probs[0].astype(BF))
            if t:
                total = total + jnp.sum(probs[1], axis=0, keepdims=True)
                mixed = mixed + dot_nn(value_t[kv, :, 0:low], probs[1].astype(BF))
            mixed = mixed * (1.0 / total)
            attended_t[h, :, low:high] = mixed.astype(BF)
            attended[h, 2 * t : 2 * t + 2] = mixed.T.astype(BF).reshape(2, BLOCK, HEAD_WIDTH)
            log_total[h, :, low:high] = jnp.broadcast_to(top + jnp.log2(total), (8, TILE))


def attend_back(r, first_head, last_head):
    query, key, key_t, value = r.query, r.key, r.key_t, r.value
    d_attended, log_total, d_query = r.d_attended, r.log_total, r.d_query
    d_key, d_value = r.d_key, r.d_value
    factor = HEAD_WIDTH ** (-0.5) * LOG2E
    plain = HEAD_WIDTH ** (-0.5)

    @pl.loop(first_head, last_head)
    def _(h):
        kv = lax.div(h, 2)
        for t in range(SEQ // TILE):
            low, high = t * TILE, (t + 1) * TILE
            q = query[h, low:high]
            da = d_attended[h, low:high]
            total = log_total[h, 0:1, low:high]
            spans = [(low, high)] + ([(0, low)] if t else [])
            probs, mixes = [], []
            for n, (first, last) in enumerate(spans):
                scores = dot_nt(key[kv, first:last], q)
                if n == 0:
                    scores = causal(scores)
                p = jnp.exp2(scores * factor - total)
                d_value[kv, first:last] += dot_nn(p.astype(BF), da)
                probs.append(p)
                mixes.append(p * dot_nt(value[kv, first:last], da))
            delta = jnp.sum(mixes[0], axis=0, keepdims=True)
            if t:
                delta = delta + jnp.sum(mixes[1], axis=0, keepdims=True)
            back = None
            for (first, last), p, mix in zip(spans, probs, mixes):
                ds = (mix - p * delta).astype(BF)
                d_key[kv, first:last] += dot_nn(ds, q)
                part = dot_nn(key_t[kv, :, first:last], ds)
                back = part if back is None else back + part
            d_query[h, low:high] = (back * plain).T


GAINS = 2 * D + 2 * HEAD_WIDTH
smem = pl.BlockSpec(memory_space=pltpu.SMEM)
regular = pltpu.SemaphoreType.DMA


class Names:
    def __init__(self, names, refs):
        self.__dict__.update(zip(names, refs))


def named_call(kernel, which, name, given, spaces, outputs, scratch):
    names = list(given) + ["out_" + n for n in outputs] + list(scratch)
    results = pl.pallas_call(
        lambda *refs: kernel(Names(names, refs)),
        out_shape=tuple(jax.ShapeDtypeStruct(shape, kind) for shape, kind, _ in outputs.values()),
        in_specs=[spaces.get(n, vmem) for n in given],
        out_specs=tuple(space for _, _, space in outputs.values()),
        scratch_shapes=list(scratch.values()),
        compiler_params=params(which),
        name=name,
    )(*given.values())
    return dict(zip(outputs, results))


SAVED = {
    "wq_all": ((4, 4, 2, 32, 1152), BF),
    "wo_all": ((4, 2, 64, D), BF),
    "hidden": ((SEQ, D), BF),
    "raw": ((OWN_HEADS + OWN_KV, SEQ, HEAD_WIDTH), BF),
    "query": ((OWN_HEADS, SEQ, HEAD_WIDTH), BF),
    "key": ((OWN_KV, SEQ, HEAD_WIDTH), BF),
    "key_t": ((OWN_KV, HEAD_WIDTH, SEQ), BF),
    "value": ((OWN_KV, SEQ, HEAD_WIDTH), BF),
    "attended_t": ((OWN_HEADS, HEAD_WIDTH, SEQ), BF),
    "log_total": ((OWN_HEADS, 8, SEQ), F32),
}


def heads_of(ref, count, at):
    return jnp.concatenate([ref[h, at] for h in range(count)], axis=1)


def row_tile(r, size):
    return pl.ds(pl.multiple_of(r * size, size), size)


def from_to(half, low, split, high):
    return pl.ds(low, split - low) if half == 0 else pl.ds(split, high - split)


def not_here(condition, other, coordinate):
    return jnp.logical_not(jnp.logical_and(condition, coordinate == other))


def pack_gateup(w, out):
    for k in range(2):
        for side in range(2):
            pieces = [w[:, FF * side + 96 * n : FF * side + 96 * n + 96] for n in range(k, 32, 2)]
            columns = jnp.concatenate(pieces, axis=1)
            for b in range(3):
                out[k, b, :, 512 * side : 512 * side + 512] = columns[:, 512 * b : 512 * b + 512]


def unpack_gateup(packed):
    sides = []
    for side in range(2):
        cores = [
            jnp.concatenate([packed[k, b, :, 512 * side : 512 * side + 512] for b in range(3)], axis=1)
            for k in range(2)
        ]
        sides += [cores[n % 2][:, 96 * (n // 2) : 96 * (n // 2) + 96] for n in range(32)]
    return jnp.concatenate(sides, axis=1)


def forward_kernel(r):
    place = Place()
    z, x, k, y = (place[a] for a in "zxky")
    near = neighbours(place, "xyzk")
    diagonal = z == y
    plane = [theirs_at(place, *o) for o in THEIRS]
    greet(near + [place.peer("y", 2)] + plane)
    for other in range(4):

        @pl.when(not_here(diagonal, other, y))
        def _():
            greet([place.device(z=y, y=jnp.int32(other))])

    for i in range(4):
        r.q_send[i, :, 0:512] = r.wq[:, 512 * i : 512 * i + 512]
        r.q_send[i, :, 512:768] = r.wq[:, 2048 + 256 * i : 2304 + 256 * i]
        r.q_send[i, :, 768:1024] = r.wq[:, 3072 + 256 * i : 3328 + 256 * i]
        r.q_send[i, :, 1024:1152] = jnp.zeros((8, 128), F32)
        r.q_send[i, 0:1, 1024:1042] = r.gains[...]
    pack_gateup(r.wgu, r.packed)
    r.q_recv[y] = r.q_send[y]
    r.o_send[...] = r.wo[...].astype(BF)
    r.tok_all[pl.ds(2 * y, 2)] = r.tok[...].reshape(2, BLOCK, D)
    await_greetings(len(near) + 1 + len(plane) + jnp.where(diagonal, 3, 4))

    g_prep = remote(r.packed.at[1 - k], r.g_recv, r.pair.at[0], r.pair.at[1], place.sibling())
    g_prep.start()
    q_prep = [
        remote(r.q_send.at[place.moved("y", n)], r.q_recv.at[y], r.qp_s.at[n], r.qp_r.at[y], place.peer("y", n))
        for n in (1, 3, 2)
    ]
    for copy in q_prep:
        copy.start()

    def o_slot(source):
        return r.wo_all.at[x, k, row_tile(source, 16)]

    for other in range(4):

        @pl.when(not_here(diagonal, other, z))
        def _():
            remote(r.o_send, o_slot(y), r.op_s.at[other], r.op_r.at[y], place.device(z=jnp.int32(other), y=z)).start()

    @pl.when(diagonal)
    def _():
        r.wo_all[x, k, row_tile(y, 16)] = r.o_send[...]

    cot_copy = remote(r.cot, r.out_cot_pair.at[pl.ds(ROWS, ROWS)], r.pair.at[2], r.pair.at[3], place.sibling())
    cot_copy.start()
    cot_own = pltpu.make_async_copy(r.cot, r.out_cot_pair.at[pl.ds(0, ROWS)], r.pair.at[6])
    cot_own.start()

    g_prep.wait_recv()
    g_own, g_other, lower = r.packed[k], r.g_recv[...], k == 0
    both = jnp.concatenate([jnp.where(lower, g_own, g_other), jnp.where(lower, g_other, g_own)], axis=1)
    r.g_y[y] = both[0:2].reshape(32, D).astype(BF)
    r.w_c[y, 4 * z + x] = both[2].astype(BF)
    c_x = Gather(place, "x", lambda i, h: r.w_c.at[y, 4 * z + i, :, pl.ds(512 * h, 512)], (r.cx_s, r.cx_r))
    c_z = Gather(place, "z", lambda i, h: r.w_c.at[y, pl.ds(4 * i + 2 * h, 2)], (r.cz_s, r.cz_r))
    c_y = Gather(place, "y", lambda i, h: r.w_c.at[i, pl.ds(8 * h, 8)], (r.cy_s, r.cy_r))
    r.d_y[y] = r.wd[...]
    g_ring = Gather(place, "y", lambda i, h: r.g_y.at[i, pl.ds(16 * h, 16)], (r.gy_s, r.gy_r))
    d_ring = Gather(place, "y", lambda i, h: r.d_y.at[i, from_to(h, 0, 16, 24)], (r.dy_s, r.dy_r))
    g_ring.start()
    d_ring.start()
    c_x.start()

    for n in (1, 3, 2):
        source = place.moved("y", n)
        remote(r.q_send.at[0], r.q_recv.at[source], r.qp_s.at[n], r.qp_r.at[source], place.peer("y", n)).wait_recv()
    r.wq_all[z, x, k] = r.q_recv[...].reshape(32, 1152).astype(BF)
    q_direct = []
    for n, (dz, dx) in enumerate(THEIRS):
        unit = r.wq_all.at[z, x, k]
        q_direct.append(remote(unit, unit, r.qd_s.at[n], r.qd_r.at[4 * z + x], theirs_at(place, dz, dx)))
    for copy in q_direct:
        copy.start()

    def q_core(at_z, at_x, core):
        unit, which = r.wq_all.at[at_z, at_x, core], 4 * at_z + at_x
        return remote(unit, unit, r.qc_s.at[which], r.qc_r.at[which], place.sibling())

    q_core(z, x, k).start()
    tokens = Gather(place, "y", lambda i, h: r.tok_all.at[2 * i + h], (r.t_s, r.t_r))
    tokens.start()

    for other in range(4):

        @pl.when(not_here(diagonal, other, y))
        def _():
            remote(r.o_send, o_slot(other), r.op_s.at[0], r.op_r.at[other], place.device(z=y, y=jnp.int32(other))).wait_recv()

    o_x = Gather(place, "x", lambda i, h: r.wo_all.at[i, k, pl.ds(32 * h, 32)], (r.ox_s, r.ox_r))
    o_x.start()
    g_ring.forward()
    d_ring.forward()
    c_x.forward()
    c_x.finish()
    c_z.start()
    o_x.forward()
    g_ring.finish()
    d_ring.finish()

    for b in range(2):
        pieces = [r.g_y[c, 16 * b : 16 * b + 16].astype(F32) for c in range(4)]
        for core_row in range(2):
            rows = jnp.concatenate([piece[8 * core_row : 8 * core_row + 8] for piece in pieces], axis=0)
            at = 64 * b + 32 * core_row
            r.unit[at : at + 32] = rows.astype(BF)
    r.unit[DOWN:UNIT] = r.d_y[...].reshape(96, D).astype(BF)
    w_all = r.out_w_all
    u_own = pltpu.make_async_copy(r.unit, w_all.at[z, x], r.pair.at[4])
    u_own.start()
    a_one = Gather(
        place, "x", lambda i, h: w_all.at[z, i, from_to(h, 0, 64, PART_A)], (r.a1_s, r.a1_r),
        own=lambda h: r.unit.at[from_to(h, 0, 64, PART_A)],
    )
    b_one = Gather(
        place, "z", lambda i, h: w_all.at[i, x, from_to(h, PART_A, 160, UNIT)], (r.b1_s, r.b1_r),
        own=lambda h: r.unit.at[from_to(h, PART_A, 160, UNIT)],
    )
    a_one.start()
    b_one.start()
    tokens.forward()
    c_z.forward()
    o_x.finish()
    o_core = remote(r.wo_all.at[:, k], r.wo_all.at[:, k], r.core.at[0], r.core.at[1], place.sibling())
    o_core.start()
    a_one.forward()
    b_one.forward()
    for dz, dx in sorted(THEIRS, key=lambda o: min(o[0], 4 - o[0]) + min(o[1], 4 - o[1])):
        at_z, at_x = place.moved("z", dz), place.moved("x", dx)
        other = r.wq_all.at[at_z, at_x, k]
        remote(other, other, r.qd_s.at[0], r.qd_r.at[4 * at_z + at_x], theirs_at(place, dz, dx)).wait_recv()
        q_core(at_z, at_x, k).start()
    a_one.finish()
    b_one.finish()
    u_own.wait()
    a_two = Gather(place, "z", lambda i, h: w_all.at[i, pl.ds(2 * h, 2), pl.ds(0, PART_A)], (r.a2_s, r.a2_r))
    b_two = Gather(place, "x", lambda i, h: w_all.at[pl.ds(2 * h, 2), i, pl.ds(PART_A, UNIT - PART_A)], (r.b2_s, r.b2_r))
    a_two.start()
    b_two.start()
    c_z.finish()
    c_y.start()
    remote(r.wo_all.at[:, 1 - k], r.wo_all.at[:, 1 - k], r.core.at[0], r.core.at[1], place.sibling()).wait_recv()
    for at_z in range(4):
        for at_x in range(4):
            q_core(at_z, at_x, 1 - k).wait_recv()
    tokens.finish()

    lanes = r.wq_all[:, :, :, :, D:1152].reshape(128, 8, 128).astype(F32)
    spread = dot_nn(jnp.sum(lanes, axis=1).astype(BF), r.spread[...])
    owner = lax.broadcasted_iota(jnp.int32, (128, GAINS), 0) * 18
    spot = lax.broadcasted_iota(jnp.int32, (128, GAINS), 1)
    mine = jnp.logical_and(spot >= owner, spot < owner + 18)
    r.out_gain_row[...] = jnp.sum(jnp.where(mine, spread, 0.0), axis=0, keepdims=True)
    gain = r.out_gain_row
    project(r, gain.at[:, 0:D], gain.at[:, 2 * D : 2 * D + 128], gain.at[:, 2 * D + 128 : GAINS])
    attend(r, 0, 2)
    c_y.forward()
    a_two.forward()
    b_two.forward()
    attend(r, 2, 4)

    wo = r.wo_all[...].reshape(OWN_HEADS * HEAD_WIDTH, D)

    @pl.loop(0, 4)
    def _(i):
        rows = jnp.concatenate(
            [heads_of(r.attended, OWN_HEADS, r.span[2 * i + n]) for n in range(2)], axis=0
        )
        r.terms[i] = dot_nn(rows, wo).astype(BF)

    reduce = Scatter(
        place, "y", lambda i, h: r.terms.at[i, pl.ds(128 * h, 128)],
        [r.boxes.at[n] for n in range(6)], (r.y_s, r.y_r),
    )
    reduce.start()
    saves = [
        pltpu.make_async_copy(getattr(r, n), getattr(r, "out_" + n), r.save.at[i]) for i, n in enumerate(SAVED)
    ]
    for copy in saves:
        copy.start()
    c_y.finish()

    @pl.loop(0, 16)
    def _(j):
        pieces = [r.w_c[c, j].astype(F32) for c in range(4)]
        rows = [piece[8 * core_row : 8 * core_row + 8] for core_row in range(2) for piece in pieces]
        r.w_two[j] = jnp.concatenate(rows, axis=0).astype(BF)

    two_copy = pltpu.make_async_copy(r.w_two, r.out_w_two, r.pair.at[5])
    two_copy.start()
    reduce.forward()
    reduce.finish(lambda h: r.total.at[pl.ds(128 * h, 128)])

    hid_copies = []
    for half in range(2):

        @pl.loop(0, BLOCK // 32)
        def _(t):
            at = row_tile(4 * half + t, 32)
            rows = r.tok[at].astype(F32) + r.total[at]
            r.total[at] = rows
            scale = lax.rsqrt(jnp.mean(rows * rows, axis=-1, keepdims=True) + norm_eps)
            r.hid[at] = (rows * scale * gain[:, D : 2 * D]).astype(BF)

        here, there = pl.ds(BLOCK * half, BLOCK), pl.ds(ROWS + BLOCK * half, BLOCK)
        hid_copies += [
            remote(r.hid.at[here], r.out_hidden_pair.at[there], r.hid_sem.at[4 * half], r.hid_sem.at[4 * half + 1], place.sibling()),
            pltpu.make_async_copy(r.hid.at[here], r.out_hidden_pair.at[here], r.hid_sem.at[4 * half + 2]),
            pltpu.make_async_copy(r.total.at[here], r.out_middle.at[here], r.hid_sem.at[4 * half + 3]),
        ]
        for copy in hid_copies[3 * half :]:
            copy.start()

    a_two.finish()
    b_two.finish()
    two_copy.wait()
    for copy in saves:
        copy.wait()
    for copy in q_prep + q_direct + [g_prep, o_core]:
        copy.wait_send()
    for at_z in range(4):
        for at_x in range(4):
            q_core(at_z, at_x, k).wait_send()
    cot_copy.wait()
    cot_own.wait()
    for copy in hid_copies:
        copy.wait()
    for other in range(4):

        @pl.when(not_here(diagonal, other, z))
        def _():
            remote(r.o_send, o_slot(y), r.op_s.at[other], r.op_r.at[y], place.device(z=jnp.int32(other), y=z)).wait_send()


def rings(*names):
    return {f"{name}_{end}": dma(6) for name in names for end in "sr"}


def forward_step(**given):
    outputs = {
        "middle": ((ROWS, D), F32, hbm),
        "hidden_pair": ((2 * ROWS, D), BF, hbm),
        "cot_pair": ((2 * ROWS, D), BF, hbm),
        "gain_row": ((1, GAINS), F32, vmem),
        "w_all": ((4, 4, UNIT, D), BF, hbm),
        "w_two": ((16, 64, D), BF, hbm),
        **{n: (*what, hbm) for n, what in SAVED.items()},
    }
    scratch = {
        "q_send": pltpu.VMEM((4, 8, 1152), F32),
        "q_recv": pltpu.VMEM((4, 8, 1152), F32),
        "o_send": pltpu.VMEM((16, D), BF),
        "packed": pltpu.VMEM((2, 3, 8, D), F32),
        "g_recv": pltpu.VMEM((3, 8, D), F32),
        "g_y": pltpu.VMEM((4, 32, D), BF),
        "w_c": pltpu.VMEM((4, 16, 16, D), BF),
        "w_two": pltpu.VMEM((16, 64, D), BF),
        "d_y": pltpu.VMEM((4, 24, D), F32),
        "unit": pltpu.VMEM((UNIT, D), BF),
        "tok_all": pltpu.VMEM((8, BLOCK, D), BF),
        "value_t": pltpu.VMEM((OWN_KV, HEAD_WIDTH, SEQ), BF),
        "attended": pltpu.VMEM((OWN_HEADS, 8, BLOCK, HEAD_WIDTH), BF),
        "terms": pltpu.VMEM((4, ROWS, D), BF),
        "boxes": pltpu.VMEM((6, BLOCK, D), BF),
        "total": pltpu.VMEM((ROWS, D), F32),
        **{n: pltpu.VMEM(*what) for n, what in SAVED.items()},
        "hid": pltpu.VMEM((ROWS, D), BF),
        "pair": dma(7),
        "core": dma(2),
        "hid_sem": dma(8),
        **{"qc_s": dma(16), "qc_r": dma(16)},
        "save": dma(len(SAVED)),
        **{n: dma(4) for n in ("qp_s", "qp_r", "op_s", "op_r")},
        **{"qd_s": dma(15), "qd_r": dma(16)},
        **rings("gy", "dy", "cx", "cz", "cy", "ox", "t", "a1", "b1", "a2", "b2", "y"),
    }
    spaces = {"span": smem}
    return named_call(forward_kernel, 1, "forward_attention", given, spaces, outputs, scratch)


def sum_everywhere(r, place):
    z, x, k, y = (place[a] for a in "zxky")

    def stage(source, slots, send, recv, offsets, device, me, slot_of):
        slots[me] = source[...]
        copies = [
            remote(source, slots.at[me], send.at[n], recv.at[me], device(*offset))
            for n, offset in enumerate(offsets)
        ]
        for copy in copies:
            copy.start()
        for n, offset in enumerate(offsets):
            slot = slot_of(*offset)
            remote(source, slots.at[slot], send.at[n], recv.at[slot], device(*offset)).wait_recv()
        for copy in copies:
            copy.wait_send()

    stage(r.value_row, r.first, r.s1_s, r.s1_r, OURS, lambda *o: ours_at(place, *o), y * 2 + k,
          lambda dy, dk: place.moved("y", dy) * 2 + lax.rem(k + dk, 2))
    r.held[...] = jnp.sum(r.first[...], axis=0)
    stage(r.held, r.second, r.s2_s, r.s2_r, THEIRS, lambda *o: theirs_at(place, *o), z * 4 + x,
          lambda dz, dx: place.moved("z", dz) * 4 + place.moved("x", dx))
    r.out_sums[...] = jnp.sum(r.second[...], axis=0)


OURS = [(dy, dk) for dy in range(4) for dk in range(2) if (dy, dk) != (0, 0)]
THEIRS = [(dz, dx) for dz in range(4) for dx in range(4) if (dz, dx) != (0, 0)]


def ours_at(place, dy, dk):
    return place.device(y=place.moved("y", dy), k=lax.rem(place["k"] + dk, 2))


def theirs_at(place, dz, dx):
    return place.device(z=place.moved("z", dz), x=place.moved("x", dx))


def by_eights(rows):
    return jnp.sum(rows.reshape(rows.shape[0] // 8, 8, D), axis=0)


def back_through_norm(r, gain, half):
    @pl.loop(0, BLOCK // 32)
    def _(t):
        at = row_tile(4 * half + t, 32)
        rows = r.middle[at]
        scale = lax.rsqrt(jnp.mean(rows * rows, axis=-1, keepdims=True) + norm_eps)
        normed = rows * scale
        incoming = r.out_input_grad[at] + r.dh_box[at].astype(F32)
        r.mlp_gain[...] += by_eights(incoming * normed)
        incoming = incoming * gain[:, D : 2 * D]
        mean = jnp.mean(incoming * normed, axis=-1, keepdims=True)
        d_mid = r.cot[at].astype(F32) + scale * (incoming - normed * mean)
        r.out_input_grad[at] = d_mid
        r.own[at] = d_mid.astype(BF)


def back_to_input(r, gain):
    r.attn_gain[...] = jnp.zeros_like(r.attn_gain)

    @pl.loop(0, ROWS // 32)
    def _(t):
        at = row_tile(t, 32)
        rows = r.tok[at].astype(F32)
        scale = lax.rsqrt(jnp.mean(rows * rows, axis=-1, keepdims=True) + norm_eps)
        normed = rows * scale
        incoming = r.dh_total[at]
        r.attn_gain[...] += by_eights(incoming * normed)
        incoming = incoming * gain[:, 0:D]
        mean = jnp.mean(incoming * normed, axis=-1, keepdims=True)
        r.out_input_grad[at] += scale * (incoming - normed * mean)


def back_to_projections(r, gain):
    plain = HEAD_WIDTH ** (-0.5)
    r.head_gain[...] = jnp.zeros_like(r.head_gain)

    @pl.loop(0, SEQ // TILE)
    def _(t):
        at = row_tile(t, TILE)
        cos_t, sin_t = r.cosine[at], r.sine[at]
        for h in range(OWN_HEADS + OWN_KV):
            mine = h < OWN_HEADS
            d_rows = r.d_query[h, at] if mine else r.d_key[h - OWN_HEADS, at] * plain
            first = 2 * D if mine else 2 * D + HEAD_WIDTH
            d_gained = d_rows * cos_t - turn(d_rows) * sin_t
            normed, scale = head_norm(r.raw[h, at].astype(F32))
            product = d_gained * normed
            r.head_gain[0 if mine else 1] += jnp.sum(product.reshape(TILE // 8, 8, HEAD_WIDTH), axis=0)
            incoming = d_gained * gain[:, first : first + HEAD_WIDTH]
            mean = jnp.mean(incoming * normed, axis=-1, keepdims=True)
            r.d_proj[pl.ds(2 * t, 2), :, 128 * h : 128 * h + 128] = (
                (scale * (incoming - normed * mean)).astype(BF).reshape(2, BLOCK, HEAD_WIDTH)
            )
        for h in range(OWN_KV):
            r.d_proj[pl.ds(2 * t, 2), :, 768 + 128 * h : 896 + 128 * h] = (
                r.d_value[h, at].astype(BF).reshape(2, BLOCK, HEAD_WIDTH)
            )


def block_weights(r, b):
    if b == 2:
        return r.c[...].reshape(D, D)
    return r.w[:, :, 64 * b : 64 * b + 64].reshape(D, D)


def block_down(r, b):
    return r.w[:, :, DOWN:UNIT].reshape(FF // 2, D)[512 * b : 512 * b + 512]


def product_rows(r, first, last):
    parts = []
    if first < D:
        parts.append(r.d_o[...].reshape(2 * ROWS, D)[:, first : min(last, D)])
    if last > D:
        parts.append(r.d_q[2:4].reshape(2 * ROWS, D)[:, max(first, D) - D : last - D])
    return parts[0] if len(parts) == 1 else jnp.concatenate(parts, axis=1)


def d_gate_up_rows(r, b, t):
    if b < 2:
        return r.d_proj[pl.ds(4 * b + 2 * t, 2)].reshape(ROWS, D)
    return r.d_q[t].reshape(ROWS, D)


def feed_forward(r, w_loads):
    w_loads[0].wait()
    w_loads[1].wait()
    for b in range(3):
        if b:
            w_loads[1 + b].wait()
        weights, down = block_weights(r, b), block_down(r, b)

        @pl.loop(0, 2)
        def _(t):
            gate_up = dot_nn(r.hidden[row_tile(t, ROWS)], weights)
            d_product = dot_nt(r.hidden[row_tile(2 + t, ROWS)], down)
            gate, up = gate_up[:, :512], gate_up[:, 512:]
            sigmoid = 1.0 / (1.0 + jnp.exp(-gate))
            active = gate * sigmoid
            product = (active * up).astype(BF).reshape(4, 64, 512)
            if b < 2:
                r.d_o[pl.ds(2 * t, 2), :, :, 512 * b : 512 * b + 512] = product.reshape(2, 2, 64, 512)
            else:
                r.d_q[2 + t, :, :, :, 0:512] = product.reshape(4, 2, 32, 512)
            d_gate = d_product * up * sigmoid * (1.0 + gate * (1.0 - sigmoid))
            d_both = jnp.concatenate([d_gate, d_product * active], axis=1).astype(BF)
            if b < 2:
                r.d_proj[pl.ds(4 * b + 2 * t, 2)] = d_both.reshape(2, BLOCK, D)
            else:
                r.d_q[t] = d_both.reshape(4, 2, 32, D)


def feed_forward_inputs(r):
    def half(t):
        total = dot_nt(d_gate_up_rows(r, 0, t), block_weights(r, 0))
        for b in (1, 2):
            total = total + dot_nt(d_gate_up_rows(r, b, t), block_weights(r, b))
        return total

    r.dh_sib[...] = half(1).astype(BF)
    r.out_input_grad[...] = half(0)


def feed_forward_outputs(r):
    down = r.w[:, :, DOWN:UNIT].reshape(FF // 2, D)

    def half(t):
        first = dot_nn(r.d_o[2 * t : 2 * t + 2].reshape(ROWS, D), down[:D])
        return first + dot_nn(r.d_q[2 + t, :, :, :, 0:512].reshape(ROWS, 512), down[D:])

    r.out_sib[...] = half(1).astype(BF)
    r.dh_total[...] = half(0)


def dot_tn(left, right):
    return lax.dot_general(left, right, (((0,), (0,)), ((), ())), preferred_element_type=F32)


def down_gradients(r):
    cot = r.hidden[2 * ROWS : SEQ]
    for i in range(4):
        left = product_rows(r, 384 * i, 384 * i + 384)
        r.w[i, :, DOWN:UNIT] = dot_tn(left, cot).astype(BF).reshape(4, 96, D)


def block_gradients(r, b):
    d_both = jnp.concatenate([d_gate_up_rows(r, b, 0), d_gate_up_rows(r, b, 1)], axis=0)

    @pl.loop(0, 4)
    def _(i):
        columns = pl.ds(pl.multiple_of(i * 256, 256), 256)
        rows = dot_tn(r.hidden[0 : 2 * ROWS, columns], d_both)
        if b < 2:
            r.w[i, :, 64 * b : 64 * b + 64] = rows.astype(BF).reshape(4, 64, D)
        else:
            rows = rows.reshape(4, 2, 4, 8, D)
            for c in range(4):
                r.c[c, pl.ds(4 * i, 4)] = rows[:, :, c].reshape(4, 16, D).astype(BF)


def backward_kernel(r):
    place = Place()
    z, x, k, y = (place[a] for a in "zxky")
    diagonal = z == y
    gain = r.gain_row
    near = neighbours(place, "xyzk")
    everyone = [ours_at(place, *o) for o in OURS] + [theirs_at(place, *o) for o in THEIRS]
    greet(near + everyone)
    for other in range(4):

        @pl.when(not_here(diagonal, other, z))
        def _():
            greet([place.device(z=jnp.int32(other), y=z)])

    loads = {
        n: pltpu.make_async_copy(getattr(r, "in_" + n), getattr(r, n), r.load.at[i]) for i, n in enumerate(SAVED)
    }
    pair_loads = [
        pltpu.make_async_copy(pair, r.hidden.at[rows], r.w_sem.at[4 + i])
        for i, (pair, rows) in enumerate([(r.hidden_pair, pl.ds(0, 2 * ROWS)), (r.cot_pair, pl.ds(2 * ROWS, 2 * ROWS))])
    ]
    w_loads = [
        pltpu.make_async_copy(r.w_all.at[:, :, rows], r.w.at[:, :, rows], r.w_sem.at[i])
        for i, rows in enumerate([pl.ds(0, 64), pl.ds(DOWN, 96), pl.ds(64, 64)])
    ]
    w_loads.append(pltpu.make_async_copy(r.w_two, r.c, r.w_sem.at[3]))
    hidden_load = loads.pop("hidden")
    for copy in pair_loads + w_loads + list(loads.values()):
        copy.start()

    def a_part(i, h):
        return r.w.at[i, pl.ds(2 * h, 2), pl.ds(0, PART_A)]

    def b_part(i, h):
        return r.w.at[pl.ds(2 * h, 2), i, pl.ds(PART_A, UNIT - PART_A)]

    a_one = Scatter(place, "z", a_part, [r.a_box.at[n] for n in range(6)], (r.a1_s, r.a1_r))
    b_one = Scatter(place, "x", b_part, [r.b_box.at[n] for n in range(6)], (r.b1_s, r.b1_r))
    await_greetings(len(near) + len(everyone) + jnp.where(diagonal, 3, 4))

    dh_copy = remote(r.dh_sib, r.dh_box, r.core.at[0], r.core.at[1], place.sibling())
    out_copy = remote(r.out_sib, r.out_box, r.core.at[2], r.core.at[3], place.sibling())
    for copy in pair_loads:
        copy.wait()
    feed_forward(r, w_loads)
    feed_forward_inputs(r)
    dh_copy.start()
    feed_forward_outputs(r)
    out_copy.start()
    dh_copy.wait_recv()
    ring = Gather(
        place, "y", lambda i, h: r.d_attn_all.at[2 * i + h], (r.t_s, r.t_r),
        own=lambda h: r.own.at[pl.ds(BLOCK * h, BLOCK)],
    )
    r.mlp_gain[...] = jnp.zeros_like(r.mlp_gain)
    for half in range(2):
        back_through_norm(r, gain, half)
        ring.start([half])
    r.d_attn_all[pl.ds(2 * y, 2)] = r.own[...].reshape(2, BLOCK, D)
    down_gradients(r)
    block_gradients(r, 1)
    b_one.start()
    block_gradients(r, 0)
    a_one.start()
    block_gradients(r, 2)
    hidden_load.start()
    out_copy.wait_recv()

    @pl.loop(0, ROWS // 16)
    def _(t):
        at = row_tile(t, 16)
        r.out_layer_out[at] = (r.middle[at] + r.dh_total[at] + r.out_box[at].astype(F32)).astype(BF)

    for copy in [hidden_load, *loads.values()]:
        copy.wait()
    r.d_key[...] = jnp.zeros_like(r.d_key)
    r.d_value[...] = jnp.zeros_like(r.d_value)
    ring.forward()
    a_one.forward()
    b_one.forward()
    ring.finish()
    c_y = Scatter(
        place, "y", lambda i, h: r.c.at[i, pl.ds(8 * h, 8)],
        [r.cy_box.at[n] for n in range(6)], (r.cy_s, r.cy_r),
    )
    c_z = Scatter(
        place, "z", lambda i, h: r.c.at[y, pl.ds(4 * i + 2 * h, 2)],
        [r.cz_box.at[n] for n in range(6)], (r.cz_s, r.cz_r),
    )
    c_x = Scatter(
        place, "x", lambda i, h: r.c.at[y, 4 * z + i, :, pl.ds(512 * h, 512)],
        [r.cx_box.at[n] for n in range(6)], (r.cx_s, r.cx_r),
    )
    c_y.start()

    wo = r.wo_all[...].reshape(OWN_HEADS * HEAD_WIDTH, D)

    @pl.loop(0, SEQ // TILE)
    def _(t):
        at = row_tile(t, TILE)
        rows = pair_of(r.d_attn_all, r.span, t)
        r.d_q[t] = rows.reshape(4, 2, 32, D)
        both = dot_nt(rows, wo)
        for h in range(OWN_HEADS):
            r.d_attended[h, at] = both[:, 128 * h : 128 * h + 128].astype(BF)

    d_sorted = r.d_q[...].reshape(SEQ, D)

    @pl.loop(0, 4)
    def _(i):
        r.d_o[i] = dot_nn(r.attended_t[i], d_sorted).astype(BF).reshape(2, 64, D)

    o_core = remote(r.d_o.at[:, 1 - k], r.o_box, r.core.at[4], r.core.at[5], place.sibling())
    o_core.start()
    attend_back(r, 0, 2)
    c_y.forward()
    o_core.wait_recv()

    @pl.loop(0, 4)
    def _(i):
        add_rows(r.o_box.at[i], [r.o_box.at[i], r.d_o.at[i, k]])

    o_x = Scatter(
        place, "x", lambda i, h: r.o_box.at[i, pl.ds(32 * h, 32)],
        [r.ox_box.at[n] for n in range(6)], (r.ox_s, r.ox_r),
    )
    o_x.start()
    a_one.finish(lambda h: a_part(z, h))
    b_one.finish(lambda h: b_part(x, h))
    a_two = Scatter(
        place, "x", lambda i, h: r.w.at[z, i, from_to(h, 0, 64, PART_A)],
        [r.a_box2.at[n, pl.ds(0, 64 if n in (0, 3, 4) else 48)] for n in range(6)], (r.a2_s, r.a2_r),
    )
    b_two = Scatter(
        place, "z", lambda i, h: r.w.at[i, x, from_to(h, PART_A, 160, UNIT)],
        [r.b_box2.at[n, pl.ds(0, 48 if n in (0, 3, 4) else 64)] for n in range(6)], (r.b2_s, r.b2_r),
    )
    a_two.start()
    b_two.start()
    attend_back(r, 2, 4)
    c_y.finish(lambda h: r.c.at[y, pl.ds(8 * h, 8)])
    c_z.start()
    o_x.forward()
    back_to_projections(r, gain)

    wq = r.wq_all[:, :, :, :, 0:D].reshape(D, D)

    @pl.loop(0, 4)
    def _(i):
        rows = jnp.concatenate([r.d_proj[r.span[2 * i + n]] for n in range(2)], axis=0)
        r.d_attn_all[pl.ds(2 * i, 2)] = dot_nt(rows, wq).astype(BF).reshape(2, BLOCK, D)

    dh_ring = Scatter(
        place, "y", lambda i, h: r.d_attn_all.at[2 * i + h],
        [r.y_box.at[n] for n in range(6)], (r.y_s, r.y_r),
    )
    dh_ring.start()

    d_proj = r.d_proj[...].reshape(SEQ, D)
    planes = [place.moved("z", dz) for dz in (1, 2, 3, 0)]
    q_core = [
        remote(r.d_q.at[plane, :, 1 - k], r.q_box.at[plane], r.qk_s.at[n], r.qk_r.at[n], place.sibling())
        for n, plane in enumerate(planes)
    ]

    @pl.loop(0, 4)
    def _(n):
        plane = place.moved("z", n + 1)
        left = r.hidden[:, row_tile(plane, 256)]
        r.d_q[plane] = dot_tn(left, d_proj).astype(BF).reshape(4, 2, 32, D)
        remote(r.d_q.at[plane, :, 1 - k], r.q_box.at[plane], r.qk_s.at[n], r.qk_r.at[n], place.sibling()).start()

    q_direct = []
    for n, plane in enumerate(planes):
        q_core[n].wait_recv()

        @pl.loop(0, 4)
        def _(j):
            add_rows(r.q_box.at[plane, j], [r.q_box.at[plane, j], r.d_q.at[plane, j, k]])

        for dx in range(1 if n == 3 else 0, 4):
            to = place.moved("x", dx)
            q_direct.append(
                remote(
                    r.q_box.at[plane, to], r.q_slots.at[4 * z + x], r.qd_s.at[len(q_direct)], r.qd_r.at[4 * z + x],
                    place.device(z=plane, x=to),
                )
            )
            q_direct[-1].start()
    r.q_slots[4 * z + x] = r.q_box[z, x]
    c_z.forward()
    a_two.forward()
    b_two.forward()
    dh_ring.forward()
    c_z.finish(lambda h: r.c.at[y, pl.ds(4 * z + 2 * h, 2)])
    c_x.start()
    o_x.finish(lambda h: r.o_two.at[pl.ds(32 * h, 32)])

    def o_target(other):
        return place.device(z=y, y=jnp.int32(other))

    for other in range(4):
        piece = r.o_two.at[pl.ds(16 * other, 16)]

        @pl.when(not_here(diagonal, other, y))
        def _():
            remote(piece, r.o_slots.at[z], r.oy_s.at[other], r.oy_r.at[z], o_target(other)).start()

    @pl.when(diagonal)
    def _():
        r.o_slots[z] = r.o_two[row_tile(y, 16)]

    c_x.forward()

    a_two.finish(lambda h: r.total.at[from_to(h, 0, 64, PART_A)])
    b_two.finish(lambda h: r.total.at[from_to(h, PART_A, 160, UNIT)])
    for c in range(4):
        for b in range(2):
            at = 64 * b + 8 * c
            rows = jnp.concatenate([r.total[at : at + 8], r.total[at + 32 : at + 40]], axis=0)
            r.g_send[c, 16 * b : 16 * b + 16] = rows.astype(BF)
    r.g_slots[y] = r.g_send[y]

    def down_rows(c):
        return pl.ds(pl.multiple_of(DOWN + 24 * c, 8), 24)

    r.d_slots[y] = r.total[down_rows(y)]
    y_copies = []
    for n in (1, 3, 2):
        to = place.moved("y", n)
        y_copies.append(remote(r.g_send.at[to], r.g_slots.at[y], r.gy_s.at[n], r.gy_r.at[y], place.peer("y", n)))
        y_copies.append(remote(r.total.at[down_rows(to)], r.d_slots.at[y], r.dy_s.at[n], r.dy_r.at[y], place.peer("y", n)))
    for copy in y_copies:
        copy.start()
    c_x.finish(lambda h: r.c_sum.at[:, pl.ds(512 * h, 512)])
    dh_ring.finish(lambda h: r.dh_total.at[pl.ds(BLOCK * h, BLOCK)])
    back_to_input(r, gain)

    for n in (1, 3, 2):
        source = place.moved("y", n)
        remote(r.g_send.at[0], r.g_slots.at[source], r.gy_s.at[n], r.gy_r.at[source], place.peer("y", n)).wait_recv()
        remote(r.total.at[pl.ds(DOWN, 24)], r.d_slots.at[source], r.dy_s.at[n], r.dy_r.at[source], place.peer("y", n)).wait_recv()
    r.out_d_out[...] = r.d_slots[0] + r.d_slots[1] + r.d_slots[2] + r.d_slots[3]
    summed = r.g_slots[0].astype(F32)
    for c in range(1, 4):
        summed = summed + r.g_slots[c].astype(F32)
    summed = summed.reshape(2, 2, 8, D)
    last = r.c_sum[...].reshape(2, 8, D)
    for n in range(2):
        r.g_sum[n, 0:2] = summed[:, n]
        r.g_sum[n, 2] = last[n]
    r.out_g_out[k] = r.g_sum[k]
    g_core = remote(r.g_sum.at[1 - k], r.out_g_out.at[k], r.core.at[8], r.core.at[9], place.sibling())
    g_core.start()
    for other in range(4):

        @pl.when(not_here(diagonal, other, z))
        def _():
            remote(r.o_two.at[pl.ds(0, 16)], r.o_slots.at[other], r.oy_s.at[0], r.oy_r.at[other], place.device(z=jnp.int32(other), y=z)).wait_recv()

    o_sum = r.o_slots[0].astype(F32)
    for c in range(1, 4):
        o_sum = o_sum + r.o_slots[c].astype(F32)
    r.out_o_out[...] = o_sum

    for dz, dx in THEIRS:
        at = 4 * place.moved("z", dz) + place.moved("x", dx)
        remote(r.q_box.at[0, 0], r.q_slots.at[at], r.qd_s.at[0], r.qd_r.at[at], theirs_at(place, dz, dx)).wait_recv()

    @pl.loop(0, 2)
    def _(t):
        at = row_tile(t, 16)
        total = r.q_slots[0, at].astype(F32)
        for n in range(1, 16):
            total = total + r.q_slots[n, at].astype(F32)
        r.q_three[at] = total

    r.out_q_out[y] = r.q_three[row_tile(y, 8)]
    q_copies = [
        remote(r.q_three.at[row_tile(place.moved("y", n), 8)], r.out_q_out.at[y], r.qy_s.at[n], r.qy_r.at[y], place.peer("y", n))
        for n in (1, 3, 2)
    ]
    for copy in q_copies:
        copy.start()
    squares = jnp.zeros((8, D), F32)
    for part in [r.q_three[8 * c : 8 * c + 8] for c in range(4)] + [r.g_sum[c, b] for c in range(2) for b in range(3)]:
        squares = squares + part * part
    for c in range(2):
        part = r.out_o_out[8 * c : 8 * c + 8]
        squares = squares + part * part
    for c in range(3):
        part = r.out_d_out[8 * c : 8 * c + 8]
        squares = squares + part * part
    attn = jnp.sum(r.attn_gain[...], axis=0, keepdims=True)
    mlp = jnp.sum(r.mlp_gain[...], axis=0, keepdims=True)
    squares = jnp.sum(squares, axis=0, keepdims=True)
    r.value_row[...] = jnp.zeros_like(r.value_row)
    lanes = jnp.zeros((1, 128), F32)
    for c in range(8):
        at = slice(128 * c, 128 * c + 128)
        r.value_row[c : c + 1] = attn[:, at]
        r.value_row[8 + c : 9 + c] = mlp[:, at]
        lanes = lanes + squares[:, at]
    for c in range(2):
        r.value_row[16 + c : 17 + c] = jnp.sum(r.head_gain[c], axis=0, keepdims=True)
    r.value_row[18:19] = lanes
    sum_everywhere(r, place)

    remote(r.g_sum.at[0], r.out_g_out.at[1 - k], r.core.at[8], r.core.at[9], place.sibling()).wait_recv()
    for n in (1, 3, 2):
        source = place.moved("y", n)
        remote(r.q_three.at[pl.ds(0, 8)], r.out_q_out.at[source], r.qy_s.at[n], r.qy_r.at[source], place.peer("y", n)).wait_recv()
    for copy in [dh_copy, out_copy, o_core, g_core] + y_copies + q_copies + q_core + q_direct:
        copy.wait_send()
    for other in range(4):

        @pl.when(not_here(diagonal, other, y))
        def _():
            remote(r.o_two.at[pl.ds(16 * other, 16)], r.o_slots.at[z], r.oy_s.at[other], r.oy_r.at[z], o_target(other)).wait_send()


def backward_step(**given):
    given = {("in_" + n if n in SAVED else n): v for n, v in given.items()}
    outputs = {
        "layer_out": ((ROWS, D), BF, vmem),
        "input_grad": ((ROWS, D), F32, vmem),
        "q_out": ((4, 8, D), F32, vmem),
        "o_out": ((16, D), F32, vmem),
        "g_out": ((2, 3, 8, D), F32, vmem),
        "d_out": ((24, D), F32, vmem),
        "sums": ((24, 128), F32, vmem),
    }
    head_rows = (OWN_HEADS, SEQ, HEAD_WIDTH)
    kv_rows = (OWN_KV, SEQ, HEAD_WIDTH)
    scratch = {
        **{n: pltpu.VMEM(*what) for n, what in SAVED.items()},
        "out_box": pltpu.VMEM((ROWS, D), BF),
        "dh_box": pltpu.VMEM((ROWS, D), BF),
        "own": pltpu.VMEM((ROWS, D), BF),
        "d_attn_all": pltpu.VMEM((8, BLOCK, D), BF),
        "d_attended": pltpu.VMEM(head_rows, BF),
        "d_query": pltpu.VMEM(head_rows, F32),
        "d_key": pltpu.VMEM(kv_rows, F32),
        "d_value": pltpu.VMEM(kv_rows, F32),
        "d_proj": pltpu.VMEM((8, BLOCK, D), BF),
        "y_box": pltpu.VMEM((6, BLOCK, D), BF),
        "dh_total": pltpu.VMEM((ROWS, D), F32),
        "a_box": pltpu.VMEM((6, 2, PART_A, D), BF),
        "b_box": pltpu.VMEM((6, 2, PART_A, D), BF),
        "w": pltpu.VMEM((4, 4, UNIT, D), BF),
        "out_sib": pltpu.VMEM((ROWS, D), BF),
        "dh_sib": pltpu.VMEM((ROWS, D), BF),
        "a_box2": pltpu.VMEM((6, 64, D), BF),
        "b_box2": pltpu.VMEM((6, 64, D), BF),
        "total": pltpu.VMEM((UNIT, D), F32),
        "g_send": pltpu.VMEM((4, 32, D), BF),
        "g_slots": pltpu.VMEM((4, 32, D), BF),
        "d_slots": pltpu.VMEM((4, 24, D), F32),
        "g_sum": pltpu.VMEM((2, 3, 8, D), F32),
        "d_q": pltpu.VMEM((4, 4, 2, 32, D), BF),
        "d_o": pltpu.VMEM((4, 2, 64, D), BF),
        "q_box": pltpu.VMEM((4, 4, 32, D), BF),
        "q_slots": pltpu.VMEM((16, 32, D), BF),
        "c": pltpu.VMEM((4, 16, 16, D), BF),
        "cy_box": pltpu.VMEM((6, 8, 16, D), BF),
        "cz_box": pltpu.VMEM((6, 2, 16, D), BF),
        "cx_box": pltpu.VMEM((6, 16, 512), BF),
        "c_sum": pltpu.VMEM((16, D), F32),
        "q_three": pltpu.VMEM((32, D), F32),
        "o_box": pltpu.VMEM((4, 64, D), BF),
        "ox_box": pltpu.VMEM((6, 32, D), BF),
        "o_two": pltpu.VMEM((64, D), BF),
        "o_slots": pltpu.VMEM((4, 16, D), BF),
        "mlp_gain": pltpu.VMEM((8, D), F32),
        "attn_gain": pltpu.VMEM((8, D), F32),
        "head_gain": pltpu.VMEM((2, 8, HEAD_WIDTH), F32),
        "value_row": pltpu.VMEM((24, 128), F32),
        "first": pltpu.VMEM((8, 24, 128), F32),
        "second": pltpu.VMEM((16, 24, 128), F32),
        "held": pltpu.VMEM((24, 128), F32),
        "core": dma(10),
        "load": dma(len(SAVED)),
        "w_sem": dma(6),
        **{n: dma(4) for n in ("gy_s", "gy_r", "dy_s", "dy_r", "qy_s", "qy_r", "oy_s", "oy_r")},
        **{"s1_s": dma(7), "s1_r": dma(8), "s2_s": dma(15), "s2_r": dma(16)},
        **{"qd_s": dma(15), "qd_r": dma(16), "qk_s": dma(4), "qk_r": dma(4)},
        **rings("t", "y", "a1", "b1", "a2", "b2", "cx", "cy", "cz", "ox"),
    }
    spaces = {"span": smem, "w_all": hbm, "w_two": hbm, "hidden_pair": hbm, "cot_pair": hbm, **{"in_" + n: hbm for n in SAVED}}
    return named_call(backward_kernel, 2, "backward_attention", given, spaces, outputs, scratch)


def gain_spread():
    return jnp.asarray(np.arange(128)[:, None] == np.arange(GAINS)[None, :] % 18, BF)


def rope_tables():
    middle = HEAD_WIDTH // 2
    frequency = rope_base ** (-(np.arange(middle) * 2.0) / HEAD_WIDTH)
    angle = np.arange(SEQ)[:, None] * frequency[None, :]
    cosine, sine = np.cos(angle), np.sin(angle)
    return (
        jnp.asarray(np.concatenate([cosine, cosine], axis=1), F32),
        jnp.asarray(np.concatenate([-sine, sine], axis=1), F32),
    )


MATRICES = {"qkv": matrix_rate, "out": out_rate, "gateup": matrix_rate, "down": matrix_rate}


def adam_update(weight, first, second, grad, factor, rate, decay):
    clipped = grad * factor
    new_first = beta_one * first + (1.0 - beta_one) * clipped
    new_second = beta_two * second + (1.0 - beta_two) * clipped * clipped
    direction = (
        new_first
        / (1.0 - beta_one**STEP)
        / (jnp.sqrt(new_second / (1.0 - beta_two**STEP)) + adam_eps)
    )
    return (weight - rate * (direction + decay * weight), new_first, new_second)


def update_kernel(r):
    hand_on = [
        pltpu.make_async_copy(r.layer_out, r.out_layer_out, r.sems.at[0]),
        pltpu.make_async_copy(r.input_grad, r.out_input_grad, r.sems.at[1]),
    ]
    for copy in hand_on:
        copy.start()
    sums = r.sums[...]
    row = lax.broadcasted_iota(jnp.int32, (24, 128), 0)
    squares = jnp.where(row < 18, sums * sums, jnp.where(row == 18, sums, 0.0))
    norm = jnp.sqrt(jnp.sum(jnp.sum(squares, axis=0, keepdims=True), axis=1, keepdims=True))
    r.out_norm[...] = norm
    factor = jnp.minimum(1.0, clip_at / (norm + 1e-06))

    place = row * 128 + lax.broadcasted_iota(jnp.int32, (24, 128), 1)
    start = (lax.axis_index("dp") * 4 + lax.axis_index("ctx")) * 18
    lane = lax.broadcasted_iota(jnp.int32, (1, 128), 1)
    mine = jnp.zeros((1, 128), F32)
    for n in range(18):
        entry = jnp.sum(jnp.where(place == start + n, sums, 0.0), axis=0, keepdims=True)
        mine = jnp.where(lane == n, jnp.sum(entry, axis=1, keepdims=True), mine)
    grads = {
        "qkv": jnp.concatenate(
            [r.q_out[c, :, 0:512] for c in range(4)]
            + [r.q_out[c, :, 512:768] for c in range(4)]
            + [r.q_out[c, :, 768:1024] for c in range(4)],
            axis=1,
        ),
        "out": r.o_out[...],
        "gateup": unpack_gateup(r.g_out),
        "down": r.d_out[...],
        "gains": mine[:, 0:18],
    }
    for name, grad in grads.items():
        rate, decay = (MATRICES[name], matrix_decay) if name in MATRICES else (gain_rate, 0.0)
        refs = [getattr(r, kind + name) for kind in ("w_", "first_", "second_")]
        news = adam_update(*[ref[...] for ref in refs], grad, factor, rate, decay)
        for kind, new in zip(("w_", "first_", "second_"), news):
            getattr(r, "out_" + kind + name)[...] = new
    for copy in hand_on:
        copy.wait()


def update_step(**given):
    outputs = {
        "layer_out": ((ROWS, D), BF, hbm),
        "input_grad": ((ROWS, D), F32, hbm),
        "norm": ((1, 1), F32, vmem),
        **{n: (v.shape, F32, vmem) for n, v in given.items() if n.split("_")[0] in ("w", "first", "second")},
    }
    return named_call(update_kernel, None, "update", given, {}, outputs, {"sems": dma(2)})


def body(
    tokens, cotangent, span_order,
    w_qkv, w_out, w_gateup, w_down, gains,
    first_qkv, first_out, first_gateup, first_down, first_gains,
    second_qkv, second_out, second_gateup, second_down, second_gains,
):
    cosine, sine = rope_tables()
    fwd = forward_step(
        span=span_order, tok=tokens, cot=cotangent, wq=w_qkv, wo=w_out, wgu=w_gateup, wd=w_down,
        gains=gains[None, :], spread=gain_spread(), cosine=cosine, sine=sine,
    )
    bwd = backward_step(
        span=span_order, tok=tokens, cot=cotangent, middle=fwd["middle"],
        gain_row=fwd["gain_row"], cosine=cosine, sine=sine,
        hidden_pair=fwd["hidden_pair"], cot_pair=fwd["cot_pair"], w_all=fwd["w_all"],
        w_two=fwd["w_two"].reshape(4, 16, 16, D),
        **{name: fwd[name] for name in SAVED},
    )
    names = ("qkv", "out", "gateup", "down", "gains")
    state = {
        "w_": (w_qkv, w_out, w_gateup, w_down, gains[None, :]),
        "first_": (first_qkv, first_out, first_gateup, first_down, first_gains[None, :]),
        "second_": (second_qkv, second_out, second_gateup, second_down, second_gains[None, :]),
    }
    new = update_step(
        **bwd, **{kind + name: value for kind, values in state.items() for name, value in zip(names, values)}
    )
    results = [
        new[kind + name] if name != "gains" else new[kind + name][0] for kind in state for name in names
    ]
    return (new["layer_out"], new["input_grad"], *results, new["norm"][0, 0])


def solution(mesh):
    rows, flat = P(("dp", "ctx"), None), P(("dp", "ctx"))
    state = (rows, rows, rows, rows, flat)
    in_specs = (rows, rows, P()) + state * 3
    out_specs = (rows, rows) + state * 3 + (P(),)
    return jax.shard_map(body, mesh=mesh, in_specs=in_specs, out_specs=out_specs, check_vma=False)
```

```python
import jax
import jax.numpy as jnp
import numpy as np
from jax import lax
from jax.experimental import pallas as pl
from jax.experimental.pallas import tpu as pltpu
from jax.sharding import PartitionSpec as P

D = 1024
HEADS = 16
KV_HEADS = 8
HEAD_WIDTH = 128
FF = 3072
STEP = 10

norm_eps = 1e-06
rope_base = 1000000.0
beta_one = 0.9
beta_two = 0.999
adam_eps = 1e-08
clip_at = 1.0
matrix_rate = 0.05
out_rate = 0.25
matrix_decay = 0.1
gain_rate = 0.5
masked_score = -1e30

MESH = pl.DeviceIdType.MESH
BF = jnp.bfloat16
F32 = jnp.float32
ROWS = 256
UNIT = 224
PART_A = 112
DOWN = 128
VMEM_LIMIT = 62 * 2**20
vmem = pl.BlockSpec(memory_space=pltpu.VMEM)
hbm = pl.BlockSpec(memory_space=pl.ANY)


class Place:
    def __init__(self):
        dp = lax.axis_index("dp")
        self.at = {
            "z": lax.div(dp, 8),
            "x": lax.rem(lax.div(dp, 2), 4),
            "k": lax.rem(dp, 2),
            "y": lax.axis_index("ctx"),
        }

    def __getitem__(self, axis):
        return self.at[axis]

    def device(self, **other):
        c = {**self.at, **other}
        return (c["z"] * 8 + c["x"] * 2 + c["k"], c["y"])

    def moved(self, axis, steps):
        return lax.rem(self.at[axis] + steps, 4)

    def peer(self, axis, steps):
        return self.device(**{axis: self.moved(axis, steps)})

    def sibling(self):
        return self.device(k=1 - self.at["k"])


def greet(devices):
    barrier = pltpu.get_barrier_semaphore()
    for device in devices:
        pl.semaphore_signal(barrier, inc=1, device_id=device, device_id_type=MESH)


def await_greetings(count):
    pl.semaphore_wait(pltpu.get_barrier_semaphore(), count)


def neighbours(place, axes):
    found = []
    for axis in axes:
        if axis == "k":
            found.append(place.sibling())
        else:
            found += [place.peer(axis, 1), place.peer(axis, 3)]
    return found


def remote(src, dst, send, recv, device):
    return pltpu.make_async_remote_copy(
        src_ref=src, dst_ref=dst, send_sem=send, recv_sem=recv, device_id=device, device_id_type=MESH
    )


class Gather:
    def __init__(self, place, axis, part, sems, own=None):
        self.part, self.send, self.recv = part, sems[0], sems[1]
        self.own = own or (lambda half: part(place[axis], half))
        self.next, self.prev = place.peer(axis, 1), place.peer(axis, 3)
        self.me, self.up, self.down, self.far = (place.moved(axis, n) for n in (0, 1, 3, 2))

    def copy(self, n, slot, half, device, src=None):
        view = self.part(slot, half)
        return remote(src if src is not None else view, view, self.send.at[n], self.recv.at[n], device)

    def outgoing(self, n):
        slot, half, device = [
            (self.me, 0, self.next),
            (self.me, 1, self.prev),
            (self.me, 1, self.next),
            (self.me, 0, self.prev),
            (self.down, 0, self.next),
            (self.up, 1, self.prev),
        ][n]
        return self.copy(n, slot, half, device, self.own(half) if n < 4 else None)

    def start(self, halves=(0, 1)):
        for half in halves:
            for n in ((0, 3), (1, 2))[half]:
                self.outgoing(n).start()

    def forward(self):
        self.copy(0, self.down, 0, self.prev).wait_recv()
        self.outgoing(4).start()
        self.copy(1, self.up, 1, self.next).wait_recv()
        self.outgoing(5).start()

    def finish(self):
        self.copy(2, self.down, 1, self.prev).wait_recv()
        self.copy(3, self.up, 0, self.next).wait_recv()
        self.copy(4, self.far, 0, self.prev).wait_recv()
        self.copy(5, self.far, 1, self.next).wait_recv()
        for n in range(6):
            self.outgoing(n).wait_send()


class Scatter:
    def __init__(self, place, axis, part, boxes, sems, mine=None):
        self.part, self.boxes = part, boxes
        self.send, self.recv = sems[0], sems[1]
        self.next, self.prev = place.peer(axis, 1), place.peer(axis, 3)
        self.me, self.up, self.down, self.far = (place.moved(axis, n) for n in (0, 1, 3, 2))
        self.mine = mine or self.own_part

    def own_part(self, n):
        slot, half = [(self.down, 0), (self.up, 1), (self.me, 0), (self.me, 1)][n]
        return self.part(slot, half)

    def copy(self, n, src, device):
        return remote(src, self.boxes[n], self.send.at[n], self.recv.at[n], device)

    def outgoing(self, n):
        source, device = [
            (lambda: self.part(self.far, 0), self.prev),
            (lambda: self.part(self.far, 1), self.next),
            (lambda: self.part(self.down, 1), self.prev),
            (lambda: self.part(self.up, 0), self.next),
            (lambda: self.boxes[0], self.prev),
            (lambda: self.boxes[1], self.next),
        ][n]
        return self.copy(n, source(), device)

    def start(self):
        for n in range(4):
            self.outgoing(n).start()

    def forward(self):
        for n in range(2):
            self.outgoing(n).wait_recv()
            add_rows(self.boxes[n], [self.boxes[n], self.mine(n)])
            self.outgoing(4 + n).start()

    def finish(self, result):
        for n in (2, 3, 4, 5):
            self.outgoing(n).wait_recv()
        add_rows(result(0), [self.mine(2), self.boxes[3], self.boxes[4]])
        add_rows(result(1), [self.mine(3), self.boxes[2], self.boxes[5]])
        for n in range(6):
            self.outgoing(n).wait_send()


def add_rows(out, terms):
    shape = out.shape
    rows = shape[-2]

    def block(at):
        total = terms[0][at].astype(F32)
        for term in terms[1:]:
            total = total + term[at].astype(F32)
        out[at] = total.astype(out.dtype)

    if len(shape) == 2:

        @pl.loop(0, rows // 16)
        def _(r):
            block((pl.ds(pl.multiple_of(r * 16, 16), 16), slice(None)))

    else:

        @pl.loop(0, shape[0])
        def _(lead):
            @pl.loop(0, rows // 16)
            def _(r):
                block((lead, pl.ds(pl.multiple_of(r * 16, 16), 16), slice(None)))


def dma(*shape):
    return pltpu.SemaphoreType.DMA(shape)


def ring_sems():
    return [dma(6), dma(6)]


def params(which):
    if which is None:
        return pltpu.CompilerParams(vmem_limit_bytes=VMEM_LIMIT)
    return pltpu.CompilerParams(
        collective_id=which, has_side_effects=True, vmem_limit_bytes=VMEM_LIMIT
    )


TILE = 256
SEQ = 4 * ROWS
BLOCK = ROWS // 2
OWN_HEADS = HEADS // 4
OWN_KV = KV_HEADS // 4
LOG2E = 1.4426950408889634


def turn(value_rows):
    return pltpu.roll(value_rows, HEAD_WIDTH // 2, 1)


def head_norm(raw):
    scale = lax.rsqrt(jnp.mean(raw * raw, axis=-1, keepdims=True) + norm_eps)
    return raw * scale, scale


def stored_block(span, position):
    found = jnp.int32(0)
    for block in range(1, 8):
        found = jnp.where(span[block] == position, block, found)
    return found


def pair_of(ref, span, tile):
    return jnp.concatenate([ref[stored_block(span, 2 * tile + n)] for n in range(2)], axis=0)


def dot_nt(left, right):
    return lax.dot_general(left, right, (((1,), (1,)), ((), ())), preferred_element_type=F32)


def dot_nn(left, right):
    return jnp.dot(left, right, preferred_element_type=F32)


def causal(scores):
    keys = lax.broadcasted_iota(jnp.int32, scores.shape, 0)
    queries = lax.broadcasted_iota(jnp.int32, scores.shape, 1)
    return jnp.where(keys <= queries, scores, masked_score)


def project(r, g_attn, g_query, g_key):
    span, tok, cosine, sine = r.span, r.tok_all, r.cosine, r.sine
    hidden, raw, query, key, key_t = r.hidden, r.raw, r.query, r.key, r.key_t
    value, value_t = r.value, r.value_t

    def columns(pair):
        return r.wq_all[:, :, :, :, 256 * pair : 256 * pair + 256].reshape(D, 256)

    @pl.loop(0, SEQ // TILE)
    def _(t):
        at = pl.ds(pl.multiple_of(t * TILE, TILE), TILE)
        rows = pair_of(tok, span, t).astype(F32)
        scale = lax.rsqrt(jnp.mean(rows * rows, axis=-1, keepdims=True) + norm_eps)
        hid = (rows * scale * g_attn[...]).astype(BF)
        hidden[at] = hid
        cos_t, sin_t = cosine[at], sine[at]
        for pair in range(OWN_HEADS // 2):
            both = dot_nn(hid, columns(pair))
            for n in range(2):
                h, part = 2 * pair + n, both[:, 128 * n : 128 * n + 128]
                raw[h, at] = part.astype(BF)
                normed = head_norm(part)[0] * g_query[...]
                query[h, at] = (normed * cos_t + turn(normed) * sin_t).astype(BF)
        both = dot_nn(hid, columns(2))
        for h in range(OWN_KV):
            part = both[:, 128 * h : 128 * h + 128]
            raw[OWN_HEADS + h, at] = part.astype(BF)
            normed = head_norm(part)[0] * g_key[...]
            rotated = normed * cos_t + turn(normed) * sin_t
            key[h, at] = rotated.astype(BF)
            key_t[h, :, at] = rotated.T.astype(BF)
        both = dot_nn(hid, columns(3))
        for h in range(OWN_KV):
            part = both[:, 128 * h : 128 * h + 128]
            value[h, at] = part.astype(BF)
            value_t[h, :, at] = part.T.astype(BF)


def attend(r, first_head, last_head):
    query, key, value_t, attended = r.query, r.key, r.value_t, r.attended
    attended_t, log_total = r.attended_t, r.log_total
    factor = HEAD_WIDTH ** (-0.5) * LOG2E

    @pl.loop(first_head, last_head)
    def _(h):
        kv = lax.div(h, 2)
        for t in range(SEQ // TILE):
            low, high = t * TILE, (t + 1) * TILE
            q = query[h, low:high]
            scores = [causal(dot_nt(key[kv, low:high], q))]
            if t:
                scores.append(dot_nt(key[kv, 0:low], q))
            top = jnp.max(scores[0], axis=0, keepdims=True)
            if t:
                top = jnp.maximum(top, jnp.max(scores[1], axis=0, keepdims=True))
            top = top * factor
            probs = [jnp.exp2(s * factor - top) for s in scores]
            total = jnp.sum(probs[0], axis=0, keepdims=True)
            mixed = dot_nn(value_t[kv, :, low:high], probs[0].astype(BF))
            if t:
                total = total + jnp.sum(probs[1], axis=0, keepdims=True)
                mixed = mixed + dot_nn(value_t[kv, :, 0:low], probs[1].astype(BF))
            mixed = mixed * (1.0 / total)
            attended_t[h, :, low:high] = mixed.astype(BF)
            attended[h, 2 * t : 2 * t + 2] = mixed.T.astype(BF).reshape(2, BLOCK, HEAD_WIDTH)
            log_total[h, :, low:high] = jnp.broadcast_to(top + jnp.log2(total), (8, TILE))


def attend_back(r, first_head, last_head):
    query, key, key_t, value = r.query, r.key, r.key_t, r.value
    d_attended, log_total, d_query = r.d_attended, r.log_total, r.d_query
    d_key, d_value = r.d_key, r.d_value
    factor = HEAD_WIDTH ** (-0.5) * LOG2E
    plain = HEAD_WIDTH ** (-0.5)

    @pl.loop(first_head, last_head)
    def _(h):
        kv = lax.div(h, 2)
        for t in range(SEQ // TILE):
            low, high = t * TILE, (t + 1) * TILE
            q = query[h, low:high]
            da = d_attended[h, low:high]
            total = log_total[h, 0:1, low:high]
            spans = [(low, high)] + ([(0, low)] if t else [])
            probs, mixes = [], []
            for n, (first, last) in enumerate(spans):
                scores = dot_nt(key[kv, first:last], q)
                if n == 0:
                    scores = causal(scores)
                p = jnp.exp2(scores * factor - total)
                d_value[kv, first:last] += dot_nn(p.astype(BF), da)
                probs.append(p)
                mixes.append(p * dot_nt(value[kv, first:last], da))
            delta = jnp.sum(mixes[0], axis=0, keepdims=True)
            if t:
                delta = delta + jnp.sum(mixes[1], axis=0, keepdims=True)
            back = None
            for (first, last), p, mix in zip(spans, probs, mixes):
                ds = (mix - p * delta).astype(BF)
                d_key[kv, first:last] += dot_nn(ds, q)
                part = dot_nn(key_t[kv, :, first:last], ds)
                back = part if back is None else back + part
            d_query[h, low:high] = (back * plain).T


GAINS = 2 * D + 2 * HEAD_WIDTH
smem = pl.BlockSpec(memory_space=pltpu.SMEM)
regular = pltpu.SemaphoreType.DMA


class Names:
    def __init__(self, names, refs):
        self.__dict__.update(zip(names, refs))


def named_call(kernel, which, name, given, spaces, outputs, scratch):
    names = list(given) + ["out_" + n for n in outputs] + list(scratch)
    results = pl.pallas_call(
        lambda *refs: kernel(Names(names, refs)),
        out_shape=tuple(jax.ShapeDtypeStruct(shape, kind) for shape, kind, _ in outputs.values()),
        in_specs=[spaces.get(n, vmem) for n in given],
        out_specs=tuple(space for _, _, space in outputs.values()),
        scratch_shapes=list(scratch.values()),
        compiler_params=params(which),
        name=name,
    )(*given.values())
    return dict(zip(outputs, results))


SAVED = {
    "wq_all": ((4, 4, 2, 32, 1152), BF),
    "wo_all": ((4, 2, 64, D), BF),
    "hidden": ((SEQ, D), BF),
    "raw": ((OWN_HEADS + OWN_KV, SEQ, HEAD_WIDTH), BF),
    "query": ((OWN_HEADS, SEQ, HEAD_WIDTH), BF),
    "key": ((OWN_KV, SEQ, HEAD_WIDTH), BF),
    "key_t": ((OWN_KV, HEAD_WIDTH, SEQ), BF),
    "value": ((OWN_KV, SEQ, HEAD_WIDTH), BF),
    "attended_t": ((OWN_HEADS, HEAD_WIDTH, SEQ), BF),
    "log_total": ((OWN_HEADS, 8, SEQ), F32),
}


def heads_of(ref, count, at):
    return jnp.concatenate([ref[h, at] for h in range(count)], axis=1)


def row_tile(r, size):
    return pl.ds(pl.multiple_of(r * size, size), size)


def from_to(half, low, split, high):
    return pl.ds(low, split - low) if half == 0 else pl.ds(split, high - split)


def not_here(condition, other, coordinate):
    return jnp.logical_not(jnp.logical_and(condition, coordinate == other))


def pack_gateup(w, out):
    for k in range(2):
        for side in range(2):
            pieces = [w[:, FF * side + 96 * n : FF * side + 96 * n + 96] for n in range(k, 32, 2)]
            columns = jnp.concatenate(pieces, axis=1)
            for b in range(3):
                out[k, b, :, 512 * side : 512 * side + 512] = columns[:, 512 * b : 512 * b + 512]


def unpack_gateup(packed):
    sides = []
    for side in range(2):
        cores = [
            jnp.concatenate([packed[k, b, :, 512 * side : 512 * side + 512] for b in range(3)], axis=1)
            for k in range(2)
        ]
        sides += [cores[n % 2][:, 96 * (n // 2) : 96 * (n // 2) + 96] for n in range(32)]
    return jnp.concatenate(sides, axis=1)


def forward_kernel(r):
    place = Place()
    z, x, k, y = (place[a] for a in "zxky")
    near = neighbours(place, "xyzk")
    diagonal = z == y
    plane = [theirs_at(place, *o) for o in THEIRS]
    greet(near + [place.peer("y", 2)] + plane)
    for other in range(4):

        @pl.when(not_here(diagonal, other, y))
        def _():
            greet([place.device(z=y, y=jnp.int32(other))])

    for i in range(4):
        r.q_send[i, :, 0:512] = r.wq[:, 512 * i : 512 * i + 512]
        r.q_send[i, :, 512:768] = r.wq[:, 2048 + 256 * i : 2304 + 256 * i]
        r.q_send[i, :, 768:1024] = r.wq[:, 3072 + 256 * i : 3328 + 256 * i]
        r.q_send[i, :, 1024:1152] = jnp.zeros((8, 128), F32)
        r.q_send[i, 0:1, 1024:1042] = r.gains[...]
    pack_gateup(r.wgu, r.packed)
    r.q_recv[y] = r.q_send[y]
    r.o_send[...] = r.wo[...].astype(BF)
    r.tok_all[pl.ds(2 * y, 2)] = r.tok[...].reshape(2, BLOCK, D)
    await_greetings(len(near) + 1 + len(plane) + jnp.where(diagonal, 3, 4))

    g_prep = remote(r.packed.at[1 - k], r.g_recv, r.pair.at[0], r.pair.at[1], place.sibling())
    g_prep.start()
    q_prep = [
        remote(r.q_send.at[place.moved("y", n)], r.q_recv.at[y], r.qp_s.at[n], r.qp_r.at[y], place.peer("y", n))
        for n in (1, 3, 2)
    ]
    for copy in q_prep:
        copy.start()

    def o_slot(source):
        return r.wo_all.at[x, k, row_tile(source, 16)]

    for other in range(4):

        @pl.when(not_here(diagonal, other, z))
        def _():
            remote(r.o_send, o_slot(y), r.op_s.at[other], r.op_r.at[y], place.device(z=jnp.int32(other), y=z)).start()

    @pl.when(diagonal)
    def _():
        r.wo_all[x, k, row_tile(y, 16)] = r.o_send[...]

    cot_copy = remote(r.cot, r.out_cot_pair.at[pl.ds(ROWS, ROWS)], r.pair.at[2], r.pair.at[3], place.sibling())
    cot_copy.start()
    cot_own = pltpu.make_async_copy(r.cot, r.out_cot_pair.at[pl.ds(0, ROWS)], r.pair.at[6])
    cot_own.start()

    g_prep.wait_recv()
    g_own, g_other, lower = r.packed[k], r.g_recv[...], k == 0
    both = jnp.concatenate([jnp.where(lower, g_own, g_other), jnp.where(lower, g_other, g_own)], axis=1)
    r.g_y[y] = both[0:2].reshape(32, D).astype(BF)
    r.w_c[y, 4 * z + x] = both[2].astype(BF)
    c_x = Gather(place, "x", lambda i, h: r.w_c.at[y, 4 * z + i, :, pl.ds(512 * h, 512)], (r.cx_s, r.cx_r))
    c_z = Gather(place, "z", lambda i, h: r.w_c.at[y, pl.ds(4 * i + 2 * h, 2)], (r.cz_s, r.cz_r))
    c_y = Gather(place, "y", lambda i, h: r.w_c.at[i, pl.ds(8 * h, 8)], (r.cy_s, r.cy_r))
    r.d_y[y] = r.wd[...]
    g_ring = Gather(place, "y", lambda i, h: r.g_y.at[i, pl.ds(16 * h, 16)], (r.gy_s, r.gy_r))
    d_ring = Gather(place, "y", lambda i, h: r.d_y.at[i, from_to(h, 0, 16, 24)], (r.dy_s, r.dy_r))
    g_ring.start()
    d_ring.start()
    c_x.start()

    for n in (1, 3, 2):
        source = place.moved("y", n)
        remote(r.q_send.at[0], r.q_recv.at[source], r.qp_s.at[n], r.qp_r.at[source], place.peer("y", n)).wait_recv()
    r.wq_all[z, x, k] = r.q_recv[...].reshape(32, 1152).astype(BF)
    q_direct = []
    for n, (dz, dx) in enumerate(THEIRS):
        unit = r.wq_all.at[z, x, k]
        q_direct.append(remote(unit, unit, r.qd_s.at[n], r.qd_r.at[4 * z + x], theirs_at(place, dz, dx)))
    for copy in q_direct:
        copy.start()

    def q_core(at_z, at_x, core):
        unit, which = r.wq_all.at[at_z, at_x, core], 4 * at_z + at_x
        return remote(unit, unit, r.qc_s.at[which], r.qc_r.at[which], place.sibling())

    q_core(z, x, k).start()
    tokens = Gather(place, "y", lambda i, h: r.tok_all.at[2 * i + h], (r.t_s, r.t_r))
    tokens.start()

    for other in range(4):

        @pl.when(not_here(diagonal, other, y))
        def _():
            remote(r.o_send, o_slot(other), r.op_s.at[0], r.op_r.at[other], place.device(z=y, y=jnp.int32(other))).wait_recv()

    o_x = Gather(place, "x", lambda i, h: r.wo_all.at[i, k, pl.ds(32 * h, 32)], (r.ox_s, r.ox_r))
    o_x.start()
    g_ring.forward()
    d_ring.forward()
    c_x.forward()
    c_x.finish()
    c_z.start()
    o_x.forward()
    g_ring.finish()
    d_ring.finish()

    for b in range(2):
        pieces = [r.g_y[c, 16 * b : 16 * b + 16].astype(F32) for c in range(4)]
        for core_row in range(2):
            rows = jnp.concatenate([piece[8 * core_row : 8 * core_row + 8] for piece in pieces], axis=0)
            at = 64 * b + 32 * core_row
            r.unit[at : at + 32] = rows.astype(BF)
    r.unit[DOWN:UNIT] = r.d_y[...].reshape(96, D).astype(BF)
    w_all = r.out_w_all
    u_own = pltpu.make_async_copy(r.unit, w_all.at[z, x], r.pair.at[4])
    u_own.start()
    a_one = Gather(
        place, "x", lambda i, h: w_all.at[z, i, from_to(h, 0, 64, PART_A)], (r.a1_s, r.a1_r),
        own=lambda h: r.unit.at[from_to(h, 0, 64, PART_A)],
    )
    b_one = Gather(
        place, "z", lambda i, h: w_all.at[i, x, from_to(h, PART_A, 160, UNIT)], (r.b1_s, r.b1_r),
        own=lambda h: r.unit.at[from_to(h, PART_A, 160, UNIT)],
    )
    a_one.start()
    b_one.start()
    tokens.forward()
    c_z.forward()
    o_x.finish()
    o_core = remote(r.wo_all.at[:, k], r.wo_all.at[:, k], r.core.at[0], r.core.at[1], place.sibling())
    o_core.start()
    a_one.forward()
    b_one.forward()
    for dz, dx in sorted(THEIRS, key=lambda o: min(o[0], 4 - o[0]) + min(o[1], 4 - o[1])):
        at_z, at_x = place.moved("z", dz), place.moved("x", dx)
        other = r.wq_all.at[at_z, at_x, k]
        remote(other, other, r.qd_s.at[0], r.qd_r.at[4 * at_z + at_x], theirs_at(place, dz, dx)).wait_recv()
        q_core(at_z, at_x, k).start()
    a_one.finish()
    b_one.finish()
    u_own.wait()
    a_two = Gather(place, "z", lambda i, h: w_all.at[i, pl.ds(2 * h, 2), pl.ds(0, PART_A)], (r.a2_s, r.a2_r))
    b_two = Gather(place, "x", lambda i, h: w_all.at[pl.ds(2 * h, 2), i, pl.ds(PART_A, UNIT - PART_A)], (r.b2_s, r.b2_r))
    a_two.start()
    b_two.start()
    c_z.finish()
    c_y.start()
    remote(r.wo_all.at[:, 1 - k], r.wo_all.at[:, 1 - k], r.core.at[0], r.core.at[1], place.sibling()).wait_recv()
    for at_z in range(4):
        for at_x in range(4):
            q_core(at_z, at_x, 1 - k).wait_recv()
    tokens.finish()

    lanes = r.wq_all[:, :, :, :, D:1152].reshape(128, 8, 128).astype(F32)
    spread = dot_nn(jnp.sum(lanes, axis=1).astype(BF), r.spread[...])
    owner = lax.broadcasted_iota(jnp.int32, (128, GAINS), 0) * 18
    spot = lax.broadcasted_iota(jnp.int32, (128, GAINS), 1)
    mine = jnp.logical_and(spot >= owner, spot < owner + 18)
    r.out_gain_row[...] = jnp.sum(jnp.where(mine, spread, 0.0), axis=0, keepdims=True)
    gain = r.out_gain_row
    project(r, gain.at[:, 0:D], gain.at[:, 2 * D : 2 * D + 128], gain.at[:, 2 * D + 128 : GAINS])
    attend(r, 0, 2)
    c_y.forward()
    attend(r, 2, 4)

    wo = r.wo_all[...].reshape(OWN_HEADS * HEAD_WIDTH, D)

    @pl.loop(0, 4)
    def _(i):
        rows = jnp.concatenate(
            [heads_of(r.attended, OWN_HEADS, r.span[2 * i + n]) for n in range(2)], axis=0
        )
        r.terms[i] = dot_nn(rows, wo).astype(BF)

    reduce = Scatter(
        place, "y", lambda i, h: r.terms.at[i, pl.ds(128 * h, 128)],
        [r.boxes.at[n] for n in range(6)], (r.y_s, r.y_r),
    )
    reduce.start()
    a_two.forward()
    b_two.forward()
    saves = [
        pltpu.make_async_copy(getattr(r, n), getattr(r, "out_" + n), r.save.at[i]) for i, n in enumerate(SAVED)
    ]
    for copy in saves:
        copy.start()
    c_y.finish()

    @pl.loop(0, 16)
    def _(j):
        pieces = [r.w_c[c, j].astype(F32) for c in range(4)]
        rows = [piece[8 * core_row : 8 * core_row + 8] for core_row in range(2) for piece in pieces]
        r.w_two[j] = jnp.concatenate(rows, axis=0).astype(BF)

    two_copy = pltpu.make_async_copy(r.w_two, r.out_w_two, r.pair.at[5])
    two_copy.start()
    reduce.forward()
    reduce.finish(lambda h: r.total.at[pl.ds(128 * h, 128)])

    hid_copies = []
    for half in range(2):

        @pl.loop(0, BLOCK // 32)
        def _(t):
            at = row_tile(4 * half + t, 32)
            rows = r.tok[at].astype(F32) + r.total[at]
            r.total[at] = rows
            scale = lax.rsqrt(jnp.mean(rows * rows, axis=-1, keepdims=True) + norm_eps)
            r.hid[at] = (rows * scale * gain[:, D : 2 * D]).astype(BF)

        here, there = pl.ds(BLOCK * half, BLOCK), pl.ds(ROWS + BLOCK * half, BLOCK)
        hid_copies += [
            remote(r.hid.at[here], r.out_hidden_pair.at[there], r.hid_sem.at[4 * half], r.hid_sem.at[4 * half + 1], place.sibling()),
            pltpu.make_async_copy(r.hid.at[here], r.out_hidden_pair.at[here], r.hid_sem.at[4 * half + 2]),
            pltpu.make_async_copy(r.total.at[here], r.out_middle.at[here], r.hid_sem.at[4 * half + 3]),
        ]
        for copy in hid_copies[3 * half :]:
            copy.start()

    a_two.finish()
    b_two.finish()
    two_copy.wait()
    for copy in saves:
        copy.wait()
    for copy in q_prep + q_direct + [g_prep, o_core]:
        copy.wait_send()
    for at_z in range(4):
        for at_x in range(4):
            q_core(at_z, at_x, k).wait_send()
    cot_copy.wait()
    cot_own.wait()
    for copy in hid_copies:
        copy.wait()
    for other in range(4):

        @pl.when(not_here(diagonal, other, z))
        def _():
            remote(r.o_send, o_slot(y), r.op_s.at[other], r.op_r.at[y], place.device(z=jnp.int32(other), y=z)).wait_send()


def rings(*names):
    return {f"{name}_{end}": dma(6) for name in names for end in "sr"}


def forward_step(**given):
    outputs = {
        "middle": ((ROWS, D), F32, hbm),
        "hidden_pair": ((2 * ROWS, D), BF, hbm),
        "cot_pair": ((2 * ROWS, D), BF, hbm),
        "gain_row": ((1, GAINS), F32, vmem),
        "w_all": ((4, 4, UNIT, D), BF, hbm),
        "w_two": ((16, 64, D), BF, hbm),
        **{n: (*what, hbm) for n, what in SAVED.items()},
    }
    scratch = {
        "q_send": pltpu.VMEM((4, 8, 1152), F32),
        "q_recv": pltpu.VMEM((4, 8, 1152), F32),
        "o_send": pltpu.VMEM((16, D), BF),
        "packed": pltpu.VMEM((2, 3, 8, D), F32),
        "g_recv": pltpu.VMEM((3, 8, D), F32),
        "g_y": pltpu.VMEM((4, 32, D), BF),
        "w_c": pltpu.VMEM((4, 16, 16, D), BF),
        "w_two": pltpu.VMEM((16, 64, D), BF),
        "d_y": pltpu.VMEM((4, 24, D), F32),
        "unit": pltpu.VMEM((UNIT, D), BF),
        "tok_all": pltpu.VMEM((8, BLOCK, D), BF),
        "value_t": pltpu.VMEM((OWN_KV, HEAD_WIDTH, SEQ), BF),
        "attended": pltpu.VMEM((OWN_HEADS, 8, BLOCK, HEAD_WIDTH), BF),
        "terms": pltpu.VMEM((4, ROWS, D), BF),
        "boxes": pltpu.VMEM((6, BLOCK, D), BF),
        "total": pltpu.VMEM((ROWS, D), F32),
        **{n: pltpu.VMEM(*what) for n, what in SAVED.items()},
        "hid": pltpu.VMEM((ROWS, D), BF),
        "pair": dma(7),
        "core": dma(2),
        "hid_sem": dma(8),
        **{"qc_s": dma(16), "qc_r": dma(16)},
        "save": dma(len(SAVED)),
        **{n: dma(4) for n in ("qp_s", "qp_r", "op_s", "op_r")},
        **{"qd_s": dma(15), "qd_r": dma(16)},
        **rings("gy", "dy", "cx", "cz", "cy", "ox", "t", "a1", "b1", "a2", "b2", "y"),
    }
    spaces = {"span": smem}
    return named_call(forward_kernel, 1, "forward_attention", given, spaces, outputs, scratch)


def sum_everywhere(r, place):
    z, x, k, y = (place[a] for a in "zxky")

    def stage(source, slots, send, recv, offsets, device, me, slot_of):
        slots[me] = source[...]
        copies = [
            remote(source, slots.at[me], send.at[n], recv.at[me], device(*offset))
            for n, offset in enumerate(offsets)
        ]
        for copy in copies:
            copy.start()
        for n, offset in enumerate(offsets):
            slot = slot_of(*offset)
            remote(source, slots.at[slot], send.at[n], recv.at[slot], device(*offset)).wait_recv()
        for copy in copies:
            copy.wait_send()

    stage(r.value_row, r.first, r.s1_s, r.s1_r, OURS, lambda *o: ours_at(place, *o), y * 2 + k,
          lambda dy, dk: place.moved("y", dy) * 2 + lax.rem(k + dk, 2))
    r.held[...] = jnp.sum(r.first[...], axis=0)
    stage(r.held, r.second, r.s2_s, r.s2_r, THEIRS, lambda *o: theirs_at(place, *o), z * 4 + x,
          lambda dz, dx: place.moved("z", dz) * 4 + place.moved("x", dx))
    r.out_sums[...] = jnp.sum(r.second[...], axis=0)


OURS = [(dy, dk) for dy in range(4) for dk in range(2) if (dy, dk) != (0, 0)]
THEIRS = [(dz, dx) for dz in range(4) for dx in range(4) if (dz, dx) != (0, 0)]


def ours_at(place, dy, dk):
    return place.device(y=place.moved("y", dy), k=lax.rem(place["k"] + dk, 2))


def theirs_at(place, dz, dx):
    return place.device(z=place.moved("z", dz), x=place.moved("x", dx))


def by_eights(rows):
    return jnp.sum(rows.reshape(rows.shape[0] // 8, 8, D), axis=0)


def back_through_norm(r, gain, half):
    @pl.loop(0, BLOCK // 32)
    def _(t):
        at = row_tile(4 * half + t, 32)
        rows = r.middle[at]
        scale = lax.rsqrt(jnp.mean(rows * rows, axis=-1, keepdims=True) + norm_eps)
        normed = rows * scale
        incoming = r.out_input_grad[at] + r.dh_box[at].astype(F32)
        r.mlp_gain[...] += by_eights(incoming * normed)
        incoming = incoming * gain[:, D : 2 * D]
        mean = jnp.mean(incoming * normed, axis=-1, keepdims=True)
        d_mid = r.cot[at].astype(F32) + scale * (incoming - normed * mean)
        r.out_input_grad[at] = d_mid
        r.own[at] = d_mid.astype(BF)


def back_to_input(r, gain):
    r.attn_gain[...] = jnp.zeros_like(r.attn_gain)

    @pl.loop(0, ROWS // 32)
    def _(t):
        at = row_tile(t, 32)
        rows = r.tok[at].astype(F32)
        scale = lax.rsqrt(jnp.mean(rows * rows, axis=-1, keepdims=True) + norm_eps)
        normed = rows * scale
        incoming = r.dh_total[at]
        r.attn_gain[...] += by_eights(incoming * normed)
        incoming = incoming * gain[:, 0:D]
        mean = jnp.mean(incoming * normed, axis=-1, keepdims=True)
        r.out_input_grad[at] += scale * (incoming - normed * mean)


def back_to_projections(r, gain):
    plain = HEAD_WIDTH ** (-0.5)
    r.head_gain[...] = jnp.zeros_like(r.head_gain)

    @pl.loop(0, SEQ // TILE)
    def _(t):
        at = row_tile(t, TILE)
        cos_t, sin_t = r.cosine[at], r.sine[at]
        for h in range(OWN_HEADS + OWN_KV):
            mine = h < OWN_HEADS
            d_rows = r.d_query[h, at] if mine else r.d_key[h - OWN_HEADS, at] * plain
            first = 2 * D if mine else 2 * D + HEAD_WIDTH
            d_gained = d_rows * cos_t - turn(d_rows) * sin_t
            normed, scale = head_norm(r.raw[h, at].astype(F32))
            product = d_gained * normed
            r.head_gain[0 if mine else 1] += jnp.sum(product.reshape(TILE // 8, 8, HEAD_WIDTH), axis=0)
            incoming = d_gained * gain[:, first : first + HEAD_WIDTH]
            mean = jnp.mean(incoming * normed, axis=-1, keepdims=True)
            r.d_proj[pl.ds(2 * t, 2), :, 128 * h : 128 * h + 128] = (
                (scale * (incoming - normed * mean)).astype(BF).reshape(2, BLOCK, HEAD_WIDTH)
            )
        for h in range(OWN_KV):
            r.d_proj[pl.ds(2 * t, 2), :, 768 + 128 * h : 896 + 128 * h] = (
                r.d_value[h, at].astype(BF).reshape(2, BLOCK, HEAD_WIDTH)
            )


def block_weights(r, b):
    if b == 2:
        return r.c[...].reshape(D, D)
    return r.w[:, :, 64 * b : 64 * b + 64].reshape(D, D)


def block_down(r, b):
    return r.w[:, :, DOWN:UNIT].reshape(FF // 2, D)[512 * b : 512 * b + 512]


def product_rows(r, first, last):
    parts = []
    if first < D:
        parts.append(r.d_o[...].reshape(2 * ROWS, D)[:, first : min(last, D)])
    if last > D:
        parts.append(r.d_q[2:4].reshape(2 * ROWS, D)[:, max(first, D) - D : last - D])
    return parts[0] if len(parts) == 1 else jnp.concatenate(parts, axis=1)


def d_gate_up_rows(r, b, t):
    if b < 2:
        return r.d_proj[pl.ds(4 * b + 2 * t, 2)].reshape(ROWS, D)
    return r.d_q[t].reshape(ROWS, D)


def feed_forward(r, w_loads):
    w_loads[0].wait()
    w_loads[1].wait()
    for b in range(3):
        if b:
            w_loads[1 + b].wait()
        weights, down = block_weights(r, b), block_down(r, b)

        @pl.loop(0, 2)
        def _(t):
            gate_up = dot_nn(r.hidden[row_tile(t, ROWS)], weights)
            d_product = dot_nt(r.hidden[row_tile(2 + t, ROWS)], down)
            gate, up = gate_up[:, :512], gate_up[:, 512:]
            sigmoid = 1.0 / (1.0 + jnp.exp(-gate))
            active = gate * sigmoid
            product = (active * up).astype(BF).reshape(4, 64, 512)
            if b < 2:
                r.d_o[pl.ds(2 * t, 2), :, :, 512 * b : 512 * b + 512] = product.reshape(2, 2, 64, 512)
            else:
                r.d_q[2 + t, :, :, :, 0:512] = product.reshape(4, 2, 32, 512)
            d_gate = d_product * up * sigmoid * (1.0 + gate * (1.0 - sigmoid))
            d_both = jnp.concatenate([d_gate, d_product * active], axis=1).astype(BF)
            if b < 2:
                r.d_proj[pl.ds(4 * b + 2 * t, 2)] = d_both.reshape(2, BLOCK, D)
            else:
                r.d_q[t] = d_both.reshape(4, 2, 32, D)


def feed_forward_inputs(r):
    def half(t):
        total = dot_nt(d_gate_up_rows(r, 0, t), block_weights(r, 0))
        for b in (1, 2):
            total = total + dot_nt(d_gate_up_rows(r, b, t), block_weights(r, b))
        return total

    r.dh_sib[...] = half(1).astype(BF)
    r.out_input_grad[...] = half(0)


def feed_forward_outputs(r):
    down = r.w[:, :, DOWN:UNIT].reshape(FF // 2, D)

    def half(t):
        first = dot_nn(r.d_o[2 * t : 2 * t + 2].reshape(ROWS, D), down[:D])
        return first + dot_nn(r.d_q[2 + t, :, :, :, 0:512].reshape(ROWS, 512), down[D:])

    r.out_sib[...] = half(1).astype(BF)
    r.dh_total[...] = half(0)


def dot_tn(left, right):
    return lax.dot_general(left, right, (((0,), (0,)), ((), ())), preferred_element_type=F32)


def down_gradients(r):
    cot = r.hidden[2 * ROWS : SEQ]
    for i in range(4):
        left = product_rows(r, 384 * i, 384 * i + 384)
        r.w[i, :, DOWN:UNIT] = dot_tn(left, cot).astype(BF).reshape(4, 96, D)


def block_gradients(r, b):
    d_both = jnp.concatenate([d_gate_up_rows(r, b, 0), d_gate_up_rows(r, b, 1)], axis=0)

    @pl.loop(0, 4)
    def _(i):
        columns = pl.ds(pl.multiple_of(i * 256, 256), 256)
        rows = dot_tn(r.hidden[0 : 2 * ROWS, columns], d_both)
        if b < 2:
            r.w[i, :, 64 * b : 64 * b + 64] = rows.astype(BF).reshape(4, 64, D)
        else:
            rows = rows.reshape(4, 2, 4, 8, D)
            for c in range(4):
                r.c[c, pl.ds(4 * i, 4)] = rows[:, :, c].reshape(4, 16, D).astype(BF)


def backward_kernel(r):
    place = Place()
    z, x, k, y = (place[a] for a in "zxky")
    diagonal = z == y
    gain = r.gain_row
    near = neighbours(place, "xyzk")
    everyone = [ours_at(place, *o) for o in OURS] + [theirs_at(place, *o) for o in THEIRS]
    greet(near + everyone)
    for other in range(4):

        @pl.when(not_here(diagonal, other, z))
        def _():
            greet([place.device(z=jnp.int32(other), y=z)])

    loads = {
        n: pltpu.make_async_copy(getattr(r, "in_" + n), getattr(r, n), r.load.at[i]) for i, n in enumerate(SAVED)
    }
    pair_loads = [
        pltpu.make_async_copy(pair, r.hidden.at[rows], r.w_sem.at[4 + i])
        for i, (pair, rows) in enumerate([(r.hidden_pair, pl.ds(0, 2 * ROWS)), (r.cot_pair, pl.ds(2 * ROWS, 2 * ROWS))])
    ]
    w_loads = [
        pltpu.make_async_copy(r.w_all.at[:, :, rows], r.w.at[:, :, rows], r.w_sem.at[i])
        for i, rows in enumerate([pl.ds(0, 64), pl.ds(DOWN, 96), pl.ds(64, 64)])
    ]
    w_loads.append(pltpu.make_async_copy(r.w_two, r.c, r.w_sem.at[3]))
    hidden_load = loads.pop("hidden")
    for copy in pair_loads + w_loads:
        copy.start()

    def a_part(i, h):
        return r.w.at[i, pl.ds(2 * h, 2), pl.ds(0, PART_A)]

    def b_part(i, h):
        return r.w.at[pl.ds(2 * h, 2), i, pl.ds(PART_A, UNIT - PART_A)]

    a_one = Scatter(place, "z", a_part, [r.a_box.at[n] for n in range(6)], (r.a1_s, r.a1_r))
    b_one = Scatter(place, "x", b_part, [r.b_box.at[n] for n in range(6)], (r.b1_s, r.b1_r))
    dh_copy = remote(r.dh_sib, r.dh_box, r.core.at[0], r.core.at[1], place.sibling())
    out_copy = remote(r.out_sib, r.out_box, r.core.at[2], r.core.at[3], place.sibling())
    for copy in pair_loads:
        copy.wait()
    feed_forward(r, w_loads)
    for copy in loads.values():
        copy.start()
    feed_forward_inputs(r)
    await_greetings(len(near) + len(everyone) + jnp.where(diagonal, 3, 4))
    dh_copy.start()
    feed_forward_outputs(r)
    out_copy.start()
    dh_copy.wait_recv()
    ring = Gather(
        place, "y", lambda i, h: r.d_attn_all.at[2 * i + h], (r.t_s, r.t_r),
        own=lambda h: r.own.at[pl.ds(BLOCK * h, BLOCK)],
    )
    r.mlp_gain[...] = jnp.zeros_like(r.mlp_gain)
    for half in range(2):
        back_through_norm(r, gain, half)
        ring.start([half])
    r.d_attn_all[pl.ds(2 * y, 2)] = r.own[...].reshape(2, BLOCK, D)
    down_gradients(r)
    block_gradients(r, 1)
    b_one.start()
    block_gradients(r, 0)
    a_one.start()
    block_gradients(r, 2)
    hidden_load.start()
    out_copy.wait_recv()

    @pl.loop(0, ROWS // 16)
    def _(t):
        at = row_tile(t, 16)
        r.out_layer_out[at] = (r.middle[at] + r.dh_total[at] + r.out_box[at].astype(F32)).astype(BF)

    for copy in [hidden_load, *loads.values()]:
        copy.wait()
    r.d_key[...] = jnp.zeros_like(r.d_key)
    r.d_value[...] = jnp.zeros_like(r.d_value)
    ring.forward()
    ring.finish()
    c_y = Scatter(
        place, "y", lambda i, h: r.c.at[i, pl.ds(8 * h, 8)],
        [r.cy_box.at[n] for n in range(6)], (r.cy_s, r.cy_r),
    )
    c_z = Scatter(
        place, "z", lambda i, h: r.c.at[y, pl.ds(4 * i + 2 * h, 2)],
        [r.cz_box.at[n] for n in range(6)], (r.cz_s, r.cz_r),
    )
    c_x = Scatter(
        place, "x", lambda i, h: r.c.at[y, 4 * z + i, :, pl.ds(512 * h, 512)],
        [r.cx_box.at[n] for n in range(6)], (r.cx_s, r.cx_r),
    )
    c_y.start()

    wo = r.wo_all[...].reshape(OWN_HEADS * HEAD_WIDTH, D)

    @pl.loop(0, SEQ // TILE)
    def _(t):
        at = row_tile(t, TILE)
        rows = pair_of(r.d_attn_all, r.span, t)
        r.d_q[t] = rows.reshape(4, 2, 32, D)
        both = dot_nt(rows, wo)
        for h in range(OWN_HEADS):
            r.d_attended[h, at] = both[:, 128 * h : 128 * h + 128].astype(BF)

    d_sorted = r.d_q[...].reshape(SEQ, D)

    @pl.loop(0, 4)
    def _(i):
        r.d_o[i] = dot_nn(r.attended_t[i], d_sorted).astype(BF).reshape(2, 64, D)

    o_core = remote(r.d_o.at[:, 1 - k], r.o_box, r.core.at[4], r.core.at[5], place.sibling())
    o_core.start()
    attend_back(r, 0, 2)
    c_y.forward()
    a_one.forward()
    b_one.forward()
    o_core.wait_recv()

    @pl.loop(0, 4)
    def _(i):
        add_rows(r.o_box.at[i], [r.o_box.at[i], r.d_o.at[i, k]])

    o_x = Scatter(
        place, "x", lambda i, h: r.o_box.at[i, pl.ds(32 * h, 32)],
        [r.ox_box.at[n] for n in range(6)], (r.ox_s, r.ox_r),
    )
    o_x.start()
    attend_back(r, 2, 4)
    c_y.finish(lambda h: r.c.at[y, pl.ds(8 * h, 8)])
    c_z.start()
    o_x.forward()
    back_to_projections(r, gain)

    wq = r.wq_all[:, :, :, :, 0:D].reshape(D, D)

    @pl.loop(0, 4)
    def _(i):
        rows = jnp.concatenate([r.d_proj[r.span[2 * i + n]] for n in range(2)], axis=0)
        r.d_attn_all[pl.ds(2 * i, 2)] = dot_nt(rows, wq).astype(BF).reshape(2, BLOCK, D)

    dh_ring = Scatter(
        place, "y", lambda i, h: r.d_attn_all.at[2 * i + h],
        [r.y_box.at[n] for n in range(6)], (r.y_s, r.y_r),
    )
    dh_ring.start()
    a_one.finish(lambda h: a_part(z, h))
    b_one.finish(lambda h: b_part(x, h))
    a_two = Scatter(
        place, "x", lambda i, h: r.w.at[z, i, from_to(h, 0, 64, PART_A)],
        [r.a_box2.at[n, pl.ds(0, 64 if n in (0, 3, 4) else 48)] for n in range(6)], (r.a2_s, r.a2_r),
    )
    b_two = Scatter(
        place, "z", lambda i, h: r.w.at[i, x, from_to(h, PART_A, 160, UNIT)],
        [r.b_box2.at[n, pl.ds(0, 48 if n in (0, 3, 4) else 64)] for n in range(6)], (r.b2_s, r.b2_r),
    )
    a_two.start()
    b_two.start()

    d_proj = r.d_proj[...].reshape(SEQ, D)
    planes = [place.moved("z", dz) for dz in (1, 2, 3, 0)]
    q_core = [
        remote(r.d_q.at[plane, :, 1 - k], r.q_box.at[plane], r.qk_s.at[n], r.qk_r.at[n], place.sibling())
        for n, plane in enumerate(planes)
    ]

    @pl.loop(0, 4)
    def _(n):
        plane = place.moved("z", n + 1)
        left = r.hidden[:, row_tile(plane, 256)]
        r.d_q[plane] = dot_tn(left, d_proj).astype(BF).reshape(4, 2, 32, D)
        remote(r.d_q.at[plane, :, 1 - k], r.q_box.at[plane], r.qk_s.at[n], r.qk_r.at[n], place.sibling()).start()

    q_direct = []
    for n, plane in enumerate(planes):
        q_core[n].wait_recv()

        @pl.loop(0, 4)
        def _(j):
            add_rows(r.q_box.at[plane, j], [r.q_box.at[plane, j], r.d_q.at[plane, j, k]])

        for dx in range(1 if n == 3 else 0, 4):
            to = place.moved("x", dx)
            q_direct.append(
                remote(
                    r.q_box.at[plane, to], r.q_slots.at[4 * z + x], r.qd_s.at[len(q_direct)], r.qd_r.at[4 * z + x],
                    place.device(z=plane, x=to),
                )
            )
            q_direct[-1].start()
    r.q_slots[4 * z + x] = r.q_box[z, x]
    dh_ring.forward()
    c_z.forward()
    a_two.forward()
    b_two.forward()
    c_z.finish(lambda h: r.c.at[y, pl.ds(4 * z + 2 * h, 2)])
    c_x.start()
    o_x.finish(lambda h: r.o_two.at[pl.ds(32 * h, 32)])

    def o_target(other):
        return place.device(z=y, y=jnp.int32(other))

    for other in range(4):
        piece = r.o_two.at[pl.ds(16 * other, 16)]

        @pl.when(not_here(diagonal, other, y))
        def _():
            remote(piece, r.o_slots.at[z], r.oy_s.at[other], r.oy_r.at[z], o_target(other)).start()

    @pl.when(diagonal)
    def _():
        r.o_slots[z] = r.o_two[row_tile(y, 16)]

    c_x.forward()

    a_two.finish(lambda h: r.total.at[from_to(h, 0, 64, PART_A)])
    b_two.finish(lambda h: r.total.at[from_to(h, PART_A, 160, UNIT)])
    for c in range(4):
        for b in range(2):
            at = 64 * b + 8 * c
            rows = jnp.concatenate([r.total[at : at + 8], r.total[at + 32 : at + 40]], axis=0)
            r.g_send[c, 16 * b : 16 * b + 16] = rows.astype(BF)
    r.g_slots[y] = r.g_send[y]

    def down_rows(c):
        return pl.ds(pl.multiple_of(DOWN + 24 * c, 8), 24)

    r.d_slots[y] = r.total[down_rows(y)]
    y_copies = []
    for n in (1, 3, 2):
        to = place.moved("y", n)
        y_copies.append(remote(r.g_send.at[to], r.g_slots.at[y], r.gy_s.at[n], r.gy_r.at[y], place.peer("y", n)))
        y_copies.append(remote(r.total.at[down_rows(to)], r.d_slots.at[y], r.dy_s.at[n], r.dy_r.at[y], place.peer("y", n)))
    for copy in y_copies:
        copy.start()
    c_x.finish(lambda h: r.c_sum.at[:, pl.ds(512 * h, 512)])
    dh_ring.finish(lambda h: r.dh_total.at[pl.ds(BLOCK * h, BLOCK)])
    back_to_input(r, gain)

    for n in (1, 3, 2):
        source = place.moved("y", n)
        remote(r.g_send.at[0], r.g_slots.at[source], r.gy_s.at[n], r.gy_r.at[source], place.peer("y", n)).wait_recv()
        remote(r.total.at[pl.ds(DOWN, 24)], r.d_slots.at[source], r.dy_s.at[n], r.dy_r.at[source], place.peer("y", n)).wait_recv()
    r.out_d_out[...] = r.d_slots[0] + r.d_slots[1] + r.d_slots[2] + r.d_slots[3]
    summed = r.g_slots[0].astype(F32)
    for c in range(1, 4):
        summed = summed + r.g_slots[c].astype(F32)
    summed = summed.reshape(2, 2, 8, D)
    last = r.c_sum[...].reshape(2, 8, D)
    for n in range(2):
        r.g_sum[n, 0:2] = summed[:, n]
        r.g_sum[n, 2] = last[n]
    r.out_g_out[k] = r.g_sum[k]
    g_core = remote(r.g_sum.at[1 - k], r.out_g_out.at[k], r.core.at[8], r.core.at[9], place.sibling())
    g_core.start()
    for other in range(4):

        @pl.when(not_here(diagonal, other, z))
        def _():
            remote(r.o_two.at[pl.ds(0, 16)], r.o_slots.at[other], r.oy_s.at[0], r.oy_r.at[other], place.device(z=jnp.int32(other), y=z)).wait_recv()

    o_sum = r.o_slots[0].astype(F32)
    for c in range(1, 4):
        o_sum = o_sum + r.o_slots[c].astype(F32)
    r.out_o_out[...] = o_sum

    for dz, dx in THEIRS:
        at = 4 * place.moved("z", dz) + place.moved("x", dx)
        remote(r.q_box.at[0, 0], r.q_slots.at[at], r.qd_s.at[0], r.qd_r.at[at], theirs_at(place, dz, dx)).wait_recv()

    @pl.loop(0, 2)
    def _(t):
        at = row_tile(t, 16)
        total = r.q_slots[0, at].astype(F32)
        for n in range(1, 16):
            total = total + r.q_slots[n, at].astype(F32)
        r.q_three[at] = total

    r.out_q_out[y] = r.q_three[row_tile(y, 8)]
    q_copies = [
        remote(r.q_three.at[row_tile(place.moved("y", n), 8)], r.out_q_out.at[y], r.qy_s.at[n], r.qy_r.at[y], place.peer("y", n))
        for n in (1, 3, 2)
    ]
    for copy in q_copies:
        copy.start()
    squares = jnp.zeros((8, D), F32)
    for part in [r.q_three[8 * c : 8 * c + 8] for c in range(4)] + [r.g_sum[c, b] for c in range(2) for b in range(3)]:
        squares = squares + part * part
    for c in range(2):
        part = r.out_o_out[8 * c : 8 * c + 8]
        squares = squares + part * part
    for c in range(3):
        part = r.out_d_out[8 * c : 8 * c + 8]
        squares = squares + part * part
    attn = jnp.sum(r.attn_gain[...], axis=0, keepdims=True)
    mlp = jnp.sum(r.mlp_gain[...], axis=0, keepdims=True)
    squares = jnp.sum(squares, axis=0, keepdims=True)
    r.value_row[...] = jnp.zeros_like(r.value_row)
    lanes = jnp.zeros((1, 128), F32)
    for c in range(8):
        at = slice(128 * c, 128 * c + 128)
        r.value_row[c : c + 1] = attn[:, at]
        r.value_row[8 + c : 9 + c] = mlp[:, at]
        lanes = lanes + squares[:, at]
    for c in range(2):
        r.value_row[16 + c : 17 + c] = jnp.sum(r.head_gain[c], axis=0, keepdims=True)
    r.value_row[18:19] = lanes
    sum_everywhere(r, place)

    remote(r.g_sum.at[0], r.out_g_out.at[1 - k], r.core.at[8], r.core.at[9], place.sibling()).wait_recv()
    for n in (1, 3, 2):
        source = place.moved("y", n)
        remote(r.q_three.at[pl.ds(0, 8)], r.out_q_out.at[source], r.qy_s.at[n], r.qy_r.at[source], place.peer("y", n)).wait_recv()
    for copy in [dh_copy, out_copy, o_core, g_core] + y_copies + q_copies + q_core + q_direct:
        copy.wait_send()
    for other in range(4):

        @pl.when(not_here(diagonal, other, y))
        def _():
            remote(r.o_two.at[pl.ds(16 * other, 16)], r.o_slots.at[z], r.oy_s.at[other], r.oy_r.at[z], o_target(other)).wait_send()


def backward_step(**given):
    given = {("in_" + n if n in SAVED else n): v for n, v in given.items()}
    outputs = {
        "layer_out": ((ROWS, D), BF, vmem),
        "input_grad": ((ROWS, D), F32, vmem),
        "q_out": ((4, 8, D), F32, vmem),
        "o_out": ((16, D), F32, vmem),
        "g_out": ((2, 3, 8, D), F32, vmem),
        "d_out": ((24, D), F32, vmem),
        "sums": ((24, 128), F32, vmem),
    }
    head_rows = (OWN_HEADS, SEQ, HEAD_WIDTH)
    kv_rows = (OWN_KV, SEQ, HEAD_WIDTH)
    scratch = {
        **{n: pltpu.VMEM(*what) for n, what in SAVED.items()},
        "out_box": pltpu.VMEM((ROWS, D), BF),
        "dh_box": pltpu.VMEM((ROWS, D), BF),
        "own": pltpu.VMEM((ROWS, D), BF),
        "d_attn_all": pltpu.VMEM((8, BLOCK, D), BF),
        "d_attended": pltpu.VMEM(head_rows, BF),
        "d_query": pltpu.VMEM(head_rows, F32),
        "d_key": pltpu.VMEM(kv_rows, F32),
        "d_value": pltpu.VMEM(kv_rows, F32),
        "d_proj": pltpu.VMEM((8, BLOCK, D), BF),
        "y_box": pltpu.VMEM((6, BLOCK, D), BF),
        "dh_total": pltpu.VMEM((ROWS, D), F32),
        "a_box": pltpu.VMEM((6, 2, PART_A, D), BF),
        "b_box": pltpu.VMEM((6, 2, PART_A, D), BF),
        "w": pltpu.VMEM((4, 4, UNIT, D), BF),
        "out_sib": pltpu.VMEM((ROWS, D), BF),
        "dh_sib": pltpu.VMEM((ROWS, D), BF),
        "a_box2": pltpu.VMEM((6, 64, D), BF),
        "b_box2": pltpu.VMEM((6, 64, D), BF),
        "total": pltpu.VMEM((UNIT, D), F32),
        "g_send": pltpu.VMEM((4, 32, D), BF),
        "g_slots": pltpu.VMEM((4, 32, D), BF),
        "d_slots": pltpu.VMEM((4, 24, D), F32),
        "g_sum": pltpu.VMEM((2, 3, 8, D), F32),
        "d_q": pltpu.VMEM((4, 4, 2, 32, D), BF),
        "d_o": pltpu.VMEM((4, 2, 64, D), BF),
        "q_box": pltpu.VMEM((4, 4, 32, D), BF),
        "q_slots": pltpu.VMEM((16, 32, D), BF),
        "c": pltpu.VMEM((4, 16, 16, D), BF),
        "cy_box": pltpu.VMEM((6, 8, 16, D), BF),
        "cz_box": pltpu.VMEM((6, 2, 16, D), BF),
        "cx_box": pltpu.VMEM((6, 16, 512), BF),
        "c_sum": pltpu.VMEM((16, D), F32),
        "q_three": pltpu.VMEM((32, D), F32),
        "o_box": pltpu.VMEM((4, 64, D), BF),
        "ox_box": pltpu.VMEM((6, 32, D), BF),
        "o_two": pltpu.VMEM((64, D), BF),
        "o_slots": pltpu.VMEM((4, 16, D), BF),
        "mlp_gain": pltpu.VMEM((8, D), F32),
        "attn_gain": pltpu.VMEM((8, D), F32),
        "head_gain": pltpu.VMEM((2, 8, HEAD_WIDTH), F32),
        "value_row": pltpu.VMEM((24, 128), F32),
        "first": pltpu.VMEM((8, 24, 128), F32),
        "second": pltpu.VMEM((16, 24, 128), F32),
        "held": pltpu.VMEM((24, 128), F32),
        "core": dma(10),
        "load": dma(len(SAVED)),
        "w_sem": dma(6),
        **{n: dma(4) for n in ("gy_s", "gy_r", "dy_s", "dy_r", "qy_s", "qy_r", "oy_s", "oy_r")},
        **{"s1_s": dma(7), "s1_r": dma(8), "s2_s": dma(15), "s2_r": dma(16)},
        **{"qd_s": dma(15), "qd_r": dma(16), "qk_s": dma(4), "qk_r": dma(4)},
        **rings("t", "y", "a1", "b1", "a2", "b2", "cx", "cy", "cz", "ox"),
    }
    spaces = {"span": smem, "w_all": hbm, "w_two": hbm, "hidden_pair": hbm, "cot_pair": hbm, **{"in_" + n: hbm for n in SAVED}}
    return named_call(backward_kernel, 2, "backward_attention", given, spaces, outputs, scratch)


def gain_spread():
    return jnp.asarray(np.arange(128)[:, None] == np.arange(GAINS)[None, :] % 18, BF)


def rope_tables():
    middle = HEAD_WIDTH // 2
    frequency = rope_base ** (-(np.arange(middle) * 2.0) / HEAD_WIDTH)
    angle = np.arange(SEQ)[:, None] * frequency[None, :]
    cosine, sine = np.cos(angle), np.sin(angle)
    return (
        jnp.asarray(np.concatenate([cosine, cosine], axis=1), F32),
        jnp.asarray(np.concatenate([-sine, sine], axis=1), F32),
    )


MATRICES = {"qkv": matrix_rate, "out": out_rate, "gateup": matrix_rate, "down": matrix_rate}


def adam_update(weight, first, second, grad, factor, rate, decay):
    clipped = grad * factor
    new_first = beta_one * first + (1.0 - beta_one) * clipped
    new_second = beta_two * second + (1.0 - beta_two) * clipped * clipped
    direction = (
        new_first
        / (1.0 - beta_one**STEP)
        / (jnp.sqrt(new_second / (1.0 - beta_two**STEP)) + adam_eps)
    )
    return (weight - rate * (direction + decay * weight), new_first, new_second)


def update_kernel(r):
    hand_on = [
        pltpu.make_async_copy(r.layer_out, r.out_layer_out, r.sems.at[0]),
        pltpu.make_async_copy(r.input_grad, r.out_input_grad, r.sems.at[1]),
    ]
    for copy in hand_on:
        copy.start()
    sums = r.sums[...]
    row = lax.broadcasted_iota(jnp.int32, (24, 128), 0)
    squares = jnp.where(row < 18, sums * sums, jnp.where(row == 18, sums, 0.0))
    norm = jnp.sqrt(jnp.sum(jnp.sum(squares, axis=0, keepdims=True), axis=1, keepdims=True))
    r.out_norm[...] = norm
    factor = jnp.minimum(1.0, clip_at / (norm + 1e-06))

    place = row * 128 + lax.broadcasted_iota(jnp.int32, (24, 128), 1)
    start = (lax.axis_index("dp") * 4 + lax.axis_index("ctx")) * 18
    lane = lax.broadcasted_iota(jnp.int32, (1, 128), 1)
    mine = jnp.zeros((1, 128), F32)
    for n in range(18):
        entry = jnp.sum(jnp.where(place == start + n, sums, 0.0), axis=0, keepdims=True)
        mine = jnp.where(lane == n, jnp.sum(entry, axis=1, keepdims=True), mine)
    grads = {
        "qkv": jnp.concatenate(
            [r.q_out[c, :, 0:512] for c in range(4)]
            + [r.q_out[c, :, 512:768] for c in range(4)]
            + [r.q_out[c, :, 768:1024] for c in range(4)],
            axis=1,
        ),
        "out": r.o_out[...],
        "gateup": unpack_gateup(r.g_out),
        "down": r.d_out[...],
        "gains": mine[:, 0:18],
    }
    for name, grad in grads.items():
        rate, decay = (MATRICES[name], matrix_decay) if name in MATRICES else (gain_rate, 0.0)
        refs = [getattr(r, kind + name) for kind in ("w_", "first_", "second_")]
        news = adam_update(*[ref[...] for ref in refs], grad, factor, rate, decay)
        for kind, new in zip(("w_", "first_", "second_"), news):
            getattr(r, "out_" + kind + name)[...] = new
    for copy in hand_on:
        copy.wait()


def update_step(**given):
    outputs = {
        "layer_out": ((ROWS, D), BF, hbm),
        "input_grad": ((ROWS, D), F32, hbm),
        "norm": ((1, 1), F32, vmem),
        **{n: (v.shape, F32, vmem) for n, v in given.items() if n.split("_")[0] in ("w", "first", "second")},
    }
    return named_call(update_kernel, None, "update", given, {}, outputs, {"sems": dma(2)})


def body(
    tokens, cotangent, span_order,
    w_qkv, w_out, w_gateup, w_down, gains,
    first_qkv, first_out, first_gateup, first_down, first_gains,
    second_qkv, second_out, second_gateup, second_down, second_gains,
):
    cosine, sine = rope_tables()
    fwd = forward_step(
        span=span_order, tok=tokens, cot=cotangent, wq=w_qkv, wo=w_out, wgu=w_gateup, wd=w_down,
        gains=gains[None, :], spread=gain_spread(), cosine=cosine, sine=sine,
    )
    bwd = backward_step(
        span=span_order, tok=tokens, cot=cotangent, middle=fwd["middle"],
        gain_row=fwd["gain_row"], cosine=cosine, sine=sine,
        hidden_pair=fwd["hidden_pair"], cot_pair=fwd["cot_pair"], w_all=fwd["w_all"],
        w_two=fwd["w_two"].reshape(4, 16, 16, D),
        **{name: fwd[name] for name in SAVED},
    )
    names = ("qkv", "out", "gateup", "down", "gains")
    state = {
        "w_": (w_qkv, w_out, w_gateup, w_down, gains[None, :]),
        "first_": (first_qkv, first_out, first_gateup, first_down, first_gains[None, :]),
        "second_": (second_qkv, second_out, second_gateup, second_down, second_gains[None, :]),
    }
    new = update_step(
        **bwd, **{kind + name: value for kind, values in state.items() for name, value in zip(names, values)}
    )
    results = [
        new[kind + name] if name != "gains" else new[kind + name][0] for kind in state for name in names
    ]
    return (new["layer_out"], new["input_grad"], *results, new["norm"][0, 0])


def solution(mesh):
    rows, flat = P(("dp", "ctx"), None), P(("dp", "ctx"))
    state = (rows, rows, rows, rows, flat)
    in_specs = (rows, rows, P()) + state * 3
    out_specs = (rows, rows) + state * 3 + (P(),)
    return jax.shard_map(body, mesh=mesh, in_specs=in_specs, out_specs=out_specs, check_vma=False)
```

```python
import jax
import jax.numpy as jnp
import numpy as np
from jax import lax
from jax.experimental import pallas as pl
from jax.experimental.pallas import tpu as pltpu
from jax.sharding import PartitionSpec as P

D = 1024
HEADS = 16
KV_HEADS = 8
HEAD_WIDTH = 128
FF = 3072
STEP = 10

norm_eps = 1e-06
rope_base = 1000000.0
beta_one = 0.9
beta_two = 0.999
adam_eps = 1e-08
clip_at = 1.0
matrix_rate = 0.05
out_rate = 0.25
matrix_decay = 0.1
gain_rate = 0.5
masked_score = -1e30

MESH = pl.DeviceIdType.MESH
BF = jnp.bfloat16
F32 = jnp.float32
ROWS = 256
UNIT = 224
PART_A = 112
DOWN = 128
VMEM_LIMIT = 62 * 2**20
vmem = pl.BlockSpec(memory_space=pltpu.VMEM)
hbm = pl.BlockSpec(memory_space=pl.ANY)


class Place:
    def __init__(self):
        dp = lax.axis_index("dp")
        self.at = {
            "z": lax.div(dp, 8),
            "x": lax.rem(lax.div(dp, 2), 4),
            "k": lax.rem(dp, 2),
            "y": lax.axis_index("ctx"),
        }

    def __getitem__(self, axis):
        return self.at[axis]

    def device(self, **other):
        c = {**self.at, **other}
        return (c["z"] * 8 + c["x"] * 2 + c["k"], c["y"])

    def moved(self, axis, steps):
        return lax.rem(self.at[axis] + steps, 4)

    def peer(self, axis, steps):
        return self.device(**{axis: self.moved(axis, steps)})

    def sibling(self):
        return self.device(k=1 - self.at["k"])


def greet(devices):
    barrier = pltpu.get_barrier_semaphore()
    for device in devices:
        pl.semaphore_signal(barrier, inc=1, device_id=device, device_id_type=MESH)


def await_greetings(count):
    pl.semaphore_wait(pltpu.get_barrier_semaphore(), count)


def neighbours(place, axes):
    found = []
    for axis in axes:
        if axis == "k":
            found.append(place.sibling())
        else:
            found += [place.peer(axis, 1), place.peer(axis, 3)]
    return found


def remote(src, dst, send, recv, device):
    return pltpu.make_async_remote_copy(
        src_ref=src, dst_ref=dst, send_sem=send, recv_sem=recv, device_id=device, device_id_type=MESH
    )


class Gather:
    def __init__(self, place, axis, part, sems, own=None):
        self.part, self.send, self.recv = part, sems[0], sems[1]
        self.own = own or (lambda half: part(place[axis], half))
        self.next, self.prev = place.peer(axis, 1), place.peer(axis, 3)
        self.me, self.up, self.down, self.far = (place.moved(axis, n) for n in (0, 1, 3, 2))

    def copy(self, n, slot, half, device, src=None):
        view = self.part(slot, half)
        return remote(src if src is not None else view, view, self.send.at[n], self.recv.at[n], device)

    def outgoing(self, n):
        slot, half, device = [
            (self.me, 0, self.next),
            (self.me, 1, self.prev),
            (self.me, 1, self.next),
            (self.me, 0, self.prev),
            (self.down, 0, self.next),
            (self.up, 1, self.prev),
        ][n]
        return self.copy(n, slot, half, device, self.own(half) if n < 4 else None)

    def start(self, halves=(0, 1)):
        for half in halves:
            for n in ((0, 3), (1, 2))[half]:
                self.outgoing(n).start()

    def forward(self):
        self.copy(0, self.down, 0, self.prev).wait_recv()
        self.outgoing(4).start()
        self.copy(1, self.up, 1, self.next).wait_recv()
        self.outgoing(5).start()

    def finish(self):
        self.copy(2, self.down, 1, self.prev).wait_recv()
        self.copy(3, self.up, 0, self.next).wait_recv()
        self.copy(4, self.far, 0, self.prev).wait_recv()
        self.copy(5, self.far, 1, self.next).wait_recv()
        for n in range(6):
            self.outgoing(n).wait_send()


class Scatter:
    def __init__(self, place, axis, part, boxes, sems, mine=None):
        self.part, self.boxes = part, boxes
        self.send, self.recv = sems[0], sems[1]
        self.next, self.prev = place.peer(axis, 1), place.peer(axis, 3)
        self.me, self.up, self.down, self.far = (place.moved(axis, n) for n in (0, 1, 3, 2))
        self.mine = mine or self.own_part

    def own_part(self, n):
        slot, half = [(self.down, 0), (self.up, 1), (self.me, 0), (self.me, 1)][n]
        return self.part(slot, half)

    def copy(self, n, src, device):
        return remote(src, self.boxes[n], self.send.at[n], self.recv.at[n], device)

    def outgoing(self, n):
        source, device = [
            (lambda: self.part(self.far, 0), self.prev),
            (lambda: self.part(self.far, 1), self.next),
            (lambda: self.part(self.down, 1), self.prev),
            (lambda: self.part(self.up, 0), self.next),
            (lambda: self.boxes[0], self.prev),
            (lambda: self.boxes[1], self.next),
        ][n]
        return self.copy(n, source(), device)

    def start(self):
        for n in range(4):
            self.outgoing(n).start()

    def forward(self):
        for n in range(2):
            self.outgoing(n).wait_recv()
            add_rows(self.boxes[n], [self.boxes[n], self.mine(n)])
            self.outgoing(4 + n).start()

    def finish(self, result):
        for n in (2, 3, 4, 5):
            self.outgoing(n).wait_recv()
        add_rows(result(0), [self.mine(2), self.boxes[3], self.boxes[4]])
        add_rows(result(1), [self.mine(3), self.boxes[2], self.boxes[5]])
        for n in range(6):
            self.outgoing(n).wait_send()


def add_rows(out, terms):
    shape = out.shape
    rows = shape[-2]

    def block(at):
        total = terms[0][at].astype(F32)
        for term in terms[1:]:
            total = total + term[at].astype(F32)
        out[at] = total.astype(out.dtype)

    if len(shape) == 2:

        @pl.loop(0, rows // 16)
        def _(r):
            block((pl.ds(pl.multiple_of(r * 16, 16), 16), slice(None)))

    else:

        @pl.loop(0, shape[0])
        def _(lead):
            @pl.loop(0, rows // 16)
            def _(r):
                block((lead, pl.ds(pl.multiple_of(r * 16, 16), 16), slice(None)))


def dma(*shape):
    return pltpu.SemaphoreType.DMA(shape)


def ring_sems():
    return [dma(6), dma(6)]


def params(which):
    if which is None:
        return pltpu.CompilerParams(vmem_limit_bytes=VMEM_LIMIT)
    return pltpu.CompilerParams(
        collective_id=which, has_side_effects=True, vmem_limit_bytes=VMEM_LIMIT
    )


TILE = 256
SEQ = 4 * ROWS
BLOCK = ROWS // 2
OWN_HEADS = HEADS // 4
OWN_KV = KV_HEADS // 4
LOG2E = 1.4426950408889634


def turn(value_rows):
    return pltpu.roll(value_rows, HEAD_WIDTH // 2, 1)


def head_norm(raw):
    scale = lax.rsqrt(jnp.mean(raw * raw, axis=-1, keepdims=True) + norm_eps)
    return raw * scale, scale


def stored_block(span, position):
    found = jnp.int32(0)
    for block in range(1, 8):
        found = jnp.where(span[block] == position, block, found)
    return found


def pair_of(ref, span, tile):
    return jnp.concatenate([ref[stored_block(span, 2 * tile + n)] for n in range(2)], axis=0)


def dot_nt(left, right):
    return lax.dot_general(left, right, (((1,), (1,)), ((), ())), preferred_element_type=F32)


def dot_nn(left, right):
    return jnp.dot(left, right, preferred_element_type=F32)


def causal(scores):
    keys = lax.broadcasted_iota(jnp.int32, scores.shape, 0)
    queries = lax.broadcasted_iota(jnp.int32, scores.shape, 1)
    return jnp.where(keys <= queries, scores, masked_score)


def project(r, g_attn, g_query, g_key):
    span, tok, cosine, sine = r.span, r.tok_all, r.cosine, r.sine
    hidden, raw, query, key, key_t = r.hidden, r.raw, r.query, r.key, r.key_t
    value, value_t = r.value, r.value_t

    def columns(pair):
        return r.wq_all[:, :, :, :, 256 * pair : 256 * pair + 256].reshape(D, 256)

    @pl.loop(0, SEQ // TILE)
    def _(t):
        at = pl.ds(pl.multiple_of(t * TILE, TILE), TILE)
        rows = pair_of(tok, span, t).astype(F32)
        scale = lax.rsqrt(jnp.mean(rows * rows, axis=-1, keepdims=True) + norm_eps)
        hid = (rows * scale * g_attn[...]).astype(BF)
        hidden[at] = hid
        cos_t, sin_t = cosine[at], sine[at]
        for pair in range(OWN_HEADS // 2):
            both = dot_nn(hid, columns(pair))
            for n in range(2):
                h, part = 2 * pair + n, both[:, 128 * n : 128 * n + 128]
                raw[h, at] = part.astype(BF)
                normed = head_norm(part)[0] * g_query[...]
                query[h, at] = (normed * cos_t + turn(normed) * sin_t).astype(BF)
        both = dot_nn(hid, columns(2))
        for h in range(OWN_KV):
            part = both[:, 128 * h : 128 * h + 128]
            raw[OWN_HEADS + h, at] = part.astype(BF)
            normed = head_norm(part)[0] * g_key[...]
            rotated = normed * cos_t + turn(normed) * sin_t
            key[h, at] = rotated.astype(BF)
            key_t[h, :, at] = rotated.T.astype(BF)
        both = dot_nn(hid, columns(3))
        for h in range(OWN_KV):
            part = both[:, 128 * h : 128 * h + 128]
            value[h, at] = part.astype(BF)
            value_t[h, :, at] = part.T.astype(BF)


def attend(r, first_head, last_head):
    query, key, value_t, attended = r.query, r.key, r.value_t, r.attended
    attended_t, log_total = r.attended_t, r.log_total
    factor = HEAD_WIDTH ** (-0.5) * LOG2E

    @pl.loop(first_head, last_head)
    def _(h):
        kv = lax.div(h, 2)
        for t in range(SEQ // TILE):
            low, high = t * TILE, (t + 1) * TILE
            q = query[h, low:high]
            scores = [causal(dot_nt(key[kv, low:high], q))]
            if t:
                scores.append(dot_nt(key[kv, 0:low], q))
            top = jnp.max(scores[0], axis=0, keepdims=True)
            if t:
                top = jnp.maximum(top, jnp.max(scores[1], axis=0, keepdims=True))
            top = top * factor
            probs = [jnp.exp2(s * factor - top) for s in scores]
            total = jnp.sum(probs[0], axis=0, keepdims=True)
            mixed = dot_nn(value_t[kv, :, low:high], probs[0].astype(BF))
            if t:
                total = total + jnp.sum(probs[1], axis=0, keepdims=True)
                mixed = mixed + dot_nn(value_t[kv, :, 0:low], probs[1].astype(BF))
            mixed = mixed * (1.0 / total)
            attended_t[h, :, low:high] = mixed.astype(BF)
            attended[h, 2 * t : 2 * t + 2] = mixed.T.astype(BF).reshape(2, BLOCK, HEAD_WIDTH)
            log_total[h, :, low:high] = jnp.broadcast_to(top + jnp.log2(total), (8, TILE))


def attend_back(r, first_head, last_head):
    query, key, key_t, value = r.query, r.key, r.key_t, r.value
    d_attended, log_total, d_query = r.d_attended, r.log_total, r.d_query
    d_key, d_value = r.d_key, r.d_value
    factor = HEAD_WIDTH ** (-0.5) * LOG2E
    plain = HEAD_WIDTH ** (-0.5)

    @pl.loop(first_head, last_head)
    def _(h):
        kv = lax.div(h, 2)
        for t in range(SEQ // TILE):
            low, high = t * TILE, (t + 1) * TILE
            q = query[h, low:high]
            da = d_attended[h, low:high]
            total = log_total[h, 0:1, low:high]
            spans = [(low, high)] + ([(0, low)] if t else [])
            probs, mixes = [], []
            for n, (first, last) in enumerate(spans):
                scores = dot_nt(key[kv, first:last], q)
                if n == 0:
                    scores = causal(scores)
                p = jnp.exp2(scores * factor - total)
                d_value[kv, first:last] += dot_nn(p.astype(BF), da)
                probs.append(p)
                mixes.append(p * dot_nt(value[kv, first:last], da))
            delta = jnp.sum(mixes[0], axis=0, keepdims=True)
            if t:
                delta = delta + jnp.sum(mixes[1], axis=0, keepdims=True)
            back = None
            for (first, last), p, mix in zip(spans, probs, mixes):
                ds = (mix - p * delta).astype(BF)
                d_key[kv, first:last] += dot_nn(ds, q)
                part = dot_nn(key_t[kv, :, first:last], ds)
                back = part if back is None else back + part
            d_query[h, low:high] = (back * plain).T


GAINS = 2 * D + 2 * HEAD_WIDTH
smem = pl.BlockSpec(memory_space=pltpu.SMEM)
regular = pltpu.SemaphoreType.DMA


class Names:
    def __init__(self, names, refs):
        self.__dict__.update(zip(names, refs))


def named_call(kernel, which, name, given, spaces, outputs, scratch):
    names = list(given) + ["out_" + n for n in outputs] + list(scratch)
    results = pl.pallas_call(
        lambda *refs: kernel(Names(names, refs)),
        out_shape=tuple(jax.ShapeDtypeStruct(shape, kind) for shape, kind, _ in outputs.values()),
        in_specs=[spaces.get(n, vmem) for n in given],
        out_specs=tuple(space for _, _, space in outputs.values()),
        scratch_shapes=list(scratch.values()),
        compiler_params=params(which),
        name=name,
    )(*given.values())
    return dict(zip(outputs, results))


TABLES = {"cosine": ((SEQ, HEAD_WIDTH), F32), "sine": ((SEQ, HEAD_WIDTH), F32)}
SAVED = {
    "wq_all": ((4, 4, 2, 32, 1152), BF),
    "wo_all": ((4, 2, 64, D), BF),
    "hidden": ((SEQ, D), BF),
    "raw": ((OWN_HEADS + OWN_KV, SEQ, HEAD_WIDTH), BF),
    "query": ((OWN_HEADS, SEQ, HEAD_WIDTH), BF),
    "key": ((OWN_KV, SEQ, HEAD_WIDTH), BF),
    "key_t": ((OWN_KV, HEAD_WIDTH, SEQ), BF),
    "value": ((OWN_KV, SEQ, HEAD_WIDTH), BF),
    "attended_t": ((OWN_HEADS, HEAD_WIDTH, SEQ), BF),
    "log_total": ((OWN_HEADS, 8, SEQ), F32),
}


def heads_of(ref, count, at):
    return jnp.concatenate([ref[h, at] for h in range(count)], axis=1)


def row_tile(r, size):
    return pl.ds(pl.multiple_of(r * size, size), size)


def from_to(half, low, split, high):
    return pl.ds(low, split - low) if half == 0 else pl.ds(split, high - split)


def not_here(condition, other, coordinate):
    return jnp.logical_not(jnp.logical_and(condition, coordinate == other))


def pack_gateup(w, out):
    for k in range(2):
        for side in range(2):
            pieces = [w[:, FF * side + 96 * n : FF * side + 96 * n + 96] for n in range(k, 32, 2)]
            columns = jnp.concatenate(pieces, axis=1)
            for b in range(3):
                out[k, b, :, 512 * side : 512 * side + 512] = columns[:, 512 * b : 512 * b + 512]


def unpack_gateup(packed):
    sides = []
    for side in range(2):
        cores = [
            jnp.concatenate([packed[k, b, :, 512 * side : 512 * side + 512] for b in range(3)], axis=1)
            for k in range(2)
        ]
        sides += [cores[n % 2][:, 96 * (n // 2) : 96 * (n // 2) + 96] for n in range(32)]
    return jnp.concatenate(sides, axis=1)


def forward_kernel(r):
    place = Place()
    z, x, k, y = (place[a] for a in "zxky")
    near = neighbours(place, "xyzk")
    diagonal = z == y
    plane = [theirs_at(place, *o) for o in THEIRS]
    greet(near + [place.peer("y", 2)] + plane)
    for other in range(4):

        @pl.when(not_here(diagonal, other, y))
        def _():
            greet([place.device(z=y, y=jnp.int32(other))])

    for i in range(4):
        r.q_send[i, :, 0:512] = r.wq[:, 512 * i : 512 * i + 512]
        r.q_send[i, :, 512:768] = r.wq[:, 2048 + 256 * i : 2304 + 256 * i]
        r.q_send[i, :, 768:1024] = r.wq[:, 3072 + 256 * i : 3328 + 256 * i]
        r.q_send[i, :, 1024:1152] = jnp.zeros((8, 128), F32)
        r.q_send[i, 0:1, 1024:1042] = r.gains[...]
    pack_gateup(r.wgu, r.packed)
    tables = [
        pltpu.make_async_copy(getattr(r, "in_" + n), getattr(r, n), r.tables.at[i])
        for i, n in enumerate(("cosine", "sine", "spread"))
    ]
    for copy in tables:
        copy.start()
    r.q_recv[y] = r.q_send[y]
    r.o_send[...] = r.wo[...].astype(BF)
    r.tok_all[pl.ds(2 * y, 2)] = r.tok[...].reshape(2, BLOCK, D)
    await_greetings(len(near) + 1 + len(plane) + jnp.where(diagonal, 3, 4))

    g_prep = remote(r.packed.at[1 - k], r.g_recv, r.pair.at[0], r.pair.at[1], place.sibling())
    g_prep.start()
    q_prep = [
        remote(r.q_send.at[place.moved("y", n)], r.q_recv.at[y], r.qp_s.at[n], r.qp_r.at[y], place.peer("y", n))
        for n in (1, 3, 2)
    ]
    for copy in q_prep:
        copy.start()

    def o_slot(source):
        return r.wo_all.at[x, k, row_tile(source, 16)]

    for other in range(4):

        @pl.when(not_here(diagonal, other, z))
        def _():
            remote(r.o_send, o_slot(y), r.op_s.at[other], r.op_r.at[y], place.device(z=jnp.int32(other), y=z)).start()

    @pl.when(diagonal)
    def _():
        r.wo_all[x, k, row_tile(y, 16)] = r.o_send[...]

    cot_copy = remote(r.cot, r.out_cot_pair.at[pl.ds(ROWS, ROWS)], r.pair.at[2], r.pair.at[3], place.sibling())
    cot_copy.start()
    cot_own = pltpu.make_async_copy(r.cot, r.out_cot_pair.at[pl.ds(0, ROWS)], r.pair.at[6])
    cot_own.start()

    g_prep.wait_recv()
    g_own, g_other, lower = r.packed[k], r.g_recv[...], k == 0
    both = jnp.concatenate([jnp.where(lower, g_own, g_other), jnp.where(lower, g_other, g_own)], axis=1)
    r.g_y[y] = both[0:2].reshape(32, D).astype(BF)
    r.w_c[y, 4 * z + x] = both[2].astype(BF)
    c_x = Gather(place, "x", lambda i, h: r.w_c.at[y, 4 * z + i, :, pl.ds(512 * h, 512)], (r.cx_s, r.cx_r))
    c_z = Gather(place, "z", lambda i, h: r.w_c.at[y, pl.ds(4 * i + 2 * h, 2)], (r.cz_s, r.cz_r))
    c_y = Gather(place, "y", lambda i, h: r.w_c.at[i, pl.ds(8 * h, 8)], (r.cy_s, r.cy_r))
    r.d_y[y] = r.wd[...]
    g_ring = Gather(place, "y", lambda i, h: r.g_y.at[i, pl.ds(16 * h, 16)], (r.gy_s, r.gy_r))
    d_ring = Gather(place, "y", lambda i, h: r.d_y.at[i, from_to(h, 0, 16, 24)], (r.dy_s, r.dy_r))
    g_ring.start()
    d_ring.start()
    c_x.start()

    for n in (1, 3, 2):
        source = place.moved("y", n)
        remote(r.q_send.at[0], r.q_recv.at[source], r.qp_s.at[n], r.qp_r.at[source], place.peer("y", n)).wait_recv()
    r.wq_all[z, x, k] = r.q_recv[...].reshape(32, 1152).astype(BF)
    q_direct = []
    for n, (dz, dx) in enumerate(THEIRS):
        unit = r.wq_all.at[z, x, k]
        q_direct.append(remote(unit, unit, r.qd_s.at[n], r.qd_r.at[4 * z + x], theirs_at(place, dz, dx)))
    for copy in q_direct:
        copy.start()

    def q_core(at_z, at_x, core):
        unit, which = r.wq_all.at[at_z, at_x, core], 4 * at_z + at_x
        return remote(unit, unit, r.qc_s.at[which], r.qc_r.at[which], place.sibling())

    q_core(z, x, k).start()
    tokens = Gather(place, "y", lambda i, h: r.tok_all.at[2 * i + h], (r.t_s, r.t_r))
    tokens.start()

    for other in range(4):

        @pl.when(not_here(diagonal, other, y))
        def _():
            remote(r.o_send, o_slot(other), r.op_s.at[0], r.op_r.at[other], place.device(z=y, y=jnp.int32(other))).wait_recv()

    o_x = Gather(place, "x", lambda i, h: r.wo_all.at[i, k, pl.ds(32 * h, 32)], (r.ox_s, r.ox_r))
    o_x.start()
    g_ring.forward()
    d_ring.forward()
    c_x.forward()
    c_x.finish()
    c_z.start()
    o_x.forward()
    g_ring.finish()
    d_ring.finish()

    for b in range(2):
        pieces = [r.g_y[c, 16 * b : 16 * b + 16].astype(F32) for c in range(4)]
        for core_row in range(2):
            rows = jnp.concatenate([piece[8 * core_row : 8 * core_row + 8] for piece in pieces], axis=0)
            at = 64 * b + 32 * core_row
            r.unit[at : at + 32] = rows.astype(BF)
    r.unit[DOWN:UNIT] = r.d_y[...].reshape(96, D).astype(BF)
    w_all = r.out_w_all
    u_own = pltpu.make_async_copy(r.unit, w_all.at[z, x], r.pair.at[4])
    u_own.start()
    a_one = Gather(
        place, "x", lambda i, h: w_all.at[z, i, from_to(h, 0, 64, PART_A)], (r.a1_s, r.a1_r),
        own=lambda h: r.unit.at[from_to(h, 0, 64, PART_A)],
    )
    b_one = Gather(
        place, "z", lambda i, h: w_all.at[i, x, from_to(h, PART_A, 160, UNIT)], (r.b1_s, r.b1_r),
        own=lambda h: r.unit.at[from_to(h, PART_A, 160, UNIT)],
    )
    a_one.start()
    b_one.start()
    tokens.forward()
    c_z.forward()
    o_x.finish()
    o_core = remote(r.wo_all.at[:, k], r.wo_all.at[:, k], r.core.at[0], r.core.at[1], place.sibling())
    o_core.start()
    a_one.forward()
    b_one.forward()
    for dz, dx in sorted(THEIRS, key=lambda o: min(o[0], 4 - o[0]) + min(o[1], 4 - o[1])):
        at_z, at_x = place.moved("z", dz), place.moved("x", dx)
        other = r.wq_all.at[at_z, at_x, k]
        remote(other, other, r.qd_s.at[0], r.qd_r.at[4 * at_z + at_x], theirs_at(place, dz, dx)).wait_recv()
        q_core(at_z, at_x, k).start()
    a_one.finish()
    b_one.finish()
    u_own.wait()
    a_two = Gather(place, "z", lambda i, h: w_all.at[i, pl.ds(2 * h, 2), pl.ds(0, PART_A)], (r.a2_s, r.a2_r))
    b_two = Gather(place, "x", lambda i, h: w_all.at[pl.ds(2 * h, 2), i, pl.ds(PART_A, UNIT - PART_A)], (r.b2_s, r.b2_r))
    a_two.start()
    b_two.start()
    c_z.finish()
    c_y.start()
    remote(r.wo_all.at[:, 1 - k], r.wo_all.at[:, 1 - k], r.core.at[0], r.core.at[1], place.sibling()).wait_recv()
    for at_z in range(4):
        for at_x in range(4):
            q_core(at_z, at_x, 1 - k).wait_recv()
    tokens.finish()

    for copy in tables:
        copy.wait()

    lanes = r.wq_all[:, :, :, :, D:1152].reshape(128, 8, 128).astype(F32)
    spread = dot_nn(jnp.sum(lanes, axis=1).astype(BF), r.spread[...])
    owner = lax.broadcasted_iota(jnp.int32, (128, GAINS), 0) * 18
    spot = lax.broadcasted_iota(jnp.int32, (128, GAINS), 1)
    mine = jnp.logical_and(spot >= owner, spot < owner + 18)
    r.out_gain_row[...] = jnp.sum(jnp.where(mine, spread, 0.0), axis=0, keepdims=True)
    gain = r.out_gain_row
    project(r, gain.at[:, 0:D], gain.at[:, 2 * D : 2 * D + 128], gain.at[:, 2 * D + 128 : GAINS])
    attend(r, 0, 2)
    c_y.forward()
    attend(r, 2, 4)

    wo = r.wo_all[...].reshape(OWN_HEADS * HEAD_WIDTH, D)

    @pl.loop(0, 4)
    def _(i):
        rows = jnp.concatenate(
            [heads_of(r.attended, OWN_HEADS, r.span[2 * i + n]) for n in range(2)], axis=0
        )
        r.terms[i] = dot_nn(rows, wo).astype(BF)

    reduce = Scatter(
        place, "y", lambda i, h: r.terms.at[i, pl.ds(128 * h, 128)],
        [r.boxes.at[n] for n in range(6)], (r.y_s, r.y_r),
    )
    reduce.start()
    a_two.forward()
    b_two.forward()
    saves = [
        pltpu.make_async_copy(getattr(r, n), getattr(r, "out_" + n), r.save.at[i]) for i, n in enumerate(SAVED)
    ]
    for copy in saves:
        copy.start()
    c_y.finish()

    @pl.loop(0, 16)
    def _(j):
        pieces = [r.w_c[c, j].astype(F32) for c in range(4)]
        rows = [piece[8 * core_row : 8 * core_row + 8] for core_row in range(2) for piece in pieces]
        r.w_two[j] = jnp.concatenate(rows, axis=0).astype(BF)

    two_copy = pltpu.make_async_copy(r.w_two, r.out_w_two, r.pair.at[5])
    two_copy.start()
    reduce.forward()
    reduce.finish(lambda h: r.total.at[pl.ds(128 * h, 128)])

    hid_copies = []
    for half in range(2):

        @pl.loop(0, BLOCK // 32)
        def _(t):
            at = row_tile(4 * half + t, 32)
            rows = r.tok[at].astype(F32) + r.total[at]
            r.total[at] = rows
            scale = lax.rsqrt(jnp.mean(rows * rows, axis=-1, keepdims=True) + norm_eps)
            r.hid[at] = (rows * scale * gain[:, D : 2 * D]).astype(BF)

        here, there = pl.ds(BLOCK * half, BLOCK), pl.ds(ROWS + BLOCK * half, BLOCK)
        hid_copies += [
            remote(r.hid.at[here], r.out_hidden_pair.at[there], r.hid_sem.at[4 * half], r.hid_sem.at[4 * half + 1], place.sibling()),
            pltpu.make_async_copy(r.hid.at[here], r.out_hidden_pair.at[here], r.hid_sem.at[4 * half + 2]),
            pltpu.make_async_copy(r.total.at[here], r.out_middle.at[here], r.hid_sem.at[4 * half + 3]),
        ]
        for copy in hid_copies[3 * half :]:
            copy.start()

    a_two.finish()
    b_two.finish()
    two_copy.wait()
    for copy in saves:
        copy.wait()
    for copy in q_prep + q_direct + [g_prep, o_core]:
        copy.wait_send()
    for at_z in range(4):
        for at_x in range(4):
            q_core(at_z, at_x, k).wait_send()
    cot_copy.wait()
    cot_own.wait()
    for copy in hid_copies:
        copy.wait()
    for other in range(4):

        @pl.when(not_here(diagonal, other, z))
        def _():
            remote(r.o_send, o_slot(y), r.op_s.at[other], r.op_r.at[y], place.device(z=jnp.int32(other), y=z)).wait_send()


def rings(*names):
    return {f"{name}_{end}": dma(6) for name in names for end in "sr"}


def forward_step(**given):
    late = {**TABLES, "spread": ((128, GAINS), BF)}
    given = {("in_" + n if n in late else n): v for n, v in given.items()}
    outputs = {
        "middle": ((ROWS, D), F32, hbm),
        "hidden_pair": ((2 * ROWS, D), BF, hbm),
        "cot_pair": ((2 * ROWS, D), BF, hbm),
        "gain_row": ((1, GAINS), F32, vmem),
        "w_all": ((4, 4, UNIT, D), BF, hbm),
        "w_two": ((16, 64, D), BF, hbm),
        **{n: (*what, hbm) for n, what in SAVED.items()},
    }
    scratch = {
        "q_send": pltpu.VMEM((4, 8, 1152), F32),
        "q_recv": pltpu.VMEM((4, 8, 1152), F32),
        "o_send": pltpu.VMEM((16, D), BF),
        "packed": pltpu.VMEM((2, 3, 8, D), F32),
        "g_recv": pltpu.VMEM((3, 8, D), F32),
        "g_y": pltpu.VMEM((4, 32, D), BF),
        "w_c": pltpu.VMEM((4, 16, 16, D), BF),
        "w_two": pltpu.VMEM((16, 64, D), BF),
        "d_y": pltpu.VMEM((4, 24, D), F32),
        "unit": pltpu.VMEM((UNIT, D), BF),
        "tok_all": pltpu.VMEM((8, BLOCK, D), BF),
        "value_t": pltpu.VMEM((OWN_KV, HEAD_WIDTH, SEQ), BF),
        "attended": pltpu.VMEM((OWN_HEADS, 8, BLOCK, HEAD_WIDTH), BF),
        "terms": pltpu.VMEM((4, ROWS, D), BF),
        "boxes": pltpu.VMEM((6, BLOCK, D), BF),
        "total": pltpu.VMEM((ROWS, D), F32),
        **{n: pltpu.VMEM(*what) for n, what in SAVED.items()},
        "hid": pltpu.VMEM((ROWS, D), BF),
        **{n: pltpu.VMEM(*what) for n, what in late.items()},
        "tables": dma(3),
        "pair": dma(7),
        "core": dma(2),
        "hid_sem": dma(8),
        **{"qc_s": dma(16), "qc_r": dma(16)},
        "save": dma(len(SAVED)),
        **{n: dma(4) for n in ("qp_s", "qp_r", "op_s", "op_r")},
        **{"qd_s": dma(15), "qd_r": dma(16)},
        **rings("gy", "dy", "cx", "cz", "cy", "ox", "t", "a1", "b1", "a2", "b2", "y"),
    }
    spaces = {"span": smem, **{"in_" + n: hbm for n in late}}
    return named_call(forward_kernel, 1, "forward_attention", given, spaces, outputs, scratch)


def sum_everywhere(r, place):
    z, x, k, y = (place[a] for a in "zxky")

    def stage(source, slots, send, recv, offsets, device, me, slot_of):
        slots[me] = source[...]
        copies = [
            remote(source, slots.at[me], send.at[n], recv.at[me], device(*offset))
            for n, offset in enumerate(offsets)
        ]
        for copy in copies:
            copy.start()
        for n, offset in enumerate(offsets):
            slot = slot_of(*offset)
            remote(source, slots.at[slot], send.at[n], recv.at[slot], device(*offset)).wait_recv()
        for copy in copies:
            copy.wait_send()

    stage(r.value_row, r.first, r.s1_s, r.s1_r, OURS, lambda *o: ours_at(place, *o), y * 2 + k,
          lambda dy, dk: place.moved("y", dy) * 2 + lax.rem(k + dk, 2))
    r.held[...] = jnp.sum(r.first[...], axis=0)
    stage(r.held, r.second, r.s2_s, r.s2_r, THEIRS, lambda *o: theirs_at(place, *o), z * 4 + x,
          lambda dz, dx: place.moved("z", dz) * 4 + place.moved("x", dx))
    r.out_sums[...] = jnp.sum(r.second[...], axis=0)


OURS = [(dy, dk) for dy in range(4) for dk in range(2) if (dy, dk) != (0, 0)]
THEIRS = [(dz, dx) for dz in range(4) for dx in range(4) if (dz, dx) != (0, 0)]


def ours_at(place, dy, dk):
    return place.device(y=place.moved("y", dy), k=lax.rem(place["k"] + dk, 2))


def theirs_at(place, dz, dx):
    return place.device(z=place.moved("z", dz), x=place.moved("x", dx))


def by_eights(rows):
    return jnp.sum(rows.reshape(rows.shape[0] // 8, 8, D), axis=0)


def back_through_norm(r, gain, half):
    @pl.loop(0, BLOCK // 32)
    def _(t):
        at = row_tile(4 * half + t, 32)
        rows = r.middle[at]
        scale = lax.rsqrt(jnp.mean(rows * rows, axis=-1, keepdims=True) + norm_eps)
        normed = rows * scale
        incoming = r.grad_rows[at] + r.dh_box[at].astype(F32)
        r.mlp_gain[...] += by_eights(incoming * normed)
        incoming = incoming * gain[:, D : 2 * D]
        mean = jnp.mean(incoming * normed, axis=-1, keepdims=True)
        d_mid = r.cot[at].astype(F32) + scale * (incoming - normed * mean)
        r.grad_rows[at] = d_mid
        r.own[at] = d_mid.astype(BF)


def back_to_input(r, gain):
    r.attn_gain[...] = jnp.zeros_like(r.attn_gain)

    @pl.loop(0, ROWS // 32)
    def _(t):
        at = row_tile(t, 32)
        rows = r.tok[at].astype(F32)
        scale = lax.rsqrt(jnp.mean(rows * rows, axis=-1, keepdims=True) + norm_eps)
        normed = rows * scale
        incoming = r.dh_total[at]
        r.attn_gain[...] += by_eights(incoming * normed)
        incoming = incoming * gain[:, 0:D]
        mean = jnp.mean(incoming * normed, axis=-1, keepdims=True)
        r.grad_rows[at] += scale * (incoming - normed * mean)


def back_to_projections(r, gain):
    plain = HEAD_WIDTH ** (-0.5)
    r.head_gain[...] = jnp.zeros_like(r.head_gain)

    @pl.loop(0, SEQ // TILE)
    def _(t):
        at = row_tile(t, TILE)
        cos_t, sin_t = r.cosine[at], r.sine[at]
        for h in range(OWN_HEADS + OWN_KV):
            mine = h < OWN_HEADS
            d_rows = r.d_query[h, at] if mine else r.d_key[h - OWN_HEADS, at] * plain
            first = 2 * D if mine else 2 * D + HEAD_WIDTH
            d_gained = d_rows * cos_t - turn(d_rows) * sin_t
            normed, scale = head_norm(r.raw[h, at].astype(F32))
            product = d_gained * normed
            r.head_gain[0 if mine else 1] += jnp.sum(product.reshape(TILE // 8, 8, HEAD_WIDTH), axis=0)
            incoming = d_gained * gain[:, first : first + HEAD_WIDTH]
            mean = jnp.mean(incoming * normed, axis=-1, keepdims=True)
            r.d_proj[pl.ds(2 * t, 2), :, 128 * h : 128 * h + 128] = (
                (scale * (incoming - normed * mean)).astype(BF).reshape(2, BLOCK, HEAD_WIDTH)
            )
        for h in range(OWN_KV):
            r.d_proj[pl.ds(2 * t, 2), :, 768 + 128 * h : 896 + 128 * h] = (
                r.d_value[h, at].astype(BF).reshape(2, BLOCK, HEAD_WIDTH)
            )


def block_weights(r, b):
    if b == 2:
        return r.c[...].reshape(D, D)
    return r.w[:, :, 64 * b : 64 * b + 64].reshape(D, D)


def block_down(r, b):
    return r.w[:, :, DOWN:UNIT].reshape(FF // 2, D)[512 * b : 512 * b + 512]


def product_rows(r, first, last):
    parts = []
    if first < D:
        parts.append(r.d_o[...].reshape(2 * ROWS, D)[:, first : min(last, D)])
    if last > D:
        parts.append(r.d_q[2:4].reshape(2 * ROWS, D)[:, max(first, D) - D : last - D])
    return parts[0] if len(parts) == 1 else jnp.concatenate(parts, axis=1)


def d_gate_up_rows(r, b, t):
    if b < 2:
        return r.d_proj[pl.ds(4 * b + 2 * t, 2)].reshape(ROWS, D)
    return r.d_q[t].reshape(ROWS, D)


def feed_forward(r, w_loads):
    w_loads[0].wait()
    w_loads[1].wait()
    for b in range(3):
        if b:
            w_loads[1 + b].wait()
        weights, down = block_weights(r, b), block_down(r, b)

        @pl.loop(0, 2)
        def _(t):
            gate_up = dot_nn(r.hidden[row_tile(t, ROWS)], weights)
            d_product = dot_nt(r.hidden[row_tile(2 + t, ROWS)], down)
            gate, up = gate_up[:, :512], gate_up[:, 512:]
            sigmoid = 1.0 / (1.0 + jnp.exp(-gate))
            active = gate * sigmoid
            product = (active * up).astype(BF).reshape(4, 64, 512)
            if b < 2:
                r.d_o[pl.ds(2 * t, 2), :, :, 512 * b : 512 * b + 512] = product.reshape(2, 2, 64, 512)
            else:
                r.d_q[2 + t, :, :, :, 0:512] = product.reshape(4, 2, 32, 512)
            d_gate = d_product * up * sigmoid * (1.0 + gate * (1.0 - sigmoid))
            d_both = jnp.concatenate([d_gate, d_product * active], axis=1).astype(BF)
            if b < 2:
                r.d_proj[pl.ds(4 * b + 2 * t, 2)] = d_both.reshape(2, BLOCK, D)
            else:
                r.d_q[t] = d_both.reshape(4, 2, 32, D)


def feed_forward_inputs(r):
    def half(t):
        total = dot_nt(d_gate_up_rows(r, 0, t), block_weights(r, 0))
        for b in (1, 2):
            total = total + dot_nt(d_gate_up_rows(r, b, t), block_weights(r, b))
        return total

    r.dh_sib[...] = half(1).astype(BF)
    r.grad_rows[...] = half(0)


def feed_forward_outputs(r):
    down = r.w[:, :, DOWN:UNIT].reshape(FF // 2, D)

    def half(t):
        first = dot_nn(r.d_o[2 * t : 2 * t + 2].reshape(ROWS, D), down[:D])
        return first + dot_nn(r.d_q[2 + t, :, :, :, 0:512].reshape(ROWS, 512), down[D:])

    r.out_sib[...] = half(1).astype(BF)
    r.dh_total[...] = half(0)


def dot_tn(left, right):
    return lax.dot_general(left, right, (((0,), (0,)), ((), ())), preferred_element_type=F32)


def down_gradients(r):
    cot = r.hidden[2 * ROWS : SEQ]
    for i in range(4):
        left = product_rows(r, 384 * i, 384 * i + 384)
        r.w[i, :, DOWN:UNIT] = dot_tn(left, cot).astype(BF).reshape(4, 96, D)


def block_gradients(r, b):
    d_both = jnp.concatenate([d_gate_up_rows(r, b, 0), d_gate_up_rows(r, b, 1)], axis=0)

    @pl.loop(0, 4)
    def _(i):
        columns = pl.ds(pl.multiple_of(i * 256, 256), 256)
        rows = dot_tn(r.hidden[0 : 2 * ROWS, columns], d_both)
        if b < 2:
            r.w[i, :, 64 * b : 64 * b + 64] = rows.astype(BF).reshape(4, 64, D)
        else:
            rows = rows.reshape(4, 2, 4, 8, D)
            for c in range(4):
                r.c[c, pl.ds(4 * i, 4)] = rows[:, :, c].reshape(4, 16, D).astype(BF)


def backward_kernel(r):
    place = Place()
    z, x, k, y = (place[a] for a in "zxky")
    diagonal = z == y
    gain = r.gain_row
    near = neighbours(place, "xyzk")
    everyone = [ours_at(place, *o) for o in OURS] + [theirs_at(place, *o) for o in THEIRS]
    greet(near + everyone)
    for other in range(4):

        @pl.when(not_here(diagonal, other, z))
        def _():
            greet([place.device(z=jnp.int32(other), y=z)])

    loads = {
        n: pltpu.make_async_copy(getattr(r, "in_" + n), getattr(r, n), r.load.at[i]) for i, n in enumerate([*SAVED, *TABLES, "middle"])
    }
    pair_loads = [
        pltpu.make_async_copy(pair, r.hidden.at[rows], r.w_sem.at[4 + i])
        for i, (pair, rows) in enumerate([(r.hidden_pair, pl.ds(0, 2 * ROWS)), (r.cot_pair, pl.ds(2 * ROWS, 2 * ROWS))])
    ]
    w_loads = [
        pltpu.make_async_copy(r.w_all.at[:, :, rows], r.w.at[:, :, rows], r.w_sem.at[i])
        for i, rows in enumerate([pl.ds(0, 64), pl.ds(DOWN, 96), pl.ds(64, 64)])
    ]
    w_loads.append(pltpu.make_async_copy(r.w_two, r.c, r.w_sem.at[3]))
    hidden_load, middle_load = loads.pop("hidden"), loads.pop("middle")
    for copy in pair_loads + w_loads + [middle_load]:
        copy.start()

    def a_part(i, h):
        return r.w.at[i, pl.ds(2 * h, 2), pl.ds(0, PART_A)]

    def b_part(i, h):
        return r.w.at[pl.ds(2 * h, 2), i, pl.ds(PART_A, UNIT - PART_A)]

    a_one = Scatter(place, "z", a_part, [r.a_box.at[n] for n in range(6)], (r.a1_s, r.a1_r))
    b_one = Scatter(place, "x", b_part, [r.b_box.at[n] for n in range(6)], (r.b1_s, r.b1_r))
    dh_copy = remote(r.dh_sib, r.dh_box, r.core.at[0], r.core.at[1], place.sibling())
    out_copy = remote(r.out_sib, r.out_box, r.core.at[2], r.core.at[3], place.sibling())
    for copy in pair_loads:
        copy.wait()
    feed_forward(r, w_loads)
    for copy in loads.values():
        copy.start()
    feed_forward_inputs(r)
    await_greetings(len(near) + len(everyone) + jnp.where(diagonal, 3, 4))
    dh_copy.start()
    feed_forward_outputs(r)
    out_copy.start()
    down_gradients(r)
    dh_copy.wait_recv()
    ring = Gather(
        place, "y", lambda i, h: r.d_attn_all.at[2 * i + h], (r.t_s, r.t_r),
        own=lambda h: r.own.at[pl.ds(BLOCK * h, BLOCK)],
    )
    middle_load.wait()
    r.mlp_gain[...] = jnp.zeros_like(r.mlp_gain)
    for half in range(2):
        back_through_norm(r, gain, half)
        ring.start([half])
    r.d_attn_all[pl.ds(2 * y, 2)] = r.own[...].reshape(2, BLOCK, D)
    block_gradients(r, 1)
    b_one.start()
    block_gradients(r, 0)
    a_one.start()
    block_gradients(r, 2)
    hidden_load.start()
    out_copy.wait_recv()

    @pl.loop(0, ROWS // 16)
    def _(t):
        at = row_tile(t, 16)
        r.layer_rows[at] = (r.middle[at] + r.dh_total[at] + r.out_box[at].astype(F32)).astype(BF)

    layer_copy = pltpu.make_async_copy(r.layer_rows, r.out_layer_out, r.w_sem.at[6])
    layer_copy.start()

    for copy in [hidden_load, *loads.values()]:
        copy.wait()
    r.d_key[...] = jnp.zeros_like(r.d_key)
    r.d_value[...] = jnp.zeros_like(r.d_value)
    ring.forward()
    ring.finish()
    c_y = Scatter(
        place, "y", lambda i, h: r.c.at[i, pl.ds(8 * h, 8)],
        [r.cy_box.at[n] for n in range(6)], (r.cy_s, r.cy_r),
    )
    c_z = Scatter(
        place, "z", lambda i, h: r.c.at[y, pl.ds(4 * i + 2 * h, 2)],
        [r.cz_box.at[n] for n in range(6)], (r.cz_s, r.cz_r),
    )
    c_x = Scatter(
        place, "x", lambda i, h: r.c.at[y, 4 * z + i, :, pl.ds(512 * h, 512)],
        [r.cx_box.at[n] for n in range(6)], (r.cx_s, r.cx_r),
    )
    c_y.start()

    wo = r.wo_all[...].reshape(OWN_HEADS * HEAD_WIDTH, D)

    @pl.loop(0, SEQ // TILE)
    def _(t):
        at = row_tile(t, TILE)
        rows = pair_of(r.d_attn_all, r.span, t)
        r.d_q[t] = rows.reshape(4, 2, 32, D)
        both = dot_nt(rows, wo)
        for h in range(OWN_HEADS):
            r.d_attended[h, at] = both[:, 128 * h : 128 * h + 128].astype(BF)

    d_sorted = r.d_q[...].reshape(SEQ, D)

    @pl.loop(0, 4)
    def _(i):
        r.d_o[i] = dot_nn(r.attended_t[i], d_sorted).astype(BF).reshape(2, 64, D)

    o_core = remote(r.d_o.at[:, 1 - k], r.o_box, r.core.at[4], r.core.at[5], place.sibling())
    o_core.start()
    attend_back(r, 0, 2)
    c_y.forward()
    a_one.forward()
    b_one.forward()
    o_core.wait_recv()

    @pl.loop(0, 4)
    def _(i):
        add_rows(r.o_box.at[i], [r.o_box.at[i], r.d_o.at[i, k]])

    o_x = Scatter(
        place, "x", lambda i, h: r.o_box.at[i, pl.ds(32 * h, 32)],
        [r.ox_box.at[n] for n in range(6)], (r.ox_s, r.ox_r),
    )
    o_x.start()
    attend_back(r, 2, 4)
    c_y.finish(lambda h: r.c.at[y, pl.ds(8 * h, 8)])
    c_z.start()
    o_x.forward()
    back_to_projections(r, gain)

    wq = r.wq_all[:, :, :, :, 0:D].reshape(D, D)

    @pl.loop(0, 4)
    def _(i):
        rows = jnp.concatenate([r.d_proj[r.span[2 * i + n]] for n in range(2)], axis=0)
        r.d_attn_all[pl.ds(2 * i, 2)] = dot_nt(rows, wq).astype(BF).reshape(2, BLOCK, D)

    dh_ring = Scatter(
        place, "y", lambda i, h: r.d_attn_all.at[2 * i + h],
        [r.y_box.at[n] for n in range(6)], (r.y_s, r.y_r),
    )
    dh_ring.start()
    a_one.finish(lambda h: a_part(z, h))
    b_one.finish(lambda h: b_part(x, h))
    a_two = Scatter(
        place, "x", lambda i, h: r.w.at[z, i, from_to(h, 0, 64, PART_A)],
        [r.a_box2.at[n, pl.ds(0, 64 if n in (0, 3, 4) else 48)] for n in range(6)], (r.a2_s, r.a2_r),
    )
    b_two = Scatter(
        place, "z", lambda i, h: r.w.at[i, x, from_to(h, PART_A, 160, UNIT)],
        [r.b_box2.at[n, pl.ds(0, 48 if n in (0, 3, 4) else 64)] for n in range(6)], (r.b2_s, r.b2_r),
    )
    a_two.start()
    b_two.start()

    d_proj = r.d_proj[...].reshape(SEQ, D)
    planes = [place.moved("z", dz) for dz in (1, 2, 3, 0)]
    q_core = [
        remote(r.d_q.at[plane, :, 1 - k], r.q_box.at[plane], r.qk_s.at[n], r.qk_r.at[n], place.sibling())
        for n, plane in enumerate(planes)
    ]

    @pl.loop(0, 4)
    def _(n):
        plane = place.moved("z", n + 1)
        left = r.hidden[:, row_tile(plane, 256)]
        r.d_q[plane] = dot_tn(left, d_proj).astype(BF).reshape(4, 2, 32, D)
        remote(r.d_q.at[plane, :, 1 - k], r.q_box.at[plane], r.qk_s.at[n], r.qk_r.at[n], place.sibling()).start()

    q_direct = []
    for n, plane in enumerate(planes):
        q_core[n].wait_recv()

        @pl.loop(0, 4)
        def _(j):
            add_rows(r.q_box.at[plane, j], [r.q_box.at[plane, j], r.d_q.at[plane, j, k]])

        for dx in range(1 if n == 3 else 0, 4):
            to = place.moved("x", dx)
            q_direct.append(
                remote(
                    r.q_box.at[plane, to], r.q_slots.at[4 * z + x], r.qd_s.at[len(q_direct)], r.qd_r.at[4 * z + x],
                    place.device(z=plane, x=to),
                )
            )
            q_direct[-1].start()
    r.q_slots[4 * z + x] = r.q_box[z, x]
    dh_ring.forward()
    c_z.forward()
    a_two.forward()
    b_two.forward()
    c_z.finish(lambda h: r.c.at[y, pl.ds(4 * z + 2 * h, 2)])
    c_x.start()
    o_x.finish(lambda h: r.o_two.at[pl.ds(32 * h, 32)])

    def o_target(other):
        return place.device(z=y, y=jnp.int32(other))

    for other in range(4):
        piece = r.o_two.at[pl.ds(16 * other, 16)]

        @pl.when(not_here(diagonal, other, y))
        def _():
            remote(piece, r.o_slots.at[z], r.oy_s.at[other], r.oy_r.at[z], o_target(other)).start()

    @pl.when(diagonal)
    def _():
        r.o_slots[z] = r.o_two[row_tile(y, 16)]

    c_x.forward()

    a_two.finish(lambda h: r.total.at[from_to(h, 0, 64, PART_A)])
    b_two.finish(lambda h: r.total.at[from_to(h, PART_A, 160, UNIT)])
    for c in range(4):
        for b in range(2):
            at = 64 * b + 8 * c
            rows = jnp.concatenate([r.total[at : at + 8], r.total[at + 32 : at + 40]], axis=0)
            r.g_send[c, 16 * b : 16 * b + 16] = rows.astype(BF)
    r.g_slots[y] = r.g_send[y]

    def down_rows(c):
        return pl.ds(pl.multiple_of(DOWN + 24 * c, 8), 24)

    r.d_slots[y] = r.total[down_rows(y)]
    y_copies = []
    for n in (1, 3, 2):
        to = place.moved("y", n)
        y_copies.append(remote(r.g_send.at[to], r.g_slots.at[y], r.gy_s.at[n], r.gy_r.at[y], place.peer("y", n)))
        y_copies.append(remote(r.total.at[down_rows(to)], r.d_slots.at[y], r.dy_s.at[n], r.dy_r.at[y], place.peer("y", n)))
    for copy in y_copies:
        copy.start()
    c_x.finish(lambda h: r.c_sum.at[:, pl.ds(512 * h, 512)])
    dh_ring.finish(lambda h: r.dh_total.at[pl.ds(BLOCK * h, BLOCK)])
    back_to_input(r, gain)
    grad_copy = pltpu.make_async_copy(r.grad_rows, r.out_input_grad, r.w_sem.at[7])
    grad_copy.start()

    for n in (1, 3, 2):
        source = place.moved("y", n)
        remote(r.g_send.at[0], r.g_slots.at[source], r.gy_s.at[n], r.gy_r.at[source], place.peer("y", n)).wait_recv()
        remote(r.total.at[pl.ds(DOWN, 24)], r.d_slots.at[source], r.dy_s.at[n], r.dy_r.at[source], place.peer("y", n)).wait_recv()
    r.out_d_out[...] = r.d_slots[0] + r.d_slots[1] + r.d_slots[2] + r.d_slots[3]
    summed = r.g_slots[0].astype(F32)
    for c in range(1, 4):
        summed = summed + r.g_slots[c].astype(F32)
    summed = summed.reshape(2, 2, 8, D)
    last = r.c_sum[...].reshape(2, 8, D)
    for n in range(2):
        r.g_sum[n, 0:2] = summed[:, n]
        r.g_sum[n, 2] = last[n]
    r.out_g_out[k] = r.g_sum[k]
    g_core = remote(r.g_sum.at[1 - k], r.out_g_out.at[k], r.core.at[8], r.core.at[9], place.sibling())
    g_core.start()
    for other in range(4):

        @pl.when(not_here(diagonal, other, z))
        def _():
            remote(r.o_two.at[pl.ds(0, 16)], r.o_slots.at[other], r.oy_s.at[0], r.oy_r.at[other], place.device(z=jnp.int32(other), y=z)).wait_recv()

    o_sum = r.o_slots[0].astype(F32)
    for c in range(1, 4):
        o_sum = o_sum + r.o_slots[c].astype(F32)
    r.out_o_out[...] = o_sum

    for dz, dx in THEIRS:
        at = 4 * place.moved("z", dz) + place.moved("x", dx)
        remote(r.q_box.at[0, 0], r.q_slots.at[at], r.qd_s.at[0], r.qd_r.at[at], theirs_at(place, dz, dx)).wait_recv()

    @pl.loop(0, 2)
    def _(t):
        at = row_tile(t, 16)
        total = r.q_slots[0, at].astype(F32)
        for n in range(1, 16):
            total = total + r.q_slots[n, at].astype(F32)
        r.q_three[at] = total

    r.out_q_out[y] = r.q_three[row_tile(y, 8)]
    q_copies = [
        remote(r.q_three.at[row_tile(place.moved("y", n), 8)], r.out_q_out.at[y], r.qy_s.at[n], r.qy_r.at[y], place.peer("y", n))
        for n in (1, 3, 2)
    ]
    for copy in q_copies:
        copy.start()
    squares = jnp.zeros((8, D), F32)
    for part in [r.q_three[8 * c : 8 * c + 8] for c in range(4)] + [r.g_sum[c, b] for c in range(2) for b in range(3)]:
        squares = squares + part * part
    for c in range(2):
        part = r.out_o_out[8 * c : 8 * c + 8]
        squares = squares + part * part
    for c in range(3):
        part = r.out_d_out[8 * c : 8 * c + 8]
        squares = squares + part * part
    attn = jnp.sum(r.attn_gain[...], axis=0, keepdims=True)
    mlp = jnp.sum(r.mlp_gain[...], axis=0, keepdims=True)
    squares = jnp.sum(squares, axis=0, keepdims=True)
    r.value_row[...] = jnp.zeros_like(r.value_row)
    lanes = jnp.zeros((1, 128), F32)
    for c in range(8):
        at = slice(128 * c, 128 * c + 128)
        r.value_row[c : c + 1] = attn[:, at]
        r.value_row[8 + c : 9 + c] = mlp[:, at]
        lanes = lanes + squares[:, at]
    for c in range(2):
        r.value_row[16 + c : 17 + c] = jnp.sum(r.head_gain[c], axis=0, keepdims=True)
    r.value_row[18:19] = lanes
    sum_everywhere(r, place)

    remote(r.g_sum.at[0], r.out_g_out.at[1 - k], r.core.at[8], r.core.at[9], place.sibling()).wait_recv()
    for n in (1, 3, 2):
        source = place.moved("y", n)
        remote(r.q_three.at[pl.ds(0, 8)], r.out_q_out.at[source], r.qy_s.at[n], r.qy_r.at[source], place.peer("y", n)).wait_recv()
    layer_copy.wait()
    grad_copy.wait()
    for copy in [dh_copy, out_copy, o_core, g_core] + y_copies + q_copies + q_core + q_direct:
        copy.wait_send()
    for other in range(4):

        @pl.when(not_here(diagonal, other, y))
        def _():
            remote(r.o_two.at[pl.ds(16 * other, 16)], r.o_slots.at[z], r.oy_s.at[other], r.oy_r.at[z], o_target(other)).wait_send()


def backward_step(**given):
    late = [*SAVED, *TABLES, "middle"]
    given = {("in_" + n if n in late else n): v for n, v in given.items()}
    outputs = {
        "layer_out": ((ROWS, D), BF, hbm),
        "input_grad": ((ROWS, D), F32, hbm),
        "q_out": ((4, 8, D), F32, vmem),
        "o_out": ((16, D), F32, vmem),
        "g_out": ((2, 3, 8, D), F32, vmem),
        "d_out": ((24, D), F32, vmem),
        "sums": ((24, 128), F32, vmem),
    }
    head_rows = (OWN_HEADS, SEQ, HEAD_WIDTH)
    kv_rows = (OWN_KV, SEQ, HEAD_WIDTH)
    scratch = {
        **{n: pltpu.VMEM(*what) for n, what in SAVED.items()},
        "layer_rows": pltpu.VMEM((ROWS, D), BF),
        "grad_rows": pltpu.VMEM((ROWS, D), F32),
        **{n: pltpu.VMEM(*what) for n, what in TABLES.items()},
        "middle": pltpu.VMEM((ROWS, D), F32),
        "out_box": pltpu.VMEM((ROWS, D), BF),
        "dh_box": pltpu.VMEM((ROWS, D), BF),
        "own": pltpu.VMEM((ROWS, D), BF),
        "d_attn_all": pltpu.VMEM((8, BLOCK, D), BF),
        "d_attended": pltpu.VMEM(head_rows, BF),
        "d_query": pltpu.VMEM(head_rows, F32),
        "d_key": pltpu.VMEM(kv_rows, F32),
        "d_value": pltpu.VMEM(kv_rows, F32),
        "d_proj": pltpu.VMEM((8, BLOCK, D), BF),
        "y_box": pltpu.VMEM((6, BLOCK, D), BF),
        "dh_total": pltpu.VMEM((ROWS, D), F32),
        "a_box": pltpu.VMEM((6, 2, PART_A, D), BF),
        "b_box": pltpu.VMEM((6, 2, PART_A, D), BF),
        "w": pltpu.VMEM((4, 4, UNIT, D), BF),
        "out_sib": pltpu.VMEM((ROWS, D), BF),
        "dh_sib": pltpu.VMEM((ROWS, D), BF),
        "a_box2": pltpu.VMEM((6, 64, D), BF),
        "b_box2": pltpu.VMEM((6, 64, D), BF),
        "total": pltpu.VMEM((UNIT, D), F32),
        "g_send": pltpu.VMEM((4, 32, D), BF),
        "g_slots": pltpu.VMEM((4, 32, D), BF),
        "d_slots": pltpu.VMEM((4, 24, D), F32),
        "g_sum": pltpu.VMEM((2, 3, 8, D), F32),
        "d_q": pltpu.VMEM((4, 4, 2, 32, D), BF),
        "d_o": pltpu.VMEM((4, 2, 64, D), BF),
        "q_box": pltpu.VMEM((4, 4, 32, D), BF),
        "q_slots": pltpu.VMEM((16, 32, D), BF),
        "c": pltpu.VMEM((4, 16, 16, D), BF),
        "cy_box": pltpu.VMEM((6, 8, 16, D), BF),
        "cz_box": pltpu.VMEM((6, 2, 16, D), BF),
        "cx_box": pltpu.VMEM((6, 16, 512), BF),
        "c_sum": pltpu.VMEM((16, D), F32),
        "q_three": pltpu.VMEM((32, D), F32),
        "o_box": pltpu.VMEM((4, 64, D), BF),
        "ox_box": pltpu.VMEM((6, 32, D), BF),
        "o_two": pltpu.VMEM((64, D), BF),
        "o_slots": pltpu.VMEM((4, 16, D), BF),
        "mlp_gain": pltpu.VMEM((8, D), F32),
        "attn_gain": pltpu.VMEM((8, D), F32),
        "head_gain": pltpu.VMEM((2, 8, HEAD_WIDTH), F32),
        "value_row": pltpu.VMEM((24, 128), F32),
        "first": pltpu.VMEM((8, 24, 128), F32),
        "second": pltpu.VMEM((16, 24, 128), F32),
        "held": pltpu.VMEM((24, 128), F32),
        "core": dma(10),
        "load": dma(len(late)),
        "w_sem": dma(8),
        **{n: dma(4) for n in ("gy_s", "gy_r", "dy_s", "dy_r", "qy_s", "qy_r", "oy_s", "oy_r")},
        **{"s1_s": dma(7), "s1_r": dma(8), "s2_s": dma(15), "s2_r": dma(16)},
        **{"qd_s": dma(15), "qd_r": dma(16), "qk_s": dma(4), "qk_r": dma(4)},
        **rings("t", "y", "a1", "b1", "a2", "b2", "cx", "cy", "cz", "ox"),
    }
    spaces = {"span": smem, "w_all": hbm, "w_two": hbm, "hidden_pair": hbm, "cot_pair": hbm, **{"in_" + n: hbm for n in late}}
    return named_call(backward_kernel, 2, "backward_attention", given, spaces, outputs, scratch)


def gain_spread():
    return jnp.asarray(np.arange(128)[:, None] == np.arange(GAINS)[None, :] % 18, BF)


def rope_tables():
    middle = HEAD_WIDTH // 2
    frequency = rope_base ** (-(np.arange(middle) * 2.0) / HEAD_WIDTH)
    angle = np.arange(SEQ)[:, None] * frequency[None, :]
    cosine, sine = np.cos(angle), np.sin(angle)
    return (
        jnp.asarray(np.concatenate([cosine, cosine], axis=1), F32),
        jnp.asarray(np.concatenate([-sine, sine], axis=1), F32),
    )


MATRICES = {"qkv": matrix_rate, "out": out_rate, "gateup": matrix_rate, "down": matrix_rate}


def adam_update(weight, first, second, grad, factor, rate, decay):
    clipped = grad * factor
    new_first = beta_one * first + (1.0 - beta_one) * clipped
    new_second = beta_two * second + (1.0 - beta_two) * clipped * clipped
    direction = (
        new_first
        / (1.0 - beta_one**STEP)
        / (jnp.sqrt(new_second / (1.0 - beta_two**STEP)) + adam_eps)
    )
    return (weight - rate * (direction + decay * weight), new_first, new_second)


def update_kernel(r):
    hand_on = [
        pltpu.make_async_copy(r.layer_out, r.out_layer_out, r.sems.at[0]),
        pltpu.make_async_copy(r.input_grad, r.out_input_grad, r.sems.at[1]),
    ]
    for copy in hand_on:
        copy.start()
    sums = r.sums[...]
    row = lax.broadcasted_iota(jnp.int32, (24, 128), 0)
    squares = jnp.where(row < 18, sums * sums, jnp.where(row == 18, sums, 0.0))
    norm = jnp.sqrt(jnp.sum(jnp.sum(squares, axis=0, keepdims=True), axis=1, keepdims=True))
    r.out_norm[...] = norm
    factor = jnp.minimum(1.0, clip_at / (norm + 1e-06))

    place = row * 128 + lax.broadcasted_iota(jnp.int32, (24, 128), 1)
    start = (lax.axis_index("dp") * 4 + lax.axis_index("ctx")) * 18
    lane = lax.broadcasted_iota(jnp.int32, (1, 128), 1)
    mine = jnp.zeros((1, 128), F32)
    for n in range(18):
        entry = jnp.sum(jnp.where(place == start + n, sums, 0.0), axis=0, keepdims=True)
        mine = jnp.where(lane == n, jnp.sum(entry, axis=1, keepdims=True), mine)
    grads = {
        "qkv": jnp.concatenate(
            [r.q_out[c, :, 0:512] for c in range(4)]
            + [r.q_out[c, :, 512:768] for c in range(4)]
            + [r.q_out[c, :, 768:1024] for c in range(4)],
            axis=1,
        ),
        "out": r.o_out[...],
        "gateup": unpack_gateup(r.g_out),
        "down": r.d_out[...],
        "gains": mine[:, 0:18],
    }
    for name, grad in grads.items():
        rate, decay = (MATRICES[name], matrix_decay) if name in MATRICES else (gain_rate, 0.0)
        refs = [getattr(r, kind + name) for kind in ("w_", "first_", "second_")]
        news = adam_update(*[ref[...] for ref in refs], grad, factor, rate, decay)
        for kind, new in zip(("w_", "first_", "second_"), news):
            getattr(r, "out_" + kind + name)[...] = new
    for copy in hand_on:
        copy.wait()


def update_step(**given):
    outputs = {
        "layer_out": ((ROWS, D), BF, hbm),
        "input_grad": ((ROWS, D), F32, hbm),
        "norm": ((1, 1), F32, vmem),
        **{n: (v.shape, F32, vmem) for n, v in given.items() if n.split("_")[0] in ("w", "first", "second")},
    }
    return named_call(update_kernel, None, "update", given, {}, outputs, {"sems": dma(2)})


def body(
    tokens, cotangent, span_order,
    w_qkv, w_out, w_gateup, w_down, gains,
    first_qkv, first_out, first_gateup, first_down, first_gains,
    second_qkv, second_out, second_gateup, second_down, second_gains,
):
    cosine, sine = rope_tables()
    fwd = forward_step(
        span=span_order, tok=tokens, cot=cotangent, wq=w_qkv, wo=w_out, wgu=w_gateup, wd=w_down,
        gains=gains[None, :], spread=gain_spread(), cosine=cosine, sine=sine,
    )
    bwd = backward_step(
        span=span_order, tok=tokens, cot=cotangent, middle=fwd["middle"],
        gain_row=fwd["gain_row"], cosine=cosine, sine=sine,
        hidden_pair=fwd["hidden_pair"], cot_pair=fwd["cot_pair"], w_all=fwd["w_all"],
        w_two=fwd["w_two"].reshape(4, 16, 16, D),
        **{name: fwd[name] for name in SAVED},
    )
    names = ("qkv", "out", "gateup", "down", "gains")
    state = {
        "w_": (w_qkv, w_out, w_gateup, w_down, gains[None, :]),
        "first_": (first_qkv, first_out, first_gateup, first_down, first_gains[None, :]),
        "second_": (second_qkv, second_out, second_gateup, second_down, second_gains[None, :]),
    }
    new = update_step(
        **bwd, **{kind + name: value for kind, values in state.items() for name, value in zip(names, values)}
    )
    results = [
        new[kind + name] if name != "gains" else new[kind + name][0] for kind in state for name in names
    ]
    return (new["layer_out"], new["input_grad"], *results, new["norm"][0, 0])


def solution(mesh):
    rows, flat = P(("dp", "ctx"), None), P(("dp", "ctx"))
    state = (rows, rows, rows, rows, flat)
    in_specs = (rows, rows, P()) + state * 3
    out_specs = (rows, rows) + state * 3 + (P(),)
    return jax.shard_map(body, mesh=mesh, in_specs=in_specs, out_specs=out_specs, check_vma=False)
```

```python
import jax
import jax.numpy as jnp
import numpy as np
from jax import lax
from jax.experimental import pallas as pl
from jax.experimental.pallas import tpu as pltpu
from jax.sharding import PartitionSpec as P

D = 1024
HEADS = 16
KV_HEADS = 8
HEAD_WIDTH = 128
FF = 3072
STEP = 10

norm_eps = 1e-06
rope_base = 1000000.0
beta_one = 0.9
beta_two = 0.999
adam_eps = 1e-08
clip_at = 1.0
matrix_rate = 0.05
out_rate = 0.25
matrix_decay = 0.1
gain_rate = 0.5
masked_score = -1e30

MESH = pl.DeviceIdType.MESH
BF = jnp.bfloat16
F32 = jnp.float32
ROWS = 256
UNIT = 224
PART_A = 112
DOWN = 128
VMEM_LIMIT = 62 * 2**20
vmem = pl.BlockSpec(memory_space=pltpu.VMEM)
hbm = pl.BlockSpec(memory_space=pl.ANY)


class Place:
    def __init__(self):
        dp = lax.axis_index("dp")
        self.at = {
            "z": lax.div(dp, 8),
            "x": lax.rem(lax.div(dp, 2), 4),
            "k": lax.rem(dp, 2),
            "y": lax.axis_index("ctx"),
        }

    def __getitem__(self, axis):
        return self.at[axis]

    def device(self, **other):
        c = {**self.at, **other}
        return (c["z"] * 8 + c["x"] * 2 + c["k"], c["y"])

    def moved(self, axis, steps):
        return lax.rem(self.at[axis] + steps, 4)

    def peer(self, axis, steps):
        return self.device(**{axis: self.moved(axis, steps)})

    def sibling(self):
        return self.device(k=1 - self.at["k"])


def greet(devices):
    barrier = pltpu.get_barrier_semaphore()
    for device in devices:
        pl.semaphore_signal(barrier, inc=1, device_id=device, device_id_type=MESH)


def await_greetings(count):
    pl.semaphore_wait(pltpu.get_barrier_semaphore(), count)


def neighbours(place, axes):
    found = []
    for axis in axes:
        if axis == "k":
            found.append(place.sibling())
        else:
            found += [place.peer(axis, 1), place.peer(axis, 3)]
    return found


def remote(src, dst, send, recv, device):
    return pltpu.make_async_remote_copy(
        src_ref=src, dst_ref=dst, send_sem=send, recv_sem=recv, device_id=device, device_id_type=MESH
    )


class Gather:
    def __init__(self, place, axis, part, sems, own=None):
        self.part, self.send, self.recv = part, sems[0], sems[1]
        self.own = own or (lambda half: part(place[axis], half))
        self.next, self.prev = place.peer(axis, 1), place.peer(axis, 3)
        self.me, self.up, self.down, self.far = (place.moved(axis, n) for n in (0, 1, 3, 2))

    def copy(self, n, slot, half, device, src=None):
        view = self.part(slot, half)
        return remote(src if src is not None else view, view, self.send.at[n], self.recv.at[n], device)

    def outgoing(self, n):
        slot, half, device = [
            (self.me, 0, self.next),
            (self.me, 1, self.prev),
            (self.me, 1, self.next),
            (self.me, 0, self.prev),
            (self.down, 0, self.next),
            (self.up, 1, self.prev),
        ][n]
        return self.copy(n, slot, half, device, self.own(half) if n < 4 else None)

    def start(self, halves=(0, 1)):
        for half in halves:
            for n in ((0, 3), (1, 2))[half]:
                self.outgoing(n).start()

    def forward(self):
        self.copy(0, self.down, 0, self.prev).wait_recv()
        self.outgoing(4).start()
        self.copy(1, self.up, 1, self.next).wait_recv()
        self.outgoing(5).start()

    def finish(self):
        self.copy(2, self.down, 1, self.prev).wait_recv()
        self.copy(3, self.up, 0, self.next).wait_recv()
        self.copy(4, self.far, 0, self.prev).wait_recv()
        self.copy(5, self.far, 1, self.next).wait_recv()
        for n in range(6):
            self.outgoing(n).wait_send()


class Scatter:
    def __init__(self, place, axis, part, boxes, sems, mine=None):
        self.part, self.boxes = part, boxes
        self.send, self.recv = sems[0], sems[1]
        self.next, self.prev = place.peer(axis, 1), place.peer(axis, 3)
        self.me, self.up, self.down, self.far = (place.moved(axis, n) for n in (0, 1, 3, 2))
        self.mine = mine or self.own_part

    def own_part(self, n):
        slot, half = [(self.down, 0), (self.up, 1), (self.me, 0), (self.me, 1)][n]
        return self.part(slot, half)

    def copy(self, n, src, device):
        return remote(src, self.boxes[n], self.send.at[n], self.recv.at[n], device)

    def outgoing(self, n):
        source, device = [
            (lambda: self.part(self.far, 0), self.prev),
            (lambda: self.part(self.far, 1), self.next),
            (lambda: self.part(self.down, 1), self.prev),
            (lambda: self.part(self.up, 0), self.next),
            (lambda: self.boxes[0], self.prev),
            (lambda: self.boxes[1], self.next),
        ][n]
        return self.copy(n, source(), device)

    def start(self):
        for n in range(4):
            self.outgoing(n).start()

    def forward(self):
        for n in range(2):
            self.outgoing(n).wait_recv()
            add_rows(self.boxes[n], [self.boxes[n], self.mine(n)])
            self.outgoing(4 + n).start()

    def finish(self, result):
        for n in (2, 3, 4, 5):
            self.outgoing(n).wait_recv()
        add_rows(result(0), [self.mine(2), self.boxes[3], self.boxes[4]])
        add_rows(result(1), [self.mine(3), self.boxes[2], self.boxes[5]])
        for n in range(6):
            self.outgoing(n).wait_send()


def add_rows(out, terms):
    shape = out.shape
    rows = shape[-2]

    def block(at):
        total = terms[0][at].astype(F32)
        for term in terms[1:]:
            total = total + term[at].astype(F32)
        out[at] = total.astype(out.dtype)

    if len(shape) == 2:

        @pl.loop(0, rows // 16)
        def _(r):
            block((pl.ds(pl.multiple_of(r * 16, 16), 16), slice(None)))

    else:

        @pl.loop(0, shape[0])
        def _(lead):
            @pl.loop(0, rows // 16)
            def _(r):
                block((lead, pl.ds(pl.multiple_of(r * 16, 16), 16), slice(None)))


def dma(*shape):
    return pltpu.SemaphoreType.DMA(shape)


def ring_sems():
    return [dma(6), dma(6)]


def params(which):
    if which is None:
        return pltpu.CompilerParams(vmem_limit_bytes=VMEM_LIMIT)
    return pltpu.CompilerParams(
        collective_id=which, has_side_effects=True, vmem_limit_bytes=VMEM_LIMIT
    )


TILE = 256
SEQ = 4 * ROWS
BLOCK = ROWS // 2
OWN_HEADS = HEADS // 4
OWN_KV = KV_HEADS // 4
LOG2E = 1.4426950408889634


def turn(value_rows):
    return pltpu.roll(value_rows, HEAD_WIDTH // 2, 1)


def head_norm(raw):
    scale = lax.rsqrt(jnp.mean(raw * raw, axis=-1, keepdims=True) + norm_eps)
    return raw * scale, scale


def stored_block(span, position):
    found = jnp.int32(0)
    for block in range(1, 8):
        found = jnp.where(span[block] == position, block, found)
    return found


def pair_of(ref, span, tile):
    return jnp.concatenate([ref[stored_block(span, 2 * tile + n)] for n in range(2)], axis=0)


def dot_nt(left, right):
    return lax.dot_general(left, right, (((1,), (1,)), ((), ())), preferred_element_type=F32)


def dot_nn(left, right):
    return jnp.dot(left, right, preferred_element_type=F32)


def causal(scores):
    keys = lax.broadcasted_iota(jnp.int32, scores.shape, 0)
    queries = lax.broadcasted_iota(jnp.int32, scores.shape, 1)
    return jnp.where(keys <= queries, scores, masked_score)


def project(r, g_attn, g_query, g_key):
    span, tok, cosine, sine = r.span, r.tok_all, r.cosine, r.sine
    hidden, raw, query, key, key_t = r.hidden, r.raw, r.query, r.key, r.key_t
    value, value_t = r.value, r.value_t

    def columns(pair):
        return r.wq_all[:, :, :, :, 256 * pair : 256 * pair + 256].reshape(D, 256)

    @pl.loop(0, SEQ // TILE)
    def _(t):
        at = pl.ds(pl.multiple_of(t * TILE, TILE), TILE)
        rows = pair_of(tok, span, t).astype(F32)
        scale = lax.rsqrt(jnp.mean(rows * rows, axis=-1, keepdims=True) + norm_eps)
        hid = (rows * scale * g_attn[...]).astype(BF)
        hidden[at] = hid
        cos_t, sin_t = cosine[at], sine[at]
        for pair in range(OWN_HEADS // 2):
            both = dot_nn(hid, columns(pair))
            for n in range(2):
                h, part = 2 * pair + n, both[:, 128 * n : 128 * n + 128]
                raw[h, at] = part.astype(BF)
                normed = head_norm(part)[0] * g_query[...]
                query[h, at] = (normed * cos_t + turn(normed) * sin_t).astype(BF)
        both = dot_nn(hid, columns(2))
        for h in range(OWN_KV):
            part = both[:, 128 * h : 128 * h + 128]
            raw[OWN_HEADS + h, at] = part.astype(BF)
            normed = head_norm(part)[0] * g_key[...]
            rotated = normed * cos_t + turn(normed) * sin_t
            key[h, at] = rotated.astype(BF)
            key_t[h, :, at] = rotated.T.astype(BF)
        both = dot_nn(hid, columns(3))
        for h in range(OWN_KV):
            part = both[:, 128 * h : 128 * h + 128]
            value[h, at] = part.astype(BF)
            value_t[h, :, at] = part.T.astype(BF)


def attend(r, first_head, last_head):
    query, key, value_t, attended = r.query, r.key, r.value_t, r.attended
    attended_t, log_total = r.attended_t, r.log_total
    factor = HEAD_WIDTH ** (-0.5) * LOG2E

    @pl.loop(first_head, last_head)
    def _(h):
        kv = lax.div(h, 2)
        for t in range(SEQ // TILE):
            low, high = t * TILE, (t + 1) * TILE
            q = query[h, low:high]
            scores = [causal(dot_nt(key[kv, low:high], q))]
            if t:
                scores.append(dot_nt(key[kv, 0:low], q))
            top = jnp.max(scores[0], axis=0, keepdims=True)
            if t:
                top = jnp.maximum(top, jnp.max(scores[1], axis=0, keepdims=True))
            top = top * factor
            probs = [jnp.exp2(s * factor - top) for s in scores]
            total = jnp.sum(probs[0], axis=0, keepdims=True)
            mixed = dot_nn(value_t[kv, :, low:high], probs[0].astype(BF))
            if t:
                total = total + jnp.sum(probs[1], axis=0, keepdims=True)
                mixed = mixed + dot_nn(value_t[kv, :, 0:low], probs[1].astype(BF))
            mixed = mixed * (1.0 / total)
            attended_t[h, :, low:high] = mixed.astype(BF)
            attended[h, 2 * t : 2 * t + 2] = mixed.T.astype(BF).reshape(2, BLOCK, HEAD_WIDTH)
            log_total[h, :, low:high] = jnp.broadcast_to(top + jnp.log2(total), (8, TILE))


def attend_back(r, first_head, last_head):
    query, key, key_t, value = r.query, r.key, r.key_t, r.value
    d_attended, log_total, d_query = r.d_attended, r.log_total, r.d_query
    d_key, d_value = r.d_key, r.d_value
    factor = HEAD_WIDTH ** (-0.5) * LOG2E
    plain = HEAD_WIDTH ** (-0.5)

    @pl.loop(first_head, last_head)
    def _(h):
        kv = lax.div(h, 2)
        for t in range(SEQ // TILE):
            low, high = t * TILE, (t + 1) * TILE
            q = query[h, low:high]
            da = d_attended[h, low:high]
            total = log_total[h, 0:1, low:high]
            spans = [(low, high)] + ([(0, low)] if t else [])
            probs, mixes = [], []
            for n, (first, last) in enumerate(spans):
                scores = dot_nt(key[kv, first:last], q)
                if n == 0:
                    scores = causal(scores)
                p = jnp.exp2(scores * factor - total)
                d_value[kv, first:last] += dot_nn(p.astype(BF), da)
                probs.append(p)
                mixes.append(p * dot_nt(value[kv, first:last], da))
            delta = jnp.sum(mixes[0], axis=0, keepdims=True)
            if t:
                delta = delta + jnp.sum(mixes[1], axis=0, keepdims=True)
            back = None
            for (first, last), p, mix in zip(spans, probs, mixes):
                ds = (mix - p * delta).astype(BF)
                d_key[kv, first:last] += dot_nn(ds, q)
                part = dot_nn(key_t[kv, :, first:last], ds)
                back = part if back is None else back + part
            d_query[h, low:high] = (back * plain).T


GAINS = 2 * D + 2 * HEAD_WIDTH
smem = pl.BlockSpec(memory_space=pltpu.SMEM)
regular = pltpu.SemaphoreType.DMA


class Names:
    def __init__(self, names, refs):
        self.__dict__.update(zip(names, refs))


def named_call(kernel, which, name, given, spaces, outputs, scratch):
    names = list(given) + ["out_" + n for n in outputs] + list(scratch)
    results = pl.pallas_call(
        lambda *refs: kernel(Names(names, refs)),
        out_shape=tuple(jax.ShapeDtypeStruct(shape, kind) for shape, kind, _ in outputs.values()),
        in_specs=[spaces.get(n, vmem) for n in given],
        out_specs=tuple(space for _, _, space in outputs.values()),
        scratch_shapes=list(scratch.values()),
        compiler_params=params(which),
        name=name,
    )(*given.values())
    return dict(zip(outputs, results))


TABLES = {"cosine": ((SEQ, HEAD_WIDTH), F32), "sine": ((SEQ, HEAD_WIDTH), F32)}
SAVED = {
    "wq_all": ((4, 4, 2, 32, 1152), BF),
    "wo_all": ((4, 2, 64, D), BF),
    "hidden": ((SEQ, D), BF),
    "raw": ((OWN_HEADS + OWN_KV, SEQ, HEAD_WIDTH), BF),
    "query": ((OWN_HEADS, SEQ, HEAD_WIDTH), BF),
    "key": ((OWN_KV, SEQ, HEAD_WIDTH), BF),
    "key_t": ((OWN_KV, HEAD_WIDTH, SEQ), BF),
    "value": ((OWN_KV, SEQ, HEAD_WIDTH), BF),
    "attended_t": ((OWN_HEADS, HEAD_WIDTH, SEQ), BF),
    "log_total": ((OWN_HEADS, 8, SEQ), F32),
}


def heads_of(ref, count, at):
    return jnp.concatenate([ref[h, at] for h in range(count)], axis=1)


def row_tile(r, size):
    return pl.ds(pl.multiple_of(r * size, size), size)


def from_to(half, low, split, high):
    return pl.ds(low, split - low) if half == 0 else pl.ds(split, high - split)


def not_here(condition, other, coordinate):
    return jnp.logical_not(jnp.logical_and(condition, coordinate == other))


def pack_gateup(w, out):
    for k in range(2):
        for side in range(2):
            pieces = [w[:, FF * side + 96 * n : FF * side + 96 * n + 96] for n in range(k, 32, 2)]
            columns = jnp.concatenate(pieces, axis=1)
            for b in range(3):
                out[k, b, :, 512 * side : 512 * side + 512] = columns[:, 512 * b : 512 * b + 512]


def unpack_gateup(packed):
    sides = []
    for side in range(2):
        cores = [
            jnp.concatenate([packed[k, b, :, 512 * side : 512 * side + 512] for b in range(3)], axis=1)
            for k in range(2)
        ]
        sides += [cores[n % 2][:, 96 * (n // 2) : 96 * (n // 2) + 96] for n in range(32)]
    return jnp.concatenate(sides, axis=1)


def forward_kernel(r):
    place = Place()
    z, x, k, y = (place[a] for a in "zxky")
    near = neighbours(place, "xyzk")
    diagonal = z == y
    plane = [theirs_at(place, *o) for o in THEIRS]
    greet(near + [place.peer("y", 2)] + plane)
    for other in range(4):

        @pl.when(not_here(diagonal, other, y))
        def _():
            greet([place.device(z=y, y=jnp.int32(other))])

    for i in range(4):
        r.q_send[i, :, 0:512] = r.wq[:, 512 * i : 512 * i + 512]
        r.q_send[i, :, 512:768] = r.wq[:, 2048 + 256 * i : 2304 + 256 * i]
        r.q_send[i, :, 768:1024] = r.wq[:, 3072 + 256 * i : 3328 + 256 * i]
        r.q_send[i, :, 1024:1152] = jnp.zeros((8, 128), F32)
        r.q_send[i, 0:1, 1024:1042] = r.gains[...]
    pack_gateup(r.wgu, r.packed)
    tables = [
        pltpu.make_async_copy(getattr(r, "in_" + n), getattr(r, n), r.tables.at[i])
        for i, n in enumerate(("cosine", "sine", "spread"))
    ]
    for copy in tables:
        copy.start()
    r.q_recv[y] = r.q_send[y]
    r.o_send[...] = r.wo[...].astype(BF)
    r.tok_all[pl.ds(2 * y, 2)] = r.tok[...].reshape(2, BLOCK, D)
    await_greetings(len(near) + 1 + len(plane) + jnp.where(diagonal, 3, 4))

    g_prep = remote(r.packed.at[1 - k], r.g_recv, r.pair.at[0], r.pair.at[1], place.sibling())
    g_prep.start()
    q_prep = [
        remote(r.q_send.at[place.moved("y", n)], r.q_recv.at[y], r.qp_s.at[n], r.qp_r.at[y], place.peer("y", n))
        for n in (1, 3, 2)
    ]
    for copy in q_prep:
        copy.start()

    def o_slot(source):
        return r.wo_all.at[x, k, row_tile(source, 16)]

    for other in range(4):

        @pl.when(not_here(diagonal, other, z))
        def _():
            remote(r.o_send, o_slot(y), r.op_s.at[other], r.op_r.at[y], place.device(z=jnp.int32(other), y=z)).start()

    @pl.when(diagonal)
    def _():
        r.wo_all[x, k, row_tile(y, 16)] = r.o_send[...]

    cot_copy = remote(r.cot, r.out_cot_pair.at[pl.ds(ROWS, ROWS)], r.pair.at[2], r.pair.at[3], place.sibling())
    cot_copy.start()
    cot_own = pltpu.make_async_copy(r.cot, r.out_cot_pair.at[pl.ds(0, ROWS)], r.pair.at[6])
    cot_own.start()

    g_prep.wait_recv()
    g_own, g_other, lower = r.packed[k], r.g_recv[...], k == 0
    both = jnp.concatenate([jnp.where(lower, g_own, g_other), jnp.where(lower, g_other, g_own)], axis=1)
    r.g_y[y] = both[0:2].reshape(32, D).astype(BF)
    r.w_c[y, 4 * z + x] = both[2].astype(BF)
    c_x = Gather(place, "x", lambda i, h: r.w_c.at[y, 4 * z + i, :, pl.ds(512 * h, 512)], (r.cx_s, r.cx_r))
    c_z = Gather(place, "z", lambda i, h: r.w_c.at[y, pl.ds(4 * i + 2 * h, 2)], (r.cz_s, r.cz_r))
    c_y = Gather(place, "y", lambda i, h: r.w_c.at[i, pl.ds(8 * h, 8)], (r.cy_s, r.cy_r))
    r.d_y[y] = r.wd[...]
    g_ring = Gather(place, "y", lambda i, h: r.g_y.at[i, pl.ds(16 * h, 16)], (r.gy_s, r.gy_r))
    d_ring = Gather(place, "y", lambda i, h: r.d_y.at[i, from_to(h, 0, 16, 24)], (r.dy_s, r.dy_r))
    g_ring.start()
    d_ring.start()
    c_x.start()

    for n in (1, 3, 2):
        source = place.moved("y", n)
        remote(r.q_send.at[0], r.q_recv.at[source], r.qp_s.at[n], r.qp_r.at[source], place.peer("y", n)).wait_recv()
    r.wq_all[z, x, k] = r.q_recv[...].reshape(32, 1152).astype(BF)
    q_direct = []
    for n, (dz, dx) in enumerate(THEIRS):
        unit = r.wq_all.at[z, x, k]
        q_direct.append(remote(unit, unit, r.qd_s.at[n], r.qd_r.at[4 * z + x], theirs_at(place, dz, dx)))
    for copy in q_direct:
        copy.start()

    def q_core(at_z, at_x, core):
        unit, which = r.wq_all.at[at_z, at_x, core], 4 * at_z + at_x
        return remote(unit, unit, r.qc_s.at[which], r.qc_r.at[which], place.sibling())

    q_core(z, x, k).start()
    tokens = Gather(place, "y", lambda i, h: r.tok_all.at[2 * i + h], (r.t_s, r.t_r))
    tokens.start()

    for other in range(4):

        @pl.when(not_here(diagonal, other, y))
        def _():
            remote(r.o_send, o_slot(other), r.op_s.at[0], r.op_r.at[other], place.device(z=y, y=jnp.int32(other))).wait_recv()

    o_x = Gather(place, "x", lambda i, h: r.wo_all.at[i, k, pl.ds(32 * h, 32)], (r.ox_s, r.ox_r))
    o_x.start()
    g_ring.forward()
    d_ring.forward()
    c_x.forward()
    c_x.finish()
    c_z.start()
    o_x.forward()
    g_ring.finish()
    d_ring.finish()

    for b in range(2):
        pieces = [r.g_y[c, 16 * b : 16 * b + 16].astype(F32) for c in range(4)]
        for core_row in range(2):
            rows = jnp.concatenate([piece[8 * core_row : 8 * core_row + 8] for piece in pieces], axis=0)
            at = 64 * b + 32 * core_row
            r.unit[at : at + 32] = rows.astype(BF)
    r.unit[DOWN:UNIT] = r.d_y[...].reshape(96, D).astype(BF)
    w_all = r.out_w_all
    u_own = pltpu.make_async_copy(r.unit, w_all.at[z, x], r.pair.at[4])
    u_own.start()
    a_one = Gather(
        place, "x", lambda i, h: w_all.at[z, i, from_to(h, 0, 64, PART_A)], (r.a1_s, r.a1_r),
        own=lambda h: r.unit.at[from_to(h, 0, 64, PART_A)],
    )
    b_one = Gather(
        place, "z", lambda i, h: w_all.at[i, x, from_to(h, PART_A, 160, UNIT)], (r.b1_s, r.b1_r),
        own=lambda h: r.unit.at[from_to(h, PART_A, 160, UNIT)],
    )
    tokens.forward()
    c_z.forward()
    o_x.finish()
    o_core = remote(r.wo_all.at[:, k], r.wo_all.at[:, k], r.core.at[0], r.core.at[1], place.sibling())
    o_core.start()
    for dz, dx in sorted(THEIRS, key=lambda o: min(o[0], 4 - o[0]) + min(o[1], 4 - o[1])):
        at_z, at_x = place.moved("z", dz), place.moved("x", dx)
        other = r.wq_all.at[at_z, at_x, k]
        remote(other, other, r.qd_s.at[0], r.qd_r.at[4 * at_z + at_x], theirs_at(place, dz, dx)).wait_recv()
        q_core(at_z, at_x, k).start()
    a_one.start()
    b_one.start()
    tokens.finish()
    a_one.forward()
    b_one.forward()
    a_one.finish()
    b_one.finish()
    u_own.wait()
    a_two = Gather(place, "z", lambda i, h: w_all.at[i, pl.ds(2 * h, 2), pl.ds(0, PART_A)], (r.a2_s, r.a2_r))
    b_two = Gather(place, "x", lambda i, h: w_all.at[pl.ds(2 * h, 2), i, pl.ds(PART_A, UNIT - PART_A)], (r.b2_s, r.b2_r))
    a_two.start()
    b_two.start()
    c_z.finish()
    c_y.start()
    remote(r.wo_all.at[:, 1 - k], r.wo_all.at[:, 1 - k], r.core.at[0], r.core.at[1], place.sibling()).wait_recv()
    for at_z in range(4):
        for at_x in range(4):
            q_core(at_z, at_x, 1 - k).wait_recv()

    for copy in tables:
        copy.wait()

    lanes = r.wq_all[:, :, :, :, D:1152].reshape(128, 8, 128).astype(F32)
    spread = dot_nn(jnp.sum(lanes, axis=1).astype(BF), r.spread[...])
    owner = lax.broadcasted_iota(jnp.int32, (128, GAINS), 0) * 18
    spot = lax.broadcasted_iota(jnp.int32, (128, GAINS), 1)
    mine = jnp.logical_and(spot >= owner, spot < owner + 18)
    r.out_gain_row[...] = jnp.sum(jnp.where(mine, spread, 0.0), axis=0, keepdims=True)
    gain = r.out_gain_row
    project(r, gain.at[:, 0:D], gain.at[:, 2 * D : 2 * D + 128], gain.at[:, 2 * D + 128 : GAINS])
    attend(r, 0, 2)
    c_y.forward()
    attend(r, 2, 4)

    wo = r.wo_all[...].reshape(OWN_HEADS * HEAD_WIDTH, D)

    @pl.loop(0, 4)
    def _(i):
        rows = jnp.concatenate(
            [heads_of(r.attended, OWN_HEADS, r.span[2 * i + n]) for n in range(2)], axis=0
        )
        r.terms[i] = dot_nn(rows, wo).astype(BF)

    reduce = Scatter(
        place, "y", lambda i, h: r.terms.at[i, pl.ds(128 * h, 128)],
        [r.boxes.at[n] for n in range(6)], (r.y_s, r.y_r),
    )
    reduce.start()
    a_two.forward()
    b_two.forward()
    saves = [
        pltpu.make_async_copy(getattr(r, n), getattr(r, "out_" + n), r.save.at[i]) for i, n in enumerate(SAVED)
    ]
    for copy in saves:
        copy.start()
    c_y.finish()

    @pl.loop(0, 16)
    def _(j):
        pieces = [r.w_c[c, j].astype(F32) for c in range(4)]
        rows = [piece[8 * core_row : 8 * core_row + 8] for core_row in range(2) for piece in pieces]
        r.w_two[j] = jnp.concatenate(rows, axis=0).astype(BF)

    two_copy = pltpu.make_async_copy(r.w_two, r.out_w_two, r.pair.at[5])
    two_copy.start()
    reduce.forward()
    reduce.finish(lambda h: r.total.at[pl.ds(128 * h, 128)])

    hid_copies = []
    for half in range(2):

        @pl.loop(0, BLOCK // 32)
        def _(t):
            at = row_tile(4 * half + t, 32)
            rows = r.tok[at].astype(F32) + r.total[at]
            r.total[at] = rows
            scale = lax.rsqrt(jnp.mean(rows * rows, axis=-1, keepdims=True) + norm_eps)
            r.hid[at] = (rows * scale * gain[:, D : 2 * D]).astype(BF)

        here, there = pl.ds(BLOCK * half, BLOCK), pl.ds(ROWS + BLOCK * half, BLOCK)
        hid_copies += [
            remote(r.hid.at[here], r.out_hidden_pair.at[there], r.hid_sem.at[4 * half], r.hid_sem.at[4 * half + 1], place.sibling()),
            pltpu.make_async_copy(r.hid.at[here], r.out_hidden_pair.at[here], r.hid_sem.at[4 * half + 2]),
            pltpu.make_async_copy(r.total.at[here], r.out_middle.at[here], r.hid_sem.at[4 * half + 3]),
        ]
        for copy in hid_copies[3 * half :]:
            copy.start()

    a_two.finish()
    b_two.finish()
    two_copy.wait()
    for copy in saves:
        copy.wait()
    for copy in q_prep + q_direct + [g_prep, o_core]:
        copy.wait_send()
    for at_z in range(4):
        for at_x in range(4):
            q_core(at_z, at_x, k).wait_send()
    cot_copy.wait()
    cot_own.wait()
    for copy in hid_copies:
        copy.wait()
    for other in range(4):

        @pl.when(not_here(diagonal, other, z))
        def _():
            remote(r.o_send, o_slot(y), r.op_s.at[other], r.op_r.at[y], place.device(z=jnp.int32(other), y=z)).wait_send()


def rings(*names):
    return {f"{name}_{end}": dma(6) for name in names for end in "sr"}


def forward_step(**given):
    late = {**TABLES, "spread": ((128, GAINS), BF)}
    given = {("in_" + n if n in late else n): v for n, v in given.items()}
    outputs = {
        "middle": ((ROWS, D), F32, hbm),
        "hidden_pair": ((2 * ROWS, D), BF, hbm),
        "cot_pair": ((2 * ROWS, D), BF, hbm),
        "gain_row": ((1, GAINS), F32, vmem),
        "w_all": ((4, 4, UNIT, D), BF, hbm),
        "w_two": ((16, 64, D), BF, hbm),
        **{n: (*what, hbm) for n, what in SAVED.items()},
    }
    scratch = {
        "q_send": pltpu.VMEM((4, 8, 1152), F32),
        "q_recv": pltpu.VMEM((4, 8, 1152), F32),
        "o_send": pltpu.VMEM((16, D), BF),
        "packed": pltpu.VMEM((2, 3, 8, D), F32),
        "g_recv": pltpu.VMEM((3, 8, D), F32),
        "g_y": pltpu.VMEM((4, 32, D), BF),
        "w_c": pltpu.VMEM((4, 16, 16, D), BF),
        "w_two": pltpu.VMEM((16, 64, D), BF),
        "d_y": pltpu.VMEM((4, 24, D), F32),
        "unit": pltpu.VMEM((UNIT, D), BF),
        "tok_all": pltpu.VMEM((8, BLOCK, D), BF),
        "value_t": pltpu.VMEM((OWN_KV, HEAD_WIDTH, SEQ), BF),
        "attended": pltpu.VMEM((OWN_HEADS, 8, BLOCK, HEAD_WIDTH), BF),
        "terms": pltpu.VMEM((4, ROWS, D), BF),
        "boxes": pltpu.VMEM((6, BLOCK, D), BF),
        "total": pltpu.VMEM((ROWS, D), F32),
        **{n: pltpu.VMEM(*what) for n, what in SAVED.items()},
        "hid": pltpu.VMEM((ROWS, D), BF),
        **{n: pltpu.VMEM(*what) for n, what in late.items()},
        "tables": dma(3),
        "pair": dma(7),
        "core": dma(2),
        "hid_sem": dma(8),
        **{"qc_s": dma(16), "qc_r": dma(16)},
        "save": dma(len(SAVED)),
        **{n: dma(4) for n in ("qp_s", "qp_r", "op_s", "op_r")},
        **{"qd_s": dma(15), "qd_r": dma(16)},
        **rings("gy", "dy", "cx", "cz", "cy", "ox", "t", "a1", "b1", "a2", "b2", "y"),
    }
    spaces = {"span": smem, **{"in_" + n: hbm for n in late}}
    return named_call(forward_kernel, 1, "forward_attention", given, spaces, outputs, scratch)


def sum_everywhere(r, place):
    z, x, k, y = (place[a] for a in "zxky")

    def stage(source, slots, send, recv, offsets, device, me, slot_of):
        slots[me] = source[...]
        copies = [
            remote(source, slots.at[me], send.at[n], recv.at[me], device(*offset))
            for n, offset in enumerate(offsets)
        ]
        for copy in copies:
            copy.start()
        for n, offset in enumerate(offsets):
            slot = slot_of(*offset)
            remote(source, slots.at[slot], send.at[n], recv.at[slot], device(*offset)).wait_recv()
        for copy in copies:
            copy.wait_send()

    stage(r.value_row, r.first, r.s1_s, r.s1_r, OURS, lambda *o: ours_at(place, *o), y * 2 + k,
          lambda dy, dk: place.moved("y", dy) * 2 + lax.rem(k + dk, 2))
    r.held[...] = jnp.sum(r.first[...], axis=0)
    stage(r.held, r.second, r.s2_s, r.s2_r, THEIRS, lambda *o: theirs_at(place, *o), z * 4 + x,
          lambda dz, dx: place.moved("z", dz) * 4 + place.moved("x", dx))
    r.out_sums[...] = jnp.sum(r.second[...], axis=0)


OURS = [(dy, dk) for dy in range(4) for dk in range(2) if (dy, dk) != (0, 0)]
THEIRS = [(dz, dx) for dz in range(4) for dx in range(4) if (dz, dx) != (0, 0)]


def ours_at(place, dy, dk):
    return place.device(y=place.moved("y", dy), k=lax.rem(place["k"] + dk, 2))


def theirs_at(place, dz, dx):
    return place.device(z=place.moved("z", dz), x=place.moved("x", dx))


def by_eights(rows):
    return jnp.sum(rows.reshape(rows.shape[0] // 8, 8, D), axis=0)


def back_through_norm(r, gain, half):
    @pl.loop(0, BLOCK // 32)
    def _(t):
        at = row_tile(4 * half + t, 32)
        rows = r.middle[at]
        scale = lax.rsqrt(jnp.mean(rows * rows, axis=-1, keepdims=True) + norm_eps)
        normed = rows * scale
        incoming = r.grad_rows[at] + r.dh_box[at].astype(F32)
        r.mlp_gain[...] += by_eights(incoming * normed)
        incoming = incoming * gain[:, D : 2 * D]
        mean = jnp.mean(incoming * normed, axis=-1, keepdims=True)
        d_mid = r.cot[at].astype(F32) + scale * (incoming - normed * mean)
        r.grad_rows[at] = d_mid
        r.own[at] = d_mid.astype(BF)


def back_to_input(r, gain):
    r.attn_gain[...] = jnp.zeros_like(r.attn_gain)

    @pl.loop(0, ROWS // 32)
    def _(t):
        at = row_tile(t, 32)
        rows = r.tok[at].astype(F32)
        scale = lax.rsqrt(jnp.mean(rows * rows, axis=-1, keepdims=True) + norm_eps)
        normed = rows * scale
        incoming = r.dh_total[at]
        r.attn_gain[...] += by_eights(incoming * normed)
        incoming = incoming * gain[:, 0:D]
        mean = jnp.mean(incoming * normed, axis=-1, keepdims=True)
        r.grad_rows[at] += scale * (incoming - normed * mean)


def back_to_projections(r, gain):
    plain = HEAD_WIDTH ** (-0.5)
    r.head_gain[...] = jnp.zeros_like(r.head_gain)

    @pl.loop(0, SEQ // TILE)
    def _(t):
        at = row_tile(t, TILE)
        cos_t, sin_t = r.cosine[at], r.sine[at]
        for h in range(OWN_HEADS + OWN_KV):
            mine = h < OWN_HEADS
            d_rows = r.d_query[h, at] if mine else r.d_key[h - OWN_HEADS, at] * plain
            first = 2 * D if mine else 2 * D + HEAD_WIDTH
            d_gained = d_rows * cos_t - turn(d_rows) * sin_t
            normed, scale = head_norm(r.raw[h, at].astype(F32))
            product = d_gained * normed
            r.head_gain[0 if mine else 1] += jnp.sum(product.reshape(TILE // 8, 8, HEAD_WIDTH), axis=0)
            incoming = d_gained * gain[:, first : first + HEAD_WIDTH]
            mean = jnp.mean(incoming * normed, axis=-1, keepdims=True)
            r.d_proj[pl.ds(2 * t, 2), :, 128 * h : 128 * h + 128] = (
                (scale * (incoming - normed * mean)).astype(BF).reshape(2, BLOCK, HEAD_WIDTH)
            )
        for h in range(OWN_KV):
            r.d_proj[pl.ds(2 * t, 2), :, 768 + 128 * h : 896 + 128 * h] = (
                r.d_value[h, at].astype(BF).reshape(2, BLOCK, HEAD_WIDTH)
            )


def block_weights(r, b):
    if b == 2:
        return r.c[...].reshape(D, D)
    return r.w[:, :, 64 * b : 64 * b + 64].reshape(D, D)


def block_down(r, b):
    return r.w[:, :, DOWN:UNIT].reshape(FF // 2, D)[512 * b : 512 * b + 512]


def product_rows(r, first, last):
    parts = []
    if first < D:
        parts.append(r.d_o[...].reshape(2 * ROWS, D)[:, first : min(last, D)])
    if last > D:
        parts.append(r.d_q[2:4].reshape(2 * ROWS, D)[:, max(first, D) - D : last - D])
    return parts[0] if len(parts) == 1 else jnp.concatenate(parts, axis=1)


def d_gate_up_rows(r, b, t):
    if b < 2:
        return r.d_proj[pl.ds(4 * b + 2 * t, 2)].reshape(ROWS, D)
    return r.d_q[t].reshape(ROWS, D)


def feed_forward(r, w_loads):
    w_loads[0].wait()
    w_loads[1].wait()
    for b in range(3):
        if b:
            w_loads[1 + b].wait()
        weights, down = block_weights(r, b), block_down(r, b)

        @pl.loop(0, 2)
        def _(t):
            gate_up = dot_nn(r.hidden[row_tile(t, ROWS)], weights)
            d_product = dot_nt(r.hidden[row_tile(2 + t, ROWS)], down)
            gate, up = gate_up[:, :512], gate_up[:, 512:]
            sigmoid = 1.0 / (1.0 + jnp.exp(-gate))
            active = gate * sigmoid
            product = (active * up).astype(BF).reshape(4, 64, 512)
            if b < 2:
                r.d_o[pl.ds(2 * t, 2), :, :, 512 * b : 512 * b + 512] = product.reshape(2, 2, 64, 512)
            else:
                r.d_q[2 + t, :, :, :, 0:512] = product.reshape(4, 2, 32, 512)
            d_gate = d_product * up * sigmoid * (1.0 + gate * (1.0 - sigmoid))
            d_both = jnp.concatenate([d_gate, d_product * active], axis=1).astype(BF)
            if b < 2:
                r.d_proj[pl.ds(4 * b + 2 * t, 2)] = d_both.reshape(2, BLOCK, D)
            else:
                r.d_q[t] = d_both.reshape(4, 2, 32, D)


def feed_forward_inputs(r):
    def half(t):
        total = dot_nt(d_gate_up_rows(r, 0, t), block_weights(r, 0))
        for b in (1, 2):
            total = total + dot_nt(d_gate_up_rows(r, b, t), block_weights(r, b))
        return total

    r.dh_sib[...] = half(1).astype(BF)
    r.grad_rows[...] = half(0)


def feed_forward_outputs(r):
    down = r.w[:, :, DOWN:UNIT].reshape(FF // 2, D)

    def half(t):
        first = dot_nn(r.d_o[2 * t : 2 * t + 2].reshape(ROWS, D), down[:D])
        return first + dot_nn(r.d_q[2 + t, :, :, :, 0:512].reshape(ROWS, 512), down[D:])

    r.out_sib[...] = half(1).astype(BF)
    r.dh_total[...] = half(0)


def dot_tn(left, right):
    return lax.dot_general(left, right, (((0,), (0,)), ((), ())), preferred_element_type=F32)


def down_gradients(r):
    cot = r.hidden[2 * ROWS : SEQ]
    for i in range(4):
        left = product_rows(r, 384 * i, 384 * i + 384)
        r.w[i, :, DOWN:UNIT] = dot_tn(left, cot).astype(BF).reshape(4, 96, D)


def block_gradients(r, b):
    d_both = jnp.concatenate([d_gate_up_rows(r, b, 0), d_gate_up_rows(r, b, 1)], axis=0)

    @pl.loop(0, 4)
    def _(i):
        columns = pl.ds(pl.multiple_of(i * 256, 256), 256)
        rows = dot_tn(r.hidden[0 : 2 * ROWS, columns], d_both)
        if b < 2:
            r.w[i, :, 64 * b : 64 * b + 64] = rows.astype(BF).reshape(4, 64, D)
        else:
            rows = rows.reshape(4, 2, 4, 8, D)
            for c in range(4):
                r.c[c, pl.ds(4 * i, 4)] = rows[:, :, c].reshape(4, 16, D).astype(BF)


def backward_kernel(r):
    place = Place()
    z, x, k, y = (place[a] for a in "zxky")
    diagonal = z == y
    gain = r.gain_row
    near = neighbours(place, "xyzk")
    everyone = [ours_at(place, *o) for o in OURS] + [theirs_at(place, *o) for o in THEIRS]
    greet(near + everyone)
    for other in range(4):

        @pl.when(not_here(diagonal, other, z))
        def _():
            greet([place.device(z=jnp.int32(other), y=z)])

    loads = {
        n: pltpu.make_async_copy(getattr(r, "in_" + n), getattr(r, n), r.load.at[i]) for i, n in enumerate([*SAVED, *TABLES, "middle"])
    }
    pair_loads = [
        pltpu.make_async_copy(pair, r.hidden.at[rows], r.w_sem.at[4 + i])
        for i, (pair, rows) in enumerate([(r.hidden_pair, pl.ds(0, 2 * ROWS)), (r.cot_pair, pl.ds(2 * ROWS, 2 * ROWS))])
    ]
    w_loads = [
        pltpu.make_async_copy(r.w_all.at[:, :, rows], r.w.at[:, :, rows], r.w_sem.at[i])
        for i, rows in enumerate([pl.ds(0, 64), pl.ds(DOWN, 96), pl.ds(64, 64)])
    ]
    w_loads.append(pltpu.make_async_copy(r.w_two, r.c, r.w_sem.at[3]))
    hidden_load, middle_load = loads.pop("hidden"), loads.pop("middle")
    for copy in pair_loads + w_loads + [middle_load]:
        copy.start()

    def a_part(i, h):
        return r.w.at[i, pl.ds(2 * h, 2), pl.ds(0, PART_A)]

    def b_part(i, h):
        return r.w.at[pl.ds(2 * h, 2), i, pl.ds(PART_A, UNIT - PART_A)]

    a_one = Scatter(place, "z", a_part, [r.a_box.at[n] for n in range(6)], (r.a1_s, r.a1_r))
    b_one = Scatter(place, "x", b_part, [r.b_box.at[n] for n in range(6)], (r.b1_s, r.b1_r))
    dh_copy = remote(r.dh_sib, r.dh_box, r.core.at[0], r.core.at[1], place.sibling())
    out_copy = remote(r.out_sib, r.out_box, r.core.at[2], r.core.at[3], place.sibling())
    for copy in pair_loads:
        copy.wait()
    feed_forward(r, w_loads)
    for copy in loads.values():
        copy.start()
    feed_forward_inputs(r)
    await_greetings(len(near) + len(everyone) + jnp.where(diagonal, 3, 4))
    dh_copy.start()
    feed_forward_outputs(r)
    out_copy.start()
    down_gradients(r)
    dh_copy.wait_recv()
    ring = Gather(
        place, "y", lambda i, h: r.d_attn_all.at[2 * i + h], (r.t_s, r.t_r),
        own=lambda h: r.own.at[pl.ds(BLOCK * h, BLOCK)],
    )
    middle_load.wait()
    r.mlp_gain[...] = jnp.zeros_like(r.mlp_gain)
    for half in range(2):
        back_through_norm(r, gain, half)
        ring.start([half])
    r.d_attn_all[pl.ds(2 * y, 2)] = r.own[...].reshape(2, BLOCK, D)
    block_gradients(r, 1)
    b_one.start()
    block_gradients(r, 0)
    a_one.start()
    block_gradients(r, 2)
    hidden_load.start()
    out_copy.wait_recv()

    @pl.loop(0, ROWS // 16)
    def _(t):
        at = row_tile(t, 16)
        r.layer_rows[at] = (r.middle[at] + r.dh_total[at] + r.out_box[at].astype(F32)).astype(BF)

    layer_copy = pltpu.make_async_copy(r.layer_rows, r.out_layer_out, r.w_sem.at[6])
    layer_copy.start()

    for copy in [hidden_load, *loads.values()]:
        copy.wait()
    r.d_key[...] = jnp.zeros_like(r.d_key)
    r.d_value[...] = jnp.zeros_like(r.d_value)
    ring.forward()
    ring.finish()
    c_y = Scatter(
        place, "y", lambda i, h: r.c.at[i, pl.ds(8 * h, 8)],
        [r.cy_box.at[n] for n in range(6)], (r.cy_s, r.cy_r),
    )
    c_z = Scatter(
        place, "z", lambda i, h: r.c.at[y, pl.ds(4 * i + 2 * h, 2)],
        [r.cz_box.at[n] for n in range(6)], (r.cz_s, r.cz_r),
    )
    c_x = Scatter(
        place, "x", lambda i, h: r.c.at[y, 4 * z + i, :, pl.ds(512 * h, 512)],
        [r.cx_box.at[n] for n in range(6)], (r.cx_s, r.cx_r),
    )
    c_y.start()

    wo = r.wo_all[...].reshape(OWN_HEADS * HEAD_WIDTH, D)

    @pl.loop(0, SEQ // TILE)
    def _(t):
        at = row_tile(t, TILE)
        rows = pair_of(r.d_attn_all, r.span, t)
        r.d_q[t] = rows.reshape(4, 2, 32, D)
        both = dot_nt(rows, wo)
        for h in range(OWN_HEADS):
            r.d_attended[h, at] = both[:, 128 * h : 128 * h + 128].astype(BF)

    d_sorted = r.d_q[...].reshape(SEQ, D)

    @pl.loop(0, 4)
    def _(i):
        r.d_o[i] = dot_nn(r.attended_t[i], d_sorted).astype(BF).reshape(2, 64, D)

    o_core = remote(r.d_o.at[:, 1 - k], r.o_box, r.core.at[4], r.core.at[5], place.sibling())
    o_core.start()
    attend_back(r, 0, 2)
    c_y.forward()
    a_one.forward()
    b_one.forward()
    o_core.wait_recv()

    @pl.loop(0, 4)
    def _(i):
        add_rows(r.o_box.at[i], [r.o_box.at[i], r.d_o.at[i, k]])

    o_x = Scatter(
        place, "x", lambda i, h: r.o_box.at[i, pl.ds(32 * h, 32)],
        [r.ox_box.at[n] for n in range(6)], (r.ox_s, r.ox_r),
    )
    o_x.start()
    attend_back(r, 2, 4)
    c_y.finish(lambda h: r.c.at[y, pl.ds(8 * h, 8)])
    c_z.start()
    o_x.forward()
    back_to_projections(r, gain)

    wq = r.wq_all[:, :, :, :, 0:D].reshape(D, D)

    @pl.loop(0, 4)
    def _(i):
        rows = jnp.concatenate([r.d_proj[r.span[2 * i + n]] for n in range(2)], axis=0)
        r.d_attn_all[pl.ds(2 * i, 2)] = dot_nt(rows, wq).astype(BF).reshape(2, BLOCK, D)

    dh_ring = Scatter(
        place, "y", lambda i, h: r.d_attn_all.at[2 * i + h],
        [r.y_box.at[n] for n in range(6)], (r.y_s, r.y_r),
    )
    dh_ring.start()
    a_one.finish(lambda h: a_part(z, h))
    b_one.finish(lambda h: b_part(x, h))
    a_two = Scatter(
        place, "x", lambda i, h: r.w.at[z, i, from_to(h, 0, 64, PART_A)],
        [r.a_box2.at[n, pl.ds(0, 64 if n in (0, 3, 4) else 48)] for n in range(6)], (r.a2_s, r.a2_r),
    )
    b_two = Scatter(
        place, "z", lambda i, h: r.w.at[i, x, from_to(h, PART_A, 160, UNIT)],
        [r.b_box2.at[n, pl.ds(0, 48 if n in (0, 3, 4) else 64)] for n in range(6)], (r.b2_s, r.b2_r),
    )
    a_two.start()
    b_two.start()

    d_proj = r.d_proj[...].reshape(SEQ, D)
    planes = [place.moved("z", dz) for dz in (1, 2, 3, 0)]
    q_core = [
        remote(r.d_q.at[plane, :, 1 - k], r.q_box.at[plane], r.qk_s.at[n], r.qk_r.at[n], place.sibling())
        for n, plane in enumerate(planes)
    ]

    @pl.loop(0, 4)
    def _(n):
        plane = place.moved("z", n + 1)
        left = r.hidden[:, row_tile(plane, 256)]
        r.d_q[plane] = dot_tn(left, d_proj).astype(BF).reshape(4, 2, 32, D)
        remote(r.d_q.at[plane, :, 1 - k], r.q_box.at[plane], r.qk_s.at[n], r.qk_r.at[n], place.sibling()).start()

    q_direct = []
    for n, plane in enumerate(planes):
        q_core[n].wait_recv()

        @pl.loop(0, 4)
        def _(j):
            add_rows(r.q_box.at[plane, j], [r.q_box.at[plane, j], r.d_q.at[plane, j, k]])

        for dx in range(1 if n == 3 else 0, 4):
            to = place.moved("x", dx)
            q_direct.append(
                remote(
                    r.q_box.at[plane, to], r.q_slots.at[4 * z + x], r.qd_s.at[len(q_direct)], r.qd_r.at[4 * z + x],
                    place.device(z=plane, x=to),
                )
            )
            q_direct[-1].start()
    r.q_slots[4 * z + x] = r.q_box[z, x]
    dh_ring.forward()
    c_z.forward()
    a_two.forward()
    b_two.forward()
    c_z.finish(lambda h: r.c.at[y, pl.ds(4 * z + 2 * h, 2)])
    c_x.start()
    o_x.finish(lambda h: r.o_two.at[pl.ds(32 * h, 32)])

    def o_target(other):
        return place.device(z=y, y=jnp.int32(other))

    for other in range(4):
        piece = r.o_two.at[pl.ds(16 * other, 16)]

        @pl.when(not_here(diagonal, other, y))
        def _():
            remote(piece, r.o_slots.at[z], r.oy_s.at[other], r.oy_r.at[z], o_target(other)).start()

    @pl.when(diagonal)
    def _():
        r.o_slots[z] = r.o_two[row_tile(y, 16)]

    c_x.forward()

    a_two.finish(lambda h: r.total.at[from_to(h, 0, 64, PART_A)])
    b_two.finish(lambda h: r.total.at[from_to(h, PART_A, 160, UNIT)])
    for c in range(4):
        for b in range(2):
            at = 64 * b + 8 * c
            rows = jnp.concatenate([r.total[at : at + 8], r.total[at + 32 : at + 40]], axis=0)
            r.g_send[c, 16 * b : 16 * b + 16] = rows.astype(BF)
    r.g_slots[y] = r.g_send[y]

    def down_rows(c):
        return pl.ds(pl.multiple_of(DOWN + 24 * c, 8), 24)

    r.d_slots[y] = r.total[down_rows(y)]
    y_copies = []
    for n in (1, 3, 2):
        to = place.moved("y", n)
        y_copies.append(remote(r.g_send.at[to], r.g_slots.at[y], r.gy_s.at[n], r.gy_r.at[y], place.peer("y", n)))
        y_copies.append(remote(r.total.at[down_rows(to)], r.d_slots.at[y], r.dy_s.at[n], r.dy_r.at[y], place.peer("y", n)))
    for copy in y_copies:
        copy.start()
    c_x.finish(lambda h: r.c_sum.at[:, pl.ds(512 * h, 512)])
    dh_ring.finish(lambda h: r.dh_total.at[pl.ds(BLOCK * h, BLOCK)])
    back_to_input(r, gain)
    grad_copy = pltpu.make_async_copy(r.grad_rows, r.out_input_grad, r.w_sem.at[7])
    grad_copy.start()

    for n in (1, 3, 2):
        source = place.moved("y", n)
        remote(r.g_send.at[0], r.g_slots.at[source], r.gy_s.at[n], r.gy_r.at[source], place.peer("y", n)).wait_recv()
        remote(r.total.at[pl.ds(DOWN, 24)], r.d_slots.at[source], r.dy_s.at[n], r.dy_r.at[source], place.peer("y", n)).wait_recv()
    r.out_d_out[...] = r.d_slots[0] + r.d_slots[1] + r.d_slots[2] + r.d_slots[3]
    summed = r.g_slots[0].astype(F32)
    for c in range(1, 4):
        summed = summed + r.g_slots[c].astype(F32)
    summed = summed.reshape(2, 2, 8, D)
    last = r.c_sum[...].reshape(2, 8, D)
    for n in range(2):
        r.g_sum[n, 0:2] = summed[:, n]
        r.g_sum[n, 2] = last[n]
    r.out_g_out[k] = r.g_sum[k]
    g_core = remote(r.g_sum.at[1 - k], r.out_g_out.at[k], r.core.at[8], r.core.at[9], place.sibling())
    g_core.start()
    for other in range(4):

        @pl.when(not_here(diagonal, other, z))
        def _():
            remote(r.o_two.at[pl.ds(0, 16)], r.o_slots.at[other], r.oy_s.at[0], r.oy_r.at[other], place.device(z=jnp.int32(other), y=z)).wait_recv()

    o_sum = r.o_slots[0].astype(F32)
    for c in range(1, 4):
        o_sum = o_sum + r.o_slots[c].astype(F32)
    r.out_o_out[...] = o_sum

    for dz, dx in THEIRS:
        at = 4 * place.moved("z", dz) + place.moved("x", dx)
        remote(r.q_box.at[0, 0], r.q_slots.at[at], r.qd_s.at[0], r.qd_r.at[at], theirs_at(place, dz, dx)).wait_recv()

    @pl.loop(0, 2)
    def _(t):
        at = row_tile(t, 16)
        total = r.q_slots[0, at].astype(F32)
        for n in range(1, 16):
            total = total + r.q_slots[n, at].astype(F32)
        r.q_three[at] = total

    r.out_q_out[y] = r.q_three[row_tile(y, 8)]
    q_copies = [
        remote(r.q_three.at[row_tile(place.moved("y", n), 8)], r.out_q_out.at[y], r.qy_s.at[n], r.qy_r.at[y], place.peer("y", n))
        for n in (1, 3, 2)
    ]
    for copy in q_copies:
        copy.start()
    squares = jnp.zeros((8, D), F32)
    for part in [r.q_three[8 * c : 8 * c + 8] for c in range(4)] + [r.g_sum[c, b] for c in range(2) for b in range(3)]:
        squares = squares + part * part
    for c in range(2):
        part = r.out_o_out[8 * c : 8 * c + 8]
        squares = squares + part * part
    for c in range(3):
        part = r.out_d_out[8 * c : 8 * c + 8]
        squares = squares + part * part
    attn = jnp.sum(r.attn_gain[...], axis=0, keepdims=True)
    mlp = jnp.sum(r.mlp_gain[...], axis=0, keepdims=True)
    squares = jnp.sum(squares, axis=0, keepdims=True)
    r.value_row[...] = jnp.zeros_like(r.value_row)
    lanes = jnp.zeros((1, 128), F32)
    for c in range(8):
        at = slice(128 * c, 128 * c + 128)
        r.value_row[c : c + 1] = attn[:, at]
        r.value_row[8 + c : 9 + c] = mlp[:, at]
        lanes = lanes + squares[:, at]
    for c in range(2):
        r.value_row[16 + c : 17 + c] = jnp.sum(r.head_gain[c], axis=0, keepdims=True)
    r.value_row[18:19] = lanes
    sum_everywhere(r, place)

    remote(r.g_sum.at[0], r.out_g_out.at[1 - k], r.core.at[8], r.core.at[9], place.sibling()).wait_recv()
    for n in (1, 3, 2):
        source = place.moved("y", n)
        remote(r.q_three.at[pl.ds(0, 8)], r.out_q_out.at[source], r.qy_s.at[n], r.qy_r.at[source], place.peer("y", n)).wait_recv()
    layer_copy.wait()
    grad_copy.wait()
    for copy in [dh_copy, out_copy, o_core, g_core] + y_copies + q_copies + q_core + q_direct:
        copy.wait_send()
    for other in range(4):

        @pl.when(not_here(diagonal, other, y))
        def _():
            remote(r.o_two.at[pl.ds(16 * other, 16)], r.o_slots.at[z], r.oy_s.at[other], r.oy_r.at[z], o_target(other)).wait_send()


def backward_step(**given):
    late = [*SAVED, *TABLES, "middle"]
    given = {("in_" + n if n in late else n): v for n, v in given.items()}
    outputs = {
        "layer_out": ((ROWS, D), BF, hbm),
        "input_grad": ((ROWS, D), F32, hbm),
        "q_out": ((4, 8, D), F32, vmem),
        "o_out": ((16, D), F32, vmem),
        "g_out": ((2, 3, 8, D), F32, vmem),
        "d_out": ((24, D), F32, vmem),
        "sums": ((24, 128), F32, vmem),
    }
    head_rows = (OWN_HEADS, SEQ, HEAD_WIDTH)
    kv_rows = (OWN_KV, SEQ, HEAD_WIDTH)
    scratch = {
        **{n: pltpu.VMEM(*what) for n, what in SAVED.items()},
        "layer_rows": pltpu.VMEM((ROWS, D), BF),
        "grad_rows": pltpu.VMEM((ROWS, D), F32),
        **{n: pltpu.VMEM(*what) for n, what in TABLES.items()},
        "middle": pltpu.VMEM((ROWS, D), F32),
        "out_box": pltpu.VMEM((ROWS, D), BF),
        "dh_box": pltpu.VMEM((ROWS, D), BF),
        "own": pltpu.VMEM((ROWS, D), BF),
        "d_attn_all": pltpu.VMEM((8, BLOCK, D), BF),
        "d_attended": pltpu.VMEM(head_rows, BF),
        "d_query": pltpu.VMEM(head_rows, F32),
        "d_key": pltpu.VMEM(kv_rows, F32),
        "d_value": pltpu.VMEM(kv_rows, F32),
        "d_proj": pltpu.VMEM((8, BLOCK, D), BF),
        "y_box": pltpu.VMEM((6, BLOCK, D), BF),
        "dh_total": pltpu.VMEM((ROWS, D), F32),
        "a_box": pltpu.VMEM((6, 2, PART_A, D), BF),
        "b_box": pltpu.VMEM((6, 2, PART_A, D), BF),
        "w": pltpu.VMEM((4, 4, UNIT, D), BF),
        "out_sib": pltpu.VMEM((ROWS, D), BF),
        "dh_sib": pltpu.VMEM((ROWS, D), BF),
        "a_box2": pltpu.VMEM((6, 64, D), BF),
        "b_box2": pltpu.VMEM((6, 64, D), BF),
        "total": pltpu.VMEM((UNIT, D), F32),
        "g_send": pltpu.VMEM((4, 32, D), BF),
        "g_slots": pltpu.VMEM((4, 32, D), BF),
        "d_slots": pltpu.VMEM((4, 24, D), F32),
        "g_sum": pltpu.VMEM((2, 3, 8, D), F32),
        "d_q": pltpu.VMEM((4, 4, 2, 32, D), BF),
        "d_o": pltpu.VMEM((4, 2, 64, D), BF),
        "q_box": pltpu.VMEM((4, 4, 32, D), BF),
        "q_slots": pltpu.VMEM((16, 32, D), BF),
        "c": pltpu.VMEM((4, 16, 16, D), BF),
        "cy_box": pltpu.VMEM((6, 8, 16, D), BF),
        "cz_box": pltpu.VMEM((6, 2, 16, D), BF),
        "cx_box": pltpu.VMEM((6, 16, 512), BF),
        "c_sum": pltpu.VMEM((16, D), F32),
        "q_three": pltpu.VMEM((32, D), F32),
        "o_box": pltpu.VMEM((4, 64, D), BF),
        "ox_box": pltpu.VMEM((6, 32, D), BF),
        "o_two": pltpu.VMEM((64, D), BF),
        "o_slots": pltpu.VMEM((4, 16, D), BF),
        "mlp_gain": pltpu.VMEM((8, D), F32),
        "attn_gain": pltpu.VMEM((8, D), F32),
        "head_gain": pltpu.VMEM((2, 8, HEAD_WIDTH), F32),
        "value_row": pltpu.VMEM((24, 128), F32),
        "first": pltpu.VMEM((8, 24, 128), F32),
        "second": pltpu.VMEM((16, 24, 128), F32),
        "held": pltpu.VMEM((24, 128), F32),
        "core": dma(10),
        "load": dma(len(late)),
        "w_sem": dma(8),
        **{n: dma(4) for n in ("gy_s", "gy_r", "dy_s", "dy_r", "qy_s", "qy_r", "oy_s", "oy_r")},
        **{"s1_s": dma(7), "s1_r": dma(8), "s2_s": dma(15), "s2_r": dma(16)},
        **{"qd_s": dma(15), "qd_r": dma(16), "qk_s": dma(4), "qk_r": dma(4)},
        **rings("t", "y", "a1", "b1", "a2", "b2", "cx", "cy", "cz", "ox"),
    }
    spaces = {"span": smem, "w_all": hbm, "w_two": hbm, "hidden_pair": hbm, "cot_pair": hbm, **{"in_" + n: hbm for n in late}}
    return named_call(backward_kernel, 2, "backward_attention", given, spaces, outputs, scratch)


def gain_spread():
    return jnp.asarray(np.arange(128)[:, None] == np.arange(GAINS)[None, :] % 18, BF)


def rope_tables():
    middle = HEAD_WIDTH // 2
    frequency = rope_base ** (-(np.arange(middle) * 2.0) / HEAD_WIDTH)
    angle = np.arange(SEQ)[:, None] * frequency[None, :]
    cosine, sine = np.cos(angle), np.sin(angle)
    return (
        jnp.asarray(np.concatenate([cosine, cosine], axis=1), F32),
        jnp.asarray(np.concatenate([-sine, sine], axis=1), F32),
    )


MATRICES = {"qkv": matrix_rate, "out": out_rate, "gateup": matrix_rate, "down": matrix_rate}


def adam_update(weight, first, second, grad, factor, rate, decay):
    clipped = grad * factor
    new_first = beta_one * first + (1.0 - beta_one) * clipped
    new_second = beta_two * second + (1.0 - beta_two) * clipped * clipped
    direction = (
        new_first
        / (1.0 - beta_one**STEP)
        / (jnp.sqrt(new_second / (1.0 - beta_two**STEP)) + adam_eps)
    )
    return (weight - rate * (direction + decay * weight), new_first, new_second)


def update_kernel(r):
    hand_in = [
        pltpu.make_async_copy(r.layer_out, r.layer_rows, r.sems.at[2]),
        pltpu.make_async_copy(r.input_grad, r.grad_rows, r.sems.at[3]),
    ]
    hand_on = [
        pltpu.make_async_copy(r.layer_rows, r.out_layer_out, r.sems.at[0]),
        pltpu.make_async_copy(r.grad_rows, r.out_input_grad, r.sems.at[1]),
    ]
    for copy in hand_in:
        copy.start()
    sums = r.sums[...]
    row = lax.broadcasted_iota(jnp.int32, (24, 128), 0)
    squares = jnp.where(row < 18, sums * sums, jnp.where(row == 18, sums, 0.0))
    norm = jnp.sqrt(jnp.sum(jnp.sum(squares, axis=0, keepdims=True), axis=1, keepdims=True))
    r.out_norm[...] = norm
    factor = jnp.minimum(1.0, clip_at / (norm + 1e-06))

    place = row * 128 + lax.broadcasted_iota(jnp.int32, (24, 128), 1)
    start = (lax.axis_index("dp") * 4 + lax.axis_index("ctx")) * 18
    lane = lax.broadcasted_iota(jnp.int32, (1, 128), 1)
    mine = jnp.zeros((1, 128), F32)
    for n in range(18):
        entry = jnp.sum(jnp.where(place == start + n, sums, 0.0), axis=0, keepdims=True)
        mine = jnp.where(lane == n, jnp.sum(entry, axis=1, keepdims=True), mine)
    grads = {
        "qkv": jnp.concatenate(
            [r.q_out[c, :, 0:512] for c in range(4)]
            + [r.q_out[c, :, 512:768] for c in range(4)]
            + [r.q_out[c, :, 768:1024] for c in range(4)],
            axis=1,
        ),
        "out": r.o_out[...],
        "gateup": unpack_gateup(r.g_out),
        "down": r.d_out[...],
        "gains": mine[:, 0:18],
    }
    for arrived, copy in zip(hand_in, hand_on):
        arrived.wait()
        copy.start()
    for name, grad in grads.items():
        rate, decay = (MATRICES[name], matrix_decay) if name in MATRICES else (gain_rate, 0.0)
        refs = [getattr(r, kind + name) for kind in ("w_", "first_", "second_")]
        news = adam_update(*[ref[...] for ref in refs], grad, factor, rate, decay)
        for kind, new in zip(("w_", "first_", "second_"), news):
            getattr(r, "out_" + kind + name)[...] = new
    for copy in hand_on:
        copy.wait()


def update_step(**given):
    outputs = {
        "layer_out": ((ROWS, D), BF, hbm),
        "input_grad": ((ROWS, D), F32, hbm),
        "norm": ((1, 1), F32, vmem),
        **{n: (v.shape, F32, vmem) for n, v in given.items() if n.split("_")[0] in ("w", "first", "second")},
    }
    return named_call(
        update_kernel, None, "update", given, {"layer_out": hbm, "input_grad": hbm}, outputs,
        {"layer_rows": pltpu.VMEM((ROWS, D), BF), "grad_rows": pltpu.VMEM((ROWS, D), F32), "sems": dma(4)},
    )


def body(
    tokens, cotangent, span_order,
    w_qkv, w_out, w_gateup, w_down, gains,
    first_qkv, first_out, first_gateup, first_down, first_gains,
    second_qkv, second_out, second_gateup, second_down, second_gains,
):
    cosine, sine = rope_tables()
    fwd = forward_step(
        span=span_order, tok=tokens, cot=cotangent, wq=w_qkv, wo=w_out, wgu=w_gateup, wd=w_down,
        gains=gains[None, :], spread=gain_spread(), cosine=cosine, sine=sine,
    )
    bwd = backward_step(
        span=span_order, tok=tokens, cot=cotangent, middle=fwd["middle"],
        gain_row=fwd["gain_row"], cosine=cosine, sine=sine,
        hidden_pair=fwd["hidden_pair"], cot_pair=fwd["cot_pair"], w_all=fwd["w_all"],
        w_two=fwd["w_two"].reshape(4, 16, 16, D),
        **{name: fwd[name] for name in SAVED},
    )
    names = ("qkv", "out", "gateup", "down", "gains")
    state = {
        "w_": (w_qkv, w_out, w_gateup, w_down, gains[None, :]),
        "first_": (first_qkv, first_out, first_gateup, first_down, first_gains[None, :]),
        "second_": (second_qkv, second_out, second_gateup, second_down, second_gains[None, :]),
    }
    new = update_step(
        **bwd, **{kind + name: value for kind, values in state.items() for name, value in zip(names, values)}
    )
    results = [
        new[kind + name] if name != "gains" else new[kind + name][0] for kind in state for name in names
    ]
    return (new["layer_out"], new["input_grad"], *results, new["norm"][0, 0])


def solution(mesh):
    rows, flat = P(("dp", "ctx"), None), P(("dp", "ctx"))
    state = (rows, rows, rows, rows, flat)
    in_specs = (rows, rows, P()) + state * 3
    out_specs = (rows, rows) + state * 3 + (P(),)
    return jax.shard_map(body, mesh=mesh, in_specs=in_specs, out_specs=out_specs, check_vma=False)
```
